128 devices in a mesh: dp: 16 (over x_hi, z, core), fsdp: 8 (over y, x_lo).
Axes of the slice: x: 4 (x_hi: 2, x_lo: 2; x = x_hi * 2 + x_lo), y: 4, z: 4, core: 2. Of those that a mesh axis runs over, the one named last changes fastest.
Arguments:
- tokens: bfloat16 [16, 2048, 1152], P('dp', 'fsdp'), may hold values from -6 to 6
- text_states: bfloat16 [16, 480, 4096], P('dp', 'fsdp'), may hold values from -6 to 6
- seg_lengths: int32 [16, 3], P('dp'), may hold values from 1 to 1793, as said below
- caption_of_segment: int32 [16, 3], P('dp'), may hold values from 0 to 3
- text_lengths: int32 [16, 4], P('dp'), may hold values from 1 to 120, as said below
- ln1_gain: float32 [1152], replicated, may hold values from 0.1 to 1.9
- ln1_bias: float32 [1152], replicated, may hold values from -3 to 3
- w_query: bfloat16 [1152, 1152], P('fsdp'), may hold values from -0.1875 to 0.1875
- w_key: bfloat16 [1152, 1152], P('fsdp'), may hold values from -0.1875 to 0.1875
- w_value: bfloat16 [1152, 1152], P('fsdp'), may hold values from -0.1875 to 0.1875
- w_out: bfloat16 [1152, 1152], P('fsdp'), may hold values from -0.5 to 0.5
- ln2_gain: float32 [1152], replicated, may hold values from 0.1 to 1.9
- ln2_bias: float32 [1152], replicated, may hold values from -3 to 3
- c_query: bfloat16 [1152, 1152], P('fsdp'), may hold values from -0.1875 to 0.1875
- w_text: bfloat16 [4096, 1152], P('fsdp'), may hold values from -0.09375 to 0.09375
- c_key: bfloat16 [1152, 1152], P('fsdp'), may hold values from -0.1875 to 0.1875
- c_value: bfloat16 [1152, 1152], P('fsdp'), may hold values from -0.1875 to 0.1875
- c_out: bfloat16 [1152, 1152], P('fsdp'), may hold values from -0.5 to 0.5
- ln3_gain: float32 [1152], replicated, may hold values from 0.1 to 1.9
- ln3_bias: float32 [1152], replicated, may hold values from -3 to 3
- w_up: bfloat16 [1152, 4608], P('fsdp'), may hold values from -0.1875 to 0.1875
- w_down: bfloat16 [4608, 1152], P('fsdp'), may hold values from -0.09375 to 0.09375
- cotangent: float32 [16, 2048, 1152], P('dp', 'fsdp'), may hold values from -6 to 6
Outputs:
- outputs: float32 [16, 2048, 1152], P('dp', 'fsdp')
- grad_tokens: float32 [16, 2048, 1152], P('dp', 'fsdp')
- grad_text: float32 [16, 480, 4096], P('dp', 'fsdp')
- grad_ln1_gain: float32 [1152], replicated
- grad_ln1_bias: float32 [1152], replicated
- grad_w_query: float32 [1152, 1152], P('fsdp')
- grad_w_key: float32 [1152, 1152], P('fsdp')
- grad_w_value: float32 [1152, 1152], P('fsdp')
- grad_w_out: float32 [1152, 1152], P('fsdp')
- grad_ln2_gain: float32 [1152], replicated
- grad_ln2_bias: float32 [1152], replicated
- grad_c_query: float32 [1152, 1152], P('fsdp')
- grad_w_text: float32 [4096, 1152], P('fsdp')
- grad_c_key: float32 [1152, 1152], P('fsdp')
- grad_c_value: float32 [1152, 1152], P('fsdp')
- grad_c_out: float32 [1152, 1152], P('fsdp')
- grad_ln3_gain: float32 [1152], replicated
- grad_ln3_bias: float32 [1152], replicated
- grad_w_up: float32 [1152, 4608], P('fsdp')
- grad_w_down: float32 [4608, 1152], P('fsdp')
The draws below stay inside these ranges and needn't reach their ends.
Inputs may be any that keep to these rules, and one draw needn't show every extreme that they name: `seg_lengths`: each row's 3 lengths sum to 2048, and one item of every row holds exactly 1793 positions. `text_lengths`: every row has a caption of 120 live tokens.
All inputs are finite; a program needn't handle non-finite values.
Results may differ from the reference program's by a relative error of at most 0.03.
Values may be sent and summed in bfloat16 or wider, within the bound.
No kernel may reach another device: no remote copies, remote signals or barrier semaphores. Data moves between devices by JAX's collectives and lax.ppermute only.
A program may use at most 320 MiB of HBM per device.

```python
import jax
import jax.numpy as jnp
from jax import lax

D = 1152
HEADS = 16
HEAD = 72
FF = 4608
TEXT = 4096
CAP_LEN = 120
TOK_DEV = 256
SEGS = 3
CAPS = 4
ROWS = 16
ROW = 2048
TXT = 480


def draw_seg_lengths(key, part):
    key = jax.random.fold_in(key, 11)
    first_key, second_key = jax.random.split(key)
    short_cap = (TOK_DEV - 1) // (SEGS - 1)
    short_len = jax.random.randint(first_key, (ROWS, SEGS), 1, short_cap + 1)
    chosen = jax.random.randint(second_key, (ROWS, 1), 0, SEGS)
    slots = jnp.arange(SEGS)[None, :]
    long_slot = slots == chosen
    rest_slot = slots == (chosen + 1) % SEGS
    short_len = jnp.where(long_slot | rest_slot, 0, short_len)
    rest_len = TOK_DEV - 1 - jnp.sum(short_len, axis=1, keepdims=True)
    lengths = jnp.where(rest_slot, rest_len, short_len)
    return jnp.where(long_slot, ROW - TOK_DEV + 1, lengths).astype(jnp.int32)


def draw_text_lengths(key, part):
    key = jax.random.fold_in(key, 23)
    first_key, second_key = jax.random.split(key)
    caption_len = jax.random.randint(first_key, (ROWS, CAPS), 1, CAP_LEN + 1)
    full_one = jax.random.randint(second_key, (ROWS, 1), 0, CAPS)
    return jnp.where(jnp.arange(CAPS)[None, :] == full_one, CAP_LEN, caption_len).astype(jnp.int32)


def touch_ends(values, key, smallest, largest):
    spot = [jax.random.randint(jax.random.fold_in(key, axis), (), 0, length) for axis, length in enumerate(values.shape)]
    main_axis = values.shape.index(max(values.shape))
    next_to = spot[:main_axis] + [(spot[main_axis] + 1) % values.shape[main_axis]] + spot[main_axis + 1:]
    return values.at[tuple(spot)].set(smallest).at[tuple(next_to)].set(largest)


def block_scale(key, dims, cuts, low, top_value):
    gain = 1.0
    for position, shards_of in cuts:
        steps = jax.random.uniform(jax.random.fold_in(jax.random.fold_in(key, 6), position), (shards_of,), jnp.float32, low / len(cuts), top_value / len(cuts))
        gain = gain * jnp.repeat(jnp.exp(steps), dims[position] // shards_of).reshape((-1,) + (1,) * (len(dims) - 1 - position))
    return gain


def scatter_about(stream_key, extent, width, reach, shards=(), kind=jnp.bfloat16):
    result = width * jax.random.normal(stream_key, extent, jnp.float32)
    if shards:
        result = result * block_scale(stream_key, extent, shards, -0.22, 0.18)
    return jnp.clip(result, -reach, reach).astype(kind)


def setup_inputs(seed: int = 0) -> dict:
    streams_of = jax.random.split(jax.random.key(seed), 24)
    tokens = scatter_about(streams_of[0], (ROWS, ROW, D), 1.0, 6.0, ((0, 16), (1, 8)))
    text_states = scatter_about(streams_of[1], (ROWS, TXT, TEXT), 1.0, 6.0, ((0, 16), (1, 8)))
    seg_lengths = draw_seg_lengths(jax.random.fold_in(streams_of[23], 71), 0)
    caption_of_segment = touch_ends(jax.random.randint(streams_of[3], (ROWS, SEGS), 0, CAPS), jax.random.fold_in(streams_of[3], 1), 0, CAPS - 1).astype(jnp.int32)
    text_lengths = draw_text_lengths(jax.random.fold_in(streams_of[23], 71), 0)
    ln1_gain = jnp.clip(1.0 + 0.18 * jax.random.normal(streams_of[5], (D,), jnp.float32), 0.1, 1.9)
    ln1_bias = scatter_about(streams_of[6], (D,), 0.5, 3.0, (), jnp.float32)
    w_query = scatter_about(streams_of[7], (D, D), D ** -0.5, 0.1875, ((0, 8),))
    w_key = scatter_about(streams_of[8], (D, D), D ** -0.5, 0.1875, ((0, 8),))
    w_value = scatter_about(streams_of[9], (D, D), D ** -0.5, 0.1875, ((0, 8),))
    w_out = scatter_about(streams_of[10], (D, D), (D // 8) ** -0.5, 0.5, ((0, 8),))
    ln2_gain = jnp.clip(1.0 + 0.18 * jax.random.normal(streams_of[11], (D,), jnp.float32), 0.1, 1.9)
    ln2_bias = scatter_about(streams_of[12], (D,), 0.5, 3.0, (), jnp.float32)
    c_query = scatter_about(streams_of[13], (D, D), D ** -0.5, 0.1875, ((0, 8),))
    w_text = scatter_about(streams_of[14], (TEXT, D), TEXT ** -0.5, 0.09375, ((0, 8),))
    c_key = scatter_about(streams_of[15], (D, D), D ** -0.5, 0.1875, ((0, 8),))
    c_value = scatter_about(streams_of[16], (D, D), D ** -0.5, 0.1875, ((0, 8),))
    c_out = scatter_about(streams_of[17], (D, D), (D // 8) ** -0.5, 0.5, ((0, 8),))
    ln3_gain = jnp.clip(1.0 + 0.18 * jax.random.normal(streams_of[18], (D,), jnp.float32), 0.1, 1.9)
    ln3_bias = scatter_about(streams_of[19], (D,), 0.5, 3.0, (), jnp.float32)
    w_up = scatter_about(streams_of[20], (D, FF), D ** -0.5, 0.1875, ((0, 8),))
    w_down = scatter_about(streams_of[21], (FF, D), FF ** -0.5, 0.09375, ((0, 8),))
    cotangent = scatter_about(streams_of[22], (ROWS, ROW, D), 1.0, 6.0, ((0, 16), (1, 8)), jnp.float32)
    return dict(tokens=tokens, text_states=text_states, seg_lengths=seg_lengths, caption_of_segment=caption_of_segment, text_lengths=text_lengths, ln1_gain=ln1_gain, ln1_bias=ln1_bias, w_query=w_query, w_key=w_key, w_value=w_value, w_out=w_out, ln2_gain=ln2_gain, ln2_bias=ln2_bias, c_query=c_query, w_text=w_text, c_key=c_key, c_value=c_value, c_out=c_out, ln3_gain=ln3_gain, ln3_bias=ln3_bias, w_up=w_up, w_down=w_down, cotangent=cotangent)


@jax.custom_vjp
def low(v):
    return lax.optimization_barrier(v.astype(jnp.bfloat16)).astype(jnp.float32)

@jax.custom_vjp
def low_back(v):
    return v

def low_keep(v):
    return (low(v), None)

def low_pass(kept, grad):
    return (grad,)

def back_keep(v):
    return (v, None)

def back_low(kept, grad):
    return (low(grad),)
low.defvjp(low_keep, low_pass)
low_back.defvjp(back_keep, back_low)
norm_eps = 1e-06
masked_score = -1e+30

def matmul_high(left_side, right_side):
    return jnp.dot(left_side, right_side, precision=lax.Precision.HIGHEST, preferred_element_type=jnp.float32)

def norm_layer(values, norm_gain, norm_shift):
    center = values - lax.optimization_barrier(jnp.mean(values, axis=-1, keepdims=True))
    spread = lax.optimization_barrier(jnp.mean(center * center, axis=-1, keepdims=True))
    return center * lax.rsqrt(spread + norm_eps) * norm_gain + norm_shift

def split_heads(values):
    return values.reshape(values.shape[0], HEADS, HEAD)

def attend(query_rows, key_rows, value_rows, allowed):
    scores = jnp.einsum('qhe,khe->hqk', split_heads(query_rows), split_heads(key_rows), precision=lax.Precision.HIGHEST) * HEAD ** (-0.5)
    scores = jnp.where(allowed[None], low_back(scores), masked_score)
    weights = low(jax.nn.softmax(scores, axis=-1))
    mixed_rows = jnp.einsum('hqk,khe->qhe', weights, split_heads(value_rows), precision=lax.Precision.HIGHEST)
    return mixed_rows.reshape(mixed_rows.shape[0], HEADS * HEAD)

def self_attention(query_rows, key_rows, value_rows, segment):
    block_rows = min(512, ROW)
    blocks_total = ROW // block_rows

    def one_block(block_in):
        return attend(block_in[0], key_rows, value_rows, block_in[1][:, None] == segment[None, :])
    mixed_rows = lax.map(jax.checkpoint(one_block), (query_rows.reshape(blocks_total, block_rows, HEADS * HEAD), segment.reshape(blocks_total, block_rows)))
    return mixed_rows.reshape(ROW, HEADS * HEAD)

def row_forward(params, tokens_row, text_row, segment, text_caption, text_live, query_caption):
    ln1_gain, ln1_bias, w_query, w_key, w_value, w_out, ln2_gain, ln2_bias, c_query, w_text, c_key, c_value, c_out, ln3_gain, ln3_bias, w_up, w_down = params
    normed_one = low(norm_layer(tokens_row, ln1_gain, ln1_bias))
    query_rows = low(low_back(matmul_high(normed_one, w_query)))
    key_rows = low(low_back(matmul_high(normed_one, w_key)))
    value_rows = low(low_back(matmul_high(normed_one, w_value)))
    attended = low(low_back(self_attention(query_rows, key_rows, value_rows, segment)))
    after_self = tokens_row + low_back(matmul_high(attended, w_out))
    normed_two = low(norm_layer(after_self, ln2_gain, ln2_bias))
    cross_query = low(low_back(matmul_high(normed_two, c_query)))
    context = low(low_back(matmul_high(text_row, w_text)))
    cross_key = low(low_back(matmul_high(context, c_key)))
    cross_value = low(low_back(matmul_high(context, c_value)))
    allowed = (query_caption[:, None] == text_caption[None, :]) & text_live[None, :]
    cross_mixed = low(low_back(attend(cross_query, cross_key, cross_value, allowed)))
    after_cross = after_self + low_back(matmul_high(cross_mixed, c_out))
    normed_three = low(norm_layer(after_cross, ln3_gain, ln3_bias))
    hidden_pre = low_back(matmul_high(normed_three, w_up))
    hidden_act = low(jax.nn.gelu(hidden_pre, approximate=False))
    return after_cross + low_back(matmul_high(hidden_act, w_down))

def reference(tokens, text_states, seg_lengths, caption_of_segment, text_lengths, ln1_gain, ln1_bias, w_query, w_key, w_value, w_out, ln2_gain, ln2_bias, c_query, w_text, c_key, c_value, c_out, ln3_gain, ln3_bias, w_up, w_down, cotangent):
    params = tuple((weight_in.astype(jnp.float32) for weight_in in (ln1_gain, ln1_bias, w_query, w_key, w_value, w_out, ln2_gain, ln2_bias, c_query, w_text, c_key, c_value, c_out, ln3_gain, ln3_bias, w_up, w_down)))
    positions = jnp.arange(ROW, dtype=jnp.int32)
    text_pos = jnp.arange(TXT, dtype=jnp.int32)
    text_caption = text_pos // CAP_LEN
    seg_numbers = jnp.arange(SEGS, dtype=jnp.int32)
    cap_numbers = jnp.arange(CAPS, dtype=jnp.int32)

    def one_row(sums, row_in):
        tokens_row, text_row, lengths, captions, text_lens, cot_row = row_in
        segment_ends = jnp.cumsum(lengths).astype(jnp.int32)
        segment = lax.optimization_barrier(jnp.sum((positions[:, None] >= segment_ends[None, :]).astype(jnp.int32), axis=1))
        query_caption = lax.optimization_barrier(jnp.sum(jnp.where(segment[:, None] == seg_numbers[None, :], captions[None, :], 0), axis=1)).astype(jnp.int32)
        live_length = lax.optimization_barrier(jnp.sum(jnp.where(text_caption[:, None] == cap_numbers[None, :], text_lens[None, :], 0), axis=1)).astype(jnp.int32)
        text_live = text_pos % CAP_LEN < live_length

        def forward(params_in, rows_in, text_in):
            return row_forward(params_in, rows_in, text_in, segment, text_caption, text_live, query_caption)
        outputs, pullback = jax.vjp(forward, params, tokens_row.astype(jnp.float32), text_row.astype(jnp.float32))
        grad_params, grad_rows, grad_text = pullback(cot_row.astype(jnp.float32))
        sums = jax.tree.map(jnp.add, sums, grad_params)
        return (sums, (outputs, grad_rows, grad_text))
    zeros_start = jax.tree.map(jnp.zeros_like, params)
    sums, stacked = lax.scan(one_row, zeros_start, (tokens, text_states, seg_lengths, caption_of_segment, text_lengths, cotangent))
    return (stacked[0], stacked[1], stacked[2], sums[0], sums[1], sums[2], sums[3], sums[4], sums[5], sums[6], sums[7], sums[8], sums[9], sums[10], sums[11], sums[12], sums[13], sums[14], sums[15], sums[16])
```

```python
import functools

import jax
import jax.numpy as jnp
from jax import lax
from jax.experimental import pallas as pl
from jax.experimental.pallas import tpu as pltpu
from jax.sharding import Mesh
from jax.sharding import PartitionSpec as P

HEADS = 16
HEAD = 72
D = 1152
FF = 4608
TXT = 480
TOK = 256
ROW = 2048
CAP_LEN = 120
SEGS = 3
CAPS = 4
SHARD = 144
SLOT = 128
HID = 72
HIDP = 80
BLK = 8 * HIDP
WIN = 640
STEP = 512

bf16 = jnp.bfloat16
f32 = jnp.float32
norm_eps = 1e-06
masked_score = -1e30
scale = HEAD ** (-0.5)
log2e = 1.4426950408889634
FS = ("y", "xl")
VMEM = 60 * 1024 * 1024


def dot_nn(a, b):
    return lax.dot_general(a, b, (((1,), (0,)), ((), ())), preferred_element_type=f32)


def dot_nt(a, b):
    return lax.dot_general(a, b, (((1,), (1,)), ((), ())), preferred_element_type=f32)


def dot_tn(a, b):
    return lax.dot_general(a, b, (((0,), (0,)), ((), ())), preferred_element_type=f32)


def params():
    return pltpu.CompilerParams(vmem_limit_bytes=VMEM)


def shift(x, axis, by):
    n = lax.axis_size(axis)
    return lax.ppermute(x, axis, [(i, (i + by) % n) for i in range(n)])


def halves(x):
    h = (x.shape[0] // 2 + 15) // 16 * 16
    return x[:h], x[h:]


def gather3(x):
    x01 = shift(x, "xl", 1)
    x10 = shift(x, "y", -1)
    x30 = shift(x, "y", 1)
    x31 = shift(x01, "y", 1)
    x20 = shift(x10, "y", -1)
    x11 = shift(x10, "xl", 1)
    lo = shift(halves(x11)[0], "y", -1)
    hi = shift(halves(x31)[1], "y", 1)
    return {
        (0, 0): x, (0, 1): x01, (1, 0): x10, (3, 0): x30, (3, 1): x31, (2, 0): x20, (1, 1): x11,
        (2, 1): (lo, hi),
    }


def reduce3(chunk):
    far = chunk(2, 1)
    lo, hi = halves(far)
    lo = shift(lo, "y", 1)
    hi = shift(hi, "y", -1)
    c20 = shift(chunk(2, 0), "y", 1)
    c11 = chunk(1, 1)
    h = lo.shape[0]
    c11 = jnp.concatenate([c11[:h] + lo, c11[h:]], axis=0)
    c31 = chunk(3, 1)
    c31 = jnp.concatenate([c31[:h], c31[h:] + hi], axis=0)
    c11 = shift(c11, "xl", 1)
    c31 = shift(c31, "y", -1)
    c10 = shift(chunk(1, 0) + c20 + c11, "y", 1)
    c01 = shift(chunk(0, 1) + c31, "xl", 1)
    c30 = shift(chunk(3, 0), "y", -1)
    return (
        chunk(0, 0).astype(f32) + c10.astype(f32) + c01.astype(f32) + c30.astype(f32)
    )


def peer(dy, dx):
    return ((lax.axis_index("y") + dy) % 4) * 2 + (lax.axis_index("xl") ^ dx)


def place(pieces, parts):
    flat, whose, at = [], [], []
    for (dy, dx), piece in pieces.items():
        first = 0
        for one in piece if isinstance(piece, tuple) else (piece,):
            flat.append(one)
            whose.append(peer(dy, dx))
            at.append(first)
            first += one.shape[0]
    n_in, n_out = len(flat), len(parts)
    copies = []
    for i, one in enumerate(flat):
        for o, (r0, rows, c0, cols) in enumerate(parts):
            lo, hi = max(r0, at[i]), min(r0 + rows, at[i] + one.shape[0])
            if hi > lo:
                copies.append((i, o, lo - at[i], hi - lo, c0, cols, lo - r0, rows))

    def body(where, *refs):
        ins, outs, sem = refs[:n_in], refs[n_in : n_in + n_out], refs[-1]
        started = []
        for k, (i, o, r, n, c0, cols, off, rows) in enumerate(copies):
            to = pl.multiple_of(where[i] * rows + off, 16)
            one = pltpu.make_async_copy(
                ins[i].at[pl.ds(r, n), pl.ds(c0, cols)], outs[o].at[pl.ds(to, n), :], sem.at[k]
            )
            one.start()
            started.append(one)
        for one in started:
            one.wait()

    any_spec = pl.BlockSpec(memory_space=pl.ANY)
    return pl.pallas_call(
        body,
        in_specs=[pl.BlockSpec(memory_space=pltpu.SMEM)] + [any_spec] * n_in,
        out_specs=[pl.BlockSpec(memory_space=pltpu.VMEM)] * n_out,
        out_shape=[jax.ShapeDtypeStruct((8 * p[1], p[3]), flat[0].dtype) for p in parts],
        scratch_shapes=[pltpu.SemaphoreType.DMA((len(copies),))],
        compiler_params=params(),
    )(jnp.stack(whose).astype(jnp.int32), *flat)


def sort_cores(mine, other):
    def body(core, m, o, w_out, c_key, c_query, c_value, c_out, sem):
        def run(first, second):
            moves = (
                (first, 0, D, w_out, 0), (first, D, D, c_key, 0), (first, 2 * D, WIN, c_out, 0),
                (second, 0, D, c_query, 0), (second, D, D, c_value, 0),
                (second, 2 * D + 128, STEP, c_out, WIN),
            )
            started = []
            for k, (src, c0, cols, dst, to) in enumerate(moves):
                one = pltpu.make_async_copy(
                    src.at[:, pl.ds(c0, cols)], dst.at[:, pl.ds(to, cols)], sem.at[k]
                )
                one.start()
                started.append(one)
            for one in started:
                one.wait()

        @pl.when(core[0] == 0)
        def _():
            run(m, o)

        @pl.when(core[0] != 0)
        def _():
            run(o, m)

    any_spec = pl.BlockSpec(memory_space=pl.ANY)
    return pl.pallas_call(
        body,
        in_specs=[pl.BlockSpec(memory_space=pltpu.SMEM), any_spec, any_spec],
        out_specs=[pl.BlockSpec(memory_space=pltpu.VMEM)] * 5,
        out_shape=[jax.ShapeDtypeStruct((D, D), bf16)] * 5,
        scratch_shapes=[pltpu.SemaphoreType.DMA((6,))],
        compiler_params=params(),
    )(lax.axis_index("c").astype(jnp.int32)[None], mine, other)


def self_forward_body(seg_q, seg_k, q, kv, out, total):
    mixed = []
    for h in range(2):
        base = 3 * SLOT * h
        s = dot_nt(q[:, base : base + SLOT], kv[:, base + SLOT : base + 2 * SLOT])
        s = jnp.where(seg_q[...] == seg_k[...], s, masked_score)
        top = jnp.max(s, axis=1, keepdims=True)
        p = jnp.exp2((s - top) * (scale * log2e))
        mass = jnp.sum(p, axis=1, keepdims=True)
        value = kv[:, base + 2 * SLOT : base + 3 * SLOT]
        mixed.append((dot_nn(p.astype(bf16), value) / mass)[:, :HEAD])
        log_total = top * (scale * log2e) + jnp.log2(mass)
        total[h] = jnp.transpose(jnp.broadcast_to(log_total, (TOK, SLOT)))[0:1, :]
    out[...] = jnp.concatenate(mixed, axis=1).astype(bf16)


def self_forward(seg_q, seg_k, qkv):
    return pl.pallas_call(
        self_forward_body,
        grid=(ROW // TOK,),
        in_specs=[
            pl.BlockSpec((TOK, 1), lambda i: (i, 0)),
            pl.BlockSpec((1, ROW), lambda i: (0, 0)),
            pl.BlockSpec((TOK, 6 * SLOT), lambda i: (i, 0)),
            pl.BlockSpec((ROW, 6 * SLOT), lambda i: (0, 0)),
        ],
        out_specs=[
            pl.BlockSpec((TOK, SHARD), lambda i: (i, 0)),
            pl.BlockSpec((2, 1, TOK), lambda i: (0, 0, i)),
        ],
        out_shape=[
            jax.ShapeDtypeStruct((ROW, SHARD), bf16),
            jax.ShapeDtypeStruct((2, 1, ROW), f32),
        ],
        compiler_params=params(),
    )(seg_q, seg_k, qkv, qkv)


def self_backward_body(head, seg_k, seg_q, total, q, kv, g, grad, key_sum, value_sum, key_t):
    i = pl.program_id(0)

    @pl.when(i == 0)
    def _():
        key_sum[...] = jnp.zeros_like(key_sum)
        value_sum[...] = jnp.zeros_like(value_sum)
        key_t[...] = jnp.transpose(kv[:, SLOT : 2 * SLOT])

    rows = pl.ds(pl.multiple_of(i * TOK, TOK), TOK)
    q_h, k_h, v_h = q[:, :SLOT], kv[:, SLOT : 2 * SLOT], kv[:, 2 * SLOT :]
    g_both = g[...]
    g_h = jnp.concatenate(
        [g_both[:, HEAD * head : HEAD * (head + 1)], jnp.zeros((TOK, SLOT - HEAD), bf16)], axis=1
    )
    p = jnp.exp2(dot_nt(k_h, q_h) * (scale * log2e) - total[0])
    p = jnp.where(seg_k[...] == seg_q[...], p, 0.0)
    dp = dot_nt(v_h, g_h)
    ds = (p * (dp - jnp.sum(p * dp, axis=0, keepdims=True))).astype(bf16)
    value_sum[...] += dot_nn(p.astype(bf16), g_h)
    key_sum[...] += dot_nn(ds, q_h)
    grad[rows, :SLOT] = (jnp.transpose(dot_nn(key_t[...], ds)) * scale).astype(bf16)

    @pl.when(i == pl.num_programs(0) - 1)
    def _():
        grad[:, SLOT : 2 * SLOT] = (key_sum[...] * scale).astype(bf16)
        grad[:, 2 * SLOT :] = value_sum[...].astype(bf16)


def self_backward(head, seg_k, seg_q, total, qkv, g):
    return pl.pallas_call(
        functools.partial(self_backward_body, head),
        grid=(ROW // TOK,),
        in_specs=[
            pl.BlockSpec((ROW, 1), lambda i: (0, 0)),
            pl.BlockSpec((1, TOK), lambda i: (0, i)),
            pl.BlockSpec((1, 1, TOK), lambda i: (head, 0, i)),
            pl.BlockSpec((TOK, 3 * SLOT), lambda i: (i, head)),
            pl.BlockSpec((ROW, 3 * SLOT), lambda i: (0, head)),
            pl.BlockSpec((TOK, SHARD), lambda i: (i, 0)),
        ],
        out_specs=pl.BlockSpec((ROW, 3 * SLOT), lambda i: (0, 0)),
        out_shape=jax.ShapeDtypeStruct((ROW, 3 * SLOT), bf16),
        scratch_shapes=[
            pltpu.VMEM((ROW, SLOT), f32),
            pltpu.VMEM((ROW, SLOT), f32),
            pltpu.VMEM((SLOT, ROW), bf16),
        ],
        compiler_params=params(),
    )(seg_k, seg_q, total, qkv, qkv, g)


def cross_forward_body(cap_q, cap_t, q, k, v, out):
    allowed = cap_q[...] == cap_t[...]
    mixed = []
    for h in range(HEADS):
        a, b = HEAD * h, HEAD * (h + 1)
        s = dot_nt(q[:, a:b], k[:, a:b])
        s = jnp.where(allowed, s, masked_score)
        top = jnp.max(s, axis=1, keepdims=True)
        p = jnp.exp2((s - top) * (scale * log2e))
        mass = jnp.sum(p, axis=1, keepdims=True)
        mixed.append(dot_nn(p.astype(bf16), v[:, a:b]) / mass)
    out[...] = jnp.concatenate(mixed, axis=1).astype(bf16)


def cross_forward(cap_q, cap_t, q, k, v):
    return pl.pallas_call(
        cross_forward_body,
        out_shape=jax.ShapeDtypeStruct((TOK, D), bf16),
        compiler_params=params(),
    )(cap_q, cap_t, q, k, v)


def cross_backward_body(cap_t, cap_q, q, k, v, g, grad_q, grad_k, grad_v):
    allowed = cap_t[...] == cap_q[...]
    dq, dk, dv = [], [], []
    for h in range(HEADS):
        a, b = HEAD * h, HEAD * (h + 1)
        q_h, k_h, v_h, g_h = q[:, a:b], k[:, a:b], v[:, a:b], g[:, a:b]
        s = jnp.where(allowed, dot_nt(k_h, q_h), masked_score)
        top = jnp.max(s, axis=0, keepdims=True)
        p = jnp.exp2((s - top) * (scale * log2e))
        p = p / jnp.sum(p, axis=0, keepdims=True)
        dp = dot_nt(v_h, g_h)
        ds = (p * (dp - jnp.sum(p * dp, axis=0, keepdims=True))).astype(bf16)
        dv.append(dot_nn(p.astype(bf16), g_h))
        dk.append(dot_nn(ds, q_h) * scale)
        dq.append(dot_tn(ds, k_h) * scale)
    grad_q[...] = jnp.concatenate(dq, axis=1).astype(bf16)
    grad_k[...] = jnp.concatenate(dk, axis=1).astype(bf16)
    grad_v[...] = jnp.concatenate(dv, axis=1).astype(bf16)


def cross_backward(cap_t, cap_q, q, k, v, g):
    return pl.pallas_call(
        cross_backward_body,
        out_shape=[
            jax.ShapeDtypeStruct((TOK, D), bf16),
            jax.ShapeDtypeStruct((TXT, D), bf16),
            jax.ShapeDtypeStruct((TXT, D), bf16),
        ],
        compiler_params=params(),
    )(cap_t, cap_q, q, k, v, g)


def mlp_body(*refs):
    x, g = refs[:2]
    ups, downs = refs[2:10], refs[10:18]
    out, act_out, pre_out, grad_x = refs[18:22]
    up_buf, down_buf, sem = refs[22:]

    def fetch(k):
        return (
            pltpu.make_async_copy(ups[k], up_buf.at[k % 2], sem.at[0, k % 2]),
            pltpu.make_async_copy(downs[k], down_buf.at[k % 2], sem.at[1, k % 2]),
        )

    for one in fetch(0):
        one.start()
    out[...] = jnp.zeros_like(out)
    grad_x[...] = jnp.zeros_like(grad_x)

    def step(h, carry):
        for k in range(8):

            @pl.when(h == k)
            def _(k=k):
                if k < 7:
                    for one in fetch(k + 1):
                        one.start()
                for one in fetch(k):
                    one.wait()

        slot = lax.rem(h, 2)
        up, down = up_buf[slot], down_buf[slot]
        cols = pl.ds(pl.multiple_of(h * BLK, BLK), BLK)
        pre = dot_nn(x[...], up)
        grad_act = dot_nt(g[...], down)
        cdf = 0.5 * (1.0 + lax.erf(pre * (0.5**0.5)))
        density = jnp.exp2(pre * pre * (-0.5 * log2e)) * 0.3989422804014327
        act = (pre * cdf).astype(bf16)
        grad_pre = (grad_act * (cdf + pre * density)).astype(bf16)
        act_out[:, cols] = act
        pre_out[:, cols] = grad_pre
        out[...] += dot_nn(act, down)
        grad_x[...] += dot_nt(grad_pre, up)
        return carry

    lax.fori_loop(0, 8, step, 0)


def mlp(x, g, ups, downs):
    vmem = pl.BlockSpec(memory_space=pltpu.VMEM)
    hbm = pl.BlockSpec(memory_space=pl.ANY)
    return pl.pallas_call(
        mlp_body,
        in_specs=[vmem] * 2 + [hbm] * 16,
        out_specs=[vmem] * 4,
        out_shape=[
            jax.ShapeDtypeStruct((TOK, D), f32),
            jax.ShapeDtypeStruct((TOK, 8 * BLK), bf16),
            jax.ShapeDtypeStruct((TOK, 8 * BLK), bf16),
            jax.ShapeDtypeStruct((TOK, D), f32),
        ],
        scratch_shapes=[
            pltpu.VMEM((2, D, BLK), bf16),
            pltpu.VMEM((2, BLK, D), bf16),
            pltpu.SemaphoreType.DMA((2, 2)),
        ],
        compiler_params=params(),
    )(x, g, *ups, *downs)


def sort_hidden_body(x, up, down):
    for f in range(8):
        lanes = slice(HIDP * f, HIDP * f + HID)
        up[:, 8 * HID * f : 8 * HID * (f + 1)] = jnp.concatenate(
            [x[h, :SHARD, lanes] for h in range(8)], axis=1
        ).astype(f32)
    for h in range(8):
        rows = slice(HID * h, HID * (h + 1))
        down[rows, :BLK] = x[h, SHARD : SHARD + HID].astype(f32)
        down[rows, BLK:] = x[h, SHARD + HIDP : SHARD + HIDP + HID, : D - BLK].astype(f32)


def sort_hidden(x):
    return pl.pallas_call(
        sort_hidden_body,
        out_shape=[
            jax.ShapeDtypeStruct((SHARD, FF), f32),
            jax.ShapeDtypeStruct((8 * HID, D), f32),
        ],
        compiler_params=params(),
    )(x)


def norm_layer(values, norm_gain, norm_shift):
    center = values - jnp.mean(values, axis=-1, keepdims=True)
    spread = jnp.mean(center * center, axis=-1, keepdims=True)
    return center * lax.rsqrt(spread + norm_eps) * norm_gain + norm_shift


def row_block(x, index, rows):
    return lax.dynamic_slice_in_dim(x, index * rows, rows, axis=0)


def core_window(x, core):
    return lax.dynamic_slice_in_dim(x, core * STEP, WIN, axis=1)


def both_cores(x):
    return jnp.concatenate([x, shift(x, "c", 1)], axis=0)


def window_grad(left, right):
    core = lax.axis_index("c")
    sent = shift(core_window(right, 1 - core), "c", 1)
    rights = jnp.concatenate([core_window(right, core), sent], axis=0)
    return dot_tn(both_cores(left), rights).astype(bf16)


def scatter_grads(grads, rows):
    packed = grads[0] if len(grads) == 1 else jnp.concatenate(grads, axis=1)
    return reduce3(lambda dy, dx: row_block(packed, peer(dy, dx), rows)).astype(bf16)


def whole_columns(mine, count):
    other = shift(mine, "c", 1)
    first = lax.axis_index("c") == 0
    low = jnp.where(first, mine, other).astype(f32)
    high = jnp.where(first, other, mine).astype(f32)
    return [
        jnp.concatenate(
            [low[:, WIN * k : WIN * (k + 1)], high[:, WIN * k + 128 : WIN * (k + 1)]], axis=1
        )
        for k in range(count)
    ]


def sum_rows_over_dp(x):
    core = lax.axis_index("c")
    rows = x.shape[0] // 2
    mine = row_block(x, core, rows) + shift(row_block(x, 1 - core, rows), "c", 1)
    mine = lax.psum(mine, ("xh", "z"))
    other = shift(mine, "c", 1)
    first = core == 0
    low = jnp.where(first, mine, other)
    high = jnp.where(first, other, mine)
    return jnp.concatenate([low, high], axis=0).astype(f32)


def sum_everywhere(x):
    for axis in ("y", "xl", "z", "xh", "c"):
        n = lax.axis_size(axis)
        x = sum([shift(x, axis, k) for k in range(1, n)], x)
    return x


def after(x, *others):
    return lax.optimization_barrier((x, *others))[0]


def local(
    tokens,
    text_states,
    seg_lengths,
    caption_of_segment,
    text_lengths,
    ln1_gain,
    ln1_bias,
    w_query,
    w_key,
    w_value,
    w_out,
    ln2_gain,
    ln2_bias,
    c_query,
    w_text,
    c_key,
    c_value,
    c_out,
    ln3_gain,
    ln3_bias,
    w_up,
    w_down,
    cotangent,
):
    core = lax.axis_index("c")
    first_core = core == 0
    eighth = lax.axis_index("z") * 2 + core
    first_row = peer(0, 0) * TOK

    ends = jnp.cumsum(seg_lengths[0])
    positions = jnp.arange(ROW, dtype=jnp.int32)
    segment = jnp.sum((positions[:, None] >= ends[None, :]).astype(jnp.int32), axis=1)
    own_segment = lax.dynamic_slice_in_dim(segment, first_row, TOK)
    text_pos = jnp.arange(TXT, dtype=jnp.int32)
    text_caption = text_pos // CAP_LEN
    live = jnp.sum(
        jnp.where(
            text_caption[:, None] == jnp.arange(CAPS, dtype=jnp.int32)[None, :],
            text_lengths[0][None, :],
            0,
        ),
        axis=1,
    )
    query_caption = jnp.sum(
        jnp.where(
            own_segment[:, None] == jnp.arange(SEGS, dtype=jnp.int32)[None, :],
            caption_of_segment[0][None, :],
            0,
        ),
        axis=1,
    )
    text_key = jnp.where(text_pos % CAP_LEN < live, text_caption, -1)

    rows_in = tokens[0].astype(f32)
    normed_one, pull_one = jax.vjp(norm_layer, rows_in, ln1_gain, ln1_bias)
    normed_one = normed_one.astype(bf16)
    (normed_all,) = place(gather3(normed_one), [(0, TOK, 0, D)])

    packed = jnp.concatenate(
        [
            jnp.concatenate([w[:, SHARD * k : SHARD * (k + 1)] for k in range(8)], axis=0)
            for w in (w_query, w_key, w_value)
        ],
        axis=1,
    )
    heads_w = lax.all_to_all(packed, FS, 0, 0, tiled=True)
    blank = jnp.zeros((D, SLOT - HEAD), bf16)
    heads_w = jnp.concatenate(
        [
            part
            for h in range(2)
            for k in range(3)
            for part in (heads_w[:, SHARD * k + HEAD * h : SHARD * k + HEAD * (h + 1)], blank)
        ],
        axis=1,
    )

    text_columns = lax.all_to_all(text_states[0], FS, split_axis=1, concat_axis=0, tiled=True)
    context = lax.psum(dot_nn(text_columns, w_text).astype(bf16), FS)

    pack = jnp.where(
        first_core,
        jnp.concatenate([w_out, c_key, c_out[:, :WIN]], axis=1),
        jnp.concatenate([c_query, c_value, c_out[:, STEP:]], axis=1),
    )
    (square_mine,) = place(gather3(after(pack, normed_all)), [(0, SHARD, 0, 2 * D + WIN)])
    square_other = shift(square_mine, "c", 1)
    full_out, full_ckey, full_cquery, full_cvalue, full_cout = sort_cores(
        square_mine, square_other
    )

    gap = jnp.zeros((SHARD, HIDP - HID), bf16)
    up_own = jnp.concatenate(
        [
            part
            for k in range(8)
            for part in (
                lax.dynamic_slice(w_up, (0, 8 * HID * k + HID * eighth), (SHARD, HID)),
                gap,
            )
        ],
        axis=1,
    )
    down_own = row_block(w_down, eighth, HID)
    down_own = jnp.pad(down_own, ((0, HIDP - HID), (0, 2 * BLK - D)))
    hidden_pack = jnp.concatenate([up_own, down_own[:, :BLK], down_own[:, BLK:]], axis=0)
    up_mine, low_mine, high_mine = place(
        gather3(hidden_pack),
        [(0, SHARD, 0, BLK), (SHARD, HIDP, 0, BLK), (SHARD + HIDP, HIDP, 0, D - BLK)],
    )
    down_mine = jnp.concatenate([low_mine, high_mine], axis=1)
    ups = [up_mine, shift(up_mine, "z", 1), shift(up_mine, "z", -1)]
    downs = [down_mine, shift(down_mine, "z", 1), shift(down_mine, "z", -1)]
    ups.append(shift(ups[1], "z", 1))
    downs.append(shift(downs[2], "z", -1))
    ups += [shift(w, "c", 1) for w in ups]
    downs += [shift(w, "c", 1) for w in downs]

    qkv = dot_nn(normed_all, heads_w).astype(bf16)
    attended_heads, self_total = self_forward(segment[:, None], segment[None, :], qkv)
    attended = lax.all_to_all(attended_heads, FS, split_axis=0, concat_axis=1, tiled=True)
    after_self = rows_in + dot_nn(attended, full_out)

    normed_two, pull_two = jax.vjp(norm_layer, after_self, ln2_gain, ln2_bias)
    normed_two = normed_two.astype(bf16)
    cross_query = dot_nn(normed_two, full_cquery).astype(bf16)
    cross_key = dot_nn(context, full_ckey).astype(bf16)
    cross_value = dot_nn(context, full_cvalue).astype(bf16)
    cross_mixed = cross_forward(
        query_caption[:, None], text_key[None, :], cross_query, cross_key, cross_value
    )
    after_cross = after_self + dot_nn(cross_mixed, full_cout)

    normed_three, pull_three = jax.vjp(norm_layer, after_cross, ln3_gain, ln3_bias)
    normed_three = normed_three.astype(bf16)
    grad_out = cotangent[0]
    grad_mlp = grad_out.astype(bf16)
    mlp_out, hidden_act, grad_pre, grad_three = mlp(normed_three, grad_mlp, ups, downs)
    outputs = after_cross + mlp_out
    grad_cross_in, grad_ln3_gain, grad_ln3_bias = pull_three(grad_three)
    grad_after_cross = grad_out + grad_cross_in

    half = 4 * BLK
    both_three = both_cores(normed_three)
    both_mlp = both_cores(grad_mlp)

    def own_blocks(x):
        mine = jnp.where(first_core, x[:, :half], x[:, half:])
        theirs = jnp.where(first_core, x[:, half:], x[:, :half])
        return mine, theirs

    act_mine, act_theirs = hidden_act[:, :half], hidden_act[:, half:]
    pre_mine, pre_theirs = grad_pre[:, :half], grad_pre[:, half:]
    act_both = jnp.concatenate([act_mine, shift(act_theirs, "c", 1)], axis=0)
    pre_both = jnp.concatenate([pre_mine, shift(pre_theirs, "c", 1)], axis=0)
    grad_up = dot_tn(both_three, pre_both).astype(bf16)
    grad_down = dot_tn(act_both, both_mlp).astype(bf16)

    def up_block(k):
        return grad_up[:, BLK * k : BLK * (k + 1)]

    def down_block(k):
        return grad_down[BLK * k : BLK * (k + 1)]

    far_up = shift(up_block(3), "z", -1)
    far_down = shift(down_block(3), "z", 1)
    up_minus = shift(up_block(1) + far_up, "z", -1)
    down_minus = shift(down_block(1), "z", -1)
    up_plus = shift(up_block(2), "z", 1)
    down_plus = shift(down_block(2) + far_down, "z", 1)
    up_sum = (
        up_block(0).astype(f32) + up_minus.astype(f32) + up_plus.astype(f32)
    ).astype(bf16)
    down_sum = (
        down_block(0).astype(f32) + down_minus.astype(f32) + down_plus.astype(f32)
    ).astype(bf16)

    def hidden_chunk(dy, dx):
        p = peer(dy, dx)
        down = jnp.pad(row_block(down_sum, p, HIDP), ((0, 0), (0, 2 * BLK - D)))
        return jnp.concatenate(
            [row_block(up_sum, p, SHARD), down[:, :BLK], down[:, BLK:]], axis=0
        )

    hidden_grad = reduce3(hidden_chunk).astype(bf16)
    hidden_grad = hidden_grad + shift(hidden_grad, "xh", 1)
    hidden_grad = lax.all_gather(hidden_grad, ("z", "c"), axis=0)
    grad_w_up, grad_w_down = sort_hidden(hidden_grad)

    grad_cross_branch = grad_after_cross.astype(bf16)
    grad_cross_mixed = dot_nt(grad_cross_branch, full_cout).astype(bf16)
    grad_cquery_rows, grad_key_part, grad_value_part = cross_backward(
        text_key[:, None],
        query_caption[None, :],
        cross_query,
        cross_key,
        cross_value,
        grad_cross_mixed,
    )
    context_grad_all = lax.psum(
        (dot_nt(grad_key_part, full_ckey) + dot_nt(grad_value_part, full_cvalue)).astype(bf16), FS
    )
    grad_w_text = dot_tn(text_columns, context_grad_all).astype(bf16)
    text_part = dot_nt(context_grad_all, w_text).astype(bf16)
    grad_text = lax.all_to_all(text_part, FS, split_axis=0, concat_axis=1, tiled=True).astype(f32)
    square_cross = scatter_grads(
        [
            window_grad(cross_mixed, grad_cross_branch),
            window_grad(normed_two, grad_cquery_rows),
            window_grad(context, grad_key_part),
            window_grad(context, grad_value_part),
        ],
        SHARD,
    )
    grad_self_in, grad_ln2_gain, grad_ln2_bias = pull_two(dot_nt(grad_cquery_rows, full_cquery))
    grad_after_self = grad_after_cross + grad_self_in

    grad_self_branch = grad_after_self.astype(bf16)
    square_out = scatter_grads([window_grad(attended, grad_self_branch)], SHARD)
    grad_attended = dot_nt(grad_self_branch, full_out).astype(bf16)
    grad_heads = lax.all_to_all(grad_attended, FS, split_axis=1, concat_axis=0, tiled=True)
    grad_qkv = jnp.concatenate(
        [
            self_backward(h, segment[:, None], segment[None, :], self_total, qkv, grad_heads)
            for h in range(2)
        ],
        axis=1,
    )
    normed_part = dot_nt(grad_qkv, heads_w).astype(bf16)
    grad_heads_w = dot_tn(normed_all, grad_qkv).astype(bf16)
    grad_heads_w = jnp.concatenate(
        [
            grad_heads_w[:, SLOT * (3 * h + k) : SLOT * (3 * h + k) + HEAD]
            for k in range(3)
            for h in range(2)
        ],
        axis=1,
    )
    grad_normed_one = reduce3(lambda dy, dx: row_block(normed_part, peer(dy, dx), TOK))
    grad_rows_in, grad_ln1_gain, grad_ln1_bias = pull_one(grad_normed_one)
    grad_tokens = grad_after_self + grad_rows_in

    square = jnp.concatenate([square_cross, square_out], axis=1)
    square = lax.psum(square, ("xh", "z"))
    grad_c_out, grad_c_query, grad_c_key, grad_c_value, grad_w_out = whole_columns(square, 5)
    grad_w_text = sum_rows_over_dp(grad_w_text)
    grad_qkv_w = lax.all_to_all(grad_heads_w, FS, 0, 0, tiled=True)
    grad_qkv_w = jnp.concatenate(
        [
            grad_qkv_w[SHARD * p : SHARD * (p + 1), SHARD * k : SHARD * (k + 1)]
            for k in range(3)
            for p in range(8)
        ],
        axis=1,
    )
    grad_qkv_w = sum_rows_over_dp(after(grad_qkv_w, square))
    grad_w_query, grad_w_key, grad_w_value = (
        grad_qkv_w[:, :D],
        grad_qkv_w[:, D : 2 * D],
        grad_qkv_w[:, 2 * D :],
    )
    norms = sum_everywhere(
        jnp.stack(
            [
                grad_ln1_gain,
                grad_ln1_bias,
                grad_ln2_gain,
                grad_ln2_bias,
                grad_ln3_gain,
                grad_ln3_bias,
            ]
        )
    )
    return (
        outputs[None],
        grad_tokens[None],
        grad_text[None],
        norms[0],
        norms[1],
        grad_w_query,
        grad_w_key,
        grad_w_value,
        grad_w_out,
        norms[2],
        norms[3],
        grad_c_query,
        grad_w_text,
        grad_c_key,
        grad_c_value,
        grad_c_out,
        norms[4],
        norms[5],
        grad_w_up,
        grad_w_down,
    )


def solution(mesh):
    split = Mesh(mesh.devices.reshape(2, 4, 2, 4, 2), ("xh", "z", "c", "y", "xl"))
    dp = ("xh", "z", "c")
    rows = P(dp, FS, None)
    per_row = P(dp, None)
    weight = P(FS, None)
    rep = P()
    in_specs = (
        rows, rows, per_row, per_row, per_row,
        rep, rep, weight, weight, weight, weight,
        rep, rep, weight, weight, weight, weight, weight,
        rep, rep, weight, weight, rows,
    )
    out_specs = (
        rows, rows, rows,
        rep, rep, weight, weight, weight, weight,
        rep, rep, weight, weight, weight, weight, weight,
        rep, rep, weight, weight,
    )
    return jax.shard_map(
        local, mesh=split, in_specs=in_specs, out_specs=out_specs, check_vma=False
    )
```

```python
import functools

import jax
import jax.numpy as jnp
from jax import lax
from jax.experimental import pallas as pl
from jax.experimental.pallas import tpu as pltpu
from jax.sharding import Mesh
from jax.sharding import PartitionSpec as P

HEADS = 16
HEAD = 72
D = 1152
FF = 4608
CAP_TOK = 60
TXT_OWN = 64
TXT = 8 * TXT_OWN
TOK = 256
ROW = 2048
CAP_LEN = 120
SEGS = 3
CAPS = 4
SHARD = 144
SLOT = 128
HID = 72
HIDP = 80
BLK = 8 * HIDP
PACK = D + 2 * BLK
OWN = SHARD + 2 * HIDP
WIN = 640
STEP = 512

bf16 = jnp.bfloat16
f32 = jnp.float32
norm_eps = 1e-06
masked_score = -1e30
scale = HEAD ** (-0.5)
log2e = 1.4426950408889634
FS = ("y", "xl")
VMEM = 60 * 1024 * 1024


def dot_nn(a, b):
    return lax.dot_general(a, b, (((1,), (0,)), ((), ())), preferred_element_type=f32)


def dot_nt(a, b):
    return lax.dot_general(a, b, (((1,), (1,)), ((), ())), preferred_element_type=f32)


def dot_tn(a, b):
    return lax.dot_general(a, b, (((0,), (0,)), ((), ())), preferred_element_type=f32)


def params():
    return pltpu.CompilerParams(vmem_limit_bytes=VMEM)


def shift(x, axis, by):
    n = lax.axis_size(axis)
    return lax.ppermute(x, axis, [(i, (i + by) % n) for i in range(n)])


def halves(x):
    h = (x.shape[0] // 2 + 15) // 16 * 16
    return x[:h], x[h:]


def after(x, *others):
    return lax.optimization_barrier((x, *others))[0] if others else x


def gather3(x, second=(), third=()):
    x01 = shift(x, "xl", 1)
    x10 = shift(x, "y", -1)
    x30 = shift(x, "y", 1)
    near = after(x10, *second)
    x31 = shift(after(x01, *second), "y", 1)
    x20 = shift(near, "y", -1)
    x11 = shift(near, "xl", 1)
    lo = shift(after(halves(x11)[0], *third), "y", -1)
    hi = shift(after(halves(x31)[1], *third), "y", 1)
    return {
        (0, 0): x, (0, 1): x01, (1, 0): x10, (3, 0): x30, (3, 1): x31, (2, 0): x20, (1, 1): x11,
        (2, 1): (lo, hi),
    }


def reduce3(chunk, second=(), third=()):
    lo, hi = halves(chunk(2, 1))
    lo = after(shift(lo, "y", 1), *second)
    hi = shift(hi, "y", -1)
    h = lo.shape[0]
    c20 = shift(after(chunk(2, 0), *second), "y", 1)
    c11 = chunk(1, 1)
    c11 = jnp.concatenate([c11[:h] + lo, c11[h:]], axis=0)
    c31 = chunk(3, 1)
    c31 = jnp.concatenate([c31[:h], c31[h:] + hi], axis=0)
    c11 = after(shift(c11, "xl", 1), *third)
    c31 = shift(c31, "y", -1)
    c10 = shift(chunk(1, 0) + c20 + c11, "y", 1)
    c01 = shift(chunk(0, 1) + c31, "xl", 1)
    c30 = shift(after(chunk(3, 0), *third), "y", -1)
    return (
        chunk(0, 0).astype(f32) + c10.astype(f32) + c01.astype(f32) + c30.astype(f32)
    )


def peer(dy, dx):
    return ((lax.axis_index("y") + dy) % 4) * 2 + (lax.axis_index("xl") ^ dx)


def place(pieces, parts):
    flat, whose, at = [], [], []
    for (dy, dx), piece in pieces.items():
        first = 0
        for one in piece if isinstance(piece, tuple) else (piece,):
            flat.append(one)
            whose.append(peer(dy, dx))
            at.append(first)
            first += one.shape[0]
    n_in, cols = len(flat), flat[0].shape[1]
    copies = []
    for i, one in enumerate(flat):
        for r0, rows, base in parts:
            lo, hi = max(r0, at[i]), min(r0 + rows, at[i] + one.shape[0])
            if hi > lo:
                copies.append((i, lo - at[i], hi - lo, rows, base + lo - r0))

    def body(where, *refs):
        ins, out, sem = refs[:n_in], refs[n_in], refs[-1]
        started = []
        for k, (i, r, n, rows, base) in enumerate(copies):
            to = pl.multiple_of(where[i] * rows + base, 16)
            one = pltpu.make_async_copy(ins[i].at[pl.ds(r, n)], out.at[pl.ds(to, n)], sem.at[k])
            one.start()
            started.append(one)
        for one in started:
            one.wait()

    any_spec = pl.BlockSpec(memory_space=pl.ANY)
    total = 8 * sum(rows for _, rows, _ in parts)
    return pl.pallas_call(
        body,
        in_specs=[pl.BlockSpec(memory_space=pltpu.SMEM)] + [any_spec] * n_in,
        out_specs=pl.BlockSpec(memory_space=pltpu.VMEM),
        out_shape=jax.ShapeDtypeStruct((total, cols), flat[0].dtype),
        scratch_shapes=[pltpu.SemaphoreType.DMA((len(copies),))],
        compiler_params=params(),
    )(jnp.stack(whose).astype(jnp.int32), *flat)


def sort_cores(mine, other, moves, count):
    def body(core, m, o, *refs):
        outs, sem = refs[:count], refs[-1]

        def run(sides):
            started = []
            for k, (side, c0, cols, dst, to) in enumerate(moves):
                one = pltpu.make_async_copy(
                    sides[side].at[:, pl.ds(c0, cols)], outs[dst].at[:, pl.ds(to, cols)], sem.at[k]
                )
                one.start()
                started.append(one)
            for one in started:
                one.wait()

        @pl.when(core[0] == 0)
        def _():
            run((m, o))

        @pl.when(core[0] != 0)
        def _():
            run((o, m))

    any_spec = pl.BlockSpec(memory_space=pl.ANY)
    return pl.pallas_call(
        body,
        in_specs=[pl.BlockSpec(memory_space=pltpu.SMEM), any_spec, any_spec],
        out_specs=[pl.BlockSpec(memory_space=pltpu.VMEM)] * count,
        out_shape=[jax.ShapeDtypeStruct((D, D), bf16)] * count,
        scratch_shapes=[pltpu.SemaphoreType.DMA((len(moves),))],
        compiler_params=params(),
    )(lax.axis_index("c").astype(jnp.int32)[None], mine, other)


def self_forward_body(seg_q, seg_k, q, kv, out, total):
    s = dot_nt(q[:, :SLOT], kv[:, SLOT : 2 * SLOT])
    s = jnp.where(seg_q[...] == seg_k[...], s, masked_score)
    top = jnp.max(s, axis=1, keepdims=True)
    p = jnp.exp2((s - top) * (scale * log2e))
    mass = jnp.sum(p, axis=1, keepdims=True)
    out[...] = (dot_nn(p.astype(bf16), kv[:, 2 * SLOT :]) / mass)[:, :HEAD].astype(bf16)
    log_total = top * (scale * log2e) + jnp.log2(mass)
    total[...] = jnp.transpose(jnp.broadcast_to(log_total, (TOK, SLOT)))[0:1, :]


def self_forward(head, seg_q, seg_k, qkv):
    return pl.pallas_call(
        self_forward_body,
        grid=(ROW // TOK,),
        in_specs=[
            pl.BlockSpec((TOK, 1), lambda i: (i, 0)),
            pl.BlockSpec((1, ROW), lambda i: (0, 0)),
            pl.BlockSpec((TOK, 3 * SLOT), lambda i: (i, head)),
            pl.BlockSpec((ROW, 3 * SLOT), lambda i: (0, head)),
        ],
        out_specs=[
            pl.BlockSpec((TOK, HEAD), lambda i: (i, 0)),
            pl.BlockSpec((1, TOK), lambda i: (0, i)),
        ],
        out_shape=[
            jax.ShapeDtypeStruct((ROW, HEAD), bf16),
            jax.ShapeDtypeStruct((1, ROW), f32),
        ],
        compiler_params=params(),
    )(seg_q, seg_k, qkv, qkv)


def self_backward_body(head, seg_k, seg_q, total, q, kv, g, grad, key_sum, value_sum, key_t):
    i = pl.program_id(0)

    @pl.when(i == 0)
    def _():
        key_sum[...] = jnp.zeros_like(key_sum)
        value_sum[...] = jnp.zeros_like(value_sum)
        key_t[...] = jnp.transpose(kv[:, SLOT : 2 * SLOT])

    rows = pl.ds(pl.multiple_of(i * TOK, TOK), TOK)
    q_h, k_h, v_h = q[:, :SLOT], kv[:, SLOT : 2 * SLOT], kv[:, 2 * SLOT :]
    g_both = g[...]
    g_h = jnp.concatenate(
        [g_both[:, HEAD * head : HEAD * (head + 1)], jnp.zeros((TOK, SLOT - HEAD), bf16)], axis=1
    )
    p = jnp.exp2(dot_nt(k_h, q_h) * (scale * log2e) - total[...])
    p = jnp.where(seg_k[...] == seg_q[...], p, 0.0)
    dp = dot_nt(v_h, g_h)
    ds = (p * (dp - jnp.sum(p * dp, axis=0, keepdims=True))).astype(bf16)
    value_sum[...] += dot_nn(p.astype(bf16), g_h)
    key_sum[...] += dot_nn(ds, q_h)
    grad[rows, :SLOT] = (jnp.transpose(dot_nn(key_t[...], ds)) * scale).astype(bf16)

    @pl.when(i == pl.num_programs(0) - 1)
    def _():
        grad[:, SLOT : 2 * SLOT] = (key_sum[...] * scale).astype(bf16)
        grad[:, 2 * SLOT :] = value_sum[...].astype(bf16)


def self_backward(head, seg_k, seg_q, total, qkv, g):
    return pl.pallas_call(
        functools.partial(self_backward_body, head),
        grid=(ROW // TOK,),
        in_specs=[
            pl.BlockSpec((ROW, 1), lambda i: (0, 0)),
            pl.BlockSpec((1, TOK), lambda i: (0, i)),
            pl.BlockSpec((1, TOK), lambda i: (0, i)),
            pl.BlockSpec((TOK, 3 * SLOT), lambda i: (i, head)),
            pl.BlockSpec((ROW, 3 * SLOT), lambda i: (0, head)),
            pl.BlockSpec((TOK, SHARD), lambda i: (i, 0)),
        ],
        out_specs=pl.BlockSpec((ROW, 3 * SLOT), lambda i: (0, 0)),
        out_shape=jax.ShapeDtypeStruct((ROW, 3 * SLOT), bf16),
        scratch_shapes=[
            pltpu.VMEM((ROW, SLOT), f32),
            pltpu.VMEM((ROW, SLOT), f32),
            pltpu.VMEM((SLOT, ROW), bf16),
        ],
        compiler_params=params(),
    )(seg_k, seg_q, total, qkv, qkv, g)


def cross_forward_body(cap_q, cap_t, q, k, v, out):
    allowed = cap_q[...] == cap_t[...]
    mixed = []
    for h in range(HEADS):
        a, b = HEAD * h, HEAD * (h + 1)
        s = dot_nt(q[:, a:b], k[:, a:b])
        s = jnp.where(allowed, s, masked_score)
        top = jnp.max(s, axis=1, keepdims=True)
        p = jnp.exp2((s - top) * (scale * log2e))
        mass = jnp.sum(p, axis=1, keepdims=True)
        mixed.append(dot_nn(p.astype(bf16), v[:, a:b]) / mass)
    out[...] = jnp.concatenate(mixed, axis=1).astype(bf16)


def cross_forward(cap_q, cap_t, q, k, v):
    return pl.pallas_call(
        cross_forward_body,
        out_shape=jax.ShapeDtypeStruct((TOK, D), bf16),
        compiler_params=params(),
    )(cap_q, cap_t, q, k, v)


def cross_backward_body(cap_t, cap_q, q, k, v, g, grad_q, grad_k, grad_v):
    allowed = cap_t[...] == cap_q[...]
    dq, dk, dv = [], [], []
    for h in range(HEADS):
        a, b = HEAD * h, HEAD * (h + 1)
        q_h, k_h, v_h, g_h = q[:, a:b], k[:, a:b], v[:, a:b], g[:, a:b]
        s = jnp.where(allowed, dot_nt(k_h, q_h), masked_score)
        top = jnp.max(s, axis=0, keepdims=True)
        p = jnp.exp2((s - top) * (scale * log2e))
        p = p / jnp.sum(p, axis=0, keepdims=True)
        dp = dot_nt(v_h, g_h)
        ds = (p * (dp - jnp.sum(p * dp, axis=0, keepdims=True))).astype(bf16)
        dv.append(dot_nn(p.astype(bf16), g_h))
        dk.append(dot_nn(ds, q_h) * scale)
        dq.append(dot_tn(ds, k_h) * scale)
    grad_q[...] = jnp.concatenate(dq, axis=1).astype(bf16)
    grad_k[...] = jnp.concatenate(dk, axis=1).astype(bf16)
    grad_v[...] = jnp.concatenate(dv, axis=1).astype(bf16)


def cross_backward(cap_t, cap_q, q, k, v, g):
    return pl.pallas_call(
        cross_backward_body,
        out_shape=[
            jax.ShapeDtypeStruct((TOK, D), bf16),
            jax.ShapeDtypeStruct((TXT, D), bf16),
            jax.ShapeDtypeStruct((TXT, D), bf16),
        ],
        compiler_params=params(),
    )(cap_t, cap_q, q, k, v, g)


def mlp_body(count, first, *refs):
    x, g = refs[:2]
    blocks = refs[2 : 2 + count]
    refs = refs[2 + count :]
    if not first:
        out_before, grad_before = refs[:2]
        refs = refs[2:]
    out, act_out, pre_out, grad_x, up_buf, down_buf, sem = refs

    def fetch(k):
        slot = k % 2
        return (
            pltpu.make_async_copy(blocks[k].at[:D], up_buf.at[slot], sem.at[0, slot]),
            pltpu.make_async_copy(
                blocks[k].at[D : D + BLK], down_buf.at[slot, :, :BLK], sem.at[1, slot]
            ),
            pltpu.make_async_copy(
                blocks[k].at[D + BLK :, : D - BLK], down_buf.at[slot, :, BLK:], sem.at[2, slot]
            ),
        )

    for one in fetch(0):
        one.start()
    out[...] = jnp.zeros_like(out) if first else out_before[...]
    grad_x[...] = jnp.zeros_like(grad_x) if first else grad_before[...]

    def step(h, carry):
        for k in range(count):

            @pl.when(h == k)
            def _(k=k):
                if k < count - 1:
                    for one in fetch(k + 1):
                        one.start()
                for one in fetch(k):
                    one.wait()

        slot = lax.rem(h, 2)
        up, down = up_buf[slot], down_buf[slot]
        cols = pl.ds(pl.multiple_of(h * BLK, BLK), BLK)
        pre = dot_nn(x[...], up)
        grad_act = dot_nt(g[...], down)
        cdf = 0.5 * (1.0 + lax.erf(pre * (0.5**0.5)))
        density = jnp.exp2(pre * pre * (-0.5 * log2e)) * 0.3989422804014327
        act = (pre * cdf).astype(bf16)
        grad_pre = (grad_act * (cdf + pre * density)).astype(bf16)
        act_out[:, cols] = act
        pre_out[:, cols] = grad_pre
        out[...] += dot_nn(act, down)
        grad_x[...] += dot_nt(grad_pre, up)
        return carry

    lax.fori_loop(0, count, step, 0)


def mlp(x, g, blocks, before=()):
    vmem = pl.BlockSpec(memory_space=pltpu.VMEM)
    hbm = pl.BlockSpec(memory_space=pl.ANY)
    count = len(blocks)
    return pl.pallas_call(
        functools.partial(mlp_body, count, not before),
        in_specs=[vmem] * 2 + [hbm] * count + [vmem] * len(before),
        out_specs=[vmem] * 4,
        out_shape=[
            jax.ShapeDtypeStruct((TOK, D), f32),
            jax.ShapeDtypeStruct((TOK, count * BLK), bf16),
            jax.ShapeDtypeStruct((TOK, count * BLK), bf16),
            jax.ShapeDtypeStruct((TOK, D), f32),
        ],
        scratch_shapes=[
            pltpu.VMEM((2, D, BLK), bf16),
            pltpu.VMEM((2, BLK, D), bf16),
            pltpu.SemaphoreType.DMA((3, 2)),
        ],
        compiler_params=params(),
    )(x, g, *blocks, *before)


def mlp_grads_body(x0, x1, g0, g1, pre0, pre1, act0, act1, out):
    up = dot_tn(x0[...], pre0[...]) + dot_tn(x1[...], pre1[...])
    down = dot_tn(act0[...], g0[...]) + dot_tn(act1[...], g1[...])
    out[0, :D] = up.astype(bf16)
    out[0, D : D + BLK] = down[:, :BLK].astype(bf16)
    out[0, D + BLK :, : D - BLK] = down[:, BLK:].astype(bf16)
    out[0, D + BLK :, D - BLK :] = jnp.zeros((BLK, 2 * BLK - D), bf16)


def mlp_grads(x0, x1, g0, g1, pre0, pre1, act0, act1):
    whole = pl.BlockSpec((TOK, D), lambda k: (0, 0))
    block = pl.BlockSpec((TOK, BLK), lambda k: (0, k))
    return pl.pallas_call(
        mlp_grads_body,
        grid=(4,),
        in_specs=[whole] * 4 + [block] * 4,
        out_specs=pl.BlockSpec((1, PACK, BLK), lambda k: (k, 0, 0)),
        out_shape=jax.ShapeDtypeStruct((4, PACK, BLK), bf16),
        compiler_params=params(),
    )(x0, x1, g0, g1, pre0, pre1, act0, act1)


def sort_hidden_body(x, up, down):
    for f in range(8):
        lanes = slice(HIDP * f, HIDP * f + HID)
        up[:, 8 * HID * f : 8 * HID * (f + 1)] = jnp.concatenate(
            [x[h, :SHARD, lanes] for h in range(8)], axis=1
        ).astype(f32)
    for h in range(8):
        rows = slice(HID * h, HID * (h + 1))
        down[rows, :BLK] = x[h, SHARD : SHARD + HID].astype(f32)
        down[rows, BLK:] = x[h, SHARD + HIDP : SHARD + HIDP + HID, : D - BLK].astype(f32)


def sort_hidden(x):
    return pl.pallas_call(
        sort_hidden_body,
        out_shape=[
            jax.ShapeDtypeStruct((SHARD, FF), f32),
            jax.ShapeDtypeStruct((8 * HID, D), f32),
        ],
        compiler_params=params(),
    )(x)


def norm_layer(values, norm_gain, norm_shift):
    center = values - jnp.mean(values, axis=-1, keepdims=True)
    spread = jnp.mean(center * center, axis=-1, keepdims=True)
    return center * lax.rsqrt(spread + norm_eps) * norm_gain + norm_shift


def row_block(x, index, rows):
    return lax.dynamic_slice_in_dim(x, index * rows, rows, axis=0)


def core_window(x, core):
    return lax.dynamic_slice_in_dim(x, core * STEP, WIN, axis=1)


def both_cores(x):
    return jnp.concatenate([x, shift(x, "c", 1)], axis=0)


def window_grad(left, right):
    core = lax.axis_index("c")
    sent = shift(core_window(right, 1 - core), "c", 1)
    rights = jnp.concatenate([core_window(right, core), sent], axis=0)
    return dot_tn(both_cores(left), rights).astype(bf16)


def sum_over_dp(x):
    part = lax.psum_scatter(x, "z", scatter_dimension=0, tiled=True)
    part = part + shift(part, "xh", 1)
    return lax.all_gather(part, "z", axis=0, tiled=True)


def whole_columns(mine, count):
    other = shift(mine, "c", 1)
    first = lax.axis_index("c") == 0
    low = jnp.where(first, mine, other).astype(f32)
    high = jnp.where(first, other, mine).astype(f32)
    return [
        jnp.concatenate(
            [low[SHARD * k : SHARD * (k + 1)], high[SHARD * k : SHARD * (k + 1), 128:]], axis=1
        )
        for k in range(count)
    ]


def sum_rows_over_dp(x):
    core = lax.axis_index("c")
    rows = x.shape[0] // 2
    mine = row_block(x, core, rows) + shift(row_block(x, 1 - core, rows), "c", 1)
    mine = sum_over_dp(mine)
    other = shift(mine, "c", 1)
    first = core == 0
    low = jnp.where(first, mine, other)
    high = jnp.where(first, other, mine)
    return jnp.concatenate([low, high], axis=0).astype(f32)


def sum_everywhere(x):
    for axis in ("y", "xl", "z", "xh", "c"):
        n = lax.axis_size(axis)
        x = sum([shift(x, axis, k) for k in range(1, n)], x)
    return x


def local(
    tokens,
    text_states,
    seg_lengths,
    caption_of_segment,
    text_lengths,
    ln1_gain,
    ln1_bias,
    w_query,
    w_key,
    w_value,
    w_out,
    ln2_gain,
    ln2_bias,
    c_query,
    w_text,
    c_key,
    c_value,
    c_out,
    ln3_gain,
    ln3_bias,
    w_up,
    w_down,
    cotangent,
):
    core = lax.axis_index("c")
    first_core = core == 0
    eighth = lax.axis_index("z") * 2 + core
    first_row = peer(0, 0) * TOK

    ends = jnp.cumsum(seg_lengths[0])
    positions = jnp.arange(ROW, dtype=jnp.int32)
    segment = jnp.sum((positions[:, None] >= ends[None, :]).astype(jnp.int32), axis=1)
    own_segment = lax.dynamic_slice_in_dim(segment, first_row, TOK)
    text_row = jnp.arange(TXT, dtype=jnp.int32)
    text_pos = text_row // TXT_OWN * CAP_TOK + text_row % TXT_OWN
    text_caption = text_pos // CAP_LEN
    live = jnp.sum(
        jnp.where(
            text_caption[:, None] == jnp.arange(CAPS, dtype=jnp.int32)[None, :],
            text_lengths[0][None, :],
            0,
        ),
        axis=1,
    )
    query_caption = jnp.sum(
        jnp.where(
            own_segment[:, None] == jnp.arange(SEGS, dtype=jnp.int32)[None, :],
            caption_of_segment[0][None, :],
            0,
        ),
        axis=1,
    )
    text_live = (text_row % TXT_OWN < CAP_TOK) & (text_pos % CAP_LEN < live)
    text_key = jnp.where(text_live, text_caption, -1)

    rows_in = tokens[0].astype(f32)
    normed_one, pull_one = jax.vjp(norm_layer, rows_in, ln1_gain, ln1_bias)
    normed_one = normed_one.astype(bf16)
    normed_all = place(gather3(normed_one), [(0, TOK, 0)])

    gap = jnp.zeros((SHARD, HIDP - HID), bf16)
    up_shard = after(w_up, normed_one)
    up_own = jnp.concatenate(
        [
            part
            for k in range(8)
            for part in (
                lax.dynamic_slice(up_shard, (0, 8 * HID * k + HID * eighth), (SHARD, HID)),
                gap,
            )
        ],
        axis=1,
    )
    down_own = row_block(w_down, eighth, HID)
    down_own = jnp.pad(down_own, ((0, HIDP - HID), (0, 2 * BLK - D)))
    hidden_own = jnp.concatenate([up_own, down_own[:, :BLK], down_own[:, BLK:]], axis=0)
    hidden = place(
        gather3(hidden_own),
        [(0, SHARD, 0), (SHARD, HIDP, D), (SHARD + HIDP, HIDP, D + BLK)],
    )

    text_own = jnp.pad(after(text_states[0], normed_one), ((0, TXT_OWN - CAP_TOK), (0, 0)))
    text_columns = lax.all_to_all(text_own, FS, split_axis=1, concat_axis=0, tiled=True)
    context_own = lax.psum_scatter(
        dot_nn(text_columns, w_text).astype(bf16), FS, scatter_dimension=0, tiled=True
    )
    context = lax.all_gather(context_own, FS, axis=0, tiled=True)

    packed = jnp.concatenate(
        [
            jnp.concatenate([w[:, SHARD * k : SHARD * (k + 1)] for k in range(8)], axis=0)
            for w in (w_query, w_key, w_value)
        ],
        axis=1,
    )
    heads_w = lax.all_to_all(after(packed, text_columns), FS, 0, 0, tiled=True)
    blank = jnp.zeros((D, SLOT - HEAD), bf16)
    heads_w = jnp.concatenate(
        [
            part
            for h in range(2)
            for k in range(3)
            for part in (heads_w[:, SHARD * k + HEAD * h : SHARD * k + HEAD * (h + 1)], blank)
        ],
        axis=1,
    )

    seg_col, seg_row = segment[:, None], segment[None, :]
    qkv = dot_nn(normed_all, heads_w).astype(bf16)
    head0, total0 = self_forward(0, seg_col, seg_row, qkv)
    head1, total1 = self_forward(1, seg_col, seg_row, after(qkv, head0))
    attended = lax.all_to_all(
        jnp.concatenate([head0, head1], axis=1), FS, split_axis=0, concat_axis=1, tiled=True
    )

    pack = after(jnp.where(first_core, w_out, c_query), normed_all)
    square_mine = place(gather3(pack, (qkv,), (head0,)), [(0, SHARD, 0)])
    full_out, full_cquery = sort_cores(
        square_mine, shift(square_mine, "c", 1), [(0, 0, D, 0, 0), (1, 0, D, 1, 0)], 2
    )
    pack = jnp.where(
        first_core,
        jnp.concatenate([c_key, c_out[:, :WIN]], axis=1),
        jnp.concatenate([c_value, c_out[:, STEP:]], axis=1),
    )
    square_mine = place(
        gather3(after(pack, qkv), (head0,), (head1,)), [(0, SHARD, 0)]
    )
    full_ckey, full_cvalue, full_cout = sort_cores(
        square_mine,
        shift(square_mine, "c", 1),
        [(0, 0, D, 0, 0), (1, 0, D, 1, 0), (0, D, WIN, 2, 0), (1, D + 128, STEP, 2, WIN)],
        3,
    )

    after_self = rows_in + dot_nn(attended, full_out)

    normed_two, pull_two = jax.vjp(norm_layer, after_self, ln2_gain, ln2_bias)
    normed_two = normed_two.astype(bf16)
    cross_query = dot_nn(normed_two, full_cquery).astype(bf16)
    context = after(context, after_self)
    cross_key = dot_nn(context, full_ckey).astype(bf16)
    cross_value = dot_nn(context, full_cvalue).astype(bf16)
    cross_mixed = cross_forward(
        query_caption[:, None], text_key[None, :], cross_query, cross_key, cross_value
    )
    after_cross = after_self + dot_nn(cross_mixed, full_cout)

    minus, plus = shift(hidden, "z", 1), shift(hidden, "z", -1)
    half = PACK // 2
    far = jnp.concatenate(
        [
            shift(after(minus[:half], cross_query), "z", 1),
            shift(after(plus[half:], cross_query), "z", -1),
        ],
        axis=0,
    )
    near = [hidden, minus, plus]
    near += [shift(w, "c", 1) for w in near]
    far = [far, shift(far, "c", 1)]

    normed_three, pull_three = jax.vjp(norm_layer, after_cross, ln3_gain, ln3_bias)
    normed_three = normed_three.astype(bf16)
    grad_out = cotangent[0]
    grad_mlp = grad_out.astype(bf16)
    part_out, act_near, pre_near, part_grad = mlp(normed_three, grad_mlp, near)
    mlp_out, act_far, pre_far, grad_three = mlp(
        normed_three, grad_mlp, far, (part_out, part_grad)
    )
    outputs = after_cross + mlp_out
    grad_cross_in, grad_ln3_gain, grad_ln3_bias = pull_three(grad_three)
    grad_after_cross = grad_out + grad_cross_in
    grad_cross_branch = grad_after_cross.astype(bf16)
    grad_cross_mixed = dot_nt(grad_cross_branch, full_cout).astype(bf16)

    def mine(near, far):
        return jnp.concatenate([near[:, : 3 * BLK], far[:, :BLK]], axis=1)

    def theirs(near, far):
        return shift(jnp.concatenate([near[:, 3 * BLK :], far[:, BLK:]], axis=1), "c", 1)

    hidden_grads = mlp_grads(
        normed_three,
        shift(normed_three, "c", 1),
        grad_mlp,
        shift(grad_mlp, "c", 1),
        mine(pre_near, pre_far),
        theirs(pre_near, pre_far),
        mine(act_near, act_far),
        theirs(act_near, act_far),
    )

    grad_cquery_rows, grad_key_part, grad_value_part = cross_backward(
        text_key[:, None],
        query_caption[None, :],
        cross_query,
        cross_key,
        cross_value,
        after(grad_cross_mixed, hidden_grads),
    )
    grad_self_in, grad_ln2_gain, grad_ln2_bias = pull_two(dot_nt(grad_cquery_rows, full_cquery))
    grad_after_self = grad_after_cross + grad_self_in
    grad_self_branch = grad_after_self.astype(bf16)
    grad_attended = dot_nt(grad_self_branch, full_out).astype(bf16)
    grad_heads = lax.all_to_all(grad_attended, FS, split_axis=1, concat_axis=0, tiled=True)

    grad_head0 = self_backward(0, seg_col, seg_row, total0, qkv, grad_heads)
    grad_head1 = self_backward(1, seg_col, seg_row, total1, qkv, after(grad_heads, grad_head0))
    grad_qkv = jnp.concatenate([grad_head0, grad_head1], axis=1)
    normed_part = dot_nt(grad_qkv, heads_w).astype(bf16)
    grad_heads_w = dot_tn(normed_all, grad_qkv).astype(bf16)
    grad_heads_w = jnp.concatenate(
        [
            grad_heads_w[:, SLOT * (3 * h + k) : SLOT * (3 * h + k) + HEAD]
            for k in range(3)
            for h in range(2)
        ],
        axis=1,
    )

    far_minus = shift(hidden_grads[3, :half], "z", -1)
    far_plus = shift(hidden_grads[3, half:], "z", 1)
    far_minus, far_plus, _ = lax.optimization_barrier((far_minus, far_plus, grad_heads))
    minus = jnp.concatenate(
        [hidden_grads[1, :half] + far_minus, hidden_grads[1, half:]], axis=0
    )
    plus = jnp.concatenate([hidden_grads[2, :half], hidden_grads[2, half:] + far_plus], axis=0)
    minus, plus = shift(minus, "z", -1), shift(plus, "z", 1)
    minus, plus, _ = lax.optimization_barrier((minus, plus, grad_head1))
    hidden_sum = (
        hidden_grads[0].astype(f32) + minus.astype(f32) + plus.astype(f32)
    ).astype(bf16)

    def hidden_chunk(dy, dx):
        p = peer(dy, dx)
        return jnp.concatenate(
            [
                row_block(hidden_sum[:D], p, SHARD),
                row_block(hidden_sum[D : D + BLK], p, HIDP),
                row_block(hidden_sum[D + BLK :], p, HIDP),
            ],
            axis=0,
        )

    hidden_grad = reduce3(hidden_chunk).astype(bf16)
    hidden_grad = hidden_grad + shift(hidden_grad, "xh", 1)
    hidden_grad = lax.all_gather(hidden_grad, ("z", "c"), axis=0)
    grad_w_up, grad_w_down = sort_hidden(hidden_grad)

    square = jnp.concatenate(
        [
            window_grad(cross_mixed, grad_cross_branch),
            window_grad(normed_two, grad_cquery_rows),
            window_grad(attended, grad_self_branch),
            window_grad(context, grad_key_part),
            window_grad(context, grad_value_part),
        ],
        axis=1,
    )
    square = after(square, grad_heads)
    square = reduce3(
        lambda dy, dx: row_block(square, peer(dy, dx), SHARD), (grad_head0,), (grad_head1,)
    ).astype(bf16)
    square = jnp.concatenate(
        [square[:, WIN * k : WIN * (k + 1)] for k in range(5)]
        + [jnp.zeros((768 - 5 * SHARD, WIN), bf16)],
        axis=0,
    )
    square = sum_over_dp(square)
    grad_c_out, grad_c_query, grad_w_out, grad_c_key, grad_c_value = whole_columns(square, 5)

    context_part = dot_nt(grad_key_part, full_ckey) + dot_nt(grad_value_part, full_cvalue)
    context_grad = lax.psum_scatter(
        context_part.astype(bf16), FS, scatter_dimension=0, tiled=True
    )
    context_grad = lax.all_gather(context_grad, FS, axis=0, tiled=True)
    context_grad = after(context_grad, grad_head1)
    grad_w_text = sum_rows_over_dp(dot_tn(text_columns, context_grad).astype(bf16))
    text_part = dot_nt(context_grad, w_text).astype(bf16)
    grad_text = lax.all_to_all(text_part, FS, split_axis=0, concat_axis=1, tiled=True)
    grad_text = grad_text[:CAP_TOK].astype(f32)

    grad_normed_one = reduce3(lambda dy, dx: row_block(normed_part, peer(dy, dx), TOK))
    grad_rows_in, grad_ln1_gain, grad_ln1_bias = pull_one(grad_normed_one)
    grad_tokens = grad_after_self + grad_rows_in
    grad_qkv_w = lax.all_to_all(grad_heads_w, FS, 0, 0, tiled=True)
    grad_qkv_w = jnp.concatenate(
        [
            jnp.concatenate(
                [
                    grad_qkv_w[SHARD * p : SHARD * (p + 1), SHARD * k : SHARD * (k + 1)]
                    for p in range(8)
                ],
                axis=1,
            )
            for k in range(3)
        ]
        + [jnp.zeros((512 - 3 * SHARD, D), bf16)],
        axis=0,
    )
    grad_qkv_w = sum_rows_over_dp(grad_qkv_w)
    grad_w_query, grad_w_key, grad_w_value = (
        grad_qkv_w[SHARD * k : SHARD * (k + 1)] for k in range(3)
    )
    norms = sum_everywhere(
        jnp.stack(
            [
                grad_ln1_gain,
                grad_ln1_bias,
                grad_ln2_gain,
                grad_ln2_bias,
                grad_ln3_gain,
                grad_ln3_bias,
            ]
        )
    )
    return (
        outputs[None],
        grad_tokens[None],
        grad_text[None],
        norms[0],
        norms[1],
        grad_w_query,
        grad_w_key,
        grad_w_value,
        grad_w_out,
        norms[2],
        norms[3],
        grad_c_query,
        grad_w_text,
        grad_c_key,
        grad_c_value,
        grad_c_out,
        norms[4],
        norms[5],
        grad_w_up,
        grad_w_down,
    )


def solution(mesh):
    split = Mesh(mesh.devices.reshape(2, 4, 2, 4, 2), ("xh", "z", "c", "y", "xl"))
    dp = ("xh", "z", "c")
    rows = P(dp, FS, None)
    per_row = P(dp, None)
    weight = P(FS, None)
    rep = P()
    in_specs = (
        rows, rows, per_row, per_row, per_row,
        rep, rep, weight, weight, weight, weight,
        rep, rep, weight, weight, weight, weight, weight,
        rep, rep, weight, weight, rows,
    )
    out_specs = (
        rows, rows, rows,
        rep, rep, weight, weight, weight, weight,
        rep, rep, weight, weight, weight, weight, weight,
        rep, rep, weight, weight,
    )
    return jax.shard_map(
        local, mesh=split, in_specs=in_specs, out_specs=out_specs, check_vma=False
    )
```

```python
import functools

import jax
import jax.numpy as jnp
from jax import lax
from jax.experimental import pallas as pl
from jax.experimental.pallas import tpu as pltpu
from jax.sharding import Mesh
from jax.sharding import PartitionSpec as P

HEADS = 16
HEAD = 72
D = 1152
FF = 4608
CAP_TOK = 60
TXT_OWN = 64
TXT = 8 * TXT_OWN
TOK = 256
ROW = 2048
CAP_LEN = 120
SEGS = 3
CAPS = 4
SHARD = 144
SLOT = 128
WIN = 640
STEP = 512

bf16 = jnp.bfloat16
f32 = jnp.float32
norm_eps = 1e-06
masked_score = -1e30
scale = HEAD ** (-0.5)
log2e = 1.4426950408889634
FS = ("y", "xl")
VMEM = 60 * 1024 * 1024


def dot_nn(a, b):
    return lax.dot_general(a, b, (((1,), (0,)), ((), ())), preferred_element_type=f32)


def dot_nt(a, b):
    return lax.dot_general(a, b, (((1,), (1,)), ((), ())), preferred_element_type=f32)


def dot_tn(a, b):
    return lax.dot_general(a, b, (((0,), (0,)), ((), ())), preferred_element_type=f32)


def params():
    return pltpu.CompilerParams(vmem_limit_bytes=VMEM)


def shift(x, axis, by):
    n = lax.axis_size(axis)
    return lax.ppermute(x, axis, [(i, (i + by) % n) for i in range(n)])


def halves(x):
    h = (x.shape[0] // 2 + 15) // 16 * 16
    return x[:h], x[h:]


def after(x, *others):
    return lax.optimization_barrier((x, *others))[0] if others else x


def gather_first(x):
    return shift(x, "xl", 1), shift(x, "y", -1), shift(x, "y", 1)


def gather_second(x01, x10):
    return shift(x01, "y", 1), shift(x10, "y", -1), shift(x10, "xl", 1)


def gather_third(x31, x11):
    return shift(halves(x11)[0], "y", -1), shift(halves(x31)[1], "y", 1)


NEAR = ((0, 0), (0, 1), (1, 0), (3, 0))
NEXT = ((3, 1), (2, 0), (1, 1))
LAST = (2, 1)


def reduce_first(chunk):
    lo, hi = halves(chunk(2, 1))
    return shift(lo, "y", 1), shift(hi, "y", -1), shift(chunk(2, 0), "y", 1)


def reduce_second(chunk, lo, hi):
    h = lo.shape[0]
    c11, c31 = chunk(1, 1), chunk(3, 1)
    c11 = jnp.concatenate([c11[:h] + lo, c11[h:]], axis=0)
    c31 = jnp.concatenate([c31[:h], c31[h:] + hi], axis=0)
    return shift(c11, "xl", 1), shift(c31, "y", -1)


def reduce_third(chunk, c20, c11, c31):
    return (
        shift(chunk(1, 0) + c20 + c11, "y", 1),
        shift(chunk(0, 1) + c31, "xl", 1),
        shift(chunk(3, 0), "y", -1),
    )


def reduce_last(chunk, *parts):
    return sum([p.astype(f32) for p in parts], chunk(0, 0).astype(f32))


def every_peer(x):
    copies = jnp.broadcast_to(x[None], (8, *x.shape)).reshape(8 * x.shape[0], x.shape[1])
    return lax.all_to_all(copies, FS, 0, 0, tiled=True)


def peers_sum(x):
    parts = lax.all_to_all(x, FS, 0, 0, tiled=True)
    return jnp.sum(parts.reshape(8, -1, x.shape[1]).astype(f32), axis=0)


def reduce_z(far, minus, plus):
    lo, hi = halves(far)
    lo, hi = shift(lo, "z", -1), shift(hi, "z", 1)
    h = lo.shape[0]
    return (
        jnp.concatenate([minus[:h] + lo, minus[h:]], axis=0),
        jnp.concatenate([plus[:h], plus[h:] + hi], axis=0),
    )


def peer(dy, dx):
    return ((lax.axis_index("y") + dy) % 4) * 2 + (lax.axis_index("xl") ^ dx)


def place(pieces, outs):
    arrays, index = [], {}

    def number(x):
        if id(x) not in index:
            index[id(x)] = len(arrays)
            arrays.append(x)
        return index[id(x)]

    block = sum(rows for _, _, rows, p, _ in pieces if p == NEAR[0])
    table, copies = [], []
    for source, first, rows, p, off in pieces:
        pair = source if isinstance(source, tuple) else (source, source)
        pair = tuple(number(x) for x in pair)
        for o, parts in enumerate(outs):
            for side, c0, cols, to in parts:
                copies.append((pair, side, first, rows, len(table), off, o, c0, cols, to))
        table.append(peer(*p))
    n_in, n_out = len(arrays), len(outs)
    widths = [sum(cols for _, _, cols, _ in parts) for parts in outs]

    def body(where, core, *refs):
        ins, targets, sem = refs[:n_in], refs[n_in : n_in + n_out], refs[-1]

        def run(this):
            started = []
            for k, (pair, side, first, rows, t, off, o, c0, cols, to) in enumerate(copies):
                src = ins[pair[0] if side == this else pair[1]]
                row = pl.multiple_of(where[t] * block + off, 16)
                one = pltpu.make_async_copy(
                    src.at[pl.ds(first, rows), pl.ds(c0, cols)],
                    targets[o].at[pl.ds(row, rows), pl.ds(to, cols)],
                    sem.at[k],
                )
                one.start()
                started.append(one)
            for one in started:
                one.wait()

        @pl.when(core[0] == 0)
        def _():
            run(0)

        @pl.when(core[0] != 0)
        def _():
            run(1)

    smem = pl.BlockSpec(memory_space=pltpu.SMEM)
    return pl.pallas_call(
        body,
        in_specs=[smem, smem] + [pl.BlockSpec(memory_space=pl.ANY)] * n_in,
        out_specs=[pl.BlockSpec(memory_space=pltpu.VMEM)] * n_out,
        out_shape=[jax.ShapeDtypeStruct((8 * block, w), bf16) for w in widths],
        scratch_shapes=[pltpu.SemaphoreType.DMA((len(copies),))],
        compiler_params=params(),
    )(jnp.stack(table).astype(jnp.int32), lax.axis_index("c").astype(jnp.int32)[None], *arrays)


def self_forward_body(seg_q, seg_k, q, kv, out, total):
    s = dot_nt(q[:, :SLOT], kv[:, SLOT : 2 * SLOT])
    s = jnp.where(seg_q[...] == seg_k[...], s, masked_score)
    top = jnp.max(s, axis=1, keepdims=True)
    p = jnp.exp2((s - top) * (scale * log2e))
    mass = jnp.sum(p, axis=1, keepdims=True)
    out[...] = (dot_nn(p.astype(bf16), kv[:, 2 * SLOT :]) / mass)[:, :HEAD].astype(bf16)
    log_total = top * (scale * log2e) + jnp.log2(mass)
    total[...] = jnp.transpose(jnp.broadcast_to(log_total, (TOK, SLOT)))[0:1, :]


def self_forward(head, seg_q, seg_k, qkv):
    return pl.pallas_call(
        self_forward_body,
        grid=(ROW // TOK,),
        in_specs=[
            pl.BlockSpec((TOK, 1), lambda i: (i, 0)),
            pl.BlockSpec((1, ROW), lambda i: (0, 0)),
            pl.BlockSpec((TOK, 3 * SLOT), lambda i: (i, head)),
            pl.BlockSpec((ROW, 3 * SLOT), lambda i: (0, head)),
        ],
        out_specs=[
            pl.BlockSpec((TOK, HEAD), lambda i: (i, 0)),
            pl.BlockSpec((1, TOK), lambda i: (0, i)),
        ],
        out_shape=[
            jax.ShapeDtypeStruct((ROW, HEAD), bf16),
            jax.ShapeDtypeStruct((1, ROW), f32),
        ],
        compiler_params=params(),
    )(seg_q, seg_k, qkv, qkv)


def self_backward_body(head, seg_k, seg_q, total, q, kv, g, grad, key_sum, value_sum, key_t):
    i = pl.program_id(0)

    @pl.when(i == 0)
    def _():
        key_sum[...] = jnp.zeros_like(key_sum)
        value_sum[...] = jnp.zeros_like(value_sum)
        key_t[...] = jnp.transpose(kv[:, SLOT : 2 * SLOT])

    rows = pl.ds(pl.multiple_of(i * TOK, TOK), TOK)
    q_h, k_h, v_h = q[:, :SLOT], kv[:, SLOT : 2 * SLOT], kv[:, 2 * SLOT :]
    g_both = g[...]
    g_h = jnp.concatenate(
        [g_both[:, HEAD * head : HEAD * (head + 1)], jnp.zeros((TOK, SLOT - HEAD), bf16)], axis=1
    )
    p = jnp.exp2(dot_nt(k_h, q_h) * (scale * log2e) - total[...])
    p = jnp.where(seg_k[...] == seg_q[...], p, 0.0)
    dp = dot_nt(v_h, g_h)
    ds = (p * (dp - jnp.sum(p * dp, axis=0, keepdims=True))).astype(bf16)
    value_sum[...] += dot_nn(p.astype(bf16), g_h)
    key_sum[...] += dot_nn(ds, q_h)
    grad[rows, :SLOT] = (jnp.transpose(dot_nn(key_t[...], ds)) * scale).astype(bf16)

    @pl.when(i == pl.num_programs(0) - 1)
    def _():
        grad[:, SLOT : 2 * SLOT] = (key_sum[...] * scale).astype(bf16)
        grad[:, 2 * SLOT :] = value_sum[...].astype(bf16)


def self_backward(head, seg_k, seg_q, total, qkv, g):
    return pl.pallas_call(
        functools.partial(self_backward_body, head),
        grid=(ROW // TOK,),
        in_specs=[
            pl.BlockSpec((ROW, 1), lambda i: (0, 0)),
            pl.BlockSpec((1, TOK), lambda i: (0, i)),
            pl.BlockSpec((1, TOK), lambda i: (0, i)),
            pl.BlockSpec((TOK, 3 * SLOT), lambda i: (i, head)),
            pl.BlockSpec((ROW, 3 * SLOT), lambda i: (0, head)),
            pl.BlockSpec((TOK, SHARD), lambda i: (i, 0)),
        ],
        out_specs=pl.BlockSpec((ROW, 3 * SLOT), lambda i: (0, 0)),
        out_shape=jax.ShapeDtypeStruct((ROW, 3 * SLOT), bf16),
        scratch_shapes=[
            pltpu.VMEM((ROW, SLOT), f32),
            pltpu.VMEM((ROW, SLOT), f32),
            pltpu.VMEM((SLOT, ROW), bf16),
        ],
        compiler_params=params(),
    )(seg_k, seg_q, total, qkv, qkv, g)


def cross_forward_body(cap_q, cap_t, q, k, v, out):
    allowed = cap_q[...] == cap_t[...]
    mixed = []
    for h in range(HEADS):
        a, b = HEAD * h, HEAD * (h + 1)
        s = dot_nt(q[:, a:b], k[:, a:b])
        s = jnp.where(allowed, s, masked_score)
        top = jnp.max(s, axis=1, keepdims=True)
        p = jnp.exp2((s - top) * (scale * log2e))
        mass = jnp.sum(p, axis=1, keepdims=True)
        mixed.append(dot_nn(p.astype(bf16), v[:, a:b]) / mass)
    out[...] = jnp.concatenate(mixed, axis=1).astype(bf16)


def cross_forward(cap_q, cap_t, q, k, v):
    return pl.pallas_call(
        cross_forward_body,
        out_shape=jax.ShapeDtypeStruct((TOK, D), bf16),
        compiler_params=params(),
    )(cap_q, cap_t, q, k, v)


def cross_backward_body(cap_t, cap_q, q, k, v, g, grad_q, grad_k, grad_v):
    allowed = cap_t[...] == cap_q[...]
    dq, dk, dv = [], [], []
    for h in range(HEADS):
        a, b = HEAD * h, HEAD * (h + 1)
        q_h, k_h, v_h, g_h = q[:, a:b], k[:, a:b], v[:, a:b], g[:, a:b]
        s = jnp.where(allowed, dot_nt(k_h, q_h), masked_score)
        top = jnp.max(s, axis=0, keepdims=True)
        p = jnp.exp2((s - top) * (scale * log2e))
        p = p / jnp.sum(p, axis=0, keepdims=True)
        dp = dot_nt(v_h, g_h)
        ds = (p * (dp - jnp.sum(p * dp, axis=0, keepdims=True))).astype(bf16)
        dv.append(dot_nn(p.astype(bf16), g_h))
        dk.append(dot_nn(ds, q_h) * scale)
        dq.append(dot_tn(ds, k_h) * scale)
    grad_q[...] = jnp.concatenate(dq, axis=1).astype(bf16)
    grad_k[...] = jnp.concatenate(dk, axis=1).astype(bf16)
    grad_v[...] = jnp.concatenate(dv, axis=1).astype(bf16)


def cross_backward(cap_t, cap_q, q, k, v, g):
    return pl.pallas_call(
        cross_backward_body,
        out_shape=[
            jax.ShapeDtypeStruct((TOK, D), bf16),
            jax.ShapeDtypeStruct((TXT, D), bf16),
            jax.ShapeDtypeStruct((TXT, D), bf16),
        ],
        compiler_params=params(),
    )(cap_t, cap_q, q, k, v, g)


def mlp_body(core, x, g, mine, other, out, act_out, pre_out, grad_x, up, down, sem):
    @pl.when(pl.program_id(0) == 0)
    def _():
        def fetch(first, second):
            one = pltpu.make_async_copy(first, up, sem.at[0])
            two = pltpu.make_async_copy(second, down, sem.at[1])
            one.start()
            two.start()
            one.wait()
            two.wait()

        @pl.when(core[0] == 0)
        def _():
            fetch(mine, other)

        @pl.when(core[0] != 0)
        def _():
            fetch(other, mine)

    pre = dot_nn(x[...], up[...])
    grad_act = dot_nt(g[...], down[...])
    cdf = 0.5 * (1.0 + lax.erf(pre * (0.5**0.5)))
    density = jnp.exp2(pre * pre * (-0.5 * log2e)) * 0.3989422804014327
    act = (pre * cdf).astype(bf16)
    grad_pre = (grad_act * (cdf + pre * density)).astype(bf16)
    act_out[...] = act
    pre_out[...] = grad_pre
    out[...] = dot_nn(act, down[...]).astype(out.dtype)
    grad_x[...] = dot_nt(grad_pre, up[...]).astype(grad_x.dtype)


def mlp(core, x, g, mine, other):
    n = x.shape[0]
    rows = pl.BlockSpec((TOK, D), lambda i: (i, 0))
    hbm = pl.BlockSpec(memory_space=pl.ANY)
    return pl.pallas_call(
        mlp_body,
        grid=(n // TOK,),
        in_specs=[pl.BlockSpec(memory_space=pltpu.SMEM), rows, rows, hbm, hbm],
        out_specs=[rows] * 4,
        out_shape=[jax.ShapeDtypeStruct((n, D), bf16)] * 4,
        scratch_shapes=[
            pltpu.VMEM((D, D), bf16),
            pltpu.VMEM((D, D), bf16),
            pltpu.SemaphoreType.DMA((2,)),
        ],
        compiler_params=params(),
    )(core, x, g, mine, other)


def mlp_grads_body(core, *refs):
    xs, pres, acts, gs = refs[0:3], refs[3:6], refs[6:9], refs[9:12]
    keep, send = refs[12:]
    up = sum(dot_tn(x[...], p[...]) for x, p in zip(xs, pres)).astype(bf16)
    down = sum(dot_tn(a[...], g[...]) for a, g in zip(acts, gs)).astype(bf16)
    first = core[0] == 0

    @pl.when(first)
    def _():
        keep[...] = up
        send[...] = down

    @pl.when(jnp.logical_not(first))
    def _():
        keep[...] = down
        send[...] = up


def mlp_grads(core, xs, pres, acts, gs):
    def whole(x):
        return pl.BlockSpec(x.shape, lambda k: (0, 0))

    def part(x):
        return pl.BlockSpec((x.shape[0], 384), lambda k: (0, k))

    out = pl.BlockSpec((D, 384), lambda k: (0, k))
    return pl.pallas_call(
        mlp_grads_body,
        grid=(3,),
        in_specs=[pl.BlockSpec(memory_space=pltpu.SMEM)]
        + [whole(x) for x in xs]
        + [part(x) for x in pres]
        + [whole(x) for x in acts]
        + [part(x) for x in gs],
        out_specs=[out, out],
        out_shape=[jax.ShapeDtypeStruct((D, D), bf16)] * 2,
        compiler_params=params(),
    )(core, *xs, *pres, *acts, *gs)


def sort_hidden_body(x, up, down):
    for f in range(8):
        lanes = slice(SHARD * f, SHARD * (f + 1))
        up[:, 4 * SHARD * f : 4 * SHARD * (f + 1)] = jnp.concatenate(
            [x[2 * z, :, lanes] for z in range(4)], axis=1
        ).astype(f32)
    for z in range(4):
        down[SHARD * z : SHARD * (z + 1), :] = x[2 * z + 1].astype(f32)


def sort_hidden(x):
    return pl.pallas_call(
        sort_hidden_body,
        out_shape=[
            jax.ShapeDtypeStruct((SHARD, FF), f32),
            jax.ShapeDtypeStruct((4 * SHARD, D), f32),
        ],
        compiler_params=params(),
    )(x)


def norm_layer(values, norm_gain, norm_shift):
    center = values - jnp.mean(values, axis=-1, keepdims=True)
    spread = jnp.mean(center * center, axis=-1, keepdims=True)
    return center * lax.rsqrt(spread + norm_eps) * norm_gain + norm_shift


def row_block(x, index, rows):
    return lax.dynamic_slice_in_dim(x, index * rows, rows, axis=0)


def core_window(x, core):
    return lax.dynamic_slice_in_dim(x, core * STEP, WIN, axis=1)


def both_cores(x):
    return jnp.concatenate([x, shift(x, "c", 1)], axis=0)


def window_grad(left, right):
    core = lax.axis_index("c")
    sent = shift(core_window(right, 1 - core), "c", 1)
    rights = jnp.concatenate([core_window(right, core), sent], axis=0)
    return dot_tn(both_cores(left), rights).astype(bf16)


def sum_over_dp(x):
    part = lax.psum_scatter(x, "z", scatter_dimension=0, tiled=True)
    part = part + shift(part, "xh", 1)
    return lax.all_gather(part, "z", axis=0, tiled=True)


def whole_columns(mine, count):
    other = shift(mine, "c", 1)
    first = lax.axis_index("c") == 0
    low = jnp.where(first, mine, other).astype(f32)
    high = jnp.where(first, other, mine).astype(f32)
    return [
        jnp.concatenate(
            [low[SHARD * k : SHARD * (k + 1)], high[SHARD * k : SHARD * (k + 1), 128:]], axis=1
        )
        for k in range(count)
    ]


def sum_rows_over_dp(x):
    core = lax.axis_index("c")
    rows = x.shape[0] // 2
    mine = row_block(x, core, rows) + shift(row_block(x, 1 - core, rows), "c", 1)
    mine = sum_over_dp(mine)
    other = shift(mine, "c", 1)
    first = core == 0
    low = jnp.where(first, mine, other)
    high = jnp.where(first, other, mine)
    return jnp.concatenate([low, high], axis=0).astype(f32)


def sum_everywhere(x):
    for axis in ("y", "xl", "z", "xh", "c"):
        n = lax.axis_size(axis)
        x = sum([shift(x, axis, k) for k in range(1, n)], x)
    return x


def local(
    tokens,
    text_states,
    seg_lengths,
    caption_of_segment,
    text_lengths,
    ln1_gain,
    ln1_bias,
    w_query,
    w_key,
    w_value,
    w_out,
    ln2_gain,
    ln2_bias,
    c_query,
    w_text,
    c_key,
    c_value,
    c_out,
    ln3_gain,
    ln3_bias,
    w_up,
    w_down,
    cotangent,
):
    core = lax.axis_index("c")
    first_core = core == 0
    core_index = core.astype(jnp.int32)[None]
    quarter = lax.axis_index("z")
    first_row = peer(0, 0) * TOK

    ends = jnp.cumsum(seg_lengths[0])
    positions = jnp.arange(ROW, dtype=jnp.int32)
    segment = jnp.sum((positions[:, None] >= ends[None, :]).astype(jnp.int32), axis=1)
    own_segment = lax.dynamic_slice_in_dim(segment, first_row, TOK)
    text_row = jnp.arange(TXT, dtype=jnp.int32)
    text_pos = text_row // TXT_OWN * CAP_TOK + text_row % TXT_OWN
    text_caption = text_pos // CAP_LEN
    live = jnp.sum(
        jnp.where(
            text_caption[:, None] == jnp.arange(CAPS, dtype=jnp.int32)[None, :],
            text_lengths[0][None, :],
            0,
        ),
        axis=1,
    )
    query_caption = jnp.sum(
        jnp.where(
            own_segment[:, None] == jnp.arange(SEGS, dtype=jnp.int32)[None, :],
            caption_of_segment[0][None, :],
            0,
        ),
        axis=1,
    )
    text_live = (text_row % TXT_OWN < CAP_TOK) & (text_pos % CAP_LEN < live)
    text_key = jnp.where(text_live, text_caption, -1)

    rows_in = tokens[0].astype(f32)
    normed_one, pull_one = jax.vjp(norm_layer, rows_in, ln1_gain, ln1_bias)
    normed_one = normed_one.astype(bf16)
    n01, n10, n30 = gather_first(normed_one)

    grad_out = cotangent[0]
    grad_mlp = grad_out.astype(bf16)
    mlp_minus, mlp_plus = shift(grad_mlp, "z", 1), shift(grad_mlp, "z", -1)

    text_own = jnp.pad(after(text_states[0], normed_one), ((0, TXT_OWN - CAP_TOK), (0, 0)))
    text_columns = lax.all_to_all(text_own, FS, split_axis=1, concat_axis=0, tiled=True)
    context_part = dot_nn(text_columns, w_text).astype(bf16)
    context_own = lax.psum_scatter(context_part, FS, scatter_dimension=0, tiled=True)
    context = lax.all_gather(context_own, FS, axis=0, tiled=True)

    packed = jnp.concatenate(
        [
            jnp.concatenate([w[:, SHARD * k : SHARD * (k + 1)] for k in range(8)], axis=0)
            for w in (w_query, w_key, w_value)
        ],
        axis=1,
    )
    heads_w = lax.all_to_all(after(packed, context_part), FS, 0, 0, tiled=True)

    n31, n20, n11 = gather_second(n01, n10)
    n21 = gather_third(n31, n11)
    lo = n21[0].shape[0]
    (normed_all,) = place(
        [(x, 0, TOK, p, 0) for x, p in zip((normed_one, n01, n10, n30), NEAR)]
        + [(x, 0, TOK, p, 0) for x, p in zip((n31, n20, n11), NEXT)]
        + [(n21[0], 0, lo, LAST, 0), (n21[1], 0, TOK - lo, LAST, lo)],
        [[(0, 0, D, 0)]],
    )
    far_lo = shift(halves(mlp_minus)[0], "z", 1)
    far_hi = shift(halves(mlp_plus)[1], "z", -1)
    mlp_far = jnp.concatenate([far_lo, far_hi], axis=0)
    mlp_near = jnp.concatenate([mlp_minus, mlp_plus], axis=0)

    blank = jnp.zeros((D, SLOT - HEAD), bf16)
    heads_w = jnp.concatenate(
        [
            part
            for h in range(2)
            for k in range(3)
            for part in (heads_w[:, SHARD * k + HEAD * h : SHARD * k + HEAD * (h + 1)], blank)
        ],
        axis=1,
    )

    pack = jnp.where(
        first_core,
        jnp.concatenate([w_out, c_key, c_out[:, :WIN]], axis=1),
        jnp.concatenate([c_query, c_value, c_out[:, STEP:]], axis=1),
    )
    pack = after(pack, normed_all)
    g01, g10, g30 = gather_first(pack)

    seg_col, seg_row = segment[:, None], segment[None, :]
    qkv = dot_nn(after(normed_all, context_own, mlp_far), heads_w).astype(bf16)
    head0, total0 = self_forward(0, seg_col, seg_row, qkv)
    g01, g10, g30, head0 = lax.optimization_barrier((g01, g10, g30, head0))
    g31, g20, g11 = gather_second(g01, g10)
    near_mine = jnp.concatenate([pack, g01, g10, g30], axis=0)
    near_other = shift(near_mine, "c", 1)
    head1, total1 = self_forward(1, seg_col, seg_row, after(qkv, head0))
    attended = lax.all_to_all(
        jnp.concatenate([head0, head1], axis=1), FS, split_axis=0, concat_axis=1, tiled=True
    )
    g31, g20, g11, attended = lax.optimization_barrier((g31, g20, g11, attended))
    g21 = gather_third(g31, g11)
    next_mine = jnp.concatenate([g31, g20, g11], axis=0)
    next_other = shift(next_mine, "c", 1)
    last_other = [shift(x, "c", 1) for x in g21]
    lo = g21[0].shape[0]
    square_pieces = (
        [((near_mine, near_other), SHARD * k, SHARD, p, 0) for k, p in enumerate(NEAR)]
        + [((next_mine, next_other), SHARD * k, SHARD, p, 0) for k, p in enumerate(NEXT)]
        + [
            ((g21[0], last_other[0]), 0, lo, LAST, 0),
            ((g21[1], last_other[1]), 0, SHARD - lo, LAST, lo),
        ]
    )
    full_out, full_cquery = place(square_pieces, [[(0, 0, D, 0)], [(1, 0, D, 0)]])
    after_self = rows_in + dot_nn(attended, full_out)

    up_own = jnp.concatenate(
        [
            lax.dynamic_slice(w_up, (0, 4 * SHARD * k + SHARD * quarter), (SHARD, SHARD))
            for k in range(8)
        ],
        axis=1,
    )
    hidden_own = jnp.where(first_core, up_own, row_block(w_down, quarter, SHARD))
    hidden_mine = every_peer(after(hidden_own, attended))
    hidden_other = shift(hidden_mine, "c", 1)

    full_ckey, full_cvalue, full_cout = place(
        square_pieces,
        [
            [(0, D, D, 0)],
            [(1, D, D, 0)],
            [(0, 2 * D, WIN, 0), (1, 2 * D + 128, STEP, WIN)],
        ],
    )
    normed_two, pull_two = jax.vjp(norm_layer, after_self, ln2_gain, ln2_bias)
    normed_two = normed_two.astype(bf16)
    cross_query = dot_nn(normed_two, full_cquery).astype(bf16)
    context = after(context, after_self)
    cross_key = dot_nn(context, full_ckey).astype(bf16)
    cross_value = dot_nn(context, full_cvalue).astype(bf16)
    cross_mixed = cross_forward(
        query_caption[:, None], text_key[None, :], cross_query, cross_key, cross_value
    )
    after_cross = after_self + dot_nn(cross_mixed, full_cout)

    normed_three, pull_three = jax.vjp(norm_layer, after_cross, ln3_gain, ln3_bias)
    normed_three = normed_three.astype(bf16)
    three_minus, three_plus = shift(normed_three, "z", 1), shift(normed_three, "z", -1)
    weights = (hidden_mine, hidden_other)
    out_own, act_own, pre_own, back_own = mlp(core_index, normed_three, grad_mlp, *weights)
    three_minus, three_plus, out_own = lax.optimization_barrier(
        (three_minus, three_plus, out_own)
    )
    three_far = jnp.concatenate(
        [shift(halves(three_minus)[0], "z", 1), shift(halves(three_plus)[1], "z", -1)], axis=0
    )
    three_near = jnp.concatenate([three_minus, three_plus], axis=0)
    out_near, act_near, pre_near, back_near = mlp(core_index, three_near, mlp_near, *weights)
    out_far, act_far, pre_far, back_far = mlp(
        core_index, after(three_far, out_near), mlp_far, *weights
    )
    back_minus, back_plus = reduce_z(back_far, back_near[:TOK], back_near[TOK:])
    keep, send = mlp_grads(
        core_index,
        (normed_three, three_near, after(three_far, back_minus, back_plus)),
        (pre_own, pre_near, pre_far),
        (act_own, act_near, act_far),
        (grad_mlp, mlp_near, mlp_far),
    )
    back_minus, back_plus = shift(back_minus, "z", -1), shift(back_plus, "z", 1)
    hidden_sum = keep + shift(send, "c", 1)
    grad_three = back_own.astype(f32) + back_minus.astype(f32) + back_plus.astype(f32)
    grad_cross_in, grad_ln3_gain, grad_ln3_bias = pull_three(grad_three)
    grad_after_cross = grad_out + grad_cross_in
    grad_cross_branch = grad_after_cross.astype(bf16)
    grad_cross_mixed = dot_nt(grad_cross_branch, full_cout).astype(bf16)

    out_minus, out_plus = reduce_z(
        after(out_far, grad_cross_mixed), out_near[:TOK], out_near[TOK:]
    )

    grad_cquery_rows, grad_key_part, grad_value_part = cross_backward(
        text_key[:, None],
        query_caption[None, :],
        cross_query,
        cross_key,
        cross_value,
        after(grad_cross_mixed, hidden_sum),
    )
    out_minus, out_plus = shift(out_minus, "z", -1), shift(out_plus, "z", 1)
    hidden_grad = peers_sum(hidden_sum).astype(bf16)
    grad_self_in, grad_ln2_gain, grad_ln2_bias = pull_two(
        dot_nt(after(grad_cquery_rows, out_minus, out_plus), full_cquery)
    )
    outputs = (
        after_cross
        + out_own.astype(f32)
        + out_minus.astype(f32)
        + out_plus.astype(f32)
    )
    grad_after_self = grad_after_cross + grad_self_in
    grad_self_branch = grad_after_self.astype(bf16)
    grad_attended = dot_nt(grad_self_branch, full_out).astype(bf16)
    grad_heads = lax.all_to_all(
        after(grad_attended, hidden_grad), FS, split_axis=1, concat_axis=0, tiled=True
    )
    hidden_grad = hidden_grad + shift(hidden_grad, "xh", 1)
    hidden_grad = lax.all_gather(hidden_grad, ("z", "c"), axis=0)

    square = jnp.concatenate(
        [
            window_grad(cross_mixed, grad_cross_branch),
            window_grad(normed_two, grad_cquery_rows),
            window_grad(attended, grad_self_branch),
            window_grad(context, grad_key_part),
            window_grad(context, grad_value_part),
        ],
        axis=1,
    )
    context_part = dot_nt(after(grad_key_part, grad_attended), full_ckey) + dot_nt(
        after(grad_value_part, grad_attended), full_cvalue
    )
    context_part = context_part.astype(bf16)
    grad_heads = after(grad_heads, square, context_part)
    context_grad = peers_sum(after(context_part, grad_heads)).astype(bf16)

    def square_chunk(dy, dx):
        return row_block(square, peer(dy, dx), SHARD)

    s_lo, s_hi, s20 = reduce_first(square_chunk)

    grad_head0 = self_backward(0, seg_col, seg_row, total0, qkv, grad_heads)
    s_lo, s_hi, s20, context_grad, grad_head0 = lax.optimization_barrier(
        (s_lo, s_hi, s20, context_grad, grad_head0)
    )
    context_grad = every_peer(context_grad)
    s11, s31 = reduce_second(square_chunk, s_lo, s_hi)
    grad_head1 = self_backward(1, seg_col, seg_row, total1, qkv, after(grad_heads, grad_head0))
    s11, s31, hidden_grad, context_grad, grad_head1 = lax.optimization_barrier(
        (s11, s31, hidden_grad, context_grad, grad_head1)
    )
    square_parts = reduce_third(square_chunk, s20, s11, s31)
    grad_qkv = jnp.concatenate([grad_head0, grad_head1], axis=1)
    normed_part = dot_nt(grad_qkv, heads_w).astype(bf16)

    def normed_chunk(dy, dx):
        return row_block(normed_part, peer(dy, dx), TOK)

    n_lo, n_hi, n20 = reduce_first(normed_chunk)
    grad_heads_w = dot_tn(normed_all, grad_qkv).astype(bf16)
    grad_heads_w = jnp.concatenate(
        [
            grad_heads_w[:, SLOT * (3 * h + k) : SLOT * (3 * h + k) + HEAD]
            for k in range(3)
            for h in range(2)
        ],
        axis=1,
    )
    grad_qkv_w = lax.all_to_all(grad_heads_w, FS, 0, 0, tiled=True)
    grad_w_text = dot_tn(text_columns, context_grad).astype(bf16)
    text_part = dot_nt(context_grad, w_text).astype(bf16)
    n_lo, n_hi, *square_parts = lax.optimization_barrier((n_lo, n_hi, *square_parts))
    n11, n31 = reduce_second(normed_chunk, n_lo, n_hi)
    square = reduce_last(square_chunk, *square_parts).astype(bf16)
    square = jnp.concatenate(
        [square[:, WIN * k : WIN * (k + 1)] for k in range(5)]
        + [jnp.zeros((768 - 5 * SHARD, WIN), bf16)],
        axis=0,
    )
    square = sum_over_dp(square)
    grad_c_out, grad_c_query, grad_w_out, grad_c_key, grad_c_value = whole_columns(square, 5)
    grad_w_text = sum_rows_over_dp(grad_w_text)
    grad_w_up, grad_w_down = sort_hidden(hidden_grad)

    n11, n31, grad_qkv_w = lax.optimization_barrier((n11, n31, grad_qkv_w))
    grad_normed_one = reduce_last(normed_chunk, *reduce_third(normed_chunk, n20, n11, n31))
    grad_qkv_w = jnp.concatenate(
        [
            jnp.concatenate(
                [
                    grad_qkv_w[SHARD * p : SHARD * (p + 1), SHARD * k : SHARD * (k + 1)]
                    for p in range(8)
                ],
                axis=1,
            )
            for k in range(3)
        ]
        + [jnp.zeros((512 - 3 * SHARD, D), bf16)],
        axis=0,
    )
    grad_qkv_w = sum_rows_over_dp(grad_qkv_w)
    grad_w_query, grad_w_key, grad_w_value = (
        grad_qkv_w[SHARD * k : SHARD * (k + 1)] for k in range(3)
    )
    grad_text = lax.all_to_all(
        after(text_part, grad_qkv_w), FS, split_axis=0, concat_axis=1, tiled=True
    )
    grad_text = grad_text[:CAP_TOK].astype(f32)
    grad_rows_in, grad_ln1_gain, grad_ln1_bias = pull_one(grad_normed_one)
    grad_tokens = grad_after_self + grad_rows_in
    norms = sum_everywhere(
        jnp.stack(
            [
                grad_ln1_gain,
                grad_ln1_bias,
                grad_ln2_gain,
                grad_ln2_bias,
                grad_ln3_gain,
                grad_ln3_bias,
            ]
        )
    )
    return (
        outputs[None],
        grad_tokens[None],
        grad_text[None],
        norms[0],
        norms[1],
        grad_w_query,
        grad_w_key,
        grad_w_value,
        grad_w_out,
        norms[2],
        norms[3],
        grad_c_query,
        grad_w_text,
        grad_c_key,
        grad_c_value,
        grad_c_out,
        norms[4],
        norms[5],
        grad_w_up,
        grad_w_down,
    )


def solution(mesh):
    split = Mesh(mesh.devices.reshape(2, 4, 2, 4, 2), ("xh", "z", "c", "y", "xl"))
    dp = ("xh", "z", "c")
    rows = P(dp, FS, None)
    per_row = P(dp, None)
    weight = P(FS, None)
    rep = P()
    in_specs = (
        rows, rows, per_row, per_row, per_row,
        rep, rep, weight, weight, weight, weight,
        rep, rep, weight, weight, weight, weight, weight,
        rep, rep, weight, weight, rows,
    )
    out_specs = (
        rows, rows, rows,
        rep, rep, weight, weight, weight, weight,
        rep, rep, weight, weight, weight, weight, weight,
        rep, rep, weight, weight,
    )
    return jax.shard_map(
        local, mesh=split, in_specs=in_specs, out_specs=out_specs, check_vma=False
    )
```

```python
import functools

import jax
import jax.numpy as jnp
from jax import lax
from jax.experimental import pallas as pl
from jax.experimental.pallas import tpu as pltpu
from jax.sharding import Mesh
from jax.sharding import PartitionSpec as P

HEADS = 16
HEAD = 72
D = 1152
FF = 4608
CAP_TOK = 60
TXT_OWN = 64
TXT = 8 * TXT_OWN
TOK = 256
ROW = 2048
CAP_LEN = 120
SEGS = 3
CAPS = 4
SHARD = 144
SLOT = 128
WIN = 640
STEP = 512

bf16 = jnp.bfloat16
f32 = jnp.float32
norm_eps = 1e-06
masked_score = -1e30
scale = HEAD ** (-0.5)
log2e = 1.4426950408889634
FS = ("y", "xl")
VMEM = 60 * 1024 * 1024


def dot_nn(a, b):
    return lax.dot_general(a, b, (((1,), (0,)), ((), ())), preferred_element_type=f32)


def dot_nt(a, b):
    return lax.dot_general(a, b, (((1,), (1,)), ((), ())), preferred_element_type=f32)


def dot_tn(a, b):
    return lax.dot_general(a, b, (((0,), (0,)), ((), ())), preferred_element_type=f32)


def params():
    return pltpu.CompilerParams(vmem_limit_bytes=VMEM)


def shift(x, axis, by):
    n = lax.axis_size(axis)
    return lax.ppermute(x, axis, [(i, (i + by) % n) for i in range(n)])


def halves(x):
    h = (x.shape[0] // 2 + 15) // 16 * 16
    return x[:h], x[h:]


def after(x, *others):
    return lax.optimization_barrier((x, *others))[0] if others else x


def gather_first(x):
    return shift(x, "xl", 1), shift(x, "y", -1), shift(x, "y", 1)


def gather_second(x01, x10):
    return shift(x01, "y", 1), shift(x10, "y", -1), shift(x10, "xl", 1)


def gather_third(x31, x11):
    return shift(halves(x11)[0], "y", -1), shift(halves(x31)[1], "y", 1)


NEAR = ((0, 0), (0, 1), (1, 0), (3, 0))
NEXT = ((3, 1), (2, 0), (1, 1))
LAST = (2, 1)


def reduce_first(chunk):
    lo, hi = halves(chunk(2, 1))
    return shift(lo, "y", 1), shift(hi, "y", -1), shift(chunk(2, 0), "y", 1)


def reduce_second(chunk, lo, hi):
    h = lo.shape[0]
    c11, c31 = chunk(1, 1), chunk(3, 1)
    c11 = jnp.concatenate([c11[:h] + lo, c11[h:]], axis=0)
    c31 = jnp.concatenate([c31[:h], c31[h:] + hi], axis=0)
    return shift(c11, "xl", 1), shift(c31, "y", -1)


def reduce_third(chunk, c20, c11, c31):
    return (
        shift(chunk(1, 0) + c20 + c11, "y", 1),
        shift(chunk(0, 1) + c31, "xl", 1),
        shift(chunk(3, 0), "y", -1),
    )


def reduce_last(chunk, *parts):
    return sum([p.astype(f32) for p in parts], chunk(0, 0).astype(f32))


def every_peer(x, axes=FS):
    copies = jnp.broadcast_to(x[None], (8, *x.shape)).reshape(8 * x.shape[0], x.shape[1])
    return lax.all_to_all(copies, axes, 0, 0, tiled=True)


def peers_parts(x, axes=FS):
    return lax.all_to_all(x, axes, 0, 0, tiled=True)


def sum_parts(parts):
    return jnp.sum(parts.reshape(8, -1, parts.shape[1]).astype(f32), axis=0)


def reduce_z(far, minus, plus):
    lo, hi = halves(far)
    lo, hi = shift(lo, "z", -1), shift(hi, "z", 1)
    h = lo.shape[0]
    return (
        jnp.concatenate([minus[:h] + lo, minus[h:]], axis=0),
        jnp.concatenate([plus[:h], plus[h:] + hi], axis=0),
    )


def peer(dy, dx):
    return ((lax.axis_index("y") + dy) % 4) * 2 + (lax.axis_index("xl") ^ dx)


def place(own, first, second, third):
    lo = third[0].shape[0]
    rows, cols = own.shape
    pieces = [(x, p, 0) for x, p in zip((own, *first), NEAR)]
    pieces += [(x, p, 0) for x, p in zip(second, NEXT)]
    pieces += [(third[0], LAST, 0), (third[1], LAST, lo)]
    count = len(pieces)

    def body(where, *refs):
        ins, out, sem = refs[:count], refs[count], refs[-1]
        started = []
        for k, (x, _, off) in enumerate(pieces):
            row = pl.multiple_of(where[k] * rows + off, 16)
            one = pltpu.make_async_copy(ins[k], out.at[pl.ds(row, x.shape[0])], sem.at[k])
            one.start()
            started.append(one)
        for one in started:
            one.wait()

    return pl.pallas_call(
        body,
        in_specs=[pl.BlockSpec(memory_space=pltpu.SMEM)]
        + [pl.BlockSpec(memory_space=pl.ANY)] * count,
        out_specs=pl.BlockSpec(memory_space=pltpu.VMEM),
        out_shape=jax.ShapeDtypeStruct((8 * rows, cols), own.dtype),
        scratch_shapes=[pltpu.SemaphoreType.DMA((count,))],
        compiler_params=params(),
    )(
        jnp.stack([peer(*p) for _, p, _ in pieces]).astype(jnp.int32),
        *[x for x, _, _ in pieces],
    )


def self_forward_body(seg_q, seg_k, q, kv, out, total):
    s = dot_nt(q[:, :SLOT], kv[:, SLOT : 2 * SLOT])
    s = jnp.where(seg_q[...] == seg_k[...], s, masked_score)
    top = jnp.max(s, axis=1, keepdims=True)
    p = jnp.exp2((s - top) * (scale * log2e))
    mass = jnp.sum(p, axis=1, keepdims=True)
    out[...] = (dot_nn(p.astype(bf16), kv[:, 2 * SLOT :]) / mass)[:, :HEAD].astype(bf16)
    log_total = top * (scale * log2e) + jnp.log2(mass)
    total[...] = jnp.transpose(jnp.broadcast_to(log_total, (TOK, SLOT)))[0:1, :]


def self_forward(head, seg_q, seg_k, qkv):
    return pl.pallas_call(
        self_forward_body,
        grid=(ROW // TOK,),
        in_specs=[
            pl.BlockSpec((TOK, 1), lambda i: (i, 0)),
            pl.BlockSpec((1, ROW), lambda i: (0, 0)),
            pl.BlockSpec((TOK, 3 * SLOT), lambda i: (i, head)),
            pl.BlockSpec((ROW, 3 * SLOT), lambda i: (0, head)),
        ],
        out_specs=[
            pl.BlockSpec((TOK, HEAD), lambda i: (i, 0)),
            pl.BlockSpec((1, TOK), lambda i: (0, i)),
        ],
        out_shape=[
            jax.ShapeDtypeStruct((ROW, HEAD), bf16),
            jax.ShapeDtypeStruct((1, ROW), f32),
        ],
        compiler_params=params(),
    )(seg_q, seg_k, qkv, qkv)


def self_backward_body(head, seg_k, seg_q, total, q, kv, g, grad, key_sum, value_sum, key_t):
    i = pl.program_id(0)

    @pl.when(i == 0)
    def _():
        key_sum[...] = jnp.zeros_like(key_sum)
        value_sum[...] = jnp.zeros_like(value_sum)
        key_t[...] = jnp.transpose(kv[:, SLOT : 2 * SLOT])

    rows = pl.ds(pl.multiple_of(i * TOK, TOK), TOK)
    q_h, k_h, v_h = q[:, :SLOT], kv[:, SLOT : 2 * SLOT], kv[:, 2 * SLOT :]
    g_both = g[...]
    g_h = jnp.concatenate(
        [g_both[:, HEAD * head : HEAD * (head + 1)], jnp.zeros((TOK, SLOT - HEAD), bf16)], axis=1
    )
    p = jnp.exp2(dot_nt(k_h, q_h) * (scale * log2e) - total[...])
    p = jnp.where(seg_k[...] == seg_q[...], p, 0.0)
    dp = dot_nt(v_h, g_h)
    ds = (p * (dp - jnp.sum(p * dp, axis=0, keepdims=True))).astype(bf16)
    value_sum[...] += dot_nn(p.astype(bf16), g_h)
    key_sum[...] += dot_nn(ds, q_h)
    grad[rows, :SLOT] = (jnp.transpose(dot_nn(key_t[...], ds)) * scale).astype(bf16)

    @pl.when(i == pl.num_programs(0) - 1)
    def _():
        grad[:, SLOT : 2 * SLOT] = (key_sum[...] * scale).astype(bf16)
        grad[:, 2 * SLOT :] = value_sum[...].astype(bf16)


def self_backward(head, seg_k, seg_q, total, qkv, g):
    return pl.pallas_call(
        functools.partial(self_backward_body, head),
        grid=(ROW // TOK,),
        in_specs=[
            pl.BlockSpec((ROW, 1), lambda i: (0, 0)),
            pl.BlockSpec((1, TOK), lambda i: (0, i)),
            pl.BlockSpec((1, TOK), lambda i: (0, i)),
            pl.BlockSpec((TOK, 3 * SLOT), lambda i: (i, head)),
            pl.BlockSpec((ROW, 3 * SLOT), lambda i: (0, head)),
            pl.BlockSpec((TOK, SHARD), lambda i: (i, 0)),
        ],
        out_specs=pl.BlockSpec((ROW, 3 * SLOT), lambda i: (0, 0)),
        out_shape=jax.ShapeDtypeStruct((ROW, 3 * SLOT), bf16),
        scratch_shapes=[
            pltpu.VMEM((ROW, SLOT), f32),
            pltpu.VMEM((ROW, SLOT), f32),
            pltpu.VMEM((SLOT, ROW), bf16),
        ],
        compiler_params=params(),
    )(seg_k, seg_q, total, qkv, qkv, g)


def cross_forward_body(cap_q, cap_t, q, k, v, out):
    allowed = cap_q[...] == cap_t[...]
    mixed = []
    for h in range(HEADS):
        a, b = HEAD * h, HEAD * (h + 1)
        s = dot_nt(q[:, a:b], k[:, a:b])
        s = jnp.where(allowed, s, masked_score)
        top = jnp.max(s, axis=1, keepdims=True)
        p = jnp.exp2((s - top) * (scale * log2e))
        mass = jnp.sum(p, axis=1, keepdims=True)
        mixed.append(dot_nn(p.astype(bf16), v[:, a:b]) / mass)
    out[...] = jnp.concatenate(mixed, axis=1).astype(bf16)


def cross_forward(cap_q, cap_t, q, k, v):
    return pl.pallas_call(
        cross_forward_body,
        out_shape=jax.ShapeDtypeStruct((TOK, D), bf16),
        compiler_params=params(),
    )(cap_q, cap_t, q, k, v)


def cross_backward_body(cap_t, cap_q, q, k, v, g, grad_q, grad_k, grad_v):
    allowed = cap_t[...] == cap_q[...]
    dq, dk, dv = [], [], []
    for h in range(HEADS):
        a, b = HEAD * h, HEAD * (h + 1)
        q_h, k_h, v_h, g_h = q[:, a:b], k[:, a:b], v[:, a:b], g[:, a:b]
        s = jnp.where(allowed, dot_nt(k_h, q_h), masked_score)
        top = jnp.max(s, axis=0, keepdims=True)
        p = jnp.exp2((s - top) * (scale * log2e))
        p = p / jnp.sum(p, axis=0, keepdims=True)
        dp = dot_nt(v_h, g_h)
        ds = (p * (dp - jnp.sum(p * dp, axis=0, keepdims=True))).astype(bf16)
        dv.append(dot_nn(p.astype(bf16), g_h))
        dk.append(dot_nn(ds, q_h) * scale)
        dq.append(dot_tn(ds, k_h) * scale)
    grad_q[...] = jnp.concatenate(dq, axis=1).astype(bf16)
    grad_k[...] = jnp.concatenate(dk, axis=1).astype(bf16)
    grad_v[...] = jnp.concatenate(dv, axis=1).astype(bf16)


def cross_backward(cap_t, cap_q, q, k, v, g):
    return pl.pallas_call(
        cross_backward_body,
        out_shape=[
            jax.ShapeDtypeStruct((TOK, D), bf16),
            jax.ShapeDtypeStruct((TXT, D), bf16),
            jax.ShapeDtypeStruct((TXT, D), bf16),
        ],
        compiler_params=params(),
    )(cap_t, cap_q, q, k, v, g)


def mlp_body(core, x, g, mine, other, out, act_out, pre_out, grad_x, up, down, sem):
    @pl.when(pl.program_id(0) == 0)
    def _():
        def fetch(first, second):
            one = pltpu.make_async_copy(first, up, sem.at[0])
            two = pltpu.make_async_copy(second, down, sem.at[1])
            one.start()
            two.start()
            one.wait()
            two.wait()

        @pl.when(core[0] == 0)
        def _():
            fetch(mine, other)

        @pl.when(core[0] != 0)
        def _():
            fetch(other, mine)

    pre = dot_nn(x[...], up[...])
    grad_act = dot_nt(g[...], down[...])
    cdf = 0.5 * (1.0 + lax.erf(pre * (0.5**0.5)))
    density = jnp.exp2(pre * pre * (-0.5 * log2e)) * 0.3989422804014327
    act = (pre * cdf).astype(bf16)
    grad_pre = (grad_act * (cdf + pre * density)).astype(bf16)
    act_out[...] = act
    pre_out[...] = grad_pre
    out[...] = dot_nn(act, down[...]).astype(out.dtype)
    grad_x[...] = dot_nt(grad_pre, up[...]).astype(grad_x.dtype)


def mlp(core, x, g, mine, other):
    n = x.shape[0]
    rows = pl.BlockSpec((TOK, D), lambda i: (i, 0))
    hbm = pl.BlockSpec(memory_space=pl.ANY)
    return pl.pallas_call(
        mlp_body,
        grid=(n // TOK,),
        in_specs=[pl.BlockSpec(memory_space=pltpu.SMEM), rows, rows, hbm, hbm],
        out_specs=[rows] * 4,
        out_shape=[jax.ShapeDtypeStruct((n, D), bf16)] * 4,
        scratch_shapes=[
            pltpu.VMEM((D, D), bf16),
            pltpu.VMEM((D, D), bf16),
            pltpu.SemaphoreType.DMA((2,)),
        ],
        compiler_params=params(),
    )(core, x, g, mine, other)


def mlp_grads_body(core, *refs):
    xs, pres, acts, gs = refs[0:3], refs[3:6], refs[6:9], refs[9:12]
    keep, send = refs[12:]
    up = sum(dot_tn(x[...], p[...]) for x, p in zip(xs, pres)).astype(bf16)
    down = sum(dot_tn(a[...], g[...]) for a, g in zip(acts, gs)).astype(bf16)
    first = core[0] == 0

    @pl.when(first)
    def _():
        keep[...] = up
        send[...] = down

    @pl.when(jnp.logical_not(first))
    def _():
        keep[...] = down
        send[...] = up


def mlp_grads(core, xs, pres, acts, gs):
    def whole(x):
        return pl.BlockSpec(x.shape, lambda k: (0, 0))

    def part(x):
        return pl.BlockSpec((x.shape[0], 384), lambda k: (0, k))

    out = pl.BlockSpec((D, 384), lambda k: (0, k))
    return pl.pallas_call(
        mlp_grads_body,
        grid=(3,),
        in_specs=[pl.BlockSpec(memory_space=pltpu.SMEM)]
        + [whole(x) for x in xs]
        + [part(x) for x in pres]
        + [whole(x) for x in acts]
        + [part(x) for x in gs],
        out_specs=[out, out],
        out_shape=[jax.ShapeDtypeStruct((D, D), bf16)] * 2,
        compiler_params=params(),
    )(core, *xs, *pres, *acts, *gs)


def sort_hidden_body(x, up, down):
    for f in range(8):
        lanes = slice(SHARD * f, SHARD * (f + 1))
        up[:, 4 * SHARD * f : 4 * SHARD * (f + 1)] = jnp.concatenate(
            [x[2 * z, :, lanes] for z in range(4)], axis=1
        ).astype(f32)
    for z in range(4):
        down[SHARD * z : SHARD * (z + 1), :] = x[2 * z + 1].astype(f32)


def sort_hidden(x):
    return pl.pallas_call(
        sort_hidden_body,
        out_shape=[
            jax.ShapeDtypeStruct((SHARD, FF), f32),
            jax.ShapeDtypeStruct((4 * SHARD, D), f32),
        ],
        compiler_params=params(),
    )(x)


def norm_layer(values, norm_gain, norm_shift):
    center = values - jnp.mean(values, axis=-1, keepdims=True)
    spread = jnp.mean(center * center, axis=-1, keepdims=True)
    return center * lax.rsqrt(spread + norm_eps) * norm_gain + norm_shift


def row_block(x, index, rows):
    return lax.dynamic_slice_in_dim(x, index * rows, rows, axis=0)


def core_window(x, core):
    return lax.dynamic_slice_in_dim(x, core * STEP, WIN, axis=1)


def both_cores(x):
    return jnp.concatenate([x, shift(x, "c", 1)], axis=0)


def window_grad(left, right):
    core = lax.axis_index("c")
    sent = shift(core_window(right, 1 - core), "c", 1)
    rights = jnp.concatenate([core_window(right, core), sent], axis=0)
    return dot_tn(both_cores(left), rights).astype(bf16)


def sum_over_dp(x):
    part = lax.psum_scatter(x, "z", scatter_dimension=0, tiled=True)
    part = part + shift(part, "xh", 1)
    return lax.all_gather(part, "z", axis=0, tiled=True)


def whole_columns(mine, count):
    other = shift(mine, "c", 1)
    first = lax.axis_index("c") == 0
    low = jnp.where(first, mine, other).astype(f32)
    high = jnp.where(first, other, mine).astype(f32)
    return [
        jnp.concatenate(
            [low[SHARD * k : SHARD * (k + 1)], high[SHARD * k : SHARD * (k + 1), 128:]], axis=1
        )
        for k in range(count)
    ]


def sum_rows_over_dp(x):
    core = lax.axis_index("c")
    rows = x.shape[0] // 2
    mine = row_block(x, core, rows) + shift(row_block(x, 1 - core, rows), "c", 1)
    mine = sum_over_dp(mine)
    other = shift(mine, "c", 1)
    first = core == 0
    low = jnp.where(first, mine, other)
    high = jnp.where(first, other, mine)
    return jnp.concatenate([low, high], axis=0).astype(f32)


def sum_everywhere(x):
    for axis in ("y", "xl", "z", "xh", "c"):
        n = lax.axis_size(axis)
        x = sum([shift(x, axis, k) for k in range(1, n)], x)
    return x


def local(
    tokens,
    text_states,
    seg_lengths,
    caption_of_segment,
    text_lengths,
    ln1_gain,
    ln1_bias,
    w_query,
    w_key,
    w_value,
    w_out,
    ln2_gain,
    ln2_bias,
    c_query,
    w_text,
    c_key,
    c_value,
    c_out,
    ln3_gain,
    ln3_bias,
    w_up,
    w_down,
    cotangent,
):
    core = lax.axis_index("c")
    first_core = core == 0
    core_index = core.astype(jnp.int32)[None]
    quarter = lax.axis_index("z")
    first_row = peer(0, 0) * TOK

    ends = jnp.cumsum(seg_lengths[0])
    positions = jnp.arange(ROW, dtype=jnp.int32)
    segment = jnp.sum((positions[:, None] >= ends[None, :]).astype(jnp.int32), axis=1)
    own_segment = lax.dynamic_slice_in_dim(segment, first_row, TOK)
    text_row = jnp.arange(TXT, dtype=jnp.int32)
    text_pos = text_row // TXT_OWN * CAP_TOK + text_row % TXT_OWN
    text_caption = text_pos // CAP_LEN
    live = jnp.sum(
        jnp.where(
            text_caption[:, None] == jnp.arange(CAPS, dtype=jnp.int32)[None, :],
            text_lengths[0][None, :],
            0,
        ),
        axis=1,
    )
    query_caption = jnp.sum(
        jnp.where(
            own_segment[:, None] == jnp.arange(SEGS, dtype=jnp.int32)[None, :],
            caption_of_segment[0][None, :],
            0,
        ),
        axis=1,
    )
    text_live = (text_row % TXT_OWN < CAP_TOK) & (text_pos % CAP_LEN < live)
    text_key = jnp.where(text_live, text_caption, -1)

    rows_in = tokens[0].astype(f32)
    normed_one, pull_one = jax.vjp(norm_layer, rows_in, ln1_gain, ln1_bias)
    normed_one = normed_one.astype(bf16)
    n01, n10, n30 = gather_first(normed_one)

    packed = jnp.concatenate(
        [
            jnp.concatenate([w[:, SHARD * k : SHARD * (k + 1)] for k in range(8)], axis=0)
            for w in (w_query, w_key, w_value)
        ],
        axis=1,
    )
    heads_w = peers_parts(packed)
    n01, n10, heads_w = lax.optimization_barrier((n01, n10, heads_w))
    n31, n20, n11 = gather_second(n01, n10)

    grad_out = cotangent[0]
    grad_mlp = grad_out.astype(bf16)
    mlp_minus, mlp_plus = shift(grad_mlp, "z", 1), shift(grad_mlp, "z", -1)

    text_own = jnp.pad(after(text_states[0], heads_w), ((0, TXT_OWN - CAP_TOK), (0, 0)))
    text_columns = lax.all_to_all(text_own, FS, split_axis=1, concat_axis=0, tiled=True)
    context_part = dot_nn(text_columns, w_text).astype(bf16)
    context_own = lax.psum_scatter(context_part, FS, scatter_dimension=0, tiled=True)
    context = lax.all_gather(context_own, FS, axis=0, tiled=True)

    n31, n11, context_part = lax.optimization_barrier((n31, n11, context_part))
    n21 = gather_third(n31, n11)
    blank = jnp.zeros((D, SLOT - HEAD), bf16)
    heads_w = jnp.concatenate(
        [
            part
            for h in range(2)
            for k in range(3)
            for part in (heads_w[:, SHARD * k + HEAD * h : SHARD * k + HEAD * (h + 1)], blank)
        ],
        axis=1,
    )
    normed_all = place(normed_one, (n01, n10, n30), (n31, n20, n11), n21)
    mlp_far = jnp.concatenate(
        [shift(halves(mlp_minus)[0], "z", 1), shift(halves(mlp_plus)[1], "z", -1)], axis=0
    )
    mlp_near = jnp.concatenate([mlp_minus, mlp_plus], axis=0)

    first_mine = every_peer(after(jnp.where(first_core, w_out, c_query), context_part))
    pack = jnp.where(
        first_core,
        jnp.concatenate([c_key, c_out[:, :WIN]], axis=1),
        jnp.concatenate([c_value, c_out[:, STEP:]], axis=1),
    )
    pack = after(pack, normed_all)
    g01, g10, g30 = gather_first(pack)

    seg_col, seg_row = segment[:, None], segment[None, :]
    qkv = dot_nn(after(normed_all, context_own, mlp_far), heads_w).astype(bf16)
    head0, total0 = self_forward(0, seg_col, seg_row, qkv)
    g01, g10, g30, first_mine, head0 = lax.optimization_barrier(
        (g01, g10, g30, first_mine, head0)
    )
    first_other = shift(first_mine, "c", 1)
    g31, g20, g11 = gather_second(g01, g10)
    head1, total1 = self_forward(1, seg_col, seg_row, after(qkv, head0))
    attended = lax.all_to_all(
        jnp.concatenate([head0, head1], axis=1), FS, split_axis=0, concat_axis=1, tiled=True
    )
    g31, g20, g11, first_other, attended = lax.optimization_barrier(
        (g31, g20, g11, first_other, attended)
    )
    square_mine = place(pack, (g01, g10, g30), (g31, g20, g11), gather_third(g31, g11))
    square_other = shift(square_mine, "c", 1)
    full_out = jnp.where(first_core, first_mine, first_other)
    after_self = rows_in + dot_nn(attended, full_out)
    full_cquery = jnp.where(first_core, first_other, first_mine)

    up_own = jnp.concatenate(
        [
            lax.dynamic_slice(w_up, (0, 4 * SHARD * k + SHARD * quarter), (SHARD, SHARD))
            for k in range(8)
        ],
        axis=1,
    )
    hidden_own = jnp.where(first_core, up_own, row_block(w_down, quarter, SHARD))
    hidden_mine = every_peer(after(hidden_own, attended))
    hidden_other = shift(hidden_mine, "c", 1)

    normed_two, pull_two = jax.vjp(norm_layer, after_self, ln2_gain, ln2_bias)
    normed_two = normed_two.astype(bf16)
    cross_query = dot_nn(normed_two, full_cquery).astype(bf16)
    context = after(context, after_self, hidden_mine)
    kv_mine = dot_nn(context, square_mine[:, :D]).astype(bf16)
    kv_other = dot_nn(context, square_other[:, :D]).astype(bf16)
    cross_key = jnp.where(first_core, kv_mine, kv_other)
    cross_value = jnp.where(first_core, kv_other, kv_mine)
    full_cout = jnp.concatenate(
        [
            jnp.where(first_core, square_mine[:, D:], square_other[:, D:]),
            jnp.where(first_core, square_other[:, D + 128 :], square_mine[:, D + 128 :]),
        ],
        axis=1,
    )
    cross_mixed = cross_forward(
        query_caption[:, None], text_key[None, :], cross_query, cross_key, cross_value
    )
    after_cross = after_self + dot_nn(cross_mixed, full_cout)

    normed_three, pull_three = jax.vjp(norm_layer, after_cross, ln3_gain, ln3_bias)
    normed_three = normed_three.astype(bf16)
    three_minus, three_plus = shift(normed_three, "z", 1), shift(normed_three, "z", -1)
    weights = (hidden_mine, hidden_other)
    out_own, act_own, pre_own, back_own = mlp(core_index, normed_three, grad_mlp, *weights)
    three_minus, three_plus, out_own = lax.optimization_barrier(
        (three_minus, three_plus, out_own)
    )
    three_far = jnp.concatenate(
        [shift(halves(three_minus)[0], "z", 1), shift(halves(three_plus)[1], "z", -1)], axis=0
    )
    three_near = jnp.concatenate([three_minus, three_plus], axis=0)
    out_near, act_near, pre_near, back_near = mlp(core_index, three_near, mlp_near, *weights)
    out_far, act_far, pre_far, back_far = mlp(
        core_index, after(three_far, out_near), mlp_far, *weights
    )
    back_minus, back_plus = reduce_z(back_far, back_near[:TOK], back_near[TOK:])
    keep, send = mlp_grads(
        core_index,
        (normed_three, three_near, after(three_far, back_minus, back_plus)),
        (pre_own, pre_near, pre_far),
        (act_own, act_near, act_far),
        (grad_mlp, mlp_near, mlp_far),
    )
    back_minus, back_plus = shift(back_minus, "z", -1), shift(back_plus, "z", 1)
    hidden_sum = keep + shift(send, "c", 1)
    grad_three = back_own.astype(f32) + back_minus.astype(f32) + back_plus.astype(f32)
    grad_cross_in, grad_ln3_gain, grad_ln3_bias = pull_three(grad_three)
    grad_after_cross = grad_out + grad_cross_in
    grad_cross_branch = grad_after_cross.astype(bf16)
    grad_cross_mixed = dot_nt(grad_cross_branch, full_cout).astype(bf16)

    hidden_parts = peers_parts(hidden_sum)
    grad_cquery_rows, grad_key_part, grad_value_part = cross_backward(
        text_key[:, None],
        query_caption[None, :],
        cross_query,
        cross_key,
        cross_value,
        after(grad_cross_mixed, hidden_sum),
    )
    square = jnp.concatenate(
        [
            window_grad(cross_mixed, grad_cross_branch),
            window_grad(normed_two, grad_cquery_rows),
            window_grad(context, grad_key_part),
            window_grad(context, grad_value_part),
        ],
        axis=1,
    )

    def square_chunk(dy, dx):
        return row_block(square, peer(dy, dx), SHARD)

    grad_cquery_rows, square, hidden_parts = lax.optimization_barrier(
        (grad_cquery_rows, square, hidden_parts)
    )
    s_lo, s_hi, s20 = reduce_first(square_chunk)
    grad_self_in, grad_ln2_gain, grad_ln2_bias = pull_two(dot_nt(grad_cquery_rows, full_cquery))
    grad_after_self = grad_after_cross + grad_self_in
    grad_self_branch = grad_after_self.astype(bf16)
    grad_attended = dot_nt(grad_self_branch, full_out).astype(bf16)
    grad_heads = lax.all_to_all(grad_attended, FS, split_axis=1, concat_axis=0, tiled=True)

    hidden_grad = sum_parts(hidden_parts).astype(bf16)
    hidden_grad = hidden_grad + shift(hidden_grad, "xh", 1)
    hidden_grad = lax.all_gather(hidden_grad, ("z", "c"), axis=0)
    out_window = window_grad(attended, grad_self_branch)
    grad_m = jnp.where(first_core, grad_key_part, grad_value_part)
    grad_o = jnp.where(first_core, grad_value_part, grad_key_part)
    grad_m, grad_o, grad_attended = lax.optimization_barrier((grad_m, grad_o, grad_attended))
    context_part = dot_nt(grad_m, square_mine[:, :D]) + dot_nt(grad_o, square_other[:, :D])
    grad_heads, out_window, context_part = lax.optimization_barrier(
        (grad_heads, out_window, context_part.astype(bf16))
    )
    context_parts = peers_parts(context_part)

    grad_head0 = self_backward(0, seg_col, seg_row, total0, qkv, grad_heads)
    s_lo, s_hi, s20, context_parts, grad_head0 = lax.optimization_barrier(
        (s_lo, s_hi, s20, context_parts, grad_head0)
    )
    out_parts = peers_parts(after(out_window, context_parts))
    s11, s31 = reduce_second(square_chunk, s_lo, s_hi)
    out_minus, out_plus = reduce_z(after(out_far, grad_head0), out_near[:TOK], out_near[TOK:])
    grad_head1 = self_backward(1, seg_col, seg_row, total1, qkv, after(grad_heads, grad_head0))
    s11, s31, hidden_grad, out_parts, out_minus, out_plus, grad_head1 = lax.optimization_barrier(
        (s11, s31, hidden_grad, out_parts, out_minus, out_plus, grad_head1)
    )
    context_grad = sum_parts(context_parts).astype(bf16)
    context_grad = every_peer(after(context_grad, out_parts))
    square_parts = reduce_third(square_chunk, s20, s11, s31)
    grad_qkv = jnp.concatenate([grad_head0, grad_head1], axis=1)
    normed_part = dot_nt(grad_qkv, heads_w).astype(bf16)

    def normed_chunk(dy, dx):
        return row_block(normed_part, peer(dy, dx), TOK)

    n_lo, n_hi, n20 = reduce_first(normed_chunk)
    grad_heads_w = dot_tn(normed_all, after(grad_qkv, normed_part)).astype(bf16)
    grad_heads_w = jnp.concatenate(
        [
            grad_heads_w[:, SLOT * (3 * h + k) : SLOT * (3 * h + k) + HEAD]
            for k in range(3)
            for h in range(2)
        ],
        axis=1,
    )
    grad_qkv_w = peers_parts(after(grad_heads_w, context_grad))
    n_lo, n_hi, *square_parts = lax.optimization_barrier((n_lo, n_hi, *square_parts))
    n11, n31 = reduce_second(normed_chunk, n_lo, n_hi)
    out_minus, out_plus = shift(out_minus, "z", -1), shift(out_plus, "z", 1)
    square = reduce_last(square_chunk, *square_parts).astype(bf16)
    square = jnp.concatenate(
        [square[:, WIN * k : WIN * (k + 1)] for k in range(4)]
        + [sum_parts(out_parts).astype(bf16), jnp.zeros((768 - 5 * SHARD, WIN), bf16)],
        axis=0,
    )
    square = sum_over_dp(square)
    grad_c_out, grad_c_query, grad_c_key, grad_c_value, grad_w_out = whole_columns(square, 5)
    grad_w_text = dot_tn(text_columns, context_grad).astype(bf16)
    text_part = dot_nt(context_grad, w_text).astype(bf16)
    grad_w_text = sum_rows_over_dp(grad_w_text)
    grad_w_up, grad_w_down = sort_hidden(hidden_grad)
    outputs = (
        after_cross + out_own.astype(f32) + out_minus.astype(f32) + out_plus.astype(f32)
    )

    n11, n31, grad_qkv_w = lax.optimization_barrier((n11, n31, grad_qkv_w))
    grad_normed_one = reduce_last(normed_chunk, *reduce_third(normed_chunk, n20, n11, n31))
    grad_qkv_w = jnp.concatenate(
        [
            jnp.concatenate(
                [
                    grad_qkv_w[SHARD * p : SHARD * (p + 1), SHARD * k : SHARD * (k + 1)]
                    for p in range(8)
                ],
                axis=1,
            )
            for k in range(3)
        ]
        + [jnp.zeros((512 - 3 * SHARD, D), bf16)],
        axis=0,
    )
    half = row_block(grad_qkv_w, core, 256) + shift(
        row_block(grad_qkv_w, 1 - core, 256), "c", 1
    )
    half = sum_parts(peers_parts(half, ("xh", "z"))).astype(bf16)
    half = every_peer(half, ("xh", "z"))
    other_half = shift(half, "c", 1)
    grad_qkv_w = jnp.concatenate(
        [jnp.where(first_core, half, other_half), jnp.where(first_core, other_half, half)], axis=0
    ).astype(f32)
    grad_w_query, grad_w_key, grad_w_value = (
        grad_qkv_w[SHARD * k : SHARD * (k + 1)] for k in range(3)
    )
    grad_text = lax.all_to_all(
        after(text_part, half), FS, split_axis=0, concat_axis=1, tiled=True
    )
    grad_text = grad_text[:CAP_TOK].astype(f32)
    grad_rows_in, grad_ln1_gain, grad_ln1_bias = pull_one(grad_normed_one)
    grad_tokens = grad_after_self + grad_rows_in
    norms = sum_everywhere(
        jnp.stack(
            [
                grad_ln1_gain,
                grad_ln1_bias,
                grad_ln2_gain,
                grad_ln2_bias,
                grad_ln3_gain,
                grad_ln3_bias,
            ]
        )
    )
    return (
        outputs[None],
        grad_tokens[None],
        grad_text[None],
        norms[0],
        norms[1],
        grad_w_query,
        grad_w_key,
        grad_w_value,
        grad_w_out,
        norms[2],
        norms[3],
        grad_c_query,
        grad_w_text,
        grad_c_key,
        grad_c_value,
        grad_c_out,
        norms[4],
        norms[5],
        grad_w_up,
        grad_w_down,
    )


def solution(mesh):
    split = Mesh(mesh.devices.reshape(2, 4, 2, 4, 2), ("xh", "z", "c", "y", "xl"))
    dp = ("xh", "z", "c")
    rows = P(dp, FS, None)
    per_row = P(dp, None)
    weight = P(FS, None)
    rep = P()
    in_specs = (
        rows, rows, per_row, per_row, per_row,
        rep, rep, weight, weight, weight, weight,
        rep, rep, weight, weight, weight, weight, weight,
        rep, rep, weight, weight, rows,
    )
    out_specs = (
        rows, rows, rows,
        rep, rep, weight, weight, weight, weight,
        rep, rep, weight, weight, weight, weight, weight,
        rep, rep, weight, weight,
    )
    return jax.shard_map(
        local, mesh=split, in_specs=in_specs, out_specs=out_specs, check_vma=False
    )
```

```python
import functools

import jax
import jax.numpy as jnp
from jax import lax
from jax.experimental import pallas as pl
from jax.experimental.pallas import tpu as pltpu
from jax.sharding import Mesh
from jax.sharding import PartitionSpec as P

HEADS = 16
HEAD = 72
D = 1152
FF = 4608
CAP_TOK = 60
TXT_OWN = 64
TXT = 8 * TXT_OWN
TOK = 256
ROW = 2048
CAP_LEN = 120
SEGS = 3
CAPS = 4
SHARD = 144
SLOT = 128
WIN = 640
STEP = 512

bf16 = jnp.bfloat16
f32 = jnp.float32
norm_eps = 1e-06
masked_score = -1e30
scale = HEAD ** (-0.5)
log2e = 1.4426950408889634
FS = ("y", "xl")
VMEM = 60 * 1024 * 1024


def dot_nn(a, b):
    return lax.dot_general(a, b, (((1,), (0,)), ((), ())), preferred_element_type=f32)


def dot_nt(a, b):
    return lax.dot_general(a, b, (((1,), (1,)), ((), ())), preferred_element_type=f32)


def dot_tn(a, b):
    return lax.dot_general(a, b, (((0,), (0,)), ((), ())), preferred_element_type=f32)


def params():
    return pltpu.CompilerParams(vmem_limit_bytes=VMEM)


def shift(x, axis, by):
    n = lax.axis_size(axis)
    return lax.ppermute(x, axis, [(i, (i + by) % n) for i in range(n)])


def halves(x):
    h = (x.shape[0] // 2 + 15) // 16 * 16
    return x[:h], x[h:]


def after(x, *others):
    return lax.optimization_barrier((x, *others))[0] if others else x


def gather_first(x):
    return shift(x, "xl", 1), shift(x, "y", -1), shift(x, "y", 1)


def gather_second(x01, x10):
    return shift(x01, "y", 1), shift(x10, "y", -1), shift(x10, "xl", 1)


def gather_third(x31, x11):
    return shift(halves(x11)[0], "y", -1), shift(halves(x31)[1], "y", 1)


NEAR = ((0, 0), (0, 1), (1, 0), (3, 0))
NEXT = ((3, 1), (2, 0), (1, 1))
LAST = (2, 1)


def reduce_first(chunk):
    lo, hi = halves(chunk(2, 1))
    return shift(lo, "y", 1), shift(hi, "y", -1), shift(chunk(2, 0), "y", 1)


def reduce_second(chunk, lo, hi):
    h = lo.shape[0]
    c11, c31 = chunk(1, 1), chunk(3, 1)
    c11 = jnp.concatenate([c11[:h] + lo, c11[h:]], axis=0)
    c31 = jnp.concatenate([c31[:h], c31[h:] + hi], axis=0)
    return shift(c11, "xl", 1), shift(c31, "y", -1)


def reduce_third(chunk, c20, c11, c31):
    return (
        shift(chunk(1, 0) + c20 + c11, "y", 1),
        shift(chunk(0, 1) + c31, "xl", 1),
        shift(chunk(3, 0), "y", -1),
    )


def reduce_last(chunk, *parts):
    return sum([p.astype(f32) for p in parts], chunk(0, 0).astype(f32))


def every_peer(x, axes=FS):
    n = lax.axis_size(axes)
    copies = jnp.broadcast_to(x[None], (n, *x.shape)).reshape(n * x.shape[0], x.shape[1])
    return lax.all_to_all(copies, axes, 0, 0, tiled=True)


def peers_parts(x, axes=FS):
    return lax.all_to_all(x, axes, 0, 0, tiled=True)


def sum_parts(parts):
    return jnp.sum(parts.reshape(8, -1, parts.shape[1]).astype(f32), axis=0)


def reduce_z(far, minus, plus):
    lo, hi = halves(far)
    lo, hi = shift(lo, "z", -1), shift(hi, "z", 1)
    h = lo.shape[0]
    return (
        jnp.concatenate([minus[:h] + lo, minus[h:]], axis=0),
        jnp.concatenate([plus[:h], plus[h:] + hi], axis=0),
    )


def peer(dy, dx):
    return ((lax.axis_index("y") + dy) % 4) * 2 + (lax.axis_index("xl") ^ dx)


def place(own, first, second, third):
    lo = third[0].shape[0]
    rows, cols = own.shape
    pieces = [(x, p, 0) for x, p in zip((own, *first), NEAR)]
    pieces += [(x, p, 0) for x, p in zip(second, NEXT)]
    pieces += [(third[0], LAST, 0), (third[1], LAST, lo)]
    count = len(pieces)

    def body(where, *refs):
        ins, out, sem = refs[:count], refs[count], refs[-1]
        started = []
        for k, (x, _, off) in enumerate(pieces):
            row = pl.multiple_of(where[k] * rows + off, 16)
            one = pltpu.make_async_copy(ins[k], out.at[pl.ds(row, x.shape[0])], sem.at[k])
            one.start()
            started.append(one)
        for one in started:
            one.wait()

    return pl.pallas_call(
        body,
        in_specs=[pl.BlockSpec(memory_space=pltpu.SMEM)]
        + [pl.BlockSpec(memory_space=pl.ANY)] * count,
        out_specs=pl.BlockSpec(memory_space=pltpu.VMEM),
        out_shape=jax.ShapeDtypeStruct((8 * rows, cols), own.dtype),
        scratch_shapes=[pltpu.SemaphoreType.DMA((count,))],
        compiler_params=params(),
    )(
        jnp.stack([peer(*p) for _, p, _ in pieces]).astype(jnp.int32),
        *[x for x, _, _ in pieces],
    )


def pack_heads_body(wq, wk, wv, out):
    for p in range(8):
        rows = slice(SHARD * p, SHARD * (p + 1))
        out[rows, :] = jnp.concatenate([w[:, rows] for w in (wq, wk, wv)], axis=1)


def pack_heads(*weights):
    return pl.pallas_call(
        pack_heads_body,
        out_shape=jax.ShapeDtypeStruct((D, 3 * SHARD), bf16),
        compiler_params=params(),
    )(*weights)


def spread_heads_body(x, out):
    blank = jnp.zeros((D, SLOT - HEAD), bf16)
    for h in range(2):
        for k in range(3):
            first = SHARD * k + HEAD * h
            slot = SLOT * (3 * h + k)
            out[:, slot : slot + SLOT] = jnp.concatenate(
                [x[:, first : first + HEAD], blank], axis=1
            )


def spread_heads(x):
    return pl.pallas_call(
        spread_heads_body,
        out_shape=jax.ShapeDtypeStruct((D, 6 * SLOT), bf16),
        compiler_params=params(),
    )(x)


def self_forward_body(seg_q, seg_k, q, kv, out, total):
    s = dot_nt(q[:, :SLOT], kv[:, SLOT : 2 * SLOT])
    s = jnp.where(seg_q[...] == seg_k[...], s, masked_score)
    top = jnp.max(s, axis=1, keepdims=True)
    p = jnp.exp2((s - top) * (scale * log2e))
    mass = jnp.sum(p, axis=1, keepdims=True)
    out[...] = (dot_nn(p.astype(bf16), kv[:, 2 * SLOT :]) / mass)[:, :HEAD].astype(bf16)
    log_total = top * (scale * log2e) + jnp.log2(mass)
    total[...] = jnp.transpose(jnp.broadcast_to(log_total, (TOK, SLOT)))[0:1, :]


def self_forward(head, seg_q, seg_k, qkv):
    return pl.pallas_call(
        self_forward_body,
        grid=(ROW // TOK,),
        in_specs=[
            pl.BlockSpec((TOK, 1), lambda i: (i, 0)),
            pl.BlockSpec((1, ROW), lambda i: (0, 0)),
            pl.BlockSpec((TOK, 3 * SLOT), lambda i: (i, head)),
            pl.BlockSpec((ROW, 3 * SLOT), lambda i: (0, head)),
        ],
        out_specs=[
            pl.BlockSpec((TOK, HEAD), lambda i: (i, 0)),
            pl.BlockSpec((1, TOK), lambda i: (0, i)),
        ],
        out_shape=[
            jax.ShapeDtypeStruct((ROW, HEAD), bf16),
            jax.ShapeDtypeStruct((1, ROW), f32),
        ],
        compiler_params=params(),
    )(seg_q, seg_k, qkv, qkv)


def self_backward_body(head, seg_k, seg_q, total, q, kv, g, grad, key_sum, value_sum, key_t):
    i = pl.program_id(0)

    @pl.when(i == 0)
    def _():
        key_sum[...] = jnp.zeros_like(key_sum)
        value_sum[...] = jnp.zeros_like(value_sum)
        key_t[...] = jnp.transpose(kv[:, SLOT : 2 * SLOT])

    rows = pl.ds(pl.multiple_of(i * TOK, TOK), TOK)
    q_h, k_h, v_h = q[:, :SLOT], kv[:, SLOT : 2 * SLOT], kv[:, 2 * SLOT :]
    g_both = g[...]
    g_h = jnp.concatenate(
        [g_both[:, HEAD * head : HEAD * (head + 1)], jnp.zeros((TOK, SLOT - HEAD), bf16)], axis=1
    )
    p = jnp.exp2(dot_nt(k_h, q_h) * (scale * log2e) - total[...])
    p = jnp.where(seg_k[...] == seg_q[...], p, 0.0)
    dp = dot_nt(v_h, g_h)
    ds = (p * (dp - jnp.sum(p * dp, axis=0, keepdims=True))).astype(bf16)
    value_sum[...] += dot_nn(p.astype(bf16), g_h)
    key_sum[...] += dot_nn(ds, q_h)
    grad[rows, :SLOT] = (jnp.transpose(dot_nn(key_t[...], ds)) * scale).astype(bf16)

    @pl.when(i == pl.num_programs(0) - 1)
    def _():
        grad[:, SLOT : 2 * SLOT] = (key_sum[...] * scale).astype(bf16)
        grad[:, 2 * SLOT :] = value_sum[...].astype(bf16)


def self_backward(head, seg_k, seg_q, total, qkv, g):
    return pl.pallas_call(
        functools.partial(self_backward_body, head),
        grid=(ROW // TOK,),
        in_specs=[
            pl.BlockSpec((ROW, 1), lambda i: (0, 0)),
            pl.BlockSpec((1, TOK), lambda i: (0, i)),
            pl.BlockSpec((1, TOK), lambda i: (0, i)),
            pl.BlockSpec((TOK, 3 * SLOT), lambda i: (i, head)),
            pl.BlockSpec((ROW, 3 * SLOT), lambda i: (0, head)),
            pl.BlockSpec((TOK, SHARD), lambda i: (i, 0)),
        ],
        out_specs=pl.BlockSpec((ROW, 3 * SLOT), lambda i: (0, 0)),
        out_shape=jax.ShapeDtypeStruct((ROW, 3 * SLOT), bf16),
        scratch_shapes=[
            pltpu.VMEM((ROW, SLOT), f32),
            pltpu.VMEM((ROW, SLOT), f32),
            pltpu.VMEM((SLOT, ROW), bf16),
        ],
        compiler_params=params(),
    )(seg_k, seg_q, total, qkv, qkv, g)


def cross_forward_body(cap_q, cap_t, q, k, v, out):
    allowed = cap_q[...] == cap_t[...]
    mixed = []
    for h in range(HEADS):
        a, b = HEAD * h, HEAD * (h + 1)
        s = dot_nt(q[:, a:b], k[:, a:b])
        s = jnp.where(allowed, s, masked_score)
        top = jnp.max(s, axis=1, keepdims=True)
        p = jnp.exp2((s - top) * (scale * log2e))
        mass = jnp.sum(p, axis=1, keepdims=True)
        mixed.append(dot_nn(p.astype(bf16), v[:, a:b]) / mass)
    out[...] = jnp.concatenate(mixed, axis=1).astype(bf16)


def cross_forward(cap_q, cap_t, q, k, v):
    return pl.pallas_call(
        cross_forward_body,
        out_shape=jax.ShapeDtypeStruct((TOK, D), bf16),
        compiler_params=params(),
    )(cap_q, cap_t, q, k, v)


def cross_backward_body(cap_t, cap_q, q, k, v, g, grad_q, grad_k, grad_v):
    allowed = cap_t[...] == cap_q[...]
    dq, dk, dv = [], [], []
    for h in range(HEADS):
        a, b = HEAD * h, HEAD * (h + 1)
        q_h, k_h, v_h, g_h = q[:, a:b], k[:, a:b], v[:, a:b], g[:, a:b]
        s = jnp.where(allowed, dot_nt(k_h, q_h), masked_score)
        top = jnp.max(s, axis=0, keepdims=True)
        p = jnp.exp2((s - top) * (scale * log2e))
        p = p / jnp.sum(p, axis=0, keepdims=True)
        dp = dot_nt(v_h, g_h)
        ds = (p * (dp - jnp.sum(p * dp, axis=0, keepdims=True))).astype(bf16)
        dv.append(dot_nn(p.astype(bf16), g_h))
        dk.append(dot_nn(ds, q_h) * scale)
        dq.append(dot_tn(ds, k_h) * scale)
    grad_q[...] = jnp.concatenate(dq, axis=1).astype(bf16)
    grad_k[...] = jnp.concatenate(dk, axis=1).astype(bf16)
    grad_v[...] = jnp.concatenate(dv, axis=1).astype(bf16)


def cross_backward(cap_t, cap_q, q, k, v, g):
    return pl.pallas_call(
        cross_backward_body,
        out_shape=[
            jax.ShapeDtypeStruct((TOK, D), bf16),
            jax.ShapeDtypeStruct((TXT, D), bf16),
            jax.ShapeDtypeStruct((TXT, D), bf16),
        ],
        compiler_params=params(),
    )(cap_t, cap_q, q, k, v, g)


def mlp_body(core, x, g, mine, other, out, act_out, pre_out, grad_x, up, down, sem):
    @pl.when(pl.program_id(0) == 0)
    def _():
        def fetch(first, second):
            one = pltpu.make_async_copy(first, up, sem.at[0])
            two = pltpu.make_async_copy(second, down, sem.at[1])
            one.start()
            two.start()
            one.wait()
            two.wait()

        @pl.when(core[0] == 0)
        def _():
            fetch(mine, other)

        @pl.when(core[0] != 0)
        def _():
            fetch(other, mine)

    pre = dot_nn(x[...], up[...])
    grad_act = dot_nt(g[...], down[...])
    cdf = 0.5 * (1.0 + lax.erf(pre * (0.5**0.5)))
    density = jnp.exp2(pre * pre * (-0.5 * log2e)) * 0.3989422804014327
    act = (pre * cdf).astype(bf16)
    grad_pre = (grad_act * (cdf + pre * density)).astype(bf16)
    act_out[...] = act
    pre_out[...] = grad_pre
    out[...] = dot_nn(act, down[...]).astype(out.dtype)
    grad_x[...] = dot_nt(grad_pre, up[...]).astype(grad_x.dtype)


def mlp(core, x, g, mine, other):
    n = x.shape[0]
    rows = pl.BlockSpec((TOK, D), lambda i: (i, 0))
    hbm = pl.BlockSpec(memory_space=pl.ANY)
    return pl.pallas_call(
        mlp_body,
        grid=(n // TOK,),
        in_specs=[pl.BlockSpec(memory_space=pltpu.SMEM), rows, rows, hbm, hbm],
        out_specs=[rows] * 4,
        out_shape=[jax.ShapeDtypeStruct((n, D), bf16)] * 4,
        scratch_shapes=[
            pltpu.VMEM((D, D), bf16),
            pltpu.VMEM((D, D), bf16),
            pltpu.SemaphoreType.DMA((2,)),
        ],
        compiler_params=params(),
    )(core, x, g, mine, other)


def mlp_grads_body(core, *refs):
    xs, pres, acts, gs = refs[0:3], refs[3:6], refs[6:9], refs[9:12]
    keep, send = refs[12:]
    up = sum(dot_tn(x[...], p[...]) for x, p in zip(xs, pres)).astype(bf16)
    down = sum(dot_tn(a[...], g[...]) for a, g in zip(acts, gs)).astype(bf16)
    first = core[0] == 0

    @pl.when(first)
    def _():
        keep[...] = up
        send[...] = down

    @pl.when(jnp.logical_not(first))
    def _():
        keep[...] = down
        send[...] = up


def mlp_grads(core, xs, pres, acts, gs):
    def whole(x):
        return pl.BlockSpec(x.shape, lambda k: (0, 0))

    def part(x):
        return pl.BlockSpec((x.shape[0], 384), lambda k: (0, k))

    out = pl.BlockSpec((D, 384), lambda k: (0, k))
    return pl.pallas_call(
        mlp_grads_body,
        grid=(3,),
        in_specs=[pl.BlockSpec(memory_space=pltpu.SMEM)]
        + [whole(x) for x in xs]
        + [part(x) for x in pres]
        + [whole(x) for x in acts]
        + [part(x) for x in gs],
        out_specs=[out, out],
        out_shape=[jax.ShapeDtypeStruct((D, D), bf16)] * 2,
        compiler_params=params(),
    )(core, *xs, *pres, *acts, *gs)


def sort_hidden_body(x, up, down):
    for f in range(8):
        lanes = slice(SHARD * f, SHARD * (f + 1))
        up[:, 4 * SHARD * f : 4 * SHARD * (f + 1)] = jnp.concatenate(
            [x[2 * z, :, lanes] for z in range(4)], axis=1
        ).astype(f32)
    for z in range(4):
        down[SHARD * z : SHARD * (z + 1), :] = x[2 * z + 1].astype(f32)


def sort_hidden(x):
    return pl.pallas_call(
        sort_hidden_body,
        out_shape=[
            jax.ShapeDtypeStruct((SHARD, FF), f32),
            jax.ShapeDtypeStruct((4 * SHARD, D), f32),
        ],
        compiler_params=params(),
    )(x)


def norm_layer(values, norm_gain, norm_shift):
    center = values - jnp.mean(values, axis=-1, keepdims=True)
    spread = jnp.mean(center * center, axis=-1, keepdims=True)
    return center * lax.rsqrt(spread + norm_eps) * norm_gain + norm_shift


def row_block(x, index, rows):
    return lax.dynamic_slice_in_dim(x, index * rows, rows, axis=0)


def core_window(x, core):
    return lax.dynamic_slice_in_dim(x, core * STEP, WIN, axis=1)


def both_cores(x):
    return jnp.concatenate([x, shift(x, "c", 1)], axis=0)


def window_grad(left, right):
    core = lax.axis_index("c")
    sent = shift(core_window(right, 1 - core), "c", 1)
    rights = jnp.concatenate([core_window(right, core), sent], axis=0)
    return dot_tn(both_cores(left), rights).astype(bf16)


def sum_over_dp(x):
    part = lax.psum_scatter(x, "z", scatter_dimension=0, tiled=True)
    part = part + shift(part, "xh", 1)
    return every_peer(part, "z")


def whole_columns(mine, count):
    other = shift(mine, "c", 1)
    first = lax.axis_index("c") == 0
    low = jnp.where(first, mine, other).astype(f32)
    high = jnp.where(first, other, mine).astype(f32)
    return [
        jnp.concatenate(
            [low[SHARD * k : SHARD * (k + 1)], high[SHARD * k : SHARD * (k + 1), 128:]], axis=1
        )
        for k in range(count)
    ]


def sum_rows_over_dp(x):
    core = lax.axis_index("c")
    rows = x.shape[0] // 2
    mine = row_block(x, core, rows) + shift(row_block(x, 1 - core, rows), "c", 1)
    mine = sum_over_dp(mine)
    other = shift(mine, "c", 1)
    first = core == 0
    low = jnp.where(first, mine, other)
    high = jnp.where(first, other, mine)
    return jnp.concatenate([low, high], axis=0).astype(f32)


def sum_everywhere(x):
    for axis in ("y", "xl", "z", "xh", "c"):
        n = lax.axis_size(axis)
        x = sum([shift(x, axis, k) for k in range(1, n)], x)
    return x


def local(
    tokens,
    text_states,
    seg_lengths,
    caption_of_segment,
    text_lengths,
    ln1_gain,
    ln1_bias,
    w_query,
    w_key,
    w_value,
    w_out,
    ln2_gain,
    ln2_bias,
    c_query,
    w_text,
    c_key,
    c_value,
    c_out,
    ln3_gain,
    ln3_bias,
    w_up,
    w_down,
    cotangent,
):
    core = lax.axis_index("c")
    first_core = core == 0
    core_index = core.astype(jnp.int32)[None]
    quarter = lax.axis_index("z")
    first_row = peer(0, 0) * TOK

    ends = jnp.cumsum(seg_lengths[0])
    positions = jnp.arange(ROW, dtype=jnp.int32)
    segment = jnp.sum((positions[:, None] >= ends[None, :]).astype(jnp.int32), axis=1)
    own_segment = lax.dynamic_slice_in_dim(segment, first_row, TOK)
    text_row = jnp.arange(TXT, dtype=jnp.int32)
    text_pos = text_row // TXT_OWN * CAP_TOK + text_row % TXT_OWN
    text_caption = text_pos // CAP_LEN
    live = jnp.sum(
        jnp.where(
            text_caption[:, None] == jnp.arange(CAPS, dtype=jnp.int32)[None, :],
            text_lengths[0][None, :],
            0,
        ),
        axis=1,
    )
    query_caption = jnp.sum(
        jnp.where(
            own_segment[:, None] == jnp.arange(SEGS, dtype=jnp.int32)[None, :],
            caption_of_segment[0][None, :],
            0,
        ),
        axis=1,
    )
    text_live = (text_row % TXT_OWN < CAP_TOK) & (text_pos % CAP_LEN < live)
    text_key = jnp.where(text_live, text_caption, -1)

    rows_in = tokens[0].astype(f32)
    normed_one, pull_one = jax.vjp(norm_layer, rows_in, ln1_gain, ln1_bias)
    normed_one = normed_one.astype(bf16)
    n01, n10, n30 = gather_first(normed_one)

    heads_w = peers_parts(pack_heads(after(w_query, normed_one), w_key, w_value))
    n01, n10, n30 = lax.optimization_barrier((n01, n10, n30))
    n31, n20, n11 = gather_second(n01, n10)
    n31, n20, n11, heads_w = lax.optimization_barrier((n31, n20, n11, heads_w))
    n21 = gather_third(n31, n11)

    text_own = jnp.pad(after(text_states[0], n11), ((0, TXT_OWN - CAP_TOK), (0, 0)))
    text_columns = lax.all_to_all(text_own, FS, split_axis=1, concat_axis=0, tiled=True)
    heads_w = spread_heads(heads_w)
    normed_all = place(
        after(normed_one, text_columns), (n01, n10, n30), (n31, n20, n11), n21
    )
    context_part = dot_nn(after(text_columns, normed_all), w_text).astype(bf16)
    context_own = lax.psum_scatter(context_part, FS, scatter_dimension=0, tiled=True)

    grad_out = cotangent[0]
    grad_mlp = grad_out.astype(bf16)
    grad_sent = after(grad_mlp, normed_all)
    mlp_minus, mlp_plus = shift(grad_sent, "z", 1), shift(grad_sent, "z", -1)

    first_mine = every_peer(after(jnp.where(first_core, w_out, c_query), normed_all))
    pack = jnp.where(
        first_core,
        jnp.concatenate([c_key, c_out[:, :WIN]], axis=1),
        jnp.concatenate([c_value, c_out[:, STEP:]], axis=1),
    )
    pack = after(pack, normed_all)
    g01, g10, g30 = gather_first(pack)

    seg_col, seg_row = segment[:, None], segment[None, :]
    qkv = dot_nn(after(normed_all, context_part), heads_w).astype(bf16)
    head0, total0 = self_forward(0, seg_col, seg_row, qkv)
    g01, g10, g30, mlp_minus, mlp_plus, head0 = lax.optimization_barrier(
        (g01, g10, g30, mlp_minus, mlp_plus, head0)
    )
    g31, g20, g11 = gather_second(g01, g10)
    head1, total1 = self_forward(1, seg_col, seg_row, after(qkv, head0))
    g31, g20, g11, first_mine, head1 = lax.optimization_barrier(
        (g31, g20, g11, first_mine, head1)
    )
    first_other = shift(first_mine, "c", 1)
    attended = lax.all_to_all(
        jnp.concatenate([head0, head1], axis=1), FS, split_axis=0, concat_axis=1, tiled=True
    )
    mlp_far = jnp.concatenate(
        [shift(halves(mlp_minus)[0], "z", 1), shift(halves(mlp_plus)[1], "z", -1)], axis=0
    )
    mlp_near = jnp.concatenate([mlp_minus, mlp_plus], axis=0)
    attended, context_own = lax.optimization_barrier((attended, context_own))
    context = every_peer(context_own)
    square_mine = place(pack, (g01, g10, g30), (g31, g20, g11), gather_third(g31, g11))
    square_other = shift(square_mine, "c", 1)
    full_out = jnp.where(first_core, first_mine, first_other)
    after_self = rows_in + dot_nn(attended, full_out)
    full_cquery = jnp.where(first_core, first_other, first_mine)

    up_own = jnp.concatenate(
        [
            lax.dynamic_slice(w_up, (0, 4 * SHARD * k + SHARD * quarter), (SHARD, SHARD))
            for k in range(8)
        ],
        axis=1,
    )
    hidden_own = jnp.where(first_core, up_own, row_block(w_down, quarter, SHARD))
    hidden_mine = every_peer(after(hidden_own, context))

    normed_two, pull_two = jax.vjp(norm_layer, after_self, ln2_gain, ln2_bias)
    normed_two = normed_two.astype(bf16)
    cross_query = dot_nn(normed_two, full_cquery).astype(bf16)
    context = after(context, cross_query)
    kv_mine = dot_nn(context, square_mine[:, :D]).astype(bf16)
    kv_other = dot_nn(context, square_other[:, :D]).astype(bf16)
    cross_key = jnp.where(first_core, kv_mine, kv_other)
    cross_value = jnp.where(first_core, kv_other, kv_mine)
    full_cout = jnp.concatenate(
        [
            jnp.where(first_core, square_mine[:, D:], square_other[:, D:]),
            jnp.where(first_core, square_other[:, D + 128 :], square_mine[:, D + 128 :]),
        ],
        axis=1,
    )
    cross_mixed = cross_forward(
        query_caption[:, None],
        text_key[None, :],
        after(cross_query, mlp_far),
        cross_key,
        cross_value,
    )
    after_cross = after_self + dot_nn(cross_mixed, full_cout)

    normed_three, pull_three = jax.vjp(norm_layer, after_cross, ln3_gain, ln3_bias)
    normed_three = normed_three.astype(bf16)
    three_minus, three_plus = shift(normed_three, "z", 1), shift(normed_three, "z", -1)
    hidden_mine = after(hidden_mine, cross_mixed)
    weights = (hidden_mine, shift(hidden_mine, "c", 1))
    out_own, act_own, pre_own, back_own = mlp(core_index, normed_three, grad_mlp, *weights)
    three_minus, three_plus, out_own = lax.optimization_barrier(
        (three_minus, three_plus, out_own)
    )
    three_far = jnp.concatenate(
        [shift(halves(three_minus)[0], "z", 1), shift(halves(three_plus)[1], "z", -1)], axis=0
    )
    three_near = jnp.concatenate([three_minus, three_plus], axis=0)
    out_near, act_near, pre_near, back_near = mlp(core_index, three_near, mlp_near, *weights)
    out_far, act_far, pre_far, back_far = mlp(
        core_index, after(three_far, out_near), mlp_far, *weights
    )
    back_minus, back_plus = reduce_z(back_far, back_near[:TOK], back_near[TOK:])
    keep, send = mlp_grads(
        core_index,
        (normed_three, three_near, after(three_far, back_minus, back_plus)),
        (pre_own, pre_near, pre_far),
        (act_own, act_near, act_far),
        (grad_mlp, mlp_near, mlp_far),
    )
    back_minus, back_plus = shift(back_minus, "z", -1), shift(back_plus, "z", 1)
    hidden_sum = keep + shift(send, "c", 1)
    grad_three = back_own.astype(f32) + back_minus.astype(f32) + back_plus.astype(f32)
    grad_cross_in, grad_ln3_gain, grad_ln3_bias = pull_three(grad_three)
    grad_after_cross = grad_out + grad_cross_in
    grad_cross_branch = grad_after_cross.astype(bf16)
    grad_cross_mixed = dot_nt(grad_cross_branch, full_cout).astype(bf16)

    grad_cquery_rows, grad_key_part, grad_value_part = cross_backward(
        text_key[:, None],
        query_caption[None, :],
        cross_query,
        cross_key,
        cross_value,
        after(grad_cross_mixed, hidden_sum),
    )
    grad_self_in, grad_ln2_gain, grad_ln2_bias = pull_two(dot_nt(grad_cquery_rows, full_cquery))
    grad_after_self = grad_after_cross + grad_self_in
    grad_self_branch = grad_after_self.astype(bf16)
    grad_attended = dot_nt(grad_self_branch, full_out).astype(bf16)
    grad_heads = lax.all_to_all(grad_attended, FS, split_axis=1, concat_axis=0, tiled=True)

    key_rows, value_rows, query_rows, _ = lax.optimization_barrier(
        (grad_key_part, grad_value_part, grad_cquery_rows, grad_attended)
    )
    square = jnp.concatenate(
        [
            window_grad(cross_mixed, grad_cross_branch),
            window_grad(normed_two, query_rows),
            window_grad(context, key_rows),
            window_grad(context, value_rows),
            window_grad(attended, grad_self_branch),
        ],
        axis=1,
    )

    def square_chunk(dy, dx):
        return row_block(square, peer(dy, dx), SHARD)

    grad_heads, square = lax.optimization_barrier((grad_heads, square))
    s_lo, s_hi, s20 = reduce_first(square_chunk)
    hidden_parts = peers_parts(after(hidden_sum, grad_heads))
    grad_m = jnp.where(first_core, key_rows, value_rows)
    grad_o = jnp.where(first_core, value_rows, key_rows)
    context_part = dot_nt(grad_m, square_mine[:, :D]) + dot_nt(grad_o, square_other[:, :D])
    context_part = context_part.astype(bf16)
    context_grad = lax.psum_scatter(context_part, FS, scatter_dimension=0, tiled=True)

    grad_head0 = self_backward(
        0, seg_col, seg_row, total0, qkv, after(grad_heads, context_part)
    )
    s_lo, s_hi, s20, grad_head0 = lax.optimization_barrier((s_lo, s_hi, s20, grad_head0))
    s11, s31 = reduce_second(square_chunk, s_lo, s_hi)
    out_minus, out_plus = reduce_z(after(out_far, grad_head0), out_near[:TOK], out_near[TOK:])
    grad_head1 = self_backward(1, seg_col, seg_row, total1, qkv, after(grad_heads, grad_head0))
    s11, s31, hidden_parts, context_grad, out_minus, out_plus, grad_head1 = (
        lax.optimization_barrier(
            (s11, s31, hidden_parts, context_grad, out_minus, out_plus, grad_head1)
        )
    )
    square_parts = reduce_third(square_chunk, s20, s11, s31)
    context_grad = every_peer(context_grad)
    grad_qkv = jnp.concatenate([grad_head0, grad_head1], axis=1)
    normed_part = dot_nt(grad_qkv, heads_w).astype(bf16)

    def normed_chunk(dy, dx):
        return row_block(normed_part, peer(dy, dx), TOK)

    n_lo, n_hi, n20 = reduce_first(normed_chunk)
    hidden_grad = sum_parts(hidden_parts).astype(bf16)
    hidden_grad = hidden_grad + shift(hidden_grad, "xh", 1)
    hidden_all = lax.all_gather(hidden_grad, ("z", "c"), axis=0)
    grad_heads_w = dot_tn(
        normed_all, after(grad_qkv, normed_part, hidden_grad, context_grad)
    ).astype(bf16)
    grad_heads_w = jnp.concatenate(
        [
            grad_heads_w[:, SLOT * (3 * h + k) : SLOT * (3 * h + k) + HEAD]
            for k in range(3)
            for h in range(2)
        ],
        axis=1,
    )
    n_lo, n_hi, grad_heads_w, *square_parts = lax.optimization_barrier(
        (n_lo, n_hi, grad_heads_w, *square_parts)
    )
    grad_qkv_w = peers_parts(grad_heads_w)
    n11, n31 = reduce_second(normed_chunk, n_lo, n_hi)
    grad_w_text = dot_tn(text_columns, context_grad).astype(bf16)
    text_part = dot_nt(context_grad, w_text).astype(bf16)
    square = reduce_last(square_chunk, *square_parts).astype(bf16)
    square = jnp.concatenate(
        [square[:, WIN * k : WIN * (k + 1)] for k in range(5)]
        + [jnp.zeros((768 - 5 * SHARD, WIN), bf16)],
        axis=0,
    )
    n11, n31, n20, grad_qkv_w, grad_w_text, square = lax.optimization_barrier(
        (n11, n31, n20, grad_qkv_w, grad_w_text, square)
    )
    normed_sums = reduce_third(normed_chunk, n20, n11, n31)
    out_minus, out_plus = shift(out_minus, "z", -1), shift(out_plus, "z", 1)
    outputs = (
        after_cross + out_own.astype(f32) + out_minus.astype(f32) + out_plus.astype(f32)
    )
    grad_w_text = sum_rows_over_dp(grad_w_text)
    square = sum_over_dp(square)
    grad_c_out, grad_c_query, grad_c_key, grad_c_value, grad_w_out = whole_columns(square, 5)
    grad_w_up, grad_w_down = sort_hidden(hidden_all)

    grad_normed_one = reduce_last(normed_chunk, *normed_sums)
    grad_qkv_w = jnp.concatenate(
        [
            jnp.concatenate(
                [
                    grad_qkv_w[SHARD * p : SHARD * (p + 1), SHARD * k : SHARD * (k + 1)]
                    for p in range(8)
                ],
                axis=1,
            )
            for k in range(3)
        ]
        + [jnp.zeros((512 - 3 * SHARD, D), bf16)],
        axis=0,
    )
    half = row_block(grad_qkv_w, core, 256) + shift(
        row_block(grad_qkv_w, 1 - core, 256), "c", 1
    )
    half = sum_parts(peers_parts(half, ("xh", "z"))).astype(bf16)
    half = every_peer(half, ("xh", "z"))
    other_half = shift(half, "c", 1)
    grad_qkv_w = jnp.concatenate(
        [jnp.where(first_core, half, other_half), jnp.where(first_core, other_half, half)], axis=0
    ).astype(f32)
    grad_w_query, grad_w_key, grad_w_value = (
        grad_qkv_w[SHARD * k : SHARD * (k + 1)] for k in range(3)
    )
    grad_text = lax.all_to_all(
        after(text_part, half), FS, split_axis=0, concat_axis=1, tiled=True
    )
    grad_text = grad_text[:CAP_TOK].astype(f32)
    grad_rows_in, grad_ln1_gain, grad_ln1_bias = pull_one(grad_normed_one)
    grad_tokens = grad_after_self + grad_rows_in
    norms = sum_everywhere(
        jnp.stack(
            [
                grad_ln1_gain,
                grad_ln1_bias,
                grad_ln2_gain,
                grad_ln2_bias,
                grad_ln3_gain,
                grad_ln3_bias,
            ]
        )
    )
    return (
        outputs[None],
        grad_tokens[None],
        grad_text[None],
        norms[0],
        norms[1],
        grad_w_query,
        grad_w_key,
        grad_w_value,
        grad_w_out,
        norms[2],
        norms[3],
        grad_c_query,
        grad_w_text,
        grad_c_key,
        grad_c_value,
        grad_c_out,
        norms[4],
        norms[5],
        grad_w_up,
        grad_w_down,
    )


def solution(mesh):
    split = Mesh(mesh.devices.reshape(2, 4, 2, 4, 2), ("xh", "z", "c", "y", "xl"))
    dp = ("xh", "z", "c")
    rows = P(dp, FS, None)
    per_row = P(dp, None)
    weight = P(FS, None)
    rep = P()
    in_specs = (
        rows, rows, per_row, per_row, per_row,
        rep, rep, weight, weight, weight, weight,
        rep, rep, weight, weight, weight, weight, weight,
        rep, rep, weight, weight, rows,
    )
    out_specs = (
        rows, rows, rows,
        rep, rep, weight, weight, weight, weight,
        rep, rep, weight, weight, weight, weight, weight,
        rep, rep, weight, weight,
    )
    return jax.shard_map(
        local, mesh=split, in_specs=in_specs, out_specs=out_specs, check_vma=False
    )
```

```python
import functools

import jax
import jax.numpy as jnp
from jax import lax
from jax.experimental import pallas as pl
from jax.experimental.pallas import tpu as pltpu
from jax.sharding import Mesh
from jax.sharding import PartitionSpec as P

HEADS = 16
HEAD = 72
D = 1152
FF = 4608
CAP_TOK = 60
TXT_OWN = 64
TXT = 8 * TXT_OWN
TOK = 256
ROW = 2048
CAP_LEN = 120
SEGS = 3
CAPS = 4
SHARD = 144
SLOT = 128
WIN = 640
STEP = 512

bf16 = jnp.bfloat16
f32 = jnp.float32
norm_eps = 1e-06
masked_score = -1e30
scale = HEAD ** (-0.5)
log2e = 1.4426950408889634
FS = ("y", "xl")
VMEM = 60 * 1024 * 1024


def dot_nn(a, b):
    return lax.dot_general(a, b, (((1,), (0,)), ((), ())), preferred_element_type=f32)


def dot_nt(a, b):
    return lax.dot_general(a, b, (((1,), (1,)), ((), ())), preferred_element_type=f32)


def dot_tn(a, b):
    return lax.dot_general(a, b, (((0,), (0,)), ((), ())), preferred_element_type=f32)


def params():
    return pltpu.CompilerParams(vmem_limit_bytes=VMEM)


def shift(x, axis, by):
    n = lax.axis_size(axis)
    return lax.ppermute(x, axis, [(i, (i + by) % n) for i in range(n)])


def halves(x):
    h = (x.shape[0] // 2 + 15) // 16 * 16
    return x[:h], x[h:]


def after(x, *others):
    return lax.optimization_barrier((x, *others))[0]


def gather_first(x):
    return shift(x, "xl", 1), shift(x, "y", -1), shift(x, "y", 1)


def gather_second(x01, x10):
    return shift(x01, "y", 1), shift(x10, "y", -1), shift(x10, "xl", 1)


def gather_third(x31, x11):
    return shift(halves(x11)[0], "y", -1), shift(halves(x31)[1], "y", 1)


NEAR = ((0, 0), (0, 1), (1, 0), (3, 0))
NEXT = ((3, 1), (2, 0), (1, 1))
LAST = (2, 1)


def reduce_first(chunk):
    lo, hi = halves(chunk(2, 1))
    return shift(lo, "y", 1), shift(hi, "y", -1), shift(chunk(2, 0), "y", 1)


def reduce_second(chunk, lo, hi):
    h = lo.shape[0]
    c11, c31 = chunk(1, 1), chunk(3, 1)
    c11 = jnp.concatenate([c11[:h] + lo, c11[h:]], axis=0)
    c31 = jnp.concatenate([c31[:h], c31[h:] + hi], axis=0)
    return shift(c11, "xl", 1), shift(c31, "y", -1)


def reduce_third(chunk, c20, c11, c31):
    return (
        shift(chunk(1, 0) + c20 + c11, "y", 1),
        shift(chunk(0, 1) + c31, "xl", 1),
        shift(chunk(3, 0), "y", -1),
    )


def reduce_last(chunk, *parts):
    return sum([p.astype(f32) for p in parts], chunk(0, 0).astype(f32))


def every_peer(x, axes=FS):
    n = lax.axis_size(axes)
    copies = jnp.broadcast_to(x[None], (n, *x.shape)).reshape(n * x.shape[0], x.shape[1])
    return lax.all_to_all(copies, axes, 0, 0, tiled=True)


def peers_parts(x, axes=FS):
    return lax.all_to_all(x, axes, 0, 0, tiled=True)


def sum_parts(parts):
    return jnp.sum(parts.reshape(8, -1, parts.shape[1]).astype(f32), axis=0)


def reduce_z(far, minus, plus):
    lo, hi = halves(far)
    lo, hi = shift(lo, "z", -1), shift(hi, "z", 1)
    h = lo.shape[0]
    return (
        jnp.concatenate([minus[:h] + lo, minus[h:]], axis=0),
        jnp.concatenate([plus[:h], plus[h:] + hi], axis=0),
    )


def peer(dy, dx):
    return ((lax.axis_index("y") + dy) % 4) * 2 + (lax.axis_index("xl") ^ dx)


def place_rows(own, first, second, third, gain, bias):
    lo = third[0].shape[0]
    rows, cols = own.shape
    pieces = [(x, p, 0) for x, p in zip((own, *first), NEAR)]
    pieces += [(x, p, 0) for x, p in zip(second, NEXT)]
    pieces += [(third[0], LAST, 0), (third[1], LAST, lo)]
    count = len(pieces)

    def body(where, gain, bias, *refs):
        ins, plain, normed, sem = refs[:count], refs[count], refs[count + 1], refs[-1]
        started = []
        for k, (x, _, off) in enumerate(pieces):
            row = pl.multiple_of(where[k] * rows + off, 16)
            one = pltpu.make_async_copy(ins[k], plain.at[pl.ds(row, x.shape[0])], sem.at[k])
            one.start()
            started.append(one)
        for one in started:
            one.wait()

        def step(i, carry):
            part = pl.ds(pl.multiple_of(i * rows, rows), rows)
            normed[part, :] = (plain[part, :].astype(f32) * gain[...] + bias[...]).astype(bf16)
            return carry

        lax.fori_loop(0, 8, step, 0)

    vmem = pl.BlockSpec(memory_space=pltpu.VMEM)
    return pl.pallas_call(
        body,
        in_specs=[pl.BlockSpec(memory_space=pltpu.SMEM), vmem, vmem]
        + [pl.BlockSpec(memory_space=pl.ANY)] * count,
        out_specs=[vmem, vmem],
        out_shape=[jax.ShapeDtypeStruct((8 * rows, cols), bf16)] * 2,
        scratch_shapes=[pltpu.SemaphoreType.DMA((count,))],
        compiler_params=params(),
    )(
        jnp.stack([peer(*p) for _, p, _ in pieces]).astype(jnp.int32),
        gain,
        bias,
        *[x for x, _, _ in pieces],
    )


def pack_heads_body(wq, wk, wv, out):
    for p in range(8):
        rows = slice(SHARD * p, SHARD * (p + 1))
        out[rows, :] = jnp.concatenate([w[:, rows] for w in (wq, wk, wv)], axis=1)


def pack_heads(*weights):
    return pl.pallas_call(
        pack_heads_body,
        out_shape=jax.ShapeDtypeStruct((D, 3 * SHARD), bf16),
        compiler_params=params(),
    )(*weights)


def spread_heads_body(x, out):
    blank = jnp.zeros((D, SLOT - HEAD), bf16)
    for h in range(2):
        for k in range(3):
            first = SHARD * k + HEAD * h
            slot = SLOT * (3 * h + k)
            out[:, slot : slot + SLOT] = jnp.concatenate(
                [x[:, first : first + HEAD], blank], axis=1
            )


def spread_heads(x):
    return pl.pallas_call(
        spread_heads_body,
        out_shape=jax.ShapeDtypeStruct((D, 6 * SLOT), bf16),
        compiler_params=params(),
    )(x)


def self_forward_body(seg_q, seg_k, q, kv, out, total):
    s = dot_nt(q[:, :SLOT], kv[:, SLOT : 2 * SLOT])
    s = jnp.where(seg_q[...] == seg_k[...], s, masked_score)
    top = jnp.max(s, axis=1, keepdims=True)
    p = jnp.exp2((s - top) * (scale * log2e))
    mass = jnp.sum(p, axis=1, keepdims=True)
    out[...] = (dot_nn(p.astype(bf16), kv[:, 2 * SLOT :]) / mass)[:, :HEAD].astype(bf16)
    log_total = top * (scale * log2e) + jnp.log2(mass)
    total[...] = jnp.transpose(jnp.broadcast_to(log_total, (TOK, SLOT)))[0:1, :]


def self_forward(head, seg_q, seg_k, qkv):
    return pl.pallas_call(
        self_forward_body,
        grid=(ROW // TOK,),
        in_specs=[
            pl.BlockSpec((TOK, 1), lambda i: (i, 0)),
            pl.BlockSpec((1, ROW), lambda i: (0, 0)),
            pl.BlockSpec((TOK, 3 * SLOT), lambda i: (i, head)),
            pl.BlockSpec((ROW, 3 * SLOT), lambda i: (0, head)),
        ],
        out_specs=[
            pl.BlockSpec((TOK, HEAD), lambda i: (i, 0)),
            pl.BlockSpec((1, TOK), lambda i: (0, i)),
        ],
        out_shape=[
            jax.ShapeDtypeStruct((ROW, HEAD), bf16),
            jax.ShapeDtypeStruct((1, ROW), f32),
        ],
        compiler_params=params(),
    )(seg_q, seg_k, qkv, qkv)


def self_backward_body(head, seg_k, seg_q, total, q, kv, g, *refs):
    grad, key_sum, value_sum, key_t = refs[-4:]
    i = pl.program_id(0)

    @pl.when(i == 0)
    def _():
        key_sum[...] = jnp.zeros_like(key_sum)
        value_sum[...] = jnp.zeros_like(value_sum)
        key_t[...] = jnp.transpose(kv[:, SLOT : 2 * SLOT])

    rows = pl.ds(pl.multiple_of(i * TOK, TOK), TOK)
    q_h, k_h, v_h = q[:, :SLOT], kv[:, SLOT : 2 * SLOT], kv[:, 2 * SLOT :]
    g_both = g[...]
    g_h = jnp.concatenate(
        [g_both[:, HEAD * head : HEAD * (head + 1)], jnp.zeros((TOK, SLOT - HEAD), bf16)], axis=1
    )
    p = jnp.exp2(dot_nt(k_h, q_h) * (scale * log2e) - total[...])
    p = jnp.where(seg_k[...] == seg_q[...], p, 0.0)
    dp = dot_nt(v_h, g_h)
    ds = (p * (dp - jnp.sum(p * dp, axis=0, keepdims=True))).astype(bf16)
    value_sum[...] += dot_nn(p.astype(bf16), g_h)
    key_sum[...] += dot_nn(ds, q_h)
    grad[rows, :SLOT] = (jnp.transpose(dot_nn(key_t[...], ds)) * scale).astype(bf16)

    @pl.when(i == pl.num_programs(0) - 1)
    def _():
        grad[:, SLOT : 2 * SLOT] = (key_sum[...] * scale).astype(bf16)
        grad[:, 2 * SLOT :] = value_sum[...].astype(bf16)


def self_backward(head, seg_k, seg_q, total, qkv, g, before=()):
    return pl.pallas_call(
        functools.partial(self_backward_body, head),
        grid=(ROW // TOK,),
        in_specs=[
            pl.BlockSpec((ROW, 1), lambda i: (0, 0)),
            pl.BlockSpec((1, TOK), lambda i: (0, i)),
            pl.BlockSpec((1, TOK), lambda i: (0, i)),
            pl.BlockSpec((TOK, 3 * SLOT), lambda i: (i, head)),
            pl.BlockSpec((ROW, 3 * SLOT), lambda i: (0, head)),
            pl.BlockSpec((TOK, SHARD), lambda i: (i, 0)),
        ]
        + [pl.BlockSpec(memory_space=pl.ANY)] * len(before),
        out_specs=pl.BlockSpec((ROW, 3 * SLOT), lambda i: (0, head)),
        out_shape=jax.ShapeDtypeStruct((ROW, 6 * SLOT), bf16),
        input_output_aliases={6: 0} if before else {},
        scratch_shapes=[
            pltpu.VMEM((ROW, SLOT), f32),
            pltpu.VMEM((ROW, SLOT), f32),
            pltpu.VMEM((SLOT, ROW), bf16),
        ],
        compiler_params=params(),
    )(seg_k, seg_q, total, qkv, qkv, g, *before)


def cross_forward_body(cap_q, cap_t, q, k, v, out):
    allowed = cap_q[...] == cap_t[...]
    mixed = []
    for h in range(HEADS):
        a, b = HEAD * h, HEAD * (h + 1)
        s = dot_nt(q[:, a:b], k[:, a:b])
        s = jnp.where(allowed, s, masked_score)
        top = jnp.max(s, axis=1, keepdims=True)
        p = jnp.exp2((s - top) * (scale * log2e))
        mass = jnp.sum(p, axis=1, keepdims=True)
        mixed.append(dot_nn(p.astype(bf16), v[:, a:b]) / mass)
    out[...] = jnp.concatenate(mixed, axis=1).astype(bf16)


def cross_forward(cap_q, cap_t, q, k, v):
    return pl.pallas_call(
        cross_forward_body,
        out_shape=jax.ShapeDtypeStruct((TOK, D), bf16),
        compiler_params=params(),
    )(cap_q, cap_t, q, k, v)


def cross_backward_body(cap_t, cap_q, q, k, v, g, grad_q, grad_kv):
    allowed = cap_t[...] == cap_q[...]
    dq, dk, dv = [], [], []
    for h in range(HEADS):
        a, b = HEAD * h, HEAD * (h + 1)
        q_h, k_h, v_h, g_h = q[:, a:b], k[:, a:b], v[:, a:b], g[:, a:b]
        s = jnp.where(allowed, dot_nt(k_h, q_h), masked_score)
        top = jnp.max(s, axis=0, keepdims=True)
        p = jnp.exp2((s - top) * (scale * log2e))
        p = p / jnp.sum(p, axis=0, keepdims=True)
        dp = dot_nt(v_h, g_h)
        ds = (p * (dp - jnp.sum(p * dp, axis=0, keepdims=True))).astype(bf16)
        dv.append(dot_nn(p.astype(bf16), g_h))
        dk.append(dot_nn(ds, q_h) * scale)
        dq.append(dot_tn(ds, k_h) * scale)
    grad_q[...] = jnp.concatenate(dq, axis=1).astype(bf16)
    grad_kv[:, :D] = jnp.concatenate(dk, axis=1).astype(bf16)
    grad_kv[:, D:] = jnp.concatenate(dv, axis=1).astype(bf16)


def cross_backward(cap_t, cap_q, q, k, v, g):
    return pl.pallas_call(
        cross_backward_body,
        out_shape=[
            jax.ShapeDtypeStruct((TOK, D), bf16),
            jax.ShapeDtypeStruct((TXT, 2 * D), bf16),
        ],
        compiler_params=params(),
    )(cap_t, cap_q, q, k, v, g)


def fetch_pair(core, mine, other, first, second, sem):
    def run(a, b):
        one = pltpu.make_async_copy(a, first, sem.at[0])
        two = pltpu.make_async_copy(b, second, sem.at[1])
        one.start()
        two.start()
        one.wait()
        two.wait()

    @pl.when(core[0] == 0)
    def _():
        run(mine, other)

    @pl.when(core[0] != 0)
    def _():
        run(other, mine)


def fetch_windows(core, mine, other, whole, sem):
    def run(a, b):
        one = pltpu.make_async_copy(a, whole.at[:, pl.ds(0, WIN)], sem.at[0])
        two = pltpu.make_async_copy(
            b.at[:, pl.ds(128, STEP)], whole.at[:, pl.ds(WIN, STEP)], sem.at[1]
        )
        one.start()
        two.start()
        one.wait()
        two.wait()

    @pl.when(core[0] == 0)
    def _():
        run(mine, other)

    @pl.when(core[0] != 0)
    def _():
        run(other, mine)


def mlp_body(parts, count, core, *refs):
    xs, gs = refs[: parts * count], refs[parts * count : 2 * parts * count]
    mine, other = refs[2 * parts * count : 2 * parts * count + 2]
    outs = refs[2 * parts * count + 2 : -3]
    up, down, sem = refs[-3:]
    fetch_pair(core, mine, other, up, down, sem)
    for k in range(count):
        x = jnp.concatenate([r[...] for r in xs[parts * k : parts * (k + 1)]], axis=0)
        g = jnp.concatenate([r[...] for r in gs[parts * k : parts * (k + 1)]], axis=0)
        out, act_out, pre_out, grad_x = outs[4 * k : 4 * (k + 1)]
        pre = dot_nn(x, up[...])
        grad_act = dot_nt(g, down[...])
        cdf = 0.5 * (1.0 + lax.erf(pre * (0.5**0.5)))
        density = jnp.exp2(pre * pre * (-0.5 * log2e)) * 0.3989422804014327
        act = (pre * cdf).astype(bf16)
        grad_pre = (grad_act * (cdf + pre * density)).astype(bf16)
        act_out[...] = act
        pre_out[...] = grad_pre
        out[...] = dot_nn(act, down[...]).astype(out.dtype)
        grad_x[...] = dot_nt(grad_pre, up[...]).astype(grad_x.dtype)


def mlp(core, xs, gs, mine, other):
    parts = TOK // xs[0].shape[0]
    count = len(xs) // parts
    vmem = pl.BlockSpec(memory_space=pltpu.VMEM)
    hbm = pl.BlockSpec(memory_space=pl.ANY)
    return pl.pallas_call(
        functools.partial(mlp_body, parts, count),
        in_specs=[pl.BlockSpec(memory_space=pltpu.SMEM)]
        + [vmem] * (2 * parts * count)
        + [hbm, hbm],
        out_specs=[vmem] * (4 * count),
        out_shape=[jax.ShapeDtypeStruct((TOK, D), bf16)] * (4 * count),
        scratch_shapes=[
            pltpu.VMEM((D, D), bf16),
            pltpu.VMEM((D, D), bf16),
            pltpu.SemaphoreType.DMA((2,)),
        ],
        compiler_params=params(),
    )(core, *xs, *gs, mine, other)


def mlp_grads_body(core, *refs):
    xs, pres, acts, gs = refs[0:4], refs[4:8], refs[8:12], refs[12:16]
    keep, send = refs[16:]
    up = sum(dot_tn(x[...], p[...]) for x, p in zip(xs, pres)).astype(bf16)
    down = sum(dot_tn(a[...], g[...]) for a, g in zip(acts, gs)).astype(bf16)
    first = core[0] == 0

    @pl.when(first)
    def _():
        keep[...] = up
        send[...] = down

    @pl.when(jnp.logical_not(first))
    def _():
        keep[...] = down
        send[...] = up


def mlp_grads(core, xs, pres, acts, gs):
    def whole(x):
        return pl.BlockSpec(x.shape, lambda k: (0, 0))

    def part(x):
        return pl.BlockSpec((x.shape[0], 384), lambda k: (0, k))

    out = pl.BlockSpec((D, 384), lambda k: (0, k))
    return pl.pallas_call(
        mlp_grads_body,
        grid=(3,),
        in_specs=[pl.BlockSpec(memory_space=pltpu.SMEM)]
        + [whole(x) for x in xs]
        + [part(x) for x in pres]
        + [whole(x) for x in acts]
        + [part(x) for x in gs],
        out_specs=[out, out],
        out_shape=[jax.ShapeDtypeStruct((D, D), bf16)] * 2,
        compiler_params=params(),
    )(core, *xs, *pres, *acts, *gs)


def sort_hidden_body(core, mine, other, up, down):
    def run(ups, downs):
        for f in range(8):
            lanes = slice(SHARD * f, SHARD * (f + 1))
            up[:, 4 * SHARD * f : 4 * SHARD * (f + 1)] = jnp.concatenate(
                [ups[SHARD * z : SHARD * (z + 1), lanes] for z in range(4)], axis=1
            ).astype(f32)
        down[...] = downs[...].astype(f32)

    @pl.when(core[0] == 0)
    def _():
        run(mine, other)

    @pl.when(core[0] != 0)
    def _():
        run(other, mine)


def sort_hidden(core, mine, other):
    vmem = pl.BlockSpec(memory_space=pltpu.VMEM)
    return pl.pallas_call(
        sort_hidden_body,
        in_specs=[pl.BlockSpec(memory_space=pltpu.SMEM), vmem, vmem],
        out_specs=[vmem, vmem],
        out_shape=[
            jax.ShapeDtypeStruct((SHARD, FF), f32),
            jax.ShapeDtypeStruct((4 * SHARD, D), f32),
        ],
        compiler_params=params(),
    )(core, mine, other)


def normalize(x):
    center = x - jnp.mean(x, axis=-1, keepdims=True)
    inverse = lax.rsqrt(jnp.mean(center * center, axis=-1, keepdims=True) + norm_eps)
    return center * inverse, inverse


def norm_back(x, g, gain):
    plain, inverse = normalize(x)
    scaled = g * gain
    mixed = jnp.mean(scaled * plain, axis=-1, keepdims=True)
    grad = inverse * (scaled - jnp.mean(scaled, axis=-1, keepdims=True) - plain * mixed)
    sums = [jnp.sum(g * plain, axis=0, keepdims=True), jnp.sum(g, axis=0, keepdims=True)]
    return grad, sums


def call(body, ins, outs, scratch):
    spaces = {"vmem": pltpu.VMEM, "hbm": pl.ANY, "smem": pltpu.SMEM}
    return pl.pallas_call(
        body,
        in_specs=[pl.BlockSpec(memory_space=spaces[where]) for _, where in ins],
        out_specs=[pl.BlockSpec(memory_space=pltpu.VMEM)] * len(outs),
        out_shape=[jax.ShapeDtypeStruct(*o) for o in outs],
        scratch_shapes=scratch,
        compiler_params=params(),
    )(*[x for x, _ in ins])


def square_scratch(count):
    return [pltpu.VMEM((D, D), bf16)] * count + [pltpu.SemaphoreType.DMA((2,))]


def after_self_body(core, x, mixed, gain, bias, mine, other, total, normed, query, w1, w2, sem):
    fetch_pair(core, mine, other, w1, w2, sem)
    rows = x[...].astype(f32) + dot_nn(mixed[...], w1[...])
    total[...] = rows
    low = (normalize(rows)[0] * gain[...] + bias[...]).astype(bf16)
    normed[...] = low
    query[...] = dot_nn(low, w2[...]).astype(bf16)


def text_keys_body(core, context, mine, other, key, value, w1, w2, sem):
    fetch_pair(core, mine, other, w1, w2, sem)
    key[...] = dot_nn(context[...], w1[...]).astype(bf16)
    value[...] = dot_nn(context[...], w2[...]).astype(bf16)


def after_cross_body(core, x, mixed, gain, bias, mine, other, total, normed, w, sem):
    fetch_windows(core, mine, other, w, sem)
    rows = x[...] + dot_nn(mixed[...], w[...])
    total[...] = rows
    normed[...] = (normalize(rows)[0] * gain[...] + bias[...]).astype(bf16)


def third_back_body(core, x, g0, g1, g2, cot, gain, mine, other, grad, low, mixed, sums, w, sem):
    fetch_windows(core, mine, other, w, sem)
    g = g0[...].astype(f32) + g1[...].astype(f32) + g2[...].astype(f32)
    back, both = norm_back(x[...], g, gain[...])
    total = cot[...] + back
    grad[...] = total
    low[...] = total.astype(bf16)
    mixed[...] = dot_nt(total.astype(bf16), w[...]).astype(bf16)
    sums[...] = jnp.concatenate(both + [jnp.zeros((6, D), f32)], axis=0)


def second_back_body(core, x, gq, before, gain, mine, other, grad, low, mixed, sums, w1, w2, sem):
    fetch_pair(core, mine, other, w1, w2, sem)
    back, both = norm_back(x[...], dot_nt(gq[...], w2[...]), gain[...])
    total = before[...] + back
    grad[...] = total
    low[...] = total.astype(bf16)
    mixed[...] = dot_nt(total.astype(bf16), w1[...]).astype(bf16)
    sums[...] = jnp.concatenate(both + [jnp.zeros((6, D), f32)], axis=0)


def first_back_body(x, parts, before, gain, grad):
    g = parts[:TOK, :].astype(f32)
    for k in range(1, 8):
        g = g + parts[TOK * k : TOK * (k + 1), :].astype(f32)
    grad[...] = before[...] + norm_back(x[...].astype(f32), g, gain[...])[0]


def text_back_body(
    core, kv, cols, text, w_text, mine, other, part, grad_text, grad_kv, w1, w2, sem
):
    fetch_pair(core, mine, other, w1, w2, sem)
    low = (dot_nt(kv[:, :D], w1[...]) + dot_nt(kv[:, D:], w2[...])).astype(bf16)
    part[...] = dot_nt(low, w_text[...]).astype(bf16)
    grad_text[...] = dot_tn(text[...], low).astype(bf16)
    grad_kv[...] = dot_tn(cols[...], kv[...]).astype(bf16)


def first_part_body(g, w, plain, part, sums):
    rows = dot_nt(g[...], w[...])
    part[...] = rows.astype(bf16)
    both = [
        jnp.sum(rows * plain[...].astype(f32), axis=0, keepdims=True),
        jnp.sum(rows, axis=0, keepdims=True),
        jnp.zeros((6, D), f32),
    ]
    both = jnp.concatenate(both, axis=0)

    @pl.when(pl.program_id(0) == 0)
    def _():
        sums[...] = both

    @pl.when(pl.program_id(0) != 0)
    def _():
        sums[...] += both


def first_part(g, w, plain):
    return pl.pallas_call(
        first_part_body,
        grid=(ROW // TOK,),
        in_specs=[
            pl.BlockSpec((TOK, 6 * SLOT), lambda i: (i, 0)),
            pl.BlockSpec((D, 6 * SLOT), lambda i: (0, 0)),
            pl.BlockSpec((TOK, D), lambda i: (i, 0)),
        ],
        out_specs=[
            pl.BlockSpec((TOK, D), lambda i: (i, 0)),
            pl.BlockSpec((8, D), lambda i: (0, 0)),
        ],
        out_shape=[jax.ShapeDtypeStruct((ROW, D), bf16), jax.ShapeDtypeStruct((8, D), f32)],
        compiler_params=params(),
    )(g, w, plain)


def heads_grad_body(x, g, out):
    grad = dot_tn(x[...], g[...]).astype(bf16)
    out[...] = jnp.concatenate(
        [
            grad[:, SLOT * (3 * h + k) : SLOT * (3 * h + k) + HEAD]
            for k in range(3)
            for h in range(2)
        ],
        axis=1,
    )


def heads_grad(x, g):
    return pl.pallas_call(
        heads_grad_body,
        grid=(3,),
        in_specs=[
            pl.BlockSpec((ROW, 384), lambda i: (0, i)),
            pl.BlockSpec((ROW, 6 * SLOT), lambda i: (0, 0)),
        ],
        out_specs=pl.BlockSpec((384, 3 * SHARD), lambda i: (i, 0)),
        out_shape=jax.ShapeDtypeStruct((D, 3 * SHARD), bf16),
        compiler_params=params(),
    )(x, g)


def unpack_heads_body(x, out):
    for k in range(3):
        out[SHARD * k : SHARD * (k + 1), :] = jnp.concatenate(
            [x[SHARD * p : SHARD * (p + 1), SHARD * k : SHARD * (k + 1)] for p in range(8)], axis=1
        )


def unpack_heads(x):
    return pl.pallas_call(
        unpack_heads_body,
        out_shape=jax.ShapeDtypeStruct((3 * SHARD, D), bf16),
        compiler_params=params(),
    )(x)


def row_block(x, index, rows):
    return lax.dynamic_slice_in_dim(x, index * rows, rows, axis=0)


def core_window(x, core):
    return lax.dynamic_slice_in_dim(x, core * STEP, WIN, axis=1)


def both_cores(x):
    return jnp.concatenate([x, shift(x, "c", 1)], axis=0)


def window_grad(left, right):
    core = lax.axis_index("c")
    sent = shift(core_window(right, 1 - core), "c", 1)
    rights = jnp.concatenate([core_window(right, core), sent], axis=0)
    return dot_tn(both_cores(left), rights).astype(bf16)


def scatter_over_dp(x):
    part = lax.psum_scatter(x, "z", scatter_dimension=0, tiled=True)
    return part + shift(part, "xh", 1)


def whole_columns(mine, count):
    other = shift(mine, "c", 1)
    first = lax.axis_index("c") == 0
    low = jnp.where(first, mine, other).astype(f32)
    high = jnp.where(first, other, mine).astype(f32)
    return [
        jnp.concatenate(
            [low[SHARD * k : SHARD * (k + 1)], high[SHARD * k : SHARD * (k + 1), 128:]], axis=1
        )
        for k in range(count)
    ]


def sum_everywhere(x):
    for axis in ("y", "xl", "z", "xh", "c"):
        n = lax.axis_size(axis)
        x = sum([shift(x, axis, k) for k in range(1, n)], x)
    return x


def local(
    tokens,
    text_states,
    seg_lengths,
    caption_of_segment,
    text_lengths,
    ln1_gain,
    ln1_bias,
    w_query,
    w_key,
    w_value,
    w_out,
    ln2_gain,
    ln2_bias,
    c_query,
    w_text,
    c_key,
    c_value,
    c_out,
    ln3_gain,
    ln3_bias,
    w_up,
    w_down,
    cotangent,
):
    core = lax.axis_index("c")
    first_core = core == 0
    core_index = core.astype(jnp.int32)[None]
    quarter = lax.axis_index("z")
    first_row = peer(0, 0) * TOK

    ends = jnp.cumsum(seg_lengths[0])
    positions = jnp.arange(ROW, dtype=jnp.int32)
    segment = jnp.sum((positions[:, None] >= ends[None, :]).astype(jnp.int32), axis=1)
    own_segment = lax.dynamic_slice_in_dim(segment, first_row, TOK)
    text_row = jnp.arange(TXT, dtype=jnp.int32)
    text_pos = text_row // TXT_OWN * CAP_TOK + text_row % TXT_OWN
    text_caption = text_pos // CAP_LEN
    live = jnp.sum(
        jnp.where(
            text_caption[:, None] == jnp.arange(CAPS, dtype=jnp.int32)[None, :],
            text_lengths[0][None, :],
            0,
        ),
        axis=1,
    )
    query_caption = jnp.sum(
        jnp.where(
            own_segment[:, None] == jnp.arange(SEGS, dtype=jnp.int32)[None, :],
            caption_of_segment[0][None, :],
            0,
        ),
        axis=1,
    )
    text_live = (text_row % TXT_OWN < CAP_TOK) & (text_pos % CAP_LEN < live)
    text_key = jnp.where(text_live, text_caption, -1)

    def row(x):
        return x[None, :]

    first_mine = lax.all_gather(jnp.where(first_core, w_out, c_query), FS, axis=0, tiled=True)

    rows_in = tokens[0]
    plain = normalize(rows_in.astype(f32))[0].astype(bf16)
    n01, n10, n30 = gather_first(plain)

    heads_w = peers_parts(pack_heads(after(w_query, plain), w_key, w_value))
    n01, n10, n30 = lax.optimization_barrier((n01, n10, n30))
    n31, n20, n11 = gather_second(n01, n10)
    n31, n20, n11, heads_w = lax.optimization_barrier((n31, n20, n11, heads_w))
    n21 = gather_third(n31, n11)

    text_own = jnp.pad(after(text_states[0], n11), ((0, TXT_OWN - CAP_TOK), (0, 0)))
    text_columns = lax.all_to_all(text_own, FS, split_axis=1, concat_axis=0, tiled=True)
    heads_w = spread_heads(heads_w)
    plain_all, normed_all = place_rows(
        after(plain, text_columns),
        (n01, n10, n30),
        (n31, n20, n11),
        n21,
        row(ln1_gain),
        row(ln1_bias),
    )

    second_pack = jnp.where(first_core, c_key, c_value)
    second_pack, first_mine, normed_all = lax.optimization_barrier(
        (second_pack, first_mine, normed_all)
    )
    second_mine = lax.all_gather(second_pack, FS, axis=0, tiled=True)

    seg_col, seg_row = segment[:, None], segment[None, :]
    qkv = dot_nn(normed_all, heads_w).astype(bf16)
    context_part = dot_nn(after(text_columns, qkv), w_text).astype(bf16)
    context_parts = peers_parts(context_part)
    grad_out = cotangent[0]
    grad_mlp = grad_out.astype(bf16)
    grad_sent = after(grad_mlp, qkv)
    mlp_minus, mlp_plus = shift(grad_sent, "z", 1), shift(grad_sent, "z", -1)
    head0, total0 = self_forward(0, seg_col, seg_row, qkv)
    mlp_minus, mlp_plus, context_parts, head0 = lax.optimization_barrier(
        (mlp_minus, mlp_plus, context_parts, head0)
    )
    context = every_peer(sum_parts(context_parts).astype(bf16))
    mlp_far = (
        shift(halves(mlp_minus)[0], "z", 1),
        shift(halves(mlp_plus)[1], "z", -1),
    )
    head1, total1 = self_forward(1, seg_col, seg_row, after(qkv, head0))
    head1, context, *mlp_far = lax.optimization_barrier((head1, context, *mlp_far))
    first_other = shift(first_mine, "c", 1)
    attended = lax.all_to_all(
        jnp.concatenate([head0, head1], axis=1), FS, split_axis=0, concat_axis=1, tiled=True
    )

    up_own = jnp.concatenate(
        [
            lax.dynamic_slice(w_up, (0, 4 * SHARD * k + SHARD * quarter), (SHARD, SHARD))
            for k in range(8)
        ],
        axis=1,
    )
    hidden_own = jnp.where(first_core, up_own, row_block(w_down, quarter, SHARD))
    hidden_mine = every_peer(after(hidden_own, attended))

    after_self, normed_two, cross_query = call(
        after_self_body,
        [
            (core_index, "smem"), (rows_in, "vmem"), (attended, "vmem"),
            (row(ln2_gain), "vmem"), (row(ln2_bias), "vmem"),
            (first_mine, "hbm"), (first_other, "hbm"),
        ],
        [((TOK, D), f32), ((TOK, D), bf16), ((TOK, D), bf16)],
        square_scratch(2),
    )
    second_mine = after(second_mine, cross_query)
    second_other = shift(second_mine, "c", 1)
    third_pack = after(jnp.where(first_core, c_out[:, :WIN], c_out[:, STEP:]), second_mine)
    third_mine = lax.all_gather(third_pack, FS, axis=0, tiled=True)
    cross_key, cross_value = call(
        text_keys_body,
        [
            (core_index, "smem"), (after(context, cross_query), "vmem"),
            (second_mine, "hbm"), (second_other, "hbm"),
        ],
        [((TXT, D), bf16), ((TXT, D), bf16)],
        square_scratch(2),
    )
    cross_mixed = cross_forward(
        query_caption[:, None], text_key[None, :], cross_query, cross_key, cross_value
    )
    third_mine, hidden_mine, cross_mixed = lax.optimization_barrier(
        (third_mine, hidden_mine, cross_mixed)
    )
    third_other = shift(third_mine, "c", 1)
    weights = (hidden_mine, shift(hidden_mine, "c", 1))
    after_cross, normed_three = call(
        after_cross_body,
        [
            (core_index, "smem"), (after_self, "vmem"), (cross_mixed, "vmem"),
            (row(ln3_gain), "vmem"), (row(ln3_bias), "vmem"),
            (third_mine, "hbm"), (third_other, "hbm"),
        ],
        [((TOK, D), f32), ((TOK, D), bf16)],
        square_scratch(1),
    )

    three_minus, three_plus = shift(normed_three, "z", 1), shift(normed_three, "z", -1)
    out_own, act_own, pre_own, back_own = mlp(core_index, (normed_three,), (grad_mlp,), *weights)
    three_minus, three_plus, out_own = lax.optimization_barrier(
        (three_minus, three_plus, out_own)
    )
    three_far = (
        shift(halves(three_minus)[0], "z", 1),
        shift(halves(three_plus)[1], "z", -1),
    )
    near = mlp(core_index, (three_minus, three_plus), (mlp_minus, mlp_plus), *weights)
    out_m, act_m, pre_m, back_m, out_p, act_p, pre_p, back_p = near
    *three_far, out_m = lax.optimization_barrier((*three_far, out_m))
    out_far, act_far, pre_far, back_far = mlp(core_index, three_far, mlp_far, *weights)
    back_minus, back_plus = reduce_z(back_far, back_m, back_p)
    keep, send = mlp_grads(
        core_index,
        (
            normed_three,
            three_minus,
            three_plus,
            after(jnp.concatenate(three_far, axis=0), back_minus, back_plus),
        ),
        (pre_own, pre_m, pre_p, pre_far),
        (act_own, act_m, act_p, act_far),
        (grad_mlp, mlp_minus, mlp_plus, jnp.concatenate(mlp_far, axis=0)),
    )
    back_minus, back_plus = shift(back_minus, "z", -1), shift(back_plus, "z", 1)
    hidden_sum = keep + shift(send, "c", 1)
    grad_after_cross, grad_cross_branch, grad_cross_mixed, sums_three = call(
        third_back_body,
        [
            (core_index, "smem"), (after_cross, "vmem"), (back_own, "vmem"),
            (back_minus, "vmem"), (back_plus, "vmem"), (grad_out, "vmem"),
            (row(ln3_gain), "vmem"), (third_mine, "hbm"), (third_other, "hbm"),
        ],
        [((TOK, D), f32), ((TOK, D), bf16), ((TOK, D), bf16), ((8, D), f32)],
        square_scratch(1),
    )

    grad_cquery_rows, grad_kv = cross_backward(
        text_key[:, None],
        query_caption[None, :],
        cross_query,
        cross_key,
        cross_value,
        after(grad_cross_mixed, hidden_sum),
    )
    kv_own = lax.psum_scatter(grad_kv, FS, scatter_dimension=0, tiled=True)
    grad_after_self, grad_self_branch, grad_attended, sums_two = call(
        second_back_body,
        [
            (core_index, "smem"), (after_self, "vmem"), (grad_cquery_rows, "vmem"),
            (grad_after_cross, "vmem"), (row(ln2_gain), "vmem"),
            (first_mine, "hbm"), (first_other, "hbm"),
        ],
        [((TOK, D), f32), ((TOK, D), bf16), ((TOK, D), bf16), ((8, D), f32)],
        square_scratch(2),
    )
    grad_heads = lax.all_to_all(grad_attended, FS, split_axis=1, concat_axis=0, tiled=True)

    query_rows = after(grad_cquery_rows, grad_attended)
    square = jnp.concatenate(
        [
            window_grad(cross_mixed, grad_cross_branch),
            window_grad(normed_two, query_rows),
            window_grad(attended, grad_self_branch),
        ],
        axis=1,
    )

    def square_chunk(dy, dx):
        return row_block(square, peer(dy, dx), SHARD)

    grad_heads, square = lax.optimization_barrier((grad_heads, square))
    s_lo, s_hi, s20 = reduce_first(square_chunk)
    hidden_parts = peers_parts(after(hidden_sum, grad_heads))

    grad_qkv = self_backward(0, seg_col, seg_row, total0, qkv, grad_heads)
    s_lo, s_hi, s20, kv_own, grad_qkv = lax.optimization_barrier(
        (s_lo, s_hi, s20, kv_own, grad_qkv)
    )
    kv_all = lax.all_gather(kv_own, FS, axis=0, tiled=True)
    s11, s31 = reduce_second(square_chunk, s_lo, s_hi)
    out_minus, out_plus = reduce_z(after(out_far, grad_qkv), out_m, out_p)
    grad_qkv = self_backward(1, seg_col, seg_row, total1, qkv, grad_heads, (grad_qkv,))
    s11, s31, hidden_parts, out_minus, out_plus, grad_qkv = lax.optimization_barrier(
        (s11, s31, hidden_parts, out_minus, out_plus, grad_qkv)
    )
    square_parts = reduce_third(square_chunk, s20, s11, s31)
    heads_own = heads_grad(normed_all, grad_qkv)
    heads_part = peers_parts(heads_own)
    normed_part, sums_one = first_part(after(grad_qkv, heads_own), heads_w, plain_all)
    normed_parts = peers_parts(after(normed_part, heads_part))
    norms = sum_everywhere(
        jnp.concatenate([sums_one[:2], sums_two[:2], sums_three[:2], jnp.zeros((2, D), f32)])
    )
    square = reduce_last(square_chunk, *square_parts).astype(bf16)
    square = jnp.concatenate(
        [square[:, WIN * k : WIN * (k + 1)] for k in range(3)]
        + [jnp.zeros((512 - 3 * SHARD, WIN), bf16)],
        axis=0,
    )
    out_minus, out_plus = shift(out_minus, "z", -1), shift(out_plus, "z", 1)
    outputs = (
        after_cross + out_own.astype(f32) + out_minus.astype(f32) + out_plus.astype(f32)
    )
    hidden_grad = sum_parts(after(hidden_parts, normed_part)).astype(bf16)
    hidden_grad = hidden_grad + shift(hidden_grad, "xh", 1)
    square = scatter_over_dp(square)
    normed_parts, norms, hidden_grad, square = lax.optimization_barrier(
        (normed_parts, norms, hidden_grad, square)
    )
    square = every_peer(square, "z")
    hidden_grad = every_peer(hidden_grad, "z")
    grad_w_up, grad_w_down = sort_hidden(core_index, hidden_grad, shift(hidden_grad, "c", 1))

    own_columns = lax.dynamic_slice_in_dim(context, peer(0, 0) * SHARD, SHARD, axis=1)
    text_part, grad_w_text, grad_w_kv = call(
        text_back_body,
        [
            (core_index, "smem"), (after(kv_all, normed_part), "vmem"), (own_columns, "vmem"),
            (text_columns, "vmem"), (w_text, "vmem"),
            (second_mine, "hbm"), (second_other, "hbm"),
        ],
        [((TXT, TXT), bf16), ((TXT, D), bf16), ((SHARD, 2 * D), bf16)],
        square_scratch(2),
    )

    grad_c_out, grad_c_query, grad_w_out = whole_columns(square, 3)
    heads_rows = unpack_heads(heads_part)

    def half(which):
        kv = jnp.where(which == 0, grad_w_kv[:, :D], grad_w_kv[:, D:])
        return jnp.concatenate(
            [
                row_block(grad_w_text, which, 256),
                row_block(heads_rows, which, 216),
                kv,
                jnp.zeros((640 - 616, D), bf16),
            ],
            axis=0,
        )

    mine = scatter_over_dp(half(core) + shift(half(1 - core), "c", 1))
    mine = every_peer(after(mine, normed_parts), "z")
    other = shift(mine, "c", 1)
    low = jnp.where(first_core, mine, other).astype(f32)
    high = jnp.where(first_core, other, mine).astype(f32)
    grad_w_text = jnp.concatenate([low[:256], high[:256]], axis=0)
    grad_w_query = low[256:400]
    grad_w_key = jnp.concatenate([low[400:472], high[256:328]], axis=0)
    grad_w_value = high[328:472]
    grad_c_key, grad_c_value = low[472:616], high[472:616]

    grad_tokens = call(
        first_back_body,
        [
            (rows_in, "vmem"), (normed_parts, "vmem"), (grad_after_self, "vmem"),
            (row(ln1_gain), "vmem"),
        ],
        [((TOK, D), f32)],
        [],
    )[0]
    grad_text = lax.all_to_all(
        after(text_part, normed_parts), FS, split_axis=0, concat_axis=1, tiled=True
    )
    grad_text = grad_text[:CAP_TOK].astype(f32)
    return (
        outputs[None],
        grad_tokens[None],
        grad_text[None],
        norms[0],
        norms[1],
        grad_w_query,
        grad_w_key,
        grad_w_value,
        grad_w_out,
        norms[2],
        norms[3],
        grad_c_query,
        grad_w_text,
        grad_c_key,
        grad_c_value,
        grad_c_out,
        norms[4],
        norms[5],
        grad_w_up,
        grad_w_down,
    )


def solution(mesh):
    split = Mesh(mesh.devices.reshape(2, 4, 2, 4, 2), ("xh", "z", "c", "y", "xl"))
    dp = ("xh", "z", "c")
    rows = P(dp, FS, None)
    per_row = P(dp, None)
    weight = P(FS, None)
    rep = P()
    in_specs = (
        rows, rows, per_row, per_row, per_row,
        rep, rep, weight, weight, weight, weight,
        rep, rep, weight, weight, weight, weight, weight,
        rep, rep, weight, weight, rows,
    )
    out_specs = (
        rows, rows, rows,
        rep, rep, weight, weight, weight, weight,
        rep, rep, weight, weight, weight, weight, weight,
        rep, rep, weight, weight,
    )
    return jax.shard_map(
        local, mesh=split, in_specs=in_specs, out_specs=out_specs, check_vma=False
    )
```

```python
import functools

import jax
import jax.numpy as jnp
from jax import lax
from jax.experimental import pallas as pl
from jax.experimental.pallas import tpu as pltpu
from jax.sharding import Mesh
from jax.sharding import PartitionSpec as P

HEADS = 16
HEAD = 72
D = 1152
FF = 4608
CAP_TOK = 60
TXT_OWN = 64
TXT = 8 * TXT_OWN
TOK = 256
ROW = 2048
CAP_LEN = 120
SEGS = 3
CAPS = 4
SHARD = 144
SLOT = 128
WIN = 640
STEP = 512

bf16 = jnp.bfloat16
f32 = jnp.float32
norm_eps = 1e-06
masked_score = -1e30
scale = HEAD ** (-0.5)
log2e = 1.4426950408889634
FS = ("y", "xl")
VMEM = 60 * 1024 * 1024


def dot_nn(a, b):
    return lax.dot_general(a, b, (((1,), (0,)), ((), ())), preferred_element_type=f32)


def dot_nt(a, b):
    return lax.dot_general(a, b, (((1,), (1,)), ((), ())), preferred_element_type=f32)


def dot_tn(a, b):
    return lax.dot_general(a, b, (((0,), (0,)), ((), ())), preferred_element_type=f32)


def params():
    return pltpu.CompilerParams(vmem_limit_bytes=VMEM)


def shift(x, axis, by):
    n = lax.axis_size(axis)
    return lax.ppermute(x, axis, [(i, (i + by) % n) for i in range(n)])


def halves(x):
    h = (x.shape[0] // 2 + 15) // 16 * 16
    return x[:h], x[h:]


def after(x, *others):
    return lax.optimization_barrier((x, *others))[0]


def gather_first(x):
    return shift(x, "xl", 1), shift(x, "y", -1), shift(x, "y", 1)


def gather_second(x01, x10):
    return shift(x01, "y", 1), shift(x10, "y", -1), shift(x10, "xl", 1)


def gather_third(x31, x11):
    return shift(halves(x11)[0], "y", -1), shift(halves(x31)[1], "y", 1)


NEAR = ((0, 0), (0, 1), (1, 0), (3, 0))
NEXT = ((3, 1), (2, 0), (1, 1))
LAST = (2, 1)


def reduce_first(chunk):
    lo, hi = halves(chunk(2, 1))
    return shift(lo, "y", 1), shift(hi, "y", -1), shift(chunk(2, 0), "y", 1)


def reduce_second(chunk, lo, hi):
    h = lo.shape[0]
    c11, c31 = chunk(1, 1), chunk(3, 1)
    c11 = jnp.concatenate([c11[:h] + lo, c11[h:]], axis=0)
    c31 = jnp.concatenate([c31[:h], c31[h:] + hi], axis=0)
    return shift(c11, "xl", 1), shift(c31, "y", -1)


def reduce_third(chunk, c20, c11, c31):
    return (
        shift(chunk(1, 0) + c20 + c11, "y", 1),
        shift(chunk(0, 1) + c31, "xl", 1),
        shift(chunk(3, 0), "y", -1),
    )


def reduce_last(chunk, *parts):
    return sum([p.astype(f32) for p in parts], chunk(0, 0).astype(f32))


def every_peer(x, axes=FS):
    n = lax.axis_size(axes)
    copies = jnp.broadcast_to(x[None], (n, *x.shape)).reshape(n * x.shape[0], x.shape[1])
    return lax.all_to_all(copies, axes, 0, 0, tiled=True)


def peers_parts(x, axes=FS):
    return lax.all_to_all(x, axes, 0, 0, tiled=True)


def sum_parts(parts):
    return jnp.sum(parts.reshape(8, -1, parts.shape[1]).astype(f32), axis=0)


def neighbours(x):
    return x, shift(x, "z", 1), shift(x, "z", 2), shift(x, "z", -1)


def in_order(*around):
    rows, cols = around[0].shape

    def body(where, *refs):
        ins, out = refs[:4], refs[4]
        for k in range(4):
            row = pl.multiple_of(lax.rem(where[0] + 4 - k, 4) * rows, 16)
            out[pl.ds(row, rows), :] = ins[k][...]

    vmem = pl.BlockSpec(memory_space=pltpu.VMEM)
    return pl.pallas_call(
        body,
        in_specs=[pl.BlockSpec(memory_space=pltpu.SMEM)] + [vmem] * 4,
        out_specs=vmem,
        out_shape=jax.ShapeDtypeStruct((4 * rows, cols), bf16),
        compiler_params=params(),
    )(lax.axis_index("z").astype(jnp.int32)[None], *around)


def reduce_z(far, minus, plus):
    lo, hi = halves(far)
    lo, hi = shift(lo, "z", -1), shift(hi, "z", 1)
    h = lo.shape[0]
    return (
        jnp.concatenate([minus[:h] + lo, minus[h:]], axis=0),
        jnp.concatenate([plus[:h], plus[h:] + hi], axis=0),
    )


def peer(dy, dx):
    return ((lax.axis_index("y") + dy) % 4) * 2 + (lax.axis_index("xl") ^ dx)


def place_rows(own, first, second, third, gain, bias):
    lo = third[0].shape[0]
    rows, cols = own.shape
    pieces = [(x, p, 0) for x, p in zip((own, *first), NEAR)]
    pieces += [(x, p, 0) for x, p in zip(second, NEXT)]
    pieces += [(third[0], LAST, 0), (third[1], LAST, lo)]
    count = len(pieces)

    def body(where, gain, bias, *refs):
        ins, plain, normed, sem = refs[:count], refs[count], refs[count + 1], refs[-1]
        started = []
        for k, (x, _, off) in enumerate(pieces):
            row = pl.multiple_of(where[k] * rows + off, 16)
            one = pltpu.make_async_copy(ins[k], plain.at[pl.ds(row, x.shape[0])], sem.at[k])
            one.start()
            started.append(one)
        for one in started:
            one.wait()

        def step(i, carry):
            part = pl.ds(pl.multiple_of(i * rows, rows), rows)
            normed[part, :] = (plain[part, :].astype(f32) * gain[...] + bias[...]).astype(bf16)
            return carry

        lax.fori_loop(0, 8, step, 0)

    vmem = pl.BlockSpec(memory_space=pltpu.VMEM)
    return pl.pallas_call(
        body,
        in_specs=[pl.BlockSpec(memory_space=pltpu.SMEM), vmem, vmem]
        + [pl.BlockSpec(memory_space=pl.ANY)] * count,
        out_specs=[vmem, vmem],
        out_shape=[jax.ShapeDtypeStruct((8 * rows, cols), bf16)] * 2,
        scratch_shapes=[pltpu.SemaphoreType.DMA((count,))],
        compiler_params=params(),
    )(
        jnp.stack([peer(*p) for _, p, _ in pieces]).astype(jnp.int32),
        gain,
        bias,
        *[x for x, _, _ in pieces],
    )


QUARTER = 768


def place_quarters(*quarters):
    def body(where, own, minus, plus, far_lo, far_hi, out, sem):
        started = []
        half = far_lo.shape[0]
        for k, (ref, turn, row) in enumerate(
            ((own, 0, 0), (minus, 3, 0), (plus, 1, 0), (far_lo, 2, 0), (far_hi, 2, half))
        ):
            column = pl.multiple_of(lax.rem(where[0] + turn, 4) * QUARTER, 128)
            one = pltpu.make_async_copy(
                ref, out.at[pl.ds(row, ref.shape[0]), pl.ds(column, QUARTER)], sem.at[k]
            )
            one.start()
            started.append(one)
        for one in started:
            one.wait()

    return pl.pallas_call(
        body,
        in_specs=[pl.BlockSpec(memory_space=pltpu.SMEM)] + [pl.BlockSpec(memory_space=pl.ANY)] * 5,
        out_specs=pl.BlockSpec(memory_space=pltpu.VMEM),
        out_shape=jax.ShapeDtypeStruct((D, 4 * QUARTER), bf16),
        scratch_shapes=[pltpu.SemaphoreType.DMA((5,))],
        compiler_params=params(),
    )(lax.axis_index("z").astype(jnp.int32)[None], *quarters)


def pack_heads_body(wq, wk, wv, out):
    for p in range(8):
        rows = slice(SHARD * p, SHARD * (p + 1))
        out[rows, :] = jnp.concatenate([w[:, rows] for w in (wq, wk, wv)], axis=1)


def pack_heads(*weights):
    return pl.pallas_call(
        pack_heads_body,
        out_shape=jax.ShapeDtypeStruct((D, 3 * SHARD), bf16),
        compiler_params=params(),
    )(*weights)


def spread_heads_body(x, out):
    blank = jnp.zeros((D, SLOT - HEAD), bf16)
    for h in range(2):
        for k in range(3):
            first = SHARD * k + HEAD * h
            slot = SLOT * (3 * h + k)
            out[:, slot : slot + SLOT] = jnp.concatenate(
                [x[:, first : first + HEAD], blank], axis=1
            )


def spread_heads(x):
    return pl.pallas_call(
        spread_heads_body,
        out_shape=jax.ShapeDtypeStruct((D, 6 * SLOT), bf16),
        compiler_params=params(),
    )(x)


def self_forward_body(seg_q, seg_k, q, kv, out, total):
    s = dot_nt(q[:, :SLOT], kv[:, SLOT : 2 * SLOT])
    s = jnp.where(seg_q[...] == seg_k[...], s, masked_score)
    top = jnp.max(s, axis=1, keepdims=True)
    p = jnp.exp2((s - top) * (scale * log2e))
    mass = jnp.sum(p, axis=1, keepdims=True)
    out[...] = (dot_nn(p.astype(bf16), kv[:, 2 * SLOT :]) / mass)[:, :HEAD].astype(bf16)
    log_total = top * (scale * log2e) + jnp.log2(mass)
    total[...] = jnp.transpose(jnp.broadcast_to(log_total, (TOK, SLOT)))[0:1, :]


def self_forward(head, seg_q, seg_k, qkv):
    return pl.pallas_call(
        self_forward_body,
        grid=(ROW // TOK,),
        in_specs=[
            pl.BlockSpec((TOK, 1), lambda i: (i, 0)),
            pl.BlockSpec((1, ROW), lambda i: (0, 0)),
            pl.BlockSpec((TOK, 3 * SLOT), lambda i: (i, head)),
            pl.BlockSpec((ROW, 3 * SLOT), lambda i: (0, head)),
        ],
        out_specs=[
            pl.BlockSpec((TOK, HEAD), lambda i: (i, 0)),
            pl.BlockSpec((1, TOK), lambda i: (0, i)),
        ],
        out_shape=[
            jax.ShapeDtypeStruct((ROW, HEAD), bf16),
            jax.ShapeDtypeStruct((1, ROW), f32),
        ],
        compiler_params=params(),
    )(seg_q, seg_k, qkv, qkv)


def self_backward_body(head, seg_k, seg_q, total, q, kv, g, *refs):
    grad, key_sum, value_sum, key_t = refs[-4:]
    i = pl.program_id(0)

    @pl.when(i == 0)
    def _():
        key_sum[...] = jnp.zeros_like(key_sum)
        value_sum[...] = jnp.zeros_like(value_sum)
        key_t[...] = jnp.transpose(kv[:, SLOT : 2 * SLOT])

    rows = pl.ds(pl.multiple_of(i * TOK, TOK), TOK)
    q_h, k_h, v_h = q[:, :SLOT], kv[:, SLOT : 2 * SLOT], kv[:, 2 * SLOT :]
    g_both = g[...]
    g_h = jnp.concatenate(
        [g_both[:, HEAD * head : HEAD * (head + 1)], jnp.zeros((TOK, SLOT - HEAD), bf16)], axis=1
    )
    p = jnp.exp2(dot_nt(k_h, q_h) * (scale * log2e) - total[...])
    p = jnp.where(seg_k[...] == seg_q[...], p, 0.0)
    dp = dot_nt(v_h, g_h)
    ds = (p * (dp - jnp.sum(p * dp, axis=0, keepdims=True))).astype(bf16)
    value_sum[...] += dot_nn(p.astype(bf16), g_h)
    key_sum[...] += dot_nn(ds, q_h)
    grad[rows, :SLOT] = (jnp.transpose(dot_nn(key_t[...], ds)) * scale).astype(bf16)

    @pl.when(i == pl.num_programs(0) - 1)
    def _():
        grad[:, SLOT : 2 * SLOT] = (key_sum[...] * scale).astype(bf16)
        grad[:, 2 * SLOT :] = value_sum[...].astype(bf16)


def self_backward(head, seg_k, seg_q, total, qkv, g, before=()):
    return pl.pallas_call(
        functools.partial(self_backward_body, head),
        grid=(ROW // TOK,),
        in_specs=[
            pl.BlockSpec((ROW, 1), lambda i: (0, 0)),
            pl.BlockSpec((1, TOK), lambda i: (0, i)),
            pl.BlockSpec((1, TOK), lambda i: (0, i)),
            pl.BlockSpec((TOK, 3 * SLOT), lambda i: (i, head)),
            pl.BlockSpec((ROW, 3 * SLOT), lambda i: (0, head)),
            pl.BlockSpec((TOK, SHARD), lambda i: (i, 0)),
        ]
        + [pl.BlockSpec(memory_space=pl.ANY)] * len(before),
        out_specs=pl.BlockSpec((ROW, 3 * SLOT), lambda i: (0, head)),
        out_shape=jax.ShapeDtypeStruct((ROW, 6 * SLOT), bf16),
        input_output_aliases={6: 0} if before else {},
        scratch_shapes=[
            pltpu.VMEM((ROW, SLOT), f32),
            pltpu.VMEM((ROW, SLOT), f32),
            pltpu.VMEM((SLOT, ROW), bf16),
        ],
        compiler_params=params(),
    )(seg_k, seg_q, total, qkv, qkv, g, *before)


def cross_forward_body(cap_q, cap_t, q, k, v, out):
    allowed = cap_q[...] == cap_t[...]
    mixed = []
    for h in range(HEADS):
        a, b = HEAD * h, HEAD * (h + 1)
        s = dot_nt(q[:, a:b], k[:, a:b])
        s = jnp.where(allowed, s, masked_score)
        top = jnp.max(s, axis=1, keepdims=True)
        p = jnp.exp2((s - top) * (scale * log2e))
        mass = jnp.sum(p, axis=1, keepdims=True)
        mixed.append(dot_nn(p.astype(bf16), v[:, a:b]) / mass)
    out[...] = jnp.concatenate(mixed, axis=1).astype(bf16)


def cross_forward(cap_q, cap_t, q, k, v):
    return pl.pallas_call(
        cross_forward_body,
        out_shape=jax.ShapeDtypeStruct((TOK, D), bf16),
        compiler_params=params(),
    )(cap_q, cap_t, q, k, v)


def cross_backward_body(cap_t, cap_q, q, k, v, g, grad_q, grad_kv):
    allowed = cap_t[...] == cap_q[...]
    dq, dk, dv = [], [], []
    for h in range(HEADS):
        a, b = HEAD * h, HEAD * (h + 1)
        q_h, k_h, v_h, g_h = q[:, a:b], k[:, a:b], v[:, a:b], g[:, a:b]
        s = jnp.where(allowed, dot_nt(k_h, q_h), masked_score)
        top = jnp.max(s, axis=0, keepdims=True)
        p = jnp.exp2((s - top) * (scale * log2e))
        p = p / jnp.sum(p, axis=0, keepdims=True)
        dp = dot_nt(v_h, g_h)
        ds = (p * (dp - jnp.sum(p * dp, axis=0, keepdims=True))).astype(bf16)
        dv.append(dot_nn(p.astype(bf16), g_h))
        dk.append(dot_nn(ds, q_h) * scale)
        dq.append(dot_tn(ds, k_h) * scale)
    grad_q[...] = jnp.concatenate(dq, axis=1).astype(bf16)
    grad_kv[:, :D] = jnp.concatenate(dk, axis=1).astype(bf16)
    grad_kv[:, D:] = jnp.concatenate(dv, axis=1).astype(bf16)


def cross_backward(cap_t, cap_q, q, k, v, g):
    return pl.pallas_call(
        cross_backward_body,
        out_shape=[
            jax.ShapeDtypeStruct((TOK, D), bf16),
            jax.ShapeDtypeStruct((TXT, 2 * D), bf16),
        ],
        compiler_params=params(),
    )(cap_t, cap_q, q, k, v, g)


def fetch_pair(core, mine, other, first, second, sem, column=0):
    def run(a, b):
        columns = pl.ds(column, D)
        one = pltpu.make_async_copy(a.at[:, columns], first, sem.at[0])
        two = pltpu.make_async_copy(b.at[:, columns], second, sem.at[1])
        one.start()
        two.start()
        one.wait()
        two.wait()

    @pl.when(core[0] == 0)
    def _():
        run(mine, other)

    @pl.when(core[0] != 0)
    def _():
        run(other, mine)


def fetch_windows(core, mine, other, whole, sem):
    def run(a, b):
        one = pltpu.make_async_copy(
            a.at[:, pl.ds(2 * D, WIN)], whole.at[:, pl.ds(0, WIN)], sem.at[0]
        )
        two = pltpu.make_async_copy(
            b.at[:, pl.ds(2 * D + 128, STEP)], whole.at[:, pl.ds(WIN, STEP)], sem.at[1]
        )
        one.start()
        two.start()
        one.wait()
        two.wait()

    @pl.when(core[0] == 0)
    def _():
        run(mine, other)

    @pl.when(core[0] != 0)
    def _():
        run(other, mine)


def mlp_body(parts, count, core, *refs):
    xs, gs = refs[: parts * count], refs[parts * count : 2 * parts * count]
    mine, other = refs[2 * parts * count : 2 * parts * count + 2]
    outs = refs[2 * parts * count + 2 : -3]
    up, down, sem = refs[-3:]
    fetch_pair(core, mine, other, up, down, sem)
    for k in range(count):
        x = jnp.concatenate([r[...] for r in xs[parts * k : parts * (k + 1)]], axis=0)
        g = jnp.concatenate([r[...] for r in gs[parts * k : parts * (k + 1)]], axis=0)
        out, act_out, pre_out, grad_x = outs[4 * k : 4 * (k + 1)]
        pre = dot_nn(x, up[...])
        grad_act = dot_nt(g, down[...])
        cdf = 0.5 * (1.0 + lax.erf(pre * (0.5**0.5)))
        density = jnp.exp2(pre * pre * (-0.5 * log2e)) * 0.3989422804014327
        act = (pre * cdf).astype(bf16)
        grad_pre = (grad_act * (cdf + pre * density)).astype(bf16)
        act_out[...] = act
        pre_out[...] = grad_pre
        out[...] = dot_nn(act, down[...]).astype(out.dtype)
        grad_x[...] = dot_nt(grad_pre, up[...]).astype(grad_x.dtype)


def mlp(core, xs, gs, mine, other):
    parts = TOK // xs[0].shape[0]
    count = len(xs) // parts
    vmem = pl.BlockSpec(memory_space=pltpu.VMEM)
    hbm = pl.BlockSpec(memory_space=pl.ANY)
    return pl.pallas_call(
        functools.partial(mlp_body, parts, count),
        in_specs=[pl.BlockSpec(memory_space=pltpu.SMEM)]
        + [vmem] * (2 * parts * count)
        + [hbm, hbm],
        out_specs=[vmem] * (4 * count),
        out_shape=[jax.ShapeDtypeStruct((TOK, D), bf16)] * (4 * count),
        scratch_shapes=[
            pltpu.VMEM((D, D), bf16),
            pltpu.VMEM((D, D), bf16),
            pltpu.SemaphoreType.DMA((2,)),
        ],
        compiler_params=params(),
    )(core, *xs, *gs, mine, other)


def mlp_grad_body(which, core, *refs):
    out = refs[16]

    def run(xs, gs):
        out[...] = sum(dot_tn(x[...], g[...]) for x, g in zip(xs, gs)).astype(bf16)

    @pl.when(core[0] == which)
    def _():
        run(refs[:4], refs[4:8])

    @pl.when(core[0] != which)
    def _():
        run(refs[8:12], refs[12:16])


def mlp_grad(which, core, xs, pres, acts, gs):
    whole = [pl.BlockSpec((TOK, D), lambda k: (0, 0))] * 4
    part = [pl.BlockSpec((TOK, 384), lambda k: (0, k))] * 4
    return pl.pallas_call(
        functools.partial(mlp_grad_body, which),
        grid=(3,),
        in_specs=[pl.BlockSpec(memory_space=pltpu.SMEM)] + whole + part + whole + part,
        out_specs=pl.BlockSpec((D, 384), lambda k: (0, k)),
        out_shape=jax.ShapeDtypeStruct((D, D), bf16),
        compiler_params=params(),
    )(core, *xs, *pres, *acts, *gs)


def sort_hidden_body(core, mine, other, up, down):
    def run(ups, downs):
        for f in range(8):
            lanes = slice(SHARD * f, SHARD * (f + 1))
            up[:, 4 * SHARD * f : 4 * SHARD * (f + 1)] = jnp.concatenate(
                [ups[SHARD * z : SHARD * (z + 1), lanes] for z in range(4)], axis=1
            ).astype(f32)
        down[...] = downs[...].astype(f32)

    @pl.when(core[0] == 0)
    def _():
        run(mine, other)

    @pl.when(core[0] != 0)
    def _():
        run(other, mine)


def sort_hidden(core, mine, other):
    vmem = pl.BlockSpec(memory_space=pltpu.VMEM)
    return pl.pallas_call(
        sort_hidden_body,
        in_specs=[pl.BlockSpec(memory_space=pltpu.SMEM), vmem, vmem],
        out_specs=[vmem, vmem],
        out_shape=[
            jax.ShapeDtypeStruct((SHARD, FF), f32),
            jax.ShapeDtypeStruct((4 * SHARD, D), f32),
        ],
        compiler_params=params(),
    )(core, mine, other)


def normalize(x):
    center = x - jnp.mean(x, axis=-1, keepdims=True)
    inverse = lax.rsqrt(jnp.mean(center * center, axis=-1, keepdims=True) + norm_eps)
    return center * inverse, inverse


def norm_back(x, g, gain):
    plain, inverse = normalize(x)
    scaled = g * gain
    mixed = jnp.mean(scaled * plain, axis=-1, keepdims=True)
    grad = inverse * (scaled - jnp.mean(scaled, axis=-1, keepdims=True) - plain * mixed)
    sums = [jnp.sum(g * plain, axis=0, keepdims=True), jnp.sum(g, axis=0, keepdims=True)]
    return grad, sums


def call(body, ins, outs, scratch):
    spaces = {"vmem": pltpu.VMEM, "hbm": pl.ANY, "smem": pltpu.SMEM}
    return pl.pallas_call(
        body,
        in_specs=[pl.BlockSpec(memory_space=spaces[where]) for _, where in ins],
        out_specs=[pl.BlockSpec(memory_space=pltpu.VMEM)] * len(outs),
        out_shape=[jax.ShapeDtypeStruct(*o) for o in outs],
        scratch_shapes=scratch,
        compiler_params=params(),
    )(*[x for x, _ in ins])


def square_scratch(count):
    return [pltpu.VMEM((D, D), bf16)] * count + [pltpu.SemaphoreType.DMA((2,))]


def after_self_body(core, x, mixed, gain, bias, mine, other, total, normed, query, w1, w2, sem):
    fetch_pair(core, mine, other, w1, w2, sem)
    rows = x[...].astype(f32) + dot_nn(mixed[...], w1[...])
    total[...] = rows
    low = (normalize(rows)[0] * gain[...] + bias[...]).astype(bf16)
    normed[...] = low
    query[...] = dot_nn(low, w2[...]).astype(bf16)


def text_keys_body(core, context, mine, other, key, value, w1, w2, sem):
    fetch_pair(core, mine, other, w1, w2, sem, D)
    key[...] = dot_nn(context[...], w1[...]).astype(bf16)
    value[...] = dot_nn(context[...], w2[...]).astype(bf16)


def after_cross_body(core, x, mixed, gain, bias, mine, other, total, normed, w, sem):
    fetch_windows(core, mine, other, w, sem)
    rows = x[...] + dot_nn(mixed[...], w[...])
    total[...] = rows
    normed[...] = (normalize(rows)[0] * gain[...] + bias[...]).astype(bf16)


def third_back_body(core, x, g0, g1, g2, cot, gain, mine, other, grad, low, mixed, sums, w, sem):
    fetch_windows(core, mine, other, w, sem)
    g = g0[...].astype(f32) + g1[...].astype(f32) + g2[...].astype(f32)
    back, both = norm_back(x[...], g, gain[...])
    total = cot[...] + back
    grad[...] = total
    low[...] = total.astype(bf16)
    mixed[...] = dot_nt(total.astype(bf16), w[...]).astype(bf16)
    sums[...] = jnp.concatenate(both + [jnp.zeros((6, D), f32)], axis=0)


def second_back_body(core, x, gq, before, gain, mine, other, grad, low, mixed, sums, w1, w2, sem):
    fetch_pair(core, mine, other, w1, w2, sem)
    back, both = norm_back(x[...], dot_nt(gq[...], w2[...]), gain[...])
    total = before[...] + back
    grad[...] = total
    low[...] = total.astype(bf16)
    mixed[...] = dot_nt(total.astype(bf16), w1[...]).astype(bf16)
    sums[...] = jnp.concatenate(both + [jnp.zeros((6, D), f32)], axis=0)


def first_back_body(x, parts, before, gain, grad):
    g = parts[:TOK, :].astype(f32)
    for k in range(1, 8):
        g = g + parts[TOK * k : TOK * (k + 1), :].astype(f32)
    grad[...] = before[...] + norm_back(x[...].astype(f32), g, gain[...])[0]


def text_back_body(
    core, kv, cols, text, w_text, mine, other, part, grad_text, grad_kv, w1, w2, sem
):
    fetch_pair(core, mine, other, w1, w2, sem, D)
    low = (dot_nt(kv[:, :D], w1[...]) + dot_nt(kv[:, D:], w2[...])).astype(bf16)
    part[...] = dot_nt(low, w_text[...]).astype(bf16)
    grad_text[...] = dot_tn(text[...], low).astype(bf16)
    grad_kv[...] = dot_tn(cols[...], kv[...]).astype(bf16)


def first_part_body(g, w, plain, part, sums):
    rows = dot_nt(g[...], w[...])
    part[...] = rows.astype(bf16)
    both = [
        jnp.sum(rows * plain[...].astype(f32), axis=0, keepdims=True),
        jnp.sum(rows, axis=0, keepdims=True),
        jnp.zeros((6, D), f32),
    ]
    both = jnp.concatenate(both, axis=0)

    @pl.when(pl.program_id(0) == 0)
    def _():
        sums[...] = both

    @pl.when(pl.program_id(0) != 0)
    def _():
        sums[...] += both


def first_part(g, w, plain):
    return pl.pallas_call(
        first_part_body,
        grid=(ROW // TOK,),
        in_specs=[
            pl.BlockSpec((TOK, 6 * SLOT), lambda i: (i, 0)),
            pl.BlockSpec((D, 6 * SLOT), lambda i: (0, 0)),
            pl.BlockSpec((TOK, D), lambda i: (i, 0)),
        ],
        out_specs=[
            pl.BlockSpec((TOK, D), lambda i: (i, 0)),
            pl.BlockSpec((8, D), lambda i: (0, 0)),
        ],
        out_shape=[jax.ShapeDtypeStruct((ROW, D), bf16), jax.ShapeDtypeStruct((8, D), f32)],
        compiler_params=params(),
    )(g, w, plain)


def heads_grad_body(x, g, out):
    grad = dot_tn(x[...], g[...]).astype(bf16)
    out[...] = jnp.concatenate(
        [
            grad[:, SLOT * (3 * h + k) : SLOT * (3 * h + k) + HEAD]
            for k in range(3)
            for h in range(2)
        ],
        axis=1,
    )


def heads_grad(x, g):
    return pl.pallas_call(
        heads_grad_body,
        grid=(3,),
        in_specs=[
            pl.BlockSpec((ROW, 384), lambda i: (0, i)),
            pl.BlockSpec((ROW, 6 * SLOT), lambda i: (0, 0)),
        ],
        out_specs=pl.BlockSpec((384, 3 * SHARD), lambda i: (i, 0)),
        out_shape=jax.ShapeDtypeStruct((D, 3 * SHARD), bf16),
        compiler_params=params(),
    )(x, g)


def unpack_heads_body(x, out):
    for k in range(3):
        out[SHARD * k : SHARD * (k + 1), :] = jnp.concatenate(
            [x[SHARD * p : SHARD * (p + 1), SHARD * k : SHARD * (k + 1)] for p in range(8)], axis=1
        )


def unpack_heads(x):
    return pl.pallas_call(
        unpack_heads_body,
        out_shape=jax.ShapeDtypeStruct((3 * SHARD, D), bf16),
        compiler_params=params(),
    )(x)


def row_block(x, index, rows):
    return lax.dynamic_slice_in_dim(x, index * rows, rows, axis=0)


def core_window(x, core):
    return lax.dynamic_slice_in_dim(x, core * STEP, WIN, axis=1)


def both_cores(x):
    return jnp.concatenate([x, shift(x, "c", 1)], axis=0)


def window_grad(left, right):
    core = lax.axis_index("c")
    sent = shift(core_window(right, 1 - core), "c", 1)
    rights = jnp.concatenate([core_window(right, core), sent], axis=0)
    return dot_tn(both_cores(left), rights).astype(bf16)


def scatter_over_dp(x):
    part = lax.psum_scatter(x, "z", scatter_dimension=0, tiled=True)
    return part + shift(part, "xh", 1)


def sum_everywhere(x):
    for axis in ("y", "xl", "z", "xh", "c"):
        n = lax.axis_size(axis)
        x = sum([shift(x, axis, k) for k in range(1, n)], x)
    return x


def local(
    tokens,
    text_states,
    seg_lengths,
    caption_of_segment,
    text_lengths,
    ln1_gain,
    ln1_bias,
    w_query,
    w_key,
    w_value,
    w_out,
    ln2_gain,
    ln2_bias,
    c_query,
    w_text,
    c_key,
    c_value,
    c_out,
    ln3_gain,
    ln3_bias,
    w_up,
    w_down,
    cotangent,
):
    core = lax.axis_index("c")
    first_core = core == 0
    core_index = core.astype(jnp.int32)[None]
    quarter = lax.axis_index("z")
    first_row = peer(0, 0) * TOK

    ends = jnp.cumsum(seg_lengths[0])
    positions = jnp.arange(ROW, dtype=jnp.int32)
    segment = jnp.sum((positions[:, None] >= ends[None, :]).astype(jnp.int32), axis=1)
    own_segment = lax.dynamic_slice_in_dim(segment, first_row, TOK)
    text_row = jnp.arange(TXT, dtype=jnp.int32)
    text_pos = text_row // TXT_OWN * CAP_TOK + text_row % TXT_OWN
    text_caption = text_pos // CAP_LEN
    live = jnp.sum(
        jnp.where(
            text_caption[:, None] == jnp.arange(CAPS, dtype=jnp.int32)[None, :],
            text_lengths[0][None, :],
            0,
        ),
        axis=1,
    )
    query_caption = jnp.sum(
        jnp.where(
            own_segment[:, None] == jnp.arange(SEGS, dtype=jnp.int32)[None, :],
            caption_of_segment[0][None, :],
            0,
        ),
        axis=1,
    )
    text_live = (text_row % TXT_OWN < CAP_TOK) & (text_pos % CAP_LEN < live)
    text_key = jnp.where(text_live, text_caption, -1)

    def row(x):
        return x[None, :]

    gap = jnp.zeros((SHARD, 128), bf16)
    square_pack = jnp.where(
        first_core,
        jnp.concatenate([w_out, c_key, c_out[:, :WIN], gap], axis=1),
        jnp.concatenate([c_query, c_value, c_out[:, STEP:], gap], axis=1),
    )
    square_pack = lax.dynamic_slice_in_dim(square_pack, quarter * QUARTER, QUARTER, axis=1)
    quarter_own = lax.all_gather(square_pack, FS, axis=0, tiled=True)

    rows_in = tokens[0]
    plain = normalize(rows_in.astype(f32))[0].astype(bf16)
    n01, n10, n30 = gather_first(plain)

    heads_w = peers_parts(pack_heads(after(w_query, plain), w_key, w_value))
    n01, n10, n30 = lax.optimization_barrier((n01, n10, n30))
    n31, n20, n11 = gather_second(n01, n10)

    text_own = jnp.pad(after(text_states[0], heads_w), ((0, TXT_OWN - CAP_TOK), (0, 0)))
    text_columns = lax.all_to_all(text_own, FS, split_axis=1, concat_axis=0, tiled=True)
    n31, n20, n11, text_columns = lax.optimization_barrier((n31, n20, n11, text_columns))
    n21 = gather_third(n31, n11)
    heads_w = spread_heads(heads_w)
    context_part = dot_nn(text_columns, w_text).astype(bf16)
    context_own = lax.psum_scatter(context_part, FS, scatter_dimension=0, tiled=True)
    plain_all, normed_all = place_rows(
        after(plain, context_part),
        (n01, n10, n30),
        (n31, n20, n11),
        n21,
        row(ln1_gain),
        row(ln1_bias),
    )
    quarter_own, normed_all = lax.optimization_barrier((quarter_own, normed_all))
    quarter_minus, quarter_plus = shift(quarter_own, "z", 1), shift(quarter_own, "z", -1)

    up_own = jnp.concatenate(
        [
            lax.dynamic_slice(w_up, (0, 4 * SHARD * k + SHARD * quarter), (SHARD, SHARD))
            for k in range(8)
        ],
        axis=1,
    )
    hidden_own = jnp.where(first_core, up_own, row_block(w_down, quarter, SHARD))

    seg_col, seg_row = segment[:, None], segment[None, :]
    qkv = dot_nn(normed_all, heads_w).astype(bf16)
    head0, total0 = self_forward(0, seg_col, seg_row, qkv)
    head1, total1 = self_forward(1, seg_col, seg_row, after(qkv, head0))
    quarter_minus, quarter_plus, context_own, head1 = lax.optimization_barrier(
        (quarter_minus, quarter_plus, context_own, head1)
    )
    context = lax.all_gather(context_own, FS, axis=0, tiled=True)
    quarter_far = (
        shift(halves(quarter_minus)[0], "z", 1),
        shift(halves(quarter_plus)[1], "z", -1),
    )
    attended = lax.all_to_all(
        jnp.concatenate([head0, head1], axis=1), FS, split_axis=0, concat_axis=1, tiled=True
    )
    attended, *quarter_far = lax.optimization_barrier((attended, *quarter_far))
    square_mine = place_quarters(quarter_own, quarter_minus, quarter_plus, *quarter_far)
    square_other = shift(square_mine, "c", 1)
    grad_out = cotangent[0]
    grad_mlp = grad_out.astype(bf16)
    grad_sent = after(grad_mlp, square_mine)
    mlp_minus, mlp_plus = shift(grad_sent, "z", 1), shift(grad_sent, "z", -1)
    hidden_mine = every_peer(after(hidden_own, attended))

    after_self, normed_two, cross_query = call(
        after_self_body,
        [
            (core_index, "smem"), (rows_in, "vmem"), (attended, "vmem"),
            (row(ln2_gain), "vmem"), (row(ln2_bias), "vmem"),
            (square_mine, "hbm"), (square_other, "hbm"),
        ],
        [((TOK, D), f32), ((TOK, D), bf16), ((TOK, D), bf16)],
        square_scratch(2),
    )
    cross_key, cross_value = call(
        text_keys_body,
        [
            (core_index, "smem"), (after(context, cross_query, mlp_minus, mlp_plus), "vmem"),
            (square_mine, "hbm"), (square_other, "hbm"),
        ],
        [((TXT, D), bf16), ((TXT, D), bf16)],
        square_scratch(2),
    )
    cross_mixed = cross_forward(
        query_caption[:, None], text_key[None, :], cross_query, cross_key, cross_value
    )
    hidden_mine = after(hidden_mine, cross_mixed)
    weights = (hidden_mine, shift(hidden_mine, "c", 1))
    after_cross, normed_three = call(
        after_cross_body,
        [
            (core_index, "smem"), (after_self, "vmem"), (cross_mixed, "vmem"),
            (row(ln3_gain), "vmem"), (row(ln3_bias), "vmem"),
            (square_mine, "hbm"), (square_other, "hbm"),
        ],
        [((TOK, D), f32), ((TOK, D), bf16)],
        square_scratch(1),
    )

    mlp_sent = lax.optimization_barrier((mlp_minus, mlp_plus, cross_query))
    mlp_far = (
        shift(halves(mlp_sent[0])[0], "z", 1),
        shift(halves(mlp_sent[1])[1], "z", -1),
    )

    three_minus, three_plus = shift(normed_three, "z", 1), shift(normed_three, "z", -1)
    out_own, act_own, pre_own, back_own = mlp(core_index, (normed_three,), (grad_mlp,), *weights)
    three_minus, three_plus, out_own = lax.optimization_barrier(
        (three_minus, three_plus, out_own)
    )
    three_far = (
        shift(halves(three_minus)[0], "z", 1),
        shift(halves(three_plus)[1], "z", -1),
    )
    near = mlp(core_index, (three_minus, three_plus), (mlp_minus, mlp_plus), *weights)
    out_m, act_m, pre_m, back_m, out_p, act_p, pre_p, back_p = near
    *three_far, out_m = lax.optimization_barrier((*three_far, out_m))
    out_far, act_far, pre_far, back_far = mlp(core_index, three_far, mlp_far, *weights)
    back_minus, back_plus = reduce_z(back_far, back_m, back_p)
    three_parts = (normed_three, three_minus, three_plus, jnp.concatenate(three_far, axis=0))
    pre_parts = (pre_own, pre_m, pre_p, pre_far)
    act_parts = (act_own, act_m, act_p, act_far)
    mlp_parts = (grad_mlp, mlp_minus, mlp_plus, jnp.concatenate(mlp_far, axis=0))
    send = mlp_grad(1, core_index, three_parts, pre_parts, act_parts, mlp_parts)
    back_minus, back_plus, send = lax.optimization_barrier((back_minus, back_plus, send))
    back_minus, back_plus = shift(back_minus, "z", -1), shift(back_plus, "z", 1)
    keep = mlp_grad(
        0, core_index, three_parts, pre_parts, act_parts, (after(grad_mlp, send), *mlp_parts[1:])
    )
    back_minus, back_plus, keep = lax.optimization_barrier((back_minus, back_plus, keep))
    hidden_sum = keep + shift(send, "c", 1)
    grad_after_cross, grad_cross_branch, grad_cross_mixed, sums_three = call(
        third_back_body,
        [
            (core_index, "smem"), (after_cross, "vmem"), (back_own, "vmem"),
            (back_minus, "vmem"), (back_plus, "vmem"), (grad_out, "vmem"),
            (row(ln3_gain), "vmem"), (square_mine, "hbm"), (square_other, "hbm"),
        ],
        [((TOK, D), f32), ((TOK, D), bf16), ((TOK, D), bf16), ((8, D), f32)],
        square_scratch(1),
    )

    grad_cquery_rows, grad_kv = cross_backward(
        text_key[:, None],
        query_caption[None, :],
        cross_query,
        cross_key,
        cross_value,
        grad_cross_mixed,
    )
    kv_own = lax.psum_scatter(grad_kv, FS, scatter_dimension=0, tiled=True)
    grad_after_self, grad_self_branch, grad_attended, sums_two = call(
        second_back_body,
        [
            (core_index, "smem"), (after_self, "vmem"), (grad_cquery_rows, "vmem"),
            (grad_after_cross, "vmem"), (row(ln2_gain), "vmem"),
            (square_mine, "hbm"), (square_other, "hbm"),
        ],
        [((TOK, D), f32), ((TOK, D), bf16), ((TOK, D), bf16), ((8, D), f32)],
        square_scratch(2),
    )
    grad_heads = lax.all_to_all(grad_attended, FS, split_axis=1, concat_axis=0, tiled=True)

    square = jnp.concatenate(
        [
            window_grad(cross_mixed, after(grad_cross_branch, grad_attended)),
            window_grad(normed_two, after(grad_cquery_rows, grad_attended)),
            window_grad(attended, grad_self_branch),
        ],
        axis=1,
    )

    def square_chunk(dy, dx):
        return row_block(square, peer(dy, dx), SHARD)

    grad_heads, square = lax.optimization_barrier((grad_heads, square))
    hidden_parts = peers_parts(after(hidden_sum, grad_heads))
    grad_qkv = self_backward(0, seg_col, seg_row, total0, qkv, grad_heads)
    kv_own, grad_qkv, square = lax.optimization_barrier((kv_own, grad_qkv, square))
    s_lo, s_hi, s20 = reduce_first(square_chunk)
    kv_all = lax.all_gather(kv_own, FS, axis=0, tiled=True)
    out_minus, out_plus = reduce_z(after(out_far, kv_own), out_m, out_p)
    grad_qkv = self_backward(
        1, seg_col, seg_row, total1, qkv, after(grad_heads, kv_own), (grad_qkv,)
    )
    s_lo, s_hi, out_minus, out_plus, grad_qkv = lax.optimization_barrier(
        (s_lo, s_hi, out_minus, out_plus, grad_qkv)
    )
    s11, s31 = reduce_second(square_chunk, s_lo, s_hi)
    heads_own = heads_grad(normed_all, grad_qkv)
    heads_own, hidden_parts = lax.optimization_barrier((heads_own, hidden_parts))
    heads_part = peers_parts(heads_own)
    normed_part, sums_one = first_part(after(grad_qkv, heads_own), heads_w, plain_all)
    normed_parts = peers_parts(after(normed_part, heads_part))
    s11, s31, normed_part = lax.optimization_barrier((s11, s31, normed_part))
    square_parts = reduce_third(square_chunk, s20, s11, s31)
    square = reduce_last(square_chunk, *square_parts).astype(bf16)
    hidden_grad = sum_parts(after(hidden_parts, normed_part)).astype(bf16)
    hidden_grad = hidden_grad + shift(hidden_grad, "xh", 1)
    hidden_z = neighbours(hidden_grad)

    own_columns = lax.dynamic_slice_in_dim(context, peer(0, 0) * SHARD, SHARD, axis=1)
    text_part, grad_w_text, grad_w_kv = call(
        text_back_body,
        [
            (core_index, "smem"), (after(kv_all, normed_part), "vmem"), (own_columns, "vmem"),
            (text_columns, "vmem"), (w_text, "vmem"),
            (square_mine, "hbm"), (square_other, "hbm"),
        ],
        [((TXT, TXT), bf16), ((TXT, D), bf16), ((SHARD, 2 * D), bf16)],
        square_scratch(2),
    )

    heads_rows = unpack_heads(heads_part)
    early = row_block(heads_rows, core, 216) + shift(row_block(heads_rows, 1 - core, 216), "c", 1)
    early = jnp.concatenate([early, jnp.zeros((256 - 216, D), bf16)], axis=0)
    rest = jnp.zeros((256 - SHARD, WIN), bf16)
    square = jnp.concatenate(
        [early] + [
            jnp.concatenate([square[:, WIN * k : WIN * (k + 1)], rest], axis=0) for k in range(3)
        ],
        axis=1,
    )
    early = scatter_over_dp(square)

    def half(which):
        kv = jnp.where(which == 0, grad_w_kv[:, :D], grad_w_kv[:, D:])
        return jnp.concatenate(
            [row_block(grad_w_text, which, 256), kv, jnp.zeros((512 - 400, D), bf16)], axis=0
        )

    late = half(core) + shift(half(1 - core), "c", 1)
    late = scatter_over_dp(late)
    normed_parts, early, late, *hidden_z = lax.optimization_barrier(
        (normed_parts, early, late, *hidden_z)
    )
    early = in_order(*neighbours(early))
    late = in_order(*neighbours(late))
    hidden_grad = in_order(*hidden_z)
    grad_w_up, grad_w_down = sort_hidden(core_index, hidden_grad, shift(hidden_grad, "c", 1))
    sums_one = after(sums_one, normed_parts)
    norms = sum_everywhere(
        jnp.concatenate([sums_one[:2], sums_two[:2], sums_three[:2], jnp.zeros((2, D), f32)])
    )
    other = shift(early, "c", 1)
    low = jnp.where(first_core, early, other).astype(f32)
    high = jnp.where(first_core, other, early).astype(f32)
    grad_w_query = low[:144, :D]
    grad_w_key = jnp.concatenate([low[144:216, :D], high[:72, :D]], axis=0)
    grad_w_value = high[72:216, :D]
    grad_c_out, grad_c_query, grad_w_out = (
        jnp.concatenate(
            [
                low[:SHARD, D + WIN * k : D + WIN * (k + 1)],
                high[:SHARD, D + WIN * k + 128 : D + WIN * (k + 1)],
            ],
            axis=1,
        )
        for k in range(3)
    )

    other = shift(late, "c", 1)
    low = jnp.where(first_core, late, other).astype(f32)
    high = jnp.where(first_core, other, late).astype(f32)
    grad_w_text = jnp.concatenate([low[:256], high[:256]], axis=0)
    grad_c_key, grad_c_value = low[256:400], high[256:400]
    out_minus, out_plus = shift(out_minus, "z", -1), shift(out_plus, "z", 1)
    outputs = (
        after_cross + out_own.astype(f32) + out_minus.astype(f32) + out_plus.astype(f32)
    )

    grad_tokens = call(
        first_back_body,
        [
            (rows_in, "vmem"), (normed_parts, "vmem"), (grad_after_self, "vmem"),
            (row(ln1_gain), "vmem"),
        ],
        [((TOK, D), f32)],
        [],
    )[0]
    grad_text = lax.all_to_all(
        after(text_part, normed_parts), FS, split_axis=0, concat_axis=1, tiled=True
    )
    grad_text = grad_text[:CAP_TOK].astype(f32)
    return (
        outputs[None],
        grad_tokens[None],
        grad_text[None],
        norms[0],
        norms[1],
        grad_w_query,
        grad_w_key,
        grad_w_value,
        grad_w_out,
        norms[2],
        norms[3],
        grad_c_query,
        grad_w_text,
        grad_c_key,
        grad_c_value,
        grad_c_out,
        norms[4],
        norms[5],
        grad_w_up,
        grad_w_down,
    )


def solution(mesh):
    split = Mesh(mesh.devices.reshape(2, 4, 2, 4, 2), ("xh", "z", "c", "y", "xl"))
    dp = ("xh", "z", "c")
    rows = P(dp, FS, None)
    per_row = P(dp, None)
    weight = P(FS, None)
    rep = P()
    in_specs = (
        rows, rows, per_row, per_row, per_row,
        rep, rep, weight, weight, weight, weight,
        rep, rep, weight, weight, weight, weight, weight,
        rep, rep, weight, weight, rows,
    )
    out_specs = (
        rows, rows, rows,
        rep, rep, weight, weight, weight, weight,
        rep, rep, weight, weight, weight, weight, weight,
        rep, rep, weight, weight,
    )
    return jax.shard_map(
        local, mesh=split, in_specs=in_specs, out_specs=out_specs, check_vma=False
    )
```

```python
import functools

import jax
import jax.numpy as jnp
from jax import lax
from jax.experimental import pallas as pl
from jax.experimental.pallas import tpu as pltpu
from jax.sharding import Mesh
from jax.sharding import PartitionSpec as P

HEADS = 16
HEAD = 72
D = 1152
FF = 4608
CAP_TOK = 60
TXT_OWN = 64
TXT = 8 * TXT_OWN
TOK = 256
ROW = 2048
CAP_LEN = 120
SEGS = 3
CAPS = 4
SHARD = 144
SLOT = 128
SPLIT = 1
WIN = 640
STEP = 512

bf16 = jnp.bfloat16
f32 = jnp.float32
norm_eps = 1e-06
masked_score = -1e30
scale = HEAD ** (-0.5)
log2e = 1.4426950408889634
FS = ("y", "xl")
VMEM = 60 * 1024 * 1024


def dot_nn(a, b):
    return lax.dot_general(a, b, (((1,), (0,)), ((), ())), preferred_element_type=f32)


def dot_nt(a, b):
    return lax.dot_general(a, b, (((1,), (1,)), ((), ())), preferred_element_type=f32)


def dot_tn(a, b):
    return lax.dot_general(a, b, (((0,), (0,)), ((), ())), preferred_element_type=f32)


def params():
    return pltpu.CompilerParams(vmem_limit_bytes=VMEM)


def shift(x, axis, by):
    n = lax.axis_size(axis)
    return lax.ppermute(x, axis, [(i, (i + by) % n) for i in range(n)])


def halves(x):
    h = (x.shape[0] // 2 + 15) // 16 * 16
    return x[:h], x[h:]


def after(x, *others):
    return lax.optimization_barrier((x, *others))[0]


def gather_first(x):
    return shift(x, "xl", 1), shift(x, "y", -1), shift(x, "y", 1)


def gather_second(x01, x10):
    return shift(x01, "y", 1), shift(x10, "y", -1), shift(x10, "xl", 1)


def gather_third(x31, x11):
    return shift(halves(x11)[0], "y", -1), shift(halves(x31)[1], "y", 1)


NEAR = ((0, 0), (0, 1), (1, 0), (3, 0))
NEXT = ((3, 1), (2, 0), (1, 1))
LAST = (2, 1)


def reduce_first(chunk):
    lo, hi = halves(chunk(2, 1))
    return shift(lo, "y", 1), shift(hi, "y", -1), shift(chunk(2, 0), "y", 1)


def reduce_second(chunk, lo, hi):
    h = lo.shape[0]
    c11, c31 = chunk(1, 1), chunk(3, 1)
    c11 = jnp.concatenate([c11[:h] + lo, c11[h:]], axis=0)
    c31 = jnp.concatenate([c31[:h], c31[h:] + hi], axis=0)
    return shift(c11, "xl", 1), shift(c31, "y", -1)


def reduce_third(chunk, c20, c11, c31):
    return (
        shift(chunk(1, 0) + c20 + c11, "y", 1),
        shift(chunk(0, 1) + c31, "xl", 1),
        shift(chunk(3, 0), "y", -1),
    )


def reduce_last(chunk, *parts):
    return sum([p.astype(f32) for p in parts], chunk(0, 0).astype(f32))


def every_peer(x, axes=FS):
    n = lax.axis_size(axes)
    copies = jnp.broadcast_to(x[None], (n, *x.shape)).reshape(n * x.shape[0], x.shape[1])
    return lax.all_to_all(copies, axes, 0, 0, tiled=True)


def peers_parts(x, axes=FS):
    return lax.all_to_all(x, axes, 0, 0, tiled=True)


def sum_parts(parts):
    return jnp.sum(parts.reshape(8, -1, parts.shape[1]).astype(f32), axis=0)


def neighbours(x):
    return x, shift(x, "z", 1), shift(x, "z", 2), shift(x, "z", -1)


def in_order(*around):
    rows, cols = around[0].shape

    def body(where, *refs):
        ins, out = refs[:4], refs[4]
        for k in range(4):
            row = pl.multiple_of(lax.rem(where[0] + 4 - k, 4) * rows, 16)
            out[pl.ds(row, rows), :] = ins[k][...]

    vmem = pl.BlockSpec(memory_space=pltpu.VMEM)
    return pl.pallas_call(
        body,
        in_specs=[pl.BlockSpec(memory_space=pltpu.SMEM)] + [vmem] * 4,
        out_specs=vmem,
        out_shape=jax.ShapeDtypeStruct((4 * rows, cols), bf16),
        compiler_params=params(),
    )(lax.axis_index("z").astype(jnp.int32)[None], *around)


def reduce_z(far, minus, plus):
    lo, hi = halves(far)
    lo, hi = shift(lo, "z", -1), shift(hi, "z", 1)
    h = lo.shape[0]
    return (
        jnp.concatenate([minus[:h] + lo, minus[h:]], axis=0),
        jnp.concatenate([plus[:h], plus[h:] + hi], axis=0),
    )


def peer(dy, dx):
    return ((lax.axis_index("y") + dy) % 4) * 2 + (lax.axis_index("xl") ^ dx)


def place_rows(own, first, second, third, gain, bias):
    lo = third[0].shape[0]
    rows, cols = own.shape
    pieces = [(x, p, 0) for x, p in zip((own, *first), NEAR)]
    pieces += [(x, p, 0) for x, p in zip(second, NEXT)]
    pieces += [(third[0], LAST, 0), (third[1], LAST, lo)]
    count = len(pieces)

    def body(where, gain, bias, *refs):
        ins, plain, normed, sem = refs[:count], refs[count], refs[count + 1], refs[-1]
        started = []
        for k, (x, _, off) in enumerate(pieces):
            row = pl.multiple_of(where[k] * rows + off, 16)
            one = pltpu.make_async_copy(ins[k], plain.at[pl.ds(row, x.shape[0])], sem.at[k])
            one.start()
            started.append(one)
        for one in started:
            one.wait()

        def step(i, carry):
            part = pl.ds(pl.multiple_of(i * rows, rows), rows)
            normed[part, :] = (plain[part, :].astype(f32) * gain[...] + bias[...]).astype(bf16)
            return carry

        lax.fori_loop(0, 8, step, 0)

    vmem = pl.BlockSpec(memory_space=pltpu.VMEM)
    return pl.pallas_call(
        body,
        in_specs=[pl.BlockSpec(memory_space=pltpu.SMEM), vmem, vmem]
        + [pl.BlockSpec(memory_space=pl.ANY)] * count,
        out_specs=[vmem, vmem],
        out_shape=[jax.ShapeDtypeStruct((8 * rows, cols), bf16)] * 2,
        scratch_shapes=[pltpu.SemaphoreType.DMA((count,))],
        compiler_params=params(),
    )(
        jnp.stack([peer(*p) for _, p, _ in pieces]).astype(jnp.int32),
        gain,
        bias,
        *[x for x, _, _ in pieces],
    )


QUARTER = 768


def place_quarters(*quarters):
    def body(where, own, minus, plus, far_lo, far_hi, out, sem):
        started = []
        half = far_lo.shape[0]
        for k, (ref, turn, row) in enumerate(
            ((own, 0, 0), (minus, 3, 0), (plus, 1, 0), (far_lo, 2, 0), (far_hi, 2, half))
        ):
            column = pl.multiple_of(lax.rem(where[0] + turn, 4) * QUARTER, 128)
            one = pltpu.make_async_copy(
                ref, out.at[pl.ds(row, ref.shape[0]), pl.ds(column, QUARTER)], sem.at[k]
            )
            one.start()
            started.append(one)
        for one in started:
            one.wait()

    return pl.pallas_call(
        body,
        in_specs=[pl.BlockSpec(memory_space=pltpu.SMEM)] + [pl.BlockSpec(memory_space=pl.ANY)] * 5,
        out_specs=pl.BlockSpec(memory_space=pltpu.VMEM),
        out_shape=jax.ShapeDtypeStruct((D, 4 * QUARTER), bf16),
        scratch_shapes=[pltpu.SemaphoreType.DMA((5,))],
        compiler_params=params(),
    )(lax.axis_index("z").astype(jnp.int32)[None], *quarters)


def pack_heads_body(wq, wk, wv, out):
    for p in range(8):
        rows = slice(SHARD * p, SHARD * (p + 1))
        out[rows, :] = jnp.concatenate([w[:, rows] for w in (wq, wk, wv)], axis=1)


def pack_heads(*weights):
    return pl.pallas_call(
        pack_heads_body,
        out_shape=jax.ShapeDtypeStruct((D, 3 * SHARD), bf16),
        compiler_params=params(),
    )(*weights)


def spread_heads_body(x, out):
    blank = jnp.zeros((D, SLOT - HEAD), bf16)
    for h in range(2):
        for k in range(3):
            first = SHARD * k + HEAD * h
            slot = SLOT * (3 * h + k)
            out[:, slot : slot + SLOT] = jnp.concatenate(
                [x[:, first : first + HEAD], blank], axis=1
            )


def spread_heads(x):
    return pl.pallas_call(
        spread_heads_body,
        out_shape=jax.ShapeDtypeStruct((D, 6 * SLOT), bf16),
        compiler_params=params(),
    )(x)


def self_forward_body(seg_q, seg_k, q, kv, out, total):
    s = dot_nt(q[:, :SLOT], kv[:, SLOT : 2 * SLOT])
    s = jnp.where(seg_q[...] == seg_k[...], s, masked_score)
    top = jnp.max(s, axis=1, keepdims=True)
    p = jnp.exp2((s - top) * (scale * log2e))
    mass = jnp.sum(p, axis=1, keepdims=True)
    out[...] = (dot_nn(p.astype(bf16), kv[:, 2 * SLOT :]) / mass)[:, :HEAD].astype(bf16)
    log_total = top * (scale * log2e) + jnp.log2(mass)
    total[...] = jnp.transpose(jnp.broadcast_to(log_total, (TOK, SLOT)))[0:1, :]


def self_forward(head, seg_q, seg_k, qkv):
    return pl.pallas_call(
        self_forward_body,
        grid=(ROW // TOK,),
        in_specs=[
            pl.BlockSpec((TOK, 1), lambda i: (i, 0)),
            pl.BlockSpec((1, ROW), lambda i: (0, 0)),
            pl.BlockSpec((TOK, 3 * SLOT), lambda i: (i, head)),
            pl.BlockSpec((ROW, 3 * SLOT), lambda i: (0, head)),
        ],
        out_specs=[
            pl.BlockSpec((TOK, HEAD), lambda i: (i, 0)),
            pl.BlockSpec((1, TOK), lambda i: (0, i)),
        ],
        out_shape=[
            jax.ShapeDtypeStruct((ROW, HEAD), bf16),
            jax.ShapeDtypeStruct((1, ROW), f32),
        ],
        compiler_params=params(),
    )(seg_q, seg_k, qkv, qkv)


def self_backward_body(head, seg_k, seg_q, total, q, kv, g, *refs):
    grad, key_sum, value_sum, key_t = refs[-4:]
    i = pl.program_id(0)

    @pl.when(i == 0)
    def _():
        key_sum[...] = jnp.zeros_like(key_sum)
        value_sum[...] = jnp.zeros_like(value_sum)
        key_t[...] = jnp.transpose(kv[:, SLOT : 2 * SLOT])

    rows = pl.ds(pl.multiple_of(i * TOK, TOK), TOK)
    q_h, k_h, v_h = q[:, :SLOT], kv[:, SLOT : 2 * SLOT], kv[:, 2 * SLOT :]
    g_both = g[...]
    g_h = jnp.concatenate(
        [g_both[:, HEAD * head : HEAD * (head + 1)], jnp.zeros((TOK, SLOT - HEAD), bf16)], axis=1
    )
    p = jnp.exp2(dot_nt(k_h, q_h) * (scale * log2e) - total[...])
    p = jnp.where(seg_k[...] == seg_q[...], p, 0.0)
    dp = dot_nt(v_h, g_h)
    ds = (p * (dp - jnp.sum(p * dp, axis=0, keepdims=True))).astype(bf16)
    value_sum[...] += dot_nn(p.astype(bf16), g_h)
    key_sum[...] += dot_nn(ds, q_h)
    grad[rows, :SLOT] = (jnp.transpose(dot_nn(key_t[...], ds)) * scale).astype(bf16)

    @pl.when(i == pl.num_programs(0) - 1)
    def _():
        grad[:, SLOT : 2 * SLOT] = (key_sum[...] * scale).astype(bf16)
        grad[:, 2 * SLOT :] = value_sum[...].astype(bf16)


def self_backward(head, seg_k, seg_q, total, qkv, g, before=()):
    return pl.pallas_call(
        functools.partial(self_backward_body, head),
        grid=(ROW // TOK,),
        in_specs=[
            pl.BlockSpec((ROW, 1), lambda i: (0, 0)),
            pl.BlockSpec((1, TOK), lambda i: (0, i)),
            pl.BlockSpec((1, TOK), lambda i: (0, i)),
            pl.BlockSpec((TOK, 3 * SLOT), lambda i: (i, head)),
            pl.BlockSpec((ROW, 3 * SLOT), lambda i: (0, head)),
            pl.BlockSpec((TOK, SHARD), lambda i: (i, 0)),
        ]
        + [pl.BlockSpec(memory_space=pl.ANY)] * len(before),
        out_specs=pl.BlockSpec((ROW, 3 * SLOT), lambda i: (0, head)),
        out_shape=jax.ShapeDtypeStruct((ROW, 6 * SLOT), bf16),
        input_output_aliases={6: 0} if before else {},
        scratch_shapes=[
            pltpu.VMEM((ROW, SLOT), f32),
            pltpu.VMEM((ROW, SLOT), f32),
            pltpu.VMEM((SLOT, ROW), bf16),
        ],
        compiler_params=params(),
    )(seg_k, seg_q, total, qkv, qkv, g, *before)


def cross_forward_body(cap_q, cap_t, q, k, v, out):
    allowed = cap_q[...] == cap_t[...]
    mixed = []
    for h in range(HEADS):
        a, b = HEAD * h, HEAD * (h + 1)
        s = dot_nt(q[:, a:b], k[:, a:b])
        s = jnp.where(allowed, s, masked_score)
        top = jnp.max(s, axis=1, keepdims=True)
        p = jnp.exp2((s - top) * (scale * log2e))
        mass = jnp.sum(p, axis=1, keepdims=True)
        mixed.append(dot_nn(p.astype(bf16), v[:, a:b]) / mass)
    out[...] = jnp.concatenate(mixed, axis=1).astype(bf16)


def cross_forward(cap_q, cap_t, q, k, v):
    return pl.pallas_call(
        cross_forward_body,
        out_shape=jax.ShapeDtypeStruct((TOK, D), bf16),
        compiler_params=params(),
    )(cap_q, cap_t, q, k, v)


def cross_backward_body(cap_t, cap_q, q, k, v, g, grad_q, grad_kv):
    allowed = cap_t[...] == cap_q[...]
    dq, dk, dv = [], [], []
    for h in range(HEADS):
        a, b = HEAD * h, HEAD * (h + 1)
        q_h, k_h, v_h, g_h = q[:, a:b], k[:, a:b], v[:, a:b], g[:, a:b]
        s = jnp.where(allowed, dot_nt(k_h, q_h), masked_score)
        top = jnp.max(s, axis=0, keepdims=True)
        p = jnp.exp2((s - top) * (scale * log2e))
        p = p / jnp.sum(p, axis=0, keepdims=True)
        dp = dot_nt(v_h, g_h)
        ds = (p * (dp - jnp.sum(p * dp, axis=0, keepdims=True))).astype(bf16)
        dv.append(dot_nn(p.astype(bf16), g_h))
        dk.append(dot_nn(ds, q_h) * scale)
        dq.append(dot_tn(ds, k_h) * scale)
    grad_q[...] = jnp.concatenate(dq, axis=1).astype(bf16)
    grad_kv[:, :D] = jnp.concatenate(dk, axis=1).astype(bf16)
    grad_kv[:, D:] = jnp.concatenate(dv, axis=1).astype(bf16)


def cross_backward(cap_t, cap_q, q, k, v, g):
    return pl.pallas_call(
        cross_backward_body,
        out_shape=[
            jax.ShapeDtypeStruct((TOK, D), bf16),
            jax.ShapeDtypeStruct((TXT, 2 * D), bf16),
        ],
        compiler_params=params(),
    )(cap_t, cap_q, q, k, v, g)


def fetch_pair(core, mine, other, first, second, sem, column=0):
    def run(a, b):
        columns = pl.ds(column, D)
        one = pltpu.make_async_copy(a.at[:, columns], first, sem.at[0])
        two = pltpu.make_async_copy(b.at[:, columns], second, sem.at[1])
        one.start()
        two.start()
        one.wait()
        two.wait()

    @pl.when(core[0] == 0)
    def _():
        run(mine, other)

    @pl.when(core[0] != 0)
    def _():
        run(other, mine)


def fetch_windows(core, mine, other, whole, sem):
    def run(a, b):
        one = pltpu.make_async_copy(
            a.at[:, pl.ds(2 * D, WIN)], whole.at[:, pl.ds(0, WIN)], sem.at[0]
        )
        two = pltpu.make_async_copy(
            b.at[:, pl.ds(2 * D + 128, STEP)], whole.at[:, pl.ds(WIN, STEP)], sem.at[1]
        )
        one.start()
        two.start()
        one.wait()
        two.wait()

    @pl.when(core[0] == 0)
    def _():
        run(mine, other)

    @pl.when(core[0] != 0)
    def _():
        run(other, mine)


def mlp_body(parts, count, core, *refs):
    xs, gs = refs[: parts * count], refs[parts * count : 2 * parts * count]
    mine, other = refs[2 * parts * count : 2 * parts * count + 2]
    outs = refs[2 * parts * count + 2 : -3]
    up, down, sem = refs[-3:]
    fetch_pair(core, mine, other, up, down, sem)
    for k in range(count):
        x = jnp.concatenate([r[...] for r in xs[parts * k : parts * (k + 1)]], axis=0)
        g = jnp.concatenate([r[...] for r in gs[parts * k : parts * (k + 1)]], axis=0)
        out, act_out, pre_out, grad_x = outs[4 * k : 4 * (k + 1)]
        pre = dot_nn(x, up[...])
        grad_act = dot_nt(g, down[...])
        cdf = 0.5 * (1.0 + lax.erf(pre * (0.5**0.5)))
        density = jnp.exp2(pre * pre * (-0.5 * log2e)) * 0.3989422804014327
        act = (pre * cdf).astype(bf16)
        grad_pre = (grad_act * (cdf + pre * density)).astype(bf16)
        act_out[...] = act
        pre_out[...] = grad_pre
        out[...] = dot_nn(act, down[...]).astype(out.dtype)
        grad_x[...] = dot_nt(grad_pre, up[...]).astype(grad_x.dtype)


def mlp(core, xs, gs, mine, other):
    parts = TOK // xs[0].shape[0]
    count = len(xs) // parts
    vmem = pl.BlockSpec(memory_space=pltpu.VMEM)
    hbm = pl.BlockSpec(memory_space=pl.ANY)
    return pl.pallas_call(
        functools.partial(mlp_body, parts, count),
        in_specs=[pl.BlockSpec(memory_space=pltpu.SMEM)]
        + [vmem] * (2 * parts * count)
        + [hbm, hbm],
        out_specs=[vmem] * (4 * count),
        out_shape=[jax.ShapeDtypeStruct((TOK, D), bf16)] * (4 * count),
        scratch_shapes=[
            pltpu.VMEM((D, D), bf16),
            pltpu.VMEM((D, D), bf16),
            pltpu.SemaphoreType.DMA((2,)),
        ],
        compiler_params=params(),
    )(core, *xs, *gs, mine, other)


def mlp_grad_body(which, core, *refs):
    out = refs[16]

    def run(xs, gs):
        out[...] = sum(dot_tn(x[...], g[...]) for x, g in zip(xs, gs)).astype(bf16)

    @pl.when(core[0] == which)
    def _():
        run(refs[:4], refs[4:8])

    @pl.when(core[0] != which)
    def _():
        run(refs[8:12], refs[12:16])


def mlp_grad(which, core, xs, pres, acts, gs):
    whole = [pl.BlockSpec((TOK, D), lambda k: (0, 0))] * 4
    part = [pl.BlockSpec((TOK, 384), lambda k: (0, k))] * 4
    return pl.pallas_call(
        functools.partial(mlp_grad_body, which),
        grid=(3,),
        in_specs=[pl.BlockSpec(memory_space=pltpu.SMEM)] + whole + part + whole + part,
        out_specs=pl.BlockSpec((D, 384), lambda k: (0, k)),
        out_shape=jax.ShapeDtypeStruct((D, D), bf16),
        compiler_params=params(),
    )(core, *xs, *pres, *acts, *gs)


def sort_hidden_body(core, mine, other, up, down):
    def run(ups, downs):
        for f in range(8):
            lanes = slice(SHARD * f, SHARD * (f + 1))
            up[:, 4 * SHARD * f : 4 * SHARD * (f + 1)] = jnp.concatenate(
                [ups[SHARD * z : SHARD * (z + 1), lanes] for z in range(4)], axis=1
            ).astype(f32)
        down[...] = downs[...].astype(f32)

    @pl.when(core[0] == 0)
    def _():
        run(mine, other)

    @pl.when(core[0] != 0)
    def _():
        run(other, mine)


def sort_hidden(core, mine, other):
    vmem = pl.BlockSpec(memory_space=pltpu.VMEM)
    return pl.pallas_call(
        sort_hidden_body,
        in_specs=[pl.BlockSpec(memory_space=pltpu.SMEM), vmem, vmem],
        out_specs=[vmem, vmem],
        out_shape=[
            jax.ShapeDtypeStruct((SHARD, FF), f32),
            jax.ShapeDtypeStruct((4 * SHARD, D), f32),
        ],
        compiler_params=params(),
    )(core, mine, other)


def normalize(x):
    center = x - jnp.mean(x, axis=-1, keepdims=True)
    inverse = lax.rsqrt(jnp.mean(center * center, axis=-1, keepdims=True) + norm_eps)
    return center * inverse, inverse


def norm_back(x, g, gain):
    plain, inverse = normalize(x)
    scaled = g * gain
    mixed = jnp.mean(scaled * plain, axis=-1, keepdims=True)
    grad = inverse * (scaled - jnp.mean(scaled, axis=-1, keepdims=True) - plain * mixed)
    sums = [jnp.sum(g * plain, axis=0, keepdims=True), jnp.sum(g, axis=0, keepdims=True)]
    return grad, sums


def call(body, ins, outs, scratch):
    spaces = {"vmem": pltpu.VMEM, "hbm": pl.ANY, "smem": pltpu.SMEM}
    return pl.pallas_call(
        body,
        in_specs=[pl.BlockSpec(memory_space=spaces[where]) for _, where in ins],
        out_specs=[pl.BlockSpec(memory_space=pltpu.VMEM)] * len(outs),
        out_shape=[jax.ShapeDtypeStruct(*o) for o in outs],
        scratch_shapes=scratch,
        compiler_params=params(),
    )(*[x for x, _ in ins])


def square_scratch(count):
    return [pltpu.VMEM((D, D), bf16)] * count + [pltpu.SemaphoreType.DMA((2,))]


def after_self_body(core, x, mixed, gain, bias, mine, other, total, normed, query, w1, w2, sem):
    fetch_pair(core, mine, other, w1, w2, sem)
    rows = x[...].astype(f32) + dot_nn(mixed[...], w1[...])
    total[...] = rows
    low = (normalize(rows)[0] * gain[...] + bias[...]).astype(bf16)
    normed[...] = low
    query[...] = dot_nn(low, w2[...]).astype(bf16)


def text_keys_body(core, context, mine, other, key, value, w1, w2, sem):
    fetch_pair(core, mine, other, w1, w2, sem, D)
    key[...] = dot_nn(context[...], w1[...]).astype(bf16)
    value[...] = dot_nn(context[...], w2[...]).astype(bf16)


def after_cross_body(core, x, mixed, gain, bias, mine, other, total, normed, w, sem):
    fetch_windows(core, mine, other, w, sem)
    rows = x[...] + dot_nn(mixed[...], w[...])
    total[...] = rows
    normed[...] = (normalize(rows)[0] * gain[...] + bias[...]).astype(bf16)


def third_back_body(core, x, g0, g1, g2, cot, gain, mine, other, grad, low, mixed, sums, w, sem):
    fetch_windows(core, mine, other, w, sem)
    g = g0[...].astype(f32) + g1[...].astype(f32) + g2[...].astype(f32)
    back, both = norm_back(x[...], g, gain[...])
    total = cot[...] + back
    grad[...] = total
    low[...] = total.astype(bf16)
    mixed[...] = dot_nt(total.astype(bf16), w[...]).astype(bf16)
    sums[...] = jnp.concatenate(both + [jnp.zeros((6, D), f32)], axis=0)


def second_back_body(core, x, gq, before, gain, mine, other, grad, low, mixed, sums, w1, w2, sem):
    fetch_pair(core, mine, other, w1, w2, sem)
    back, both = norm_back(x[...], dot_nt(gq[...], w2[...]), gain[...])
    total = before[...] + back
    grad[...] = total
    low[...] = total.astype(bf16)
    mixed[...] = dot_nt(total.astype(bf16), w1[...]).astype(bf16)
    sums[...] = jnp.concatenate(both + [jnp.zeros((6, D), f32)], axis=0)


def first_back_body(x, *refs):
    before, gain, grad = refs[SPLIT:]
    size = TOK // SPLIT
    sums = []
    for parts in refs[:SPLIT]:
        g = parts[:size, :].astype(f32)
        for k in range(1, 8):
            g = g + parts[size * k : size * (k + 1), :].astype(f32)
        sums.append(g)
    g = jnp.concatenate(sums, axis=0)
    grad[...] = before[...] + norm_back(x[...].astype(f32), g, gain[...])[0]


def text_back_body(
    core, kv, cols, text, w_text, mine, other, part, grad_text, grad_kv, w1, w2, sem
):
    fetch_pair(core, mine, other, w1, w2, sem, D)
    low = (dot_nt(kv[:, :D], w1[...]) + dot_nt(kv[:, D:], w2[...])).astype(bf16)
    part[...] = dot_nt(low, w_text[...]).astype(bf16)
    grad_text[...] = dot_tn(text[...], low).astype(bf16)
    grad_kv[...] = dot_tn(cols[...], kv[...]).astype(bf16)


def first_part_body(g, w, plain, *refs):
    rows = dot_nt(g[...], w[...])
    sums = refs[-1]
    size = TOK // SPLIT
    for k in range(SPLIT):
        refs[k][...] = rows[size * k : size * (k + 1)].astype(bf16)
    both = [
        jnp.sum(rows * plain[...].astype(f32), axis=0, keepdims=True),
        jnp.sum(rows, axis=0, keepdims=True),
        jnp.zeros((6, D), f32),
    ]
    both = jnp.concatenate(both, axis=0)

    @pl.when(pl.program_id(0) == 0)
    def _():
        sums[...] = both

    @pl.when(pl.program_id(0) != 0)
    def _():
        sums[...] += both


def first_part(g, w, plain):
    return pl.pallas_call(
        first_part_body,
        grid=(ROW // TOK,),
        in_specs=[
            pl.BlockSpec((TOK, 6 * SLOT), lambda i: (i, 0)),
            pl.BlockSpec((D, 6 * SLOT), lambda i: (0, 0)),
            pl.BlockSpec((TOK, D), lambda i: (i, 0)),
        ],
        out_specs=[
            *[pl.BlockSpec((TOK // SPLIT, D), lambda i: (i, 0))] * SPLIT,
            pl.BlockSpec((8, D), lambda i: (0, 0)),
        ],
        out_shape=[jax.ShapeDtypeStruct((ROW // SPLIT, D), bf16)] * SPLIT
        + [jax.ShapeDtypeStruct((8, D), f32)],
        compiler_params=params(),
    )(g, w, plain)


def heads_grad_body(x, g, out):
    grad = dot_tn(x[...], g[...]).astype(bf16)
    out[...] = jnp.concatenate(
        [
            grad[:, SLOT * (3 * h + k) : SLOT * (3 * h + k) + HEAD]
            for k in range(3)
            for h in range(2)
        ],
        axis=1,
    )


def heads_grad(x, g):
    return pl.pallas_call(
        heads_grad_body,
        grid=(3,),
        in_specs=[
            pl.BlockSpec((ROW, 384), lambda i: (0, i)),
            pl.BlockSpec((ROW, 6 * SLOT), lambda i: (0, 0)),
        ],
        out_specs=pl.BlockSpec((384, 3 * SHARD), lambda i: (i, 0)),
        out_shape=jax.ShapeDtypeStruct((D, 3 * SHARD), bf16),
        compiler_params=params(),
    )(x, g)


def unpack_heads_body(x, out):
    for k in range(3):
        out[SHARD * k : SHARD * (k + 1), :] = jnp.concatenate(
            [x[SHARD * p : SHARD * (p + 1), SHARD * k : SHARD * (k + 1)] for p in range(8)], axis=1
        )


def unpack_heads(x):
    return pl.pallas_call(
        unpack_heads_body,
        out_shape=jax.ShapeDtypeStruct((3 * SHARD, D), bf16),
        compiler_params=params(),
    )(x)


def row_block(x, index, rows):
    return lax.dynamic_slice_in_dim(x, index * rows, rows, axis=0)


def core_window(x, core):
    return lax.dynamic_slice_in_dim(x, core * STEP, WIN, axis=1)


def both_cores(x):
    return jnp.concatenate([x, shift(x, "c", 1)], axis=0)


def window_grad(left, right):
    core = lax.axis_index("c")
    sent = shift(core_window(right, 1 - core), "c", 1)
    rights = jnp.concatenate([core_window(right, core), sent], axis=0)
    return dot_tn(both_cores(left), rights).astype(bf16)


def sum_over(x, *axes):
    for axis in axes:
        n = lax.axis_size(axis)
        x = sum([shift(x, axis, k) for k in range(1, n)], x)
    return x


def local(
    tokens,
    text_states,
    seg_lengths,
    caption_of_segment,
    text_lengths,
    ln1_gain,
    ln1_bias,
    w_query,
    w_key,
    w_value,
    w_out,
    ln2_gain,
    ln2_bias,
    c_query,
    w_text,
    c_key,
    c_value,
    c_out,
    ln3_gain,
    ln3_bias,
    w_up,
    w_down,
    cotangent,
):
    core = lax.axis_index("c")
    first_core = core == 0
    core_index = core.astype(jnp.int32)[None]
    quarter = lax.axis_index("z")
    first_row = peer(0, 0) * TOK

    ends = jnp.cumsum(seg_lengths[0])
    positions = jnp.arange(ROW, dtype=jnp.int32)
    segment = jnp.sum((positions[:, None] >= ends[None, :]).astype(jnp.int32), axis=1)
    own_segment = lax.dynamic_slice_in_dim(segment, first_row, TOK)
    text_row = jnp.arange(TXT, dtype=jnp.int32)
    text_pos = text_row // TXT_OWN * CAP_TOK + text_row % TXT_OWN
    text_caption = text_pos // CAP_LEN
    live = jnp.sum(
        jnp.where(
            text_caption[:, None] == jnp.arange(CAPS, dtype=jnp.int32)[None, :],
            text_lengths[0][None, :],
            0,
        ),
        axis=1,
    )
    query_caption = jnp.sum(
        jnp.where(
            own_segment[:, None] == jnp.arange(SEGS, dtype=jnp.int32)[None, :],
            caption_of_segment[0][None, :],
            0,
        ),
        axis=1,
    )
    text_live = (text_row % TXT_OWN < CAP_TOK) & (text_pos % CAP_LEN < live)
    text_key = jnp.where(text_live, text_caption, -1)

    def row(x):
        return x[None, :]

    gap = jnp.zeros((SHARD, 128), bf16)
    square_pack = jnp.where(
        first_core,
        jnp.concatenate([w_out, c_key, c_out[:, :WIN], gap], axis=1),
        jnp.concatenate([c_query, c_value, c_out[:, STEP:], gap], axis=1),
    )
    square_pack = lax.dynamic_slice_in_dim(square_pack, quarter * QUARTER, QUARTER, axis=1)
    quarter_own = lax.all_gather(square_pack, FS, axis=0, tiled=True)

    rows_in = tokens[0]
    plain = normalize(rows_in.astype(f32))[0].astype(bf16)
    n01, n10, n30 = gather_first(plain)

    heads_pack = pack_heads(after(w_query, plain), w_key, w_value)
    n01, n10, n30, heads_pack = lax.optimization_barrier((n01, n10, n30, heads_pack))
    heads_w = peers_parts(heads_pack)
    n31, n20, n11 = gather_second(n01, n10)

    text_own = jnp.pad(after(text_states[0], heads_w), ((0, TXT_OWN - CAP_TOK), (0, 0)))
    text_columns = lax.all_to_all(text_own, FS, split_axis=1, concat_axis=0, tiled=True)
    n31, n20, n11, text_columns = lax.optimization_barrier((n31, n20, n11, text_columns))
    n21 = gather_third(n31, n11)
    heads_w = spread_heads(heads_w)
    context_part = dot_nn(text_columns, w_text).astype(bf16)
    context_own = lax.psum_scatter(context_part, FS, scatter_dimension=0, tiled=True)
    plain_all, normed_all = place_rows(
        after(plain, context_part),
        (n01, n10, n30),
        (n31, n20, n11),
        n21,
        row(ln1_gain),
        row(ln1_bias),
    )
    quarter_own, normed_all = lax.optimization_barrier((quarter_own, normed_all))
    quarter_minus, quarter_plus = shift(quarter_own, "z", 1), shift(quarter_own, "z", -1)

    up_own = jnp.concatenate(
        [
            lax.dynamic_slice(w_up, (0, 4 * SHARD * k + SHARD * quarter), (SHARD, SHARD))
            for k in range(8)
        ],
        axis=1,
    )
    hidden_own = jnp.where(first_core, up_own, row_block(w_down, quarter, SHARD))

    seg_col, seg_row = segment[:, None], segment[None, :]
    qkv = dot_nn(normed_all, heads_w).astype(bf16)
    head0, total0 = self_forward(0, seg_col, seg_row, qkv)
    head1, total1 = self_forward(1, seg_col, seg_row, after(qkv, head0))
    quarter_minus, quarter_plus, head1 = lax.optimization_barrier(
        (quarter_minus, quarter_plus, head1)
    )
    quarter_far = (
        shift(halves(quarter_minus)[0], "z", 1),
        shift(halves(quarter_plus)[1], "z", -1),
    )
    attended = lax.all_to_all(
        jnp.concatenate([head0, head1], axis=1), FS, split_axis=0, concat_axis=1, tiled=True
    )
    attended, context_own, *quarter_far = lax.optimization_barrier(
        (attended, context_own, *quarter_far)
    )
    context = every_peer(context_own)
    square_mine = place_quarters(quarter_own, quarter_minus, quarter_plus, *quarter_far)
    square_other = shift(square_mine, "c", 1)
    grad_out = cotangent[0]
    grad_mlp = grad_out.astype(bf16)
    grad_sent = after(grad_mlp, square_mine)
    mlp_minus, mlp_plus = shift(grad_sent, "z", 1), shift(grad_sent, "z", -1)
    hidden_mine = every_peer(after(hidden_own, context))

    after_self, normed_two, cross_query = call(
        after_self_body,
        [
            (core_index, "smem"), (rows_in, "vmem"), (attended, "vmem"),
            (row(ln2_gain), "vmem"), (row(ln2_bias), "vmem"),
            (square_mine, "hbm"), (square_other, "hbm"),
        ],
        [((TOK, D), f32), ((TOK, D), bf16), ((TOK, D), bf16)],
        square_scratch(2),
    )
    cross_key, cross_value = call(
        text_keys_body,
        [
            (core_index, "smem"), (after(context, cross_query, mlp_minus, mlp_plus), "vmem"),
            (square_mine, "hbm"), (square_other, "hbm"),
        ],
        [((TXT, D), bf16), ((TXT, D), bf16)],
        square_scratch(2),
    )
    cross_mixed = cross_forward(
        query_caption[:, None], text_key[None, :], cross_query, cross_key, cross_value
    )
    hidden_mine = after(hidden_mine, cross_mixed)
    weights = (hidden_mine, shift(hidden_mine, "c", 1))
    after_cross, normed_three = call(
        after_cross_body,
        [
            (core_index, "smem"), (after_self, "vmem"), (cross_mixed, "vmem"),
            (row(ln3_gain), "vmem"), (row(ln3_bias), "vmem"),
            (square_mine, "hbm"), (square_other, "hbm"),
        ],
        [((TOK, D), f32), ((TOK, D), bf16)],
        square_scratch(1),
    )

    mlp_sent = lax.optimization_barrier((mlp_minus, mlp_plus, cross_query))
    mlp_far = (
        shift(halves(mlp_sent[0])[0], "z", 1),
        shift(halves(mlp_sent[1])[1], "z", -1),
    )

    three_minus, three_plus = shift(normed_three, "z", 1), shift(normed_three, "z", -1)
    out_own, act_own, pre_own, back_own = mlp(core_index, (normed_three,), (grad_mlp,), *weights)
    three_minus, three_plus, out_own = lax.optimization_barrier(
        (three_minus, three_plus, out_own)
    )
    three_far = (
        shift(halves(three_minus)[0], "z", 1),
        shift(halves(three_plus)[1], "z", -1),
    )
    near = mlp(core_index, (three_minus, three_plus), (mlp_minus, mlp_plus), *weights)
    out_m, act_m, pre_m, back_m, out_p, act_p, pre_p, back_p = near
    *three_far, out_m = lax.optimization_barrier((*three_far, out_m))
    out_far, act_far, pre_far, back_far = mlp(core_index, three_far, mlp_far, *weights)
    back_minus, back_plus = reduce_z(back_far, back_m, back_p)
    three_parts = (normed_three, three_minus, three_plus, jnp.concatenate(three_far, axis=0))
    pre_parts = (pre_own, pre_m, pre_p, pre_far)
    act_parts = (act_own, act_m, act_p, act_far)
    mlp_parts = (grad_mlp, mlp_minus, mlp_plus, jnp.concatenate(mlp_far, axis=0))
    send = mlp_grad(1, core_index, three_parts, pre_parts, act_parts, mlp_parts)
    back_minus, back_plus, send = lax.optimization_barrier((back_minus, back_plus, send))
    back_minus, back_plus = shift(back_minus, "z", -1), shift(back_plus, "z", 1)
    keep = mlp_grad(
        0, core_index, three_parts, pre_parts, act_parts, (after(grad_mlp, send), *mlp_parts[1:])
    )
    back_minus, back_plus, keep = lax.optimization_barrier((back_minus, back_plus, keep))
    hidden_sum = keep + shift(send, "c", 1)

    def hidden_chunk(dy, dx):
        return row_block(hidden_sum, peer(dy, dx), SHARD)

    h_lo, h_hi, h20 = reduce_first(hidden_chunk)
    grad_after_cross, grad_cross_branch, grad_cross_mixed, sums_three = call(
        third_back_body,
        [
            (core_index, "smem"), (after_cross, "vmem"), (back_own, "vmem"),
            (back_minus, "vmem"), (back_plus, "vmem"), (grad_out, "vmem"),
            (after(row(ln3_gain), hidden_sum), "vmem"), (square_mine, "hbm"), (square_other, "hbm"),
        ],
        [((TOK, D), f32), ((TOK, D), bf16), ((TOK, D), bf16), ((8, D), f32)],
        square_scratch(1),
    )

    grad_cquery_rows, grad_kv = cross_backward(
        text_key[:, None],
        query_caption[None, :],
        cross_query,
        cross_key,
        cross_value,
        after(grad_cross_mixed, h_lo, h_hi),
    )
    h11, h31 = reduce_second(hidden_chunk, h_lo, h_hi)
    kv_own = lax.psum_scatter(grad_kv, FS, scatter_dimension=0, tiled=True)
    grad_after_self, grad_self_branch, grad_attended, sums_two = call(
        second_back_body,
        [
            (core_index, "smem"), (after_self, "vmem"), (after(grad_cquery_rows, h11, h31, h20), "vmem"),
            (grad_after_cross, "vmem"), (row(ln2_gain), "vmem"),
            (square_mine, "hbm"), (square_other, "hbm"),
        ],
        [((TOK, D), f32), ((TOK, D), bf16), ((TOK, D), bf16), ((8, D), f32)],
        square_scratch(2),
    )
    hidden_parts = reduce_third(hidden_chunk, h20, h11, h31)
    grad_heads = lax.all_to_all(grad_attended, FS, split_axis=1, concat_axis=0, tiled=True)

    square = jnp.concatenate(
        [
            window_grad(cross_mixed, after(grad_cross_branch, grad_attended)),
            window_grad(normed_two, after(grad_cquery_rows, grad_attended)),
            window_grad(attended, grad_self_branch),
        ],
        axis=1,
    )

    def square_chunk(dy, dx):
        return row_block(square, peer(dy, dx), SHARD)

    grad_heads, square, *hidden_parts = lax.optimization_barrier(
        (grad_heads, square, *hidden_parts)
    )
    hidden_grad = reduce_last(hidden_chunk, *hidden_parts).astype(bf16)
    grad_qkv = self_backward(0, seg_col, seg_row, total0, qkv, grad_heads)
    kv_own, grad_qkv, square = lax.optimization_barrier((kv_own, grad_qkv, square))
    s_lo, s_hi, s20 = reduce_first(square_chunk)
    kv_all = every_peer(kv_own)
    hidden_grad = after(hidden_grad, kv_own)
    hidden_grad = hidden_grad + shift(hidden_grad, "xh", 1)
    out_minus, out_plus = reduce_z(after(out_far, kv_own), out_m, out_p)
    grad_qkv = self_backward(
        1, seg_col, seg_row, total1, qkv, after(grad_heads, kv_own), (grad_qkv,)
    )
    s_lo, s_hi, out_minus, out_plus, hidden_grad, grad_qkv = lax.optimization_barrier(
        (s_lo, s_hi, out_minus, out_plus, hidden_grad, grad_qkv)
    )
    heads_own = heads_grad(normed_all, grad_qkv)
    heads_own, kv_all = lax.optimization_barrier((heads_own, kv_all))
    heads_part = peers_parts(heads_own)
    part, sums_one = first_part(after(grad_qkv, heads_own), heads_w, plain_all)
    part, heads_part = lax.optimization_barrier((part, heads_part))
    sent = peers_parts(part)

    s11, s31 = reduce_second(square_chunk, after(s_lo, part), s_hi)
    hidden_z = neighbours(after(hidden_grad, part))
    heads_rows = unpack_heads(heads_part)
    early = row_block(heads_rows, core, 216) + shift(row_block(heads_rows, 1 - core, 216), "c", 1)
    early = jnp.concatenate([early, jnp.zeros((256 - 216, D), bf16)], axis=0)
    own_columns = lax.dynamic_slice_in_dim(context, peer(0, 0) * SHARD, SHARD, axis=1)
    text_part, grad_w_text, grad_w_kv = call(
        text_back_body,
        [
            (core_index, "smem"), (after(kv_all, part), "vmem"), (own_columns, "vmem"),
            (text_columns, "vmem"), (w_text, "vmem"),
            (square_mine, "hbm"), (square_other, "hbm"),
        ],
        [((TXT, TXT), bf16), ((TXT, D), bf16), ((SHARD, 2 * D), bf16)],
        square_scratch(2),
    )

    def half(which):
        kv = jnp.where(which == 0, grad_w_kv[:, :D], grad_w_kv[:, D:])
        return jnp.concatenate(
            [row_block(grad_w_text, which, 256), kv, jnp.zeros((512 - 400, D), bf16)], axis=0
        )

    late = half(core) + shift(half(1 - core), "c", 1)
    early = lax.psum_scatter(early, "z", scatter_dimension=0, tiled=True)
    square_parts = reduce_third(square_chunk, s20, s11, s31)
    square = reduce_last(square_chunk, *square_parts).astype(bf16)
    square = jnp.concatenate(
        [square[:, WIN * k : WIN * (k + 1)] for k in range(3)]
        + [jnp.zeros((512 - 3 * SHARD, WIN), bf16)],
        axis=0,
    )
    late = jnp.concatenate([late, square], axis=1)
    late = lax.psum_scatter(late, "z", scatter_dimension=0, tiled=True)
    part, early, late, *hidden_z = lax.optimization_barrier((sent, early, late, *hidden_z))
    early = early + shift(early, "xh", 1)
    norms = jnp.concatenate([sums_one[:2], sums_two[:2], sums_three[:2], jnp.zeros((2, D), f32)])
    norms = sum_over(after(norms, part), "z", "c")

    norms = sum_over(norms, "y", "xl", "xh")
    late = late + shift(late, "xh", 1)
    early = in_order(*neighbours(early))
    late = in_order(*neighbours(late))
    hidden_grad = in_order(*hidden_z)
    grad_w_up, grad_w_down = sort_hidden(core_index, hidden_grad, shift(hidden_grad, "c", 1))

    def by_core(x):
        other = shift(x, "c", 1)
        low, high = jnp.where(first_core, x, other), jnp.where(first_core, other, x)
        return low.astype(f32), high.astype(f32)

    low, high = by_core(early)
    grad_w_query = low[:144]
    grad_w_key = jnp.concatenate([low[144:216], high[:72]], axis=0)
    grad_w_value = high[72:216]
    low, high = by_core(late)
    grad_w_text = jnp.concatenate([low[:256, :D], high[:256, :D]], axis=0)
    grad_c_key, grad_c_value = low[256:400, :D], high[256:400, :D]
    grad_c_out, grad_c_query, grad_w_out = (
        jnp.concatenate(
            [low[SHARD * k : SHARD * (k + 1), D:], high[SHARD * k : SHARD * (k + 1), D + 128 :]],
            axis=1,
        )
        for k in range(3)
    )
    out_minus, out_plus = shift(out_minus, "z", -1), shift(out_plus, "z", 1)
    outputs = (
        after_cross + out_own.astype(f32) + out_minus.astype(f32) + out_plus.astype(f32)
    )

    grad_tokens = call(
        first_back_body,
        [
            (rows_in, "vmem"), (part, "vmem"), (grad_after_self, "vmem"),
            (row(ln1_gain), "vmem"),
        ],
        [((TOK, D), f32)],
        [],
    )[0]
    grad_text = lax.all_to_all(
        after(text_part, part), FS, split_axis=0, concat_axis=1, tiled=True
    )
    grad_text = grad_text[:CAP_TOK].astype(f32)
    return (
        outputs[None],
        grad_tokens[None],
        grad_text[None],
        norms[0],
        norms[1],
        grad_w_query,
        grad_w_key,
        grad_w_value,
        grad_w_out,
        norms[2],
        norms[3],
        grad_c_query,
        grad_w_text,
        grad_c_key,
        grad_c_value,
        grad_c_out,
        norms[4],
        norms[5],
        grad_w_up,
        grad_w_down,
    )


def solution(mesh):
    split = Mesh(mesh.devices.reshape(2, 4, 2, 4, 2), ("xh", "z", "c", "y", "xl"))
    dp = ("xh", "z", "c")
    rows = P(dp, FS, None)
    per_row = P(dp, None)
    weight = P(FS, None)
    rep = P()
    in_specs = (
        rows, rows, per_row, per_row, per_row,
        rep, rep, weight, weight, weight, weight,
        rep, rep, weight, weight, weight, weight, weight,
        rep, rep, weight, weight, rows,
    )
    out_specs = (
        rows, rows, rows,
        rep, rep, weight, weight, weight, weight,
        rep, rep, weight, weight, weight, weight, weight,
        rep, rep, weight, weight,
    )
    return jax.shard_map(
        local, mesh=split, in_specs=in_specs, out_specs=out_specs, check_vma=False
    )
```

```python
import functools

import jax
import jax.numpy as jnp
from jax import lax
from jax.experimental import pallas as pl
from jax.experimental.pallas import tpu as pltpu
from jax.sharding import Mesh
from jax.sharding import PartitionSpec as P

HEADS = 16
HEAD = 72
D = 1152
FF = 4608
CAP_TOK = 60
TXT_OWN = 64
TXT = 8 * TXT_OWN
TOK = 256
ROW = 2048
CAP_LEN = 120
SEGS = 3
CAPS = 4
SHARD = 144
SLOT = 128
SPLIT = 1
WIN = 640
STEP = 512

bf16 = jnp.bfloat16
f32 = jnp.float32
norm_eps = 1e-06
masked_score = -1e30
scale = HEAD ** (-0.5)
log2e = 1.4426950408889634
FS = ("y", "xl")
VMEM = 60 * 1024 * 1024


def dot_nn(a, b):
    return lax.dot_general(a, b, (((1,), (0,)), ((), ())), preferred_element_type=f32)


def dot_nt(a, b):
    return lax.dot_general(a, b, (((1,), (1,)), ((), ())), preferred_element_type=f32)


def dot_tn(a, b):
    return lax.dot_general(a, b, (((0,), (0,)), ((), ())), preferred_element_type=f32)


def params():
    return pltpu.CompilerParams(vmem_limit_bytes=VMEM)


def cost(micros):
    return pl.CostEstimate(flops=int(micros * 1.15e9), bytes_accessed=0, transcendentals=0)


def shift(x, axis, by):
    n = lax.axis_size(axis)
    return lax.ppermute(x, axis, [(i, (i + by) % n) for i in range(n)])


def halves(x):
    h = (x.shape[0] // 2 + 15) // 16 * 16
    return x[:h], x[h:]


def after(x, *others):
    return lax.optimization_barrier((x, *others))[0]


def gather_first(x):
    return shift(x, "xl", 1), shift(x, "y", -1), shift(x, "y", 1)


def gather_second(x01, x10):
    return shift(x01, "y", 1), shift(x10, "y", -1), shift(x10, "xl", 1)


def gather_third(x31, x11):
    return shift(halves(x11)[0], "y", -1), shift(halves(x31)[1], "y", 1)


NEAR = ((0, 0), (0, 1), (1, 0), (3, 0))
NEXT = ((3, 1), (2, 0), (1, 1))
LAST = (2, 1)


def reduce_first(chunk):
    lo, hi = halves(chunk(2, 1))
    return shift(lo, "y", 1), shift(hi, "y", -1), shift(chunk(2, 0), "y", 1)


def reduce_second(chunk, lo, hi):
    h = lo.shape[0]
    c11, c31 = chunk(1, 1), chunk(3, 1)
    c11 = jnp.concatenate([c11[:h] + lo, c11[h:]], axis=0)
    c31 = jnp.concatenate([c31[:h], c31[h:] + hi], axis=0)
    return shift(c11, "xl", 1), shift(c31, "y", -1)


def reduce_third(chunk, c20, c11, c31):
    return (
        shift(chunk(1, 0) + c20 + c11, "y", 1),
        shift(chunk(0, 1) + c31, "xl", 1),
        shift(chunk(3, 0), "y", -1),
    )


def reduce_last(chunk, *parts):
    return sum([p.astype(f32) for p in parts], chunk(0, 0).astype(f32))


def every_peer(x, axes=FS):
    n = lax.axis_size(axes)
    copies = jnp.broadcast_to(x[None], (n, *x.shape)).reshape(n * x.shape[0], x.shape[1])
    return lax.all_to_all(copies, axes, 0, 0, tiled=True)


def peers_parts(x, axes=FS):
    return lax.all_to_all(x, axes, 0, 0, tiled=True)


def sum_parts(parts):
    return jnp.sum(parts.reshape(8, -1, parts.shape[1]).astype(f32), axis=0)


def neighbours(x):
    return x, shift(x, "z", 1), shift(x, "z", 2), shift(x, "z", -1)


def in_order(*around):
    rows, cols = around[0].shape

    def body(where, *refs):
        ins, out = refs[:4], refs[4]
        for k in range(4):
            row = pl.multiple_of(lax.rem(where[0] + 4 - k, 4) * rows, 16)
            out[pl.ds(row, rows), :] = ins[k][...]

    vmem = pl.BlockSpec(memory_space=pltpu.VMEM)
    return pl.pallas_call(
        body,
        in_specs=[pl.BlockSpec(memory_space=pltpu.SMEM)] + [vmem] * 4,
        out_specs=vmem,
        out_shape=jax.ShapeDtypeStruct((4 * rows, cols), bf16),
        compiler_params=params(),
    )(lax.axis_index("z").astype(jnp.int32)[None], *around)


def reduce_z(far, minus, plus):
    lo, hi = halves(far)
    lo, hi = shift(lo, "z", -1), shift(hi, "z", 1)
    h = lo.shape[0]
    return (
        jnp.concatenate([minus[:h] + lo, minus[h:]], axis=0),
        jnp.concatenate([plus[:h], plus[h:] + hi], axis=0),
    )


def peer(dy, dx):
    return ((lax.axis_index("y") + dy) % 4) * 2 + (lax.axis_index("xl") ^ dx)


def place_rows(own, first, second, third, gain, bias):
    lo = third[0].shape[0]
    rows, cols = own.shape
    pieces = [(x, p, 0) for x, p in zip((own, *first), NEAR)]
    pieces += [(x, p, 0) for x, p in zip(second, NEXT)]
    pieces += [(third[0], LAST, 0), (third[1], LAST, lo)]
    count = len(pieces)

    def body(where, gain, bias, *refs):
        ins, plain, normed, sem = refs[:count], refs[count], refs[count + 1], refs[-1]
        started = []
        for k, (x, _, off) in enumerate(pieces):
            row = pl.multiple_of(where[k] * rows + off, 16)
            one = pltpu.make_async_copy(ins[k], plain.at[pl.ds(row, x.shape[0])], sem.at[k])
            one.start()
            started.append(one)
        for one in started:
            one.wait()

        def step(i, carry):
            part = pl.ds(pl.multiple_of(i * rows, rows), rows)
            normed[part, :] = (plain[part, :].astype(f32) * gain[...] + bias[...]).astype(bf16)
            return carry

        lax.fori_loop(0, 8, step, 0)

    vmem = pl.BlockSpec(memory_space=pltpu.VMEM)
    return pl.pallas_call(
        body,
        in_specs=[pl.BlockSpec(memory_space=pltpu.SMEM), vmem, vmem]
        + [pl.BlockSpec(memory_space=pl.ANY)] * count,
        out_specs=[vmem, vmem],
        out_shape=[jax.ShapeDtypeStruct((8 * rows, cols), bf16)] * 2,
        scratch_shapes=[pltpu.SemaphoreType.DMA((count,))],
        compiler_params=params(),
    )(
        jnp.stack([peer(*p) for _, p, _ in pieces]).astype(jnp.int32),
        gain,
        bias,
        *[x for x, _, _ in pieces],
    )


QUARTER = 768


def place_quarters(*quarters):
    def body(where, own, minus, plus, far_lo, far_hi, out, sem):
        started = []
        half = far_lo.shape[0]
        for k, (ref, turn, row) in enumerate(
            ((own, 0, 0), (minus, 3, 0), (plus, 1, 0), (far_lo, 2, 0), (far_hi, 2, half))
        ):
            column = pl.multiple_of(lax.rem(where[0] + turn, 4) * QUARTER, 128)
            one = pltpu.make_async_copy(
                ref, out.at[pl.ds(row, ref.shape[0]), pl.ds(column, QUARTER)], sem.at[k]
            )
            one.start()
            started.append(one)
        for one in started:
            one.wait()

    return pl.pallas_call(
        body,
        in_specs=[pl.BlockSpec(memory_space=pltpu.SMEM)] + [pl.BlockSpec(memory_space=pl.ANY)] * 5,
        out_specs=pl.BlockSpec(memory_space=pltpu.VMEM),
        out_shape=jax.ShapeDtypeStruct((D, 4 * QUARTER), bf16),
        scratch_shapes=[pltpu.SemaphoreType.DMA((5,))],
        compiler_params=params(),
    )(lax.axis_index("z").astype(jnp.int32)[None], *quarters)


def pack_heads_body(wq, wk, wv, out):
    for p in range(8):
        rows = slice(SHARD * p, SHARD * (p + 1))
        out[rows, :] = jnp.concatenate([w[:, rows] for w in (wq, wk, wv)], axis=1)


def pack_heads(*weights):
    return pl.pallas_call(
        pack_heads_body,
        out_shape=jax.ShapeDtypeStruct((D, 3 * SHARD), bf16),
        compiler_params=params(),
    )(*weights)


def spread_heads_body(x, out):
    blank = jnp.zeros((D, SLOT - HEAD), bf16)
    for h in range(2):
        for k in range(3):
            first = SHARD * k + HEAD * h
            slot = SLOT * (3 * h + k)
            out[:, slot : slot + SLOT] = jnp.concatenate(
                [x[:, first : first + HEAD], blank], axis=1
            )


def spread_heads(x):
    return pl.pallas_call(
        spread_heads_body,
        out_shape=jax.ShapeDtypeStruct((D, 6 * SLOT), bf16),
        compiler_params=params(),
    )(x)


def self_forward_body(seg_q, seg_k, q, kv, out, total):
    s = dot_nt(q[:, :SLOT], kv[:, SLOT : 2 * SLOT])
    s = jnp.where(seg_q[...] == seg_k[...], s, masked_score)
    top = jnp.max(s, axis=1, keepdims=True)
    p = jnp.exp2((s - top) * (scale * log2e))
    mass = jnp.sum(p, axis=1, keepdims=True)
    out[...] = (dot_nn(p.astype(bf16), kv[:, 2 * SLOT :]) / mass)[:, :HEAD].astype(bf16)
    log_total = top * (scale * log2e) + jnp.log2(mass)
    total[...] = jnp.transpose(jnp.broadcast_to(log_total, (TOK, SLOT)))[0:1, :]


def self_forward(head, seg_q, seg_k, qkv):
    return pl.pallas_call(
        self_forward_body,
        grid=(ROW // TOK,),
        in_specs=[
            pl.BlockSpec((TOK, 1), lambda i: (i, 0)),
            pl.BlockSpec((1, ROW), lambda i: (0, 0)),
            pl.BlockSpec((TOK, 3 * SLOT), lambda i: (i, head)),
            pl.BlockSpec((ROW, 3 * SLOT), lambda i: (0, head)),
        ],
        out_specs=[
            pl.BlockSpec((TOK, HEAD), lambda i: (i, 0)),
            pl.BlockSpec((1, TOK), lambda i: (0, i)),
        ],
        out_shape=[
            jax.ShapeDtypeStruct((ROW, HEAD), bf16),
            jax.ShapeDtypeStruct((1, ROW), f32),
        ],
        compiler_params=params(),
    )(seg_q, seg_k, qkv, qkv)


def self_backward_body(head, seg_k, seg_q, total, q, kv, g, *refs):
    grad, key_sum, value_sum, key_t = refs[-4:]
    i = pl.program_id(0)

    @pl.when(i == 0)
    def _():
        key_sum[...] = jnp.zeros_like(key_sum)
        value_sum[...] = jnp.zeros_like(value_sum)
        key_t[...] = jnp.transpose(kv[:, SLOT : 2 * SLOT])

    rows = pl.ds(pl.multiple_of(i * TOK, TOK), TOK)
    q_h, k_h, v_h = q[:, :SLOT], kv[:, SLOT : 2 * SLOT], kv[:, 2 * SLOT :]
    g_both = g[...]
    g_h = jnp.concatenate(
        [g_both[:, HEAD * head : HEAD * (head + 1)], jnp.zeros((TOK, SLOT - HEAD), bf16)], axis=1
    )
    p = jnp.exp2(dot_nt(k_h, q_h) * (scale * log2e) - total[...])
    p = jnp.where(seg_k[...] == seg_q[...], p, 0.0)
    dp = dot_nt(v_h, g_h)
    ds = (p * (dp - jnp.sum(p * dp, axis=0, keepdims=True))).astype(bf16)
    value_sum[...] += dot_nn(p.astype(bf16), g_h)
    key_sum[...] += dot_nn(ds, q_h)
    grad[rows, :SLOT] = (jnp.transpose(dot_nn(key_t[...], ds)) * scale).astype(bf16)

    @pl.when(i == pl.num_programs(0) - 1)
    def _():
        grad[:, SLOT : 2 * SLOT] = (key_sum[...] * scale).astype(bf16)
        grad[:, 2 * SLOT :] = value_sum[...].astype(bf16)


def self_backward(head, seg_k, seg_q, total, qkv, g, before=()):
    return pl.pallas_call(
        functools.partial(self_backward_body, head),
        grid=(ROW // TOK,),
        in_specs=[
            pl.BlockSpec((ROW, 1), lambda i: (0, 0)),
            pl.BlockSpec((1, TOK), lambda i: (0, i)),
            pl.BlockSpec((1, TOK), lambda i: (0, i)),
            pl.BlockSpec((TOK, 3 * SLOT), lambda i: (i, head)),
            pl.BlockSpec((ROW, 3 * SLOT), lambda i: (0, head)),
            pl.BlockSpec((TOK, SHARD), lambda i: (i, 0)),
        ]
        + [pl.BlockSpec(memory_space=pl.ANY)] * len(before),
        out_specs=pl.BlockSpec((ROW, 3 * SLOT), lambda i: (0, head)),
        out_shape=jax.ShapeDtypeStruct((ROW, 6 * SLOT), bf16),
        input_output_aliases={6: 0} if before else {},
        scratch_shapes=[
            pltpu.VMEM((ROW, SLOT), f32),
            pltpu.VMEM((ROW, SLOT), f32),
            pltpu.VMEM((SLOT, ROW), bf16),
        ],
        compiler_params=params(),
    )(seg_k, seg_q, total, qkv, qkv, g, *before)


def cross_forward_body(cap_q, cap_t, q, k, v, out):
    allowed = cap_q[...] == cap_t[...]
    mixed = []
    for h in range(HEADS):
        a, b = HEAD * h, HEAD * (h + 1)
        s = dot_nt(q[:, a:b], k[:, a:b])
        s = jnp.where(allowed, s, masked_score)
        top = jnp.max(s, axis=1, keepdims=True)
        p = jnp.exp2((s - top) * (scale * log2e))
        mass = jnp.sum(p, axis=1, keepdims=True)
        mixed.append(dot_nn(p.astype(bf16), v[:, a:b]) / mass)
    out[...] = jnp.concatenate(mixed, axis=1).astype(bf16)


def cross_forward(cap_q, cap_t, q, k, v):
    return pl.pallas_call(
        cross_forward_body,
        out_shape=jax.ShapeDtypeStruct((TOK, D), bf16),
        compiler_params=params(),
    )(cap_q, cap_t, q, k, v)


def cross_backward_body(cap_t, cap_q, q, k, v, g, grad_q, grad_kv):
    allowed = cap_t[...] == cap_q[...]
    dq, dk, dv = [], [], []
    for h in range(HEADS):
        a, b = HEAD * h, HEAD * (h + 1)
        q_h, k_h, v_h, g_h = q[:, a:b], k[:, a:b], v[:, a:b], g[:, a:b]
        s = jnp.where(allowed, dot_nt(k_h, q_h), masked_score)
        top = jnp.max(s, axis=0, keepdims=True)
        p = jnp.exp2((s - top) * (scale * log2e))
        p = p / jnp.sum(p, axis=0, keepdims=True)
        dp = dot_nt(v_h, g_h)
        ds = (p * (dp - jnp.sum(p * dp, axis=0, keepdims=True))).astype(bf16)
        dv.append(dot_nn(p.astype(bf16), g_h))
        dk.append(dot_nn(ds, q_h) * scale)
        dq.append(dot_tn(ds, k_h) * scale)
    grad_q[...] = jnp.concatenate(dq, axis=1).astype(bf16)
    grad_kv[:, :D] = jnp.concatenate(dk, axis=1).astype(bf16)
    grad_kv[:, D:] = jnp.concatenate(dv, axis=1).astype(bf16)


def cross_backward(cap_t, cap_q, q, k, v, g):
    return pl.pallas_call(
        cross_backward_body,
        out_shape=[
            jax.ShapeDtypeStruct((TOK, D), bf16),
            jax.ShapeDtypeStruct((TXT, 2 * D), bf16),
        ],
        compiler_params=params(),
    )(cap_t, cap_q, q, k, v, g)


def fetch_pair(core, mine, other, first, second, sem, column=0):
    def run(a, b):
        columns = pl.ds(column, D)
        one = pltpu.make_async_copy(a.at[:, columns], first, sem.at[0])
        two = pltpu.make_async_copy(b.at[:, columns], second, sem.at[1])
        one.start()
        two.start()
        one.wait()
        two.wait()

    @pl.when(core[0] == 0)
    def _():
        run(mine, other)

    @pl.when(core[0] != 0)
    def _():
        run(other, mine)


def fetch_windows(core, mine, other, whole, sem):
    def run(a, b):
        one = pltpu.make_async_copy(
            a.at[:, pl.ds(2 * D, WIN)], whole.at[:, pl.ds(0, WIN)], sem.at[0]
        )
        two = pltpu.make_async_copy(
            b.at[:, pl.ds(2 * D + 128, STEP)], whole.at[:, pl.ds(WIN, STEP)], sem.at[1]
        )
        one.start()
        two.start()
        one.wait()
        two.wait()

    @pl.when(core[0] == 0)
    def _():
        run(mine, other)

    @pl.when(core[0] != 0)
    def _():
        run(other, mine)


def mlp_body(parts, count, core, *refs):
    xs, gs = refs[: parts * count], refs[parts * count : 2 * parts * count]
    mine, other = refs[2 * parts * count : 2 * parts * count + 2]
    outs = refs[2 * parts * count + 2 : -3]
    up, down, sem = refs[-3:]
    fetch_pair(core, mine, other, up, down, sem)
    for k in range(count):
        x = jnp.concatenate([r[...] for r in xs[parts * k : parts * (k + 1)]], axis=0)
        g = jnp.concatenate([r[...] for r in gs[parts * k : parts * (k + 1)]], axis=0)
        out, act_out, pre_out, grad_x = outs[4 * k : 4 * (k + 1)]
        pre = dot_nn(x, up[...])
        grad_act = dot_nt(g, down[...])
        cdf = 0.5 * (1.0 + lax.erf(pre * (0.5**0.5)))
        density = jnp.exp2(pre * pre * (-0.5 * log2e)) * 0.3989422804014327
        act = (pre * cdf).astype(bf16)
        grad_pre = (grad_act * (cdf + pre * density)).astype(bf16)
        act_out[...] = act
        pre_out[...] = grad_pre
        out[...] = dot_nn(act, down[...]).astype(out.dtype)
        grad_x[...] = dot_nt(grad_pre, up[...]).astype(grad_x.dtype)


def mlp(core, xs, gs, mine, other):
    parts = TOK // xs[0].shape[0]
    count = len(xs) // parts
    vmem = pl.BlockSpec(memory_space=pltpu.VMEM)
    hbm = pl.BlockSpec(memory_space=pl.ANY)
    return pl.pallas_call(
        functools.partial(mlp_body, parts, count),
        in_specs=[pl.BlockSpec(memory_space=pltpu.SMEM)]
        + [vmem] * (2 * parts * count)
        + [hbm, hbm],
        out_specs=[vmem] * (4 * count),
        out_shape=[jax.ShapeDtypeStruct((TOK, D), bf16)] * (4 * count),
        scratch_shapes=[
            pltpu.VMEM((D, D), bf16),
            pltpu.VMEM((D, D), bf16),
            pltpu.SemaphoreType.DMA((2,)),
        ],
        compiler_params=params(),
    )(core, *xs, *gs, mine, other)


def mlp_grad_body(which, core, *refs):
    out = refs[16]

    def run(xs, gs):
        out[...] = sum(dot_tn(x[...], g[...]) for x, g in zip(xs, gs)).astype(bf16)

    @pl.when(core[0] == which)
    def _():
        run(refs[:4], refs[4:8])

    @pl.when(core[0] != which)
    def _():
        run(refs[8:12], refs[12:16])


def mlp_grad(which, core, xs, pres, acts, gs):
    whole = [pl.BlockSpec((TOK, D), lambda k: (0, 0))] * 4
    part = [pl.BlockSpec((TOK, 384), lambda k: (0, k))] * 4
    return pl.pallas_call(
        functools.partial(mlp_grad_body, which),
        grid=(3,),
        in_specs=[pl.BlockSpec(memory_space=pltpu.SMEM)] + whole + part + whole + part,
        out_specs=pl.BlockSpec((D, 384), lambda k: (0, k)),
        out_shape=jax.ShapeDtypeStruct((D, D), bf16),
        compiler_params=params(),
    )(core, *xs, *pres, *acts, *gs)


def sort_hidden_body(core, mine, other, up, down):
    def run(ups, downs):
        for f in range(8):
            lanes = slice(SHARD * f, SHARD * (f + 1))
            up[:, 4 * SHARD * f : 4 * SHARD * (f + 1)] = jnp.concatenate(
                [ups[SHARD * z : SHARD * (z + 1), lanes] for z in range(4)], axis=1
            ).astype(f32)
        down[...] = downs[...].astype(f32)

    @pl.when(core[0] == 0)
    def _():
        run(mine, other)

    @pl.when(core[0] != 0)
    def _():
        run(other, mine)


def sort_hidden(core, mine, other):
    vmem = pl.BlockSpec(memory_space=pltpu.VMEM)
    return pl.pallas_call(
        sort_hidden_body,
        in_specs=[pl.BlockSpec(memory_space=pltpu.SMEM), vmem, vmem],
        out_specs=[vmem, vmem],
        out_shape=[
            jax.ShapeDtypeStruct((SHARD, FF), f32),
            jax.ShapeDtypeStruct((4 * SHARD, D), f32),
        ],
        compiler_params=params(),
    )(core, mine, other)


def normalize(x):
    center = x - jnp.mean(x, axis=-1, keepdims=True)
    inverse = lax.rsqrt(jnp.mean(center * center, axis=-1, keepdims=True) + norm_eps)
    return center * inverse, inverse


def norm_back(x, g, gain):
    plain, inverse = normalize(x)
    scaled = g * gain
    mixed = jnp.mean(scaled * plain, axis=-1, keepdims=True)
    grad = inverse * (scaled - jnp.mean(scaled, axis=-1, keepdims=True) - plain * mixed)
    sums = [jnp.sum(g * plain, axis=0, keepdims=True), jnp.sum(g, axis=0, keepdims=True)]
    return grad, sums


def call(body, ins, outs, scratch):
    spaces = {"vmem": pltpu.VMEM, "hbm": pl.ANY, "smem": pltpu.SMEM}
    return pl.pallas_call(
        body,
        in_specs=[pl.BlockSpec(memory_space=spaces[where]) for _, where in ins],
        out_specs=[pl.BlockSpec(memory_space=pltpu.VMEM)] * len(outs),
        out_shape=[jax.ShapeDtypeStruct(*o) for o in outs],
        scratch_shapes=scratch,
        compiler_params=params(),
    )(*[x for x, _ in ins])


def square_scratch(count):
    return [pltpu.VMEM((D, D), bf16)] * count + [pltpu.SemaphoreType.DMA((2,))]


def after_self_body(core, x, mixed, gain, bias, mine, other, total, normed, query, w1, w2, sem):
    fetch_pair(core, mine, other, w1, w2, sem)
    rows = x[...].astype(f32) + dot_nn(mixed[...], w1[...])
    total[...] = rows
    low = (normalize(rows)[0] * gain[...] + bias[...]).astype(bf16)
    normed[...] = low
    query[...] = dot_nn(low, w2[...]).astype(bf16)


def text_keys_body(core, context, mine, other, key, value, w1, w2, sem):
    fetch_pair(core, mine, other, w1, w2, sem, D)
    key[...] = dot_nn(context[...], w1[...]).astype(bf16)
    value[...] = dot_nn(context[...], w2[...]).astype(bf16)


def after_cross_body(core, x, mixed, gain, bias, mine, other, total, normed, w, sem):
    fetch_windows(core, mine, other, w, sem)
    rows = x[...] + dot_nn(mixed[...], w[...])
    total[...] = rows
    normed[...] = (normalize(rows)[0] * gain[...] + bias[...]).astype(bf16)


def third_back_body(core, x, g0, g1, g2, cot, gain, mine, other, grad, low, mixed, sums, w, sem):
    fetch_windows(core, mine, other, w, sem)
    g = g0[...].astype(f32) + g1[...].astype(f32) + g2[...].astype(f32)
    back, both = norm_back(x[...], g, gain[...])
    total = cot[...] + back
    grad[...] = total
    low[...] = total.astype(bf16)
    mixed[...] = dot_nt(total.astype(bf16), w[...]).astype(bf16)
    sums[...] = jnp.concatenate(both + [jnp.zeros((6, D), f32)], axis=0)


def second_back_body(core, x, gq, before, gain, mine, other, grad, low, mixed, sums, w1, w2, sem):
    fetch_pair(core, mine, other, w1, w2, sem)
    back, both = norm_back(x[...], dot_nt(gq[...], w2[...]), gain[...])
    total = before[...] + back
    grad[...] = total
    low[...] = total.astype(bf16)
    mixed[...] = dot_nt(total.astype(bf16), w1[...]).astype(bf16)
    sums[...] = jnp.concatenate(both + [jnp.zeros((6, D), f32)], axis=0)


def first_back_body(x, *refs):
    before, gain, grad = refs[SPLIT:]
    size = TOK // SPLIT
    sums = []
    for parts in refs[:SPLIT]:
        g = parts[:size, :].astype(f32)
        for k in range(1, 8):
            g = g + parts[size * k : size * (k + 1), :].astype(f32)
        sums.append(g)
    g = jnp.concatenate(sums, axis=0)
    grad[...] = before[...] + norm_back(x[...].astype(f32), g, gain[...])[0]


def text_back_body(
    core, kv, cols, text, w_text, mine, other, part, grad_text, grad_kv, w1, w2, sem
):
    fetch_pair(core, mine, other, w1, w2, sem, D)
    low = (dot_nt(kv[:, :D], w1[...]) + dot_nt(kv[:, D:], w2[...])).astype(bf16)
    part[...] = dot_nt(low, w_text[...]).astype(bf16)
    grad_text[...] = dot_tn(text[...], low).astype(bf16)
    grad_kv[...] = dot_tn(cols[...], kv[...]).astype(bf16)


def first_part_body(g, w, plain, *refs):
    rows = dot_nt(g[...], w[...])
    sums = refs[-1]
    size = TOK // SPLIT
    for k in range(SPLIT):
        refs[k][...] = rows[size * k : size * (k + 1)].astype(bf16)
    both = [
        jnp.sum(rows * plain[...].astype(f32), axis=0, keepdims=True),
        jnp.sum(rows, axis=0, keepdims=True),
        jnp.zeros((6, D), f32),
    ]
    both = jnp.concatenate(both, axis=0)

    @pl.when(pl.program_id(0) == 0)
    def _():
        sums[...] = both

    @pl.when(pl.program_id(0) != 0)
    def _():
        sums[...] += both


def first_part(g, w, plain):
    return pl.pallas_call(
        first_part_body,
        grid=(ROW // TOK,),
        in_specs=[
            pl.BlockSpec((TOK, 6 * SLOT), lambda i: (i, 0)),
            pl.BlockSpec((D, 6 * SLOT), lambda i: (0, 0)),
            pl.BlockSpec((TOK, D), lambda i: (i, 0)),
        ],
        out_specs=[
            *[pl.BlockSpec((TOK // SPLIT, D), lambda i: (i, 0))] * SPLIT,
            pl.BlockSpec((8, D), lambda i: (0, 0)),
        ],
        out_shape=[jax.ShapeDtypeStruct((ROW // SPLIT, D), bf16)] * SPLIT
        + [jax.ShapeDtypeStruct((8, D), f32)],
        cost_estimate=cost(11),
        compiler_params=params(),
    )(g, w, plain)


def heads_grad_body(x, g, out):
    grad = dot_tn(x[...], g[...]).astype(bf16)
    out[...] = jnp.concatenate(
        [
            grad[:, SLOT * (3 * h + k) : SLOT * (3 * h + k) + HEAD]
            for k in range(3)
            for h in range(2)
        ],
        axis=1,
    )


def heads_grad(x, g):
    return pl.pallas_call(
        heads_grad_body,
        grid=(3,),
        in_specs=[
            pl.BlockSpec((ROW, 384), lambda i: (0, i)),
            pl.BlockSpec((ROW, 6 * SLOT), lambda i: (0, 0)),
        ],
        out_specs=pl.BlockSpec((384, 3 * SHARD), lambda i: (i, 0)),
        out_shape=jax.ShapeDtypeStruct((D, 3 * SHARD), bf16),
        cost_estimate=cost(8),
        compiler_params=params(),
    )(x, g)


def unpack_heads_body(x, out):
    for k in range(3):
        out[SHARD * k : SHARD * (k + 1), :] = jnp.concatenate(
            [x[SHARD * p : SHARD * (p + 1), SHARD * k : SHARD * (k + 1)] for p in range(8)], axis=1
        )


def unpack_heads(x):
    return pl.pallas_call(
        unpack_heads_body,
        out_shape=jax.ShapeDtypeStruct((3 * SHARD, D), bf16),
        compiler_params=params(),
    )(x)


def row_block(x, index, rows):
    return lax.dynamic_slice_in_dim(x, index * rows, rows, axis=0)


def core_window(x, core):
    return lax.dynamic_slice_in_dim(x, core * STEP, WIN, axis=1)


def both_cores(x):
    return jnp.concatenate([x, shift(x, "c", 1)], axis=0)


def window_grad(left, right):
    core = lax.axis_index("c")
    sent = shift(core_window(right, 1 - core), "c", 1)
    rights = jnp.concatenate([core_window(right, core), sent], axis=0)
    return dot_tn(both_cores(left), rights).astype(bf16)


def sum_over(x, *axes):
    for axis in axes:
        n = lax.axis_size(axis)
        x = sum([shift(x, axis, k) for k in range(1, n)], x)
    return x


def local(
    tokens,
    text_states,
    seg_lengths,
    caption_of_segment,
    text_lengths,
    ln1_gain,
    ln1_bias,
    w_query,
    w_key,
    w_value,
    w_out,
    ln2_gain,
    ln2_bias,
    c_query,
    w_text,
    c_key,
    c_value,
    c_out,
    ln3_gain,
    ln3_bias,
    w_up,
    w_down,
    cotangent,
):
    core = lax.axis_index("c")
    first_core = core == 0
    core_index = core.astype(jnp.int32)[None]
    quarter = lax.axis_index("z")
    first_row = peer(0, 0) * TOK

    ends = jnp.cumsum(seg_lengths[0])
    positions = jnp.arange(ROW, dtype=jnp.int32)
    segment = jnp.sum((positions[:, None] >= ends[None, :]).astype(jnp.int32), axis=1)
    own_segment = lax.dynamic_slice_in_dim(segment, first_row, TOK)
    text_row = jnp.arange(TXT, dtype=jnp.int32)
    text_pos = text_row // TXT_OWN * CAP_TOK + text_row % TXT_OWN
    text_caption = text_pos // CAP_LEN
    live = jnp.sum(
        jnp.where(
            text_caption[:, None] == jnp.arange(CAPS, dtype=jnp.int32)[None, :],
            text_lengths[0][None, :],
            0,
        ),
        axis=1,
    )
    query_caption = jnp.sum(
        jnp.where(
            own_segment[:, None] == jnp.arange(SEGS, dtype=jnp.int32)[None, :],
            caption_of_segment[0][None, :],
            0,
        ),
        axis=1,
    )
    text_live = (text_row % TXT_OWN < CAP_TOK) & (text_pos % CAP_LEN < live)
    text_key = jnp.where(text_live, text_caption, -1)

    def row(x):
        return x[None, :]

    gap = jnp.zeros((SHARD, 128), bf16)
    square_pack = jnp.where(
        first_core,
        jnp.concatenate([w_out, c_key, c_out[:, :WIN], gap], axis=1),
        jnp.concatenate([c_query, c_value, c_out[:, STEP:], gap], axis=1),
    )
    square_pack = lax.dynamic_slice_in_dim(square_pack, quarter * QUARTER, QUARTER, axis=1)
    quarter_own = lax.all_gather(square_pack, FS, axis=0, tiled=True)

    rows_in = tokens[0]
    plain = normalize(rows_in.astype(f32))[0].astype(bf16)
    n01, n10, n30 = gather_first(plain)

    heads_pack = pack_heads(after(w_query, plain), w_key, w_value)
    n01, n10, n30, heads_pack = lax.optimization_barrier((n01, n10, n30, heads_pack))
    heads_w = peers_parts(heads_pack)
    n31, n20, n11 = gather_second(n01, n10)

    n31, n20, n11 = lax.optimization_barrier((n31, n20, n11))
    n21 = gather_third(n31, n11)
    plain_all, normed_all = place_rows(
        plain,
        (n01, n10, n30),
        (n31, n20, n11),
        n21,
        row(ln1_gain),
        row(ln1_bias),
    )
    heads_w = spread_heads(heads_w)
    quarter_own, normed_all, heads_w = lax.optimization_barrier((quarter_own, normed_all, heads_w))
    quarter_minus, quarter_plus = shift(quarter_own, "z", 1), shift(quarter_own, "z", -1)

    text_own = jnp.pad(after(text_states[0], normed_all), ((0, TXT_OWN - CAP_TOK), (0, 0)))
    text_columns = lax.all_to_all(text_own, FS, split_axis=1, concat_axis=0, tiled=True)

    up_own = jnp.concatenate(
        [
            lax.dynamic_slice(w_up, (0, 4 * SHARD * k + SHARD * quarter), (SHARD, SHARD))
            for k in range(8)
        ],
        axis=1,
    )
    hidden_own = jnp.where(first_core, up_own, row_block(w_down, quarter, SHARD))

    seg_col, seg_row = segment[:, None], segment[None, :]
    qkv = dot_nn(normed_all, heads_w).astype(bf16)
    text_columns, qkv = lax.optimization_barrier((text_columns, qkv))
    context_part = dot_nn(text_columns, w_text).astype(bf16)
    context_own = lax.psum_scatter(context_part, FS, scatter_dimension=0, tiled=True)
    head0, total0 = self_forward(0, seg_col, seg_row, after(qkv, context_part))
    head1, total1 = self_forward(1, seg_col, seg_row, after(qkv, head0))
    quarter_minus, quarter_plus, head1 = lax.optimization_barrier(
        (quarter_minus, quarter_plus, head1)
    )
    quarter_far = (
        shift(halves(quarter_minus)[0], "z", 1),
        shift(halves(quarter_plus)[1], "z", -1),
    )
    attended = lax.all_to_all(
        jnp.concatenate([head0, head1], axis=1), FS, split_axis=0, concat_axis=1, tiled=True
    )
    attended, context_own, *quarter_far = lax.optimization_barrier(
        (attended, context_own, *quarter_far)
    )
    context = every_peer(context_own)
    square_mine = place_quarters(quarter_own, quarter_minus, quarter_plus, *quarter_far)
    square_other = shift(square_mine, "c", 1)
    grad_out = cotangent[0]
    grad_mlp = grad_out.astype(bf16)
    grad_sent = after(grad_mlp, square_mine)
    mlp_minus, mlp_plus = shift(grad_sent, "z", 1), shift(grad_sent, "z", -1)
    hidden_mine = every_peer(after(hidden_own, context))

    after_self, normed_two, cross_query = call(
        after_self_body,
        [
            (core_index, "smem"), (rows_in, "vmem"), (attended, "vmem"),
            (row(ln2_gain), "vmem"), (row(ln2_bias), "vmem"),
            (square_mine, "hbm"), (square_other, "hbm"),
        ],
        [((TOK, D), f32), ((TOK, D), bf16), ((TOK, D), bf16)],
        square_scratch(2),
    )
    cross_key, cross_value = call(
        text_keys_body,
        [
            (core_index, "smem"), (after(context, cross_query, mlp_minus, mlp_plus), "vmem"),
            (square_mine, "hbm"), (square_other, "hbm"),
        ],
        [((TXT, D), bf16), ((TXT, D), bf16)],
        square_scratch(2),
    )
    cross_mixed = cross_forward(
        query_caption[:, None], text_key[None, :], cross_query, cross_key, cross_value
    )
    hidden_mine = after(hidden_mine, cross_mixed)
    weights = (hidden_mine, shift(hidden_mine, "c", 1))
    after_cross, normed_three = call(
        after_cross_body,
        [
            (core_index, "smem"), (after_self, "vmem"), (cross_mixed, "vmem"),
            (row(ln3_gain), "vmem"), (row(ln3_bias), "vmem"),
            (square_mine, "hbm"), (square_other, "hbm"),
        ],
        [((TOK, D), f32), ((TOK, D), bf16)],
        square_scratch(1),
    )

    mlp_sent = lax.optimization_barrier((mlp_minus, mlp_plus, cross_query))
    mlp_far = (
        shift(halves(mlp_sent[0])[0], "z", 1),
        shift(halves(mlp_sent[1])[1], "z", -1),
    )

    three_minus, three_plus = shift(normed_three, "z", 1), shift(normed_three, "z", -1)
    out_own, act_own, pre_own, back_own = mlp(core_index, (normed_three,), (grad_mlp,), *weights)
    three_minus, three_plus, out_own = lax.optimization_barrier(
        (three_minus, three_plus, out_own)
    )
    three_far = (
        shift(halves(three_minus)[0], "z", 1),
        shift(halves(three_plus)[1], "z", -1),
    )
    near = mlp(core_index, (three_minus, three_plus), (mlp_minus, mlp_plus), *weights)
    out_m, act_m, pre_m, back_m, out_p, act_p, pre_p, back_p = near
    *three_far, out_m = lax.optimization_barrier((*three_far, out_m))
    out_far, act_far, pre_far, back_far = mlp(core_index, three_far, mlp_far, *weights)
    back_minus, back_plus = reduce_z(back_far, back_m, back_p)
    three_parts = (normed_three, three_minus, three_plus, jnp.concatenate(three_far, axis=0))
    pre_parts = (pre_own, pre_m, pre_p, pre_far)
    act_parts = (act_own, act_m, act_p, act_far)
    mlp_parts = (grad_mlp, mlp_minus, mlp_plus, jnp.concatenate(mlp_far, axis=0))
    send = mlp_grad(1, core_index, three_parts, pre_parts, act_parts, mlp_parts)
    back_minus, back_plus, send = lax.optimization_barrier((back_minus, back_plus, send))
    back_minus, back_plus = shift(back_minus, "z", -1), shift(back_plus, "z", 1)
    keep = mlp_grad(
        0, core_index, three_parts, pre_parts, act_parts, (after(grad_mlp, send), *mlp_parts[1:])
    )
    back_minus, back_plus, keep = lax.optimization_barrier((back_minus, back_plus, keep))
    hidden_sum = keep + shift(send, "c", 1)
    grad_after_cross, grad_cross_branch, grad_cross_mixed, sums_three = call(
        third_back_body,
        [
            (core_index, "smem"), (after_cross, "vmem"), (back_own, "vmem"),
            (back_minus, "vmem"), (back_plus, "vmem"), (grad_out, "vmem"),
            (after(row(ln3_gain), hidden_sum), "vmem"), (square_mine, "hbm"), (square_other, "hbm"),
        ],
        [((TOK, D), f32), ((TOK, D), bf16), ((TOK, D), bf16), ((8, D), f32)],
        square_scratch(1),
    )

    grad_cquery_rows, grad_kv = cross_backward(
        text_key[:, None],
        query_caption[None, :],
        cross_query,
        cross_key,
        cross_value,
        grad_cross_mixed,
    )
    kv_own = lax.psum_scatter(grad_kv, FS, scatter_dimension=0, tiled=True)
    grad_after_self, grad_self_branch, grad_attended, sums_two = call(
        second_back_body,
        [
            (core_index, "smem"), (after_self, "vmem"), (grad_cquery_rows, "vmem"),
            (grad_after_cross, "vmem"), (row(ln2_gain), "vmem"),
            (square_mine, "hbm"), (square_other, "hbm"),
        ],
        [((TOK, D), f32), ((TOK, D), bf16), ((TOK, D), bf16), ((8, D), f32)],
        square_scratch(2),
    )
    grad_heads = lax.all_to_all(grad_attended, FS, split_axis=1, concat_axis=0, tiled=True)

    square = jnp.concatenate(
        [
            window_grad(cross_mixed, after(grad_cross_branch, grad_attended)),
            window_grad(normed_two, after(grad_cquery_rows, grad_attended)),
            window_grad(attended, grad_self_branch),
        ],
        axis=1,
    )

    def square_chunk(dy, dx):
        return row_block(square, peer(dy, dx), SHARD)

    grad_heads, square = lax.optimization_barrier((grad_heads, square))
    grad_qkv = self_backward(0, seg_col, seg_row, total0, qkv, grad_heads)
    kv_own, square, grad_qkv = lax.optimization_barrier((kv_own, square, grad_qkv))
    s_lo, s_hi, s20 = reduce_first(square_chunk)
    kv_all = every_peer(kv_own)
    hidden_grad = lax.psum_scatter(after(hidden_sum, kv_own), FS, scatter_dimension=0, tiled=True)
    out_minus, out_plus = reduce_z(after(out_far, grad_qkv), out_m, out_p)
    grad_qkv = self_backward(
        1, seg_col, seg_row, total1, qkv, after(grad_heads, kv_own), (grad_qkv,)
    )
    s_lo, s_hi, s20, out_minus, out_plus, grad_qkv = lax.optimization_barrier(
        (s_lo, s_hi, s20, out_minus, out_plus, grad_qkv)
    )
    s11, s31 = reduce_second(square_chunk, s_lo, s_hi)

    heads_own = heads_grad(normed_all, grad_qkv)
    heads_own, s11, s31, kv_all = lax.optimization_barrier((heads_own, s11, s31, kv_all))
    heads_part = peers_parts(heads_own)
    square_parts = reduce_third(square_chunk, s20, s11, s31)
    part, sums_one = first_part(after(grad_qkv, heads_own), heads_w, plain_all)
    part, heads_part, kv_all, *square_parts = lax.optimization_barrier(
        (part, heads_part, kv_all, *square_parts)
    )
    sent = peers_parts(part)

    square = reduce_last(square_chunk, *square_parts).astype(bf16)
    heads_rows = unpack_heads(heads_part)
    early = row_block(heads_rows, core, 216) + shift(row_block(heads_rows, 1 - core, 216), "c", 1)
    early = jnp.concatenate([early, jnp.zeros((256 - 216, D), bf16)], axis=0)
    square = jnp.concatenate([square[:, WIN * k : WIN * (k + 1)] for k in range(3)], axis=0)
    square = jnp.concatenate([square[:216], square[216:]], axis=1)
    early = jnp.concatenate(
        [early, jnp.concatenate([square, jnp.zeros((256 - 216, 2 * WIN), bf16)], axis=0)], axis=1
    )
    early = lax.psum_scatter(early, "z", scatter_dimension=0, tiled=True)
    norms = jnp.concatenate([sums_one[:2], sums_two[:2], sums_three[:2], jnp.zeros((2, D), f32)])
    norms = sum_over(norms, "z", "c")
    own_columns = lax.dynamic_slice_in_dim(context, peer(0, 0) * SHARD, SHARD, axis=1)
    text_part, grad_w_text, grad_w_kv = call(
        text_back_body,
        [
            (core_index, "smem"), (kv_all, "vmem"), (own_columns, "vmem"),
            (text_columns, "vmem"), (w_text, "vmem"),
            (square_mine, "hbm"), (square_other, "hbm"),
        ],
        [((TXT, TXT), bf16), ((TXT, D), bf16), ((SHARD, 2 * D), bf16)],
        square_scratch(2),
    )

    def half(which):
        kv = jnp.where(which == 0, grad_w_kv[:, :D], grad_w_kv[:, D:])
        return jnp.concatenate(
            [row_block(grad_w_text, which, 256), kv, jnp.zeros((448 - 400, D), bf16)], axis=0
        )

    late = half(core) + shift(half(1 - core), "c", 1)
    late = lax.psum_scatter(late, "z", scatter_dimension=0, tiled=True)
    hidden_grad = after(hidden_grad, part)
    hidden_grad = hidden_grad + shift(hidden_grad, "xh", 1)
    part, norms, late = lax.optimization_barrier((sent, norms, late))
    early = after(early, part)
    early = early + shift(early, "xh", 1)
    hidden_grad = in_order(*neighbours(after(hidden_grad, part)))
    grad_w_up, grad_w_down = sort_hidden(core_index, hidden_grad, shift(hidden_grad, "c", 1))

    norms = sum_over(norms, "y", "xl", "xh")
    late = late + shift(late, "xh", 1)
    early = in_order(*neighbours(early))
    late = in_order(*neighbours(late))

    def by_core(x):
        other = shift(x, "c", 1)
        low, high = jnp.where(first_core, x, other), jnp.where(first_core, other, x)
        return low.astype(f32), high.astype(f32)

    low, high = by_core(early)
    grad_w_query = low[:144, :D]
    grad_w_key = jnp.concatenate([low[144:216, :D], high[:72, :D]], axis=0)
    grad_w_value = high[72:216, :D]
    low = jnp.concatenate([low[:216, D : D + WIN], low[:216, D + WIN :]], axis=0)
    high = jnp.concatenate([high[:216, D : D + WIN], high[:216, D + WIN :]], axis=0)
    grad_c_out, grad_c_query, grad_w_out = (
        jnp.concatenate(
            [low[SHARD * k : SHARD * (k + 1)], high[SHARD * k : SHARD * (k + 1), 128:]], axis=1
        )
        for k in range(3)
    )
    low, high = by_core(late)
    grad_w_text = jnp.concatenate([low[:256], high[:256]], axis=0)
    grad_c_key, grad_c_value = low[256:400], high[256:400]
    out_minus, out_plus = shift(out_minus, "z", -1), shift(out_plus, "z", 1)
    outputs = (
        after_cross + out_own.astype(f32) + out_minus.astype(f32) + out_plus.astype(f32)
    )

    grad_tokens = call(
        first_back_body,
        [
            (rows_in, "vmem"), (part, "vmem"), (grad_after_self, "vmem"),
            (row(ln1_gain), "vmem"),
        ],
        [((TOK, D), f32)],
        [],
    )[0]
    grad_text = lax.all_to_all(
        after(text_part, part), FS, split_axis=0, concat_axis=1, tiled=True
    )
    grad_text = grad_text[:CAP_TOK].astype(f32)
    return (
        outputs[None],
        grad_tokens[None],
        grad_text[None],
        norms[0],
        norms[1],
        grad_w_query,
        grad_w_key,
        grad_w_value,
        grad_w_out,
        norms[2],
        norms[3],
        grad_c_query,
        grad_w_text,
        grad_c_key,
        grad_c_value,
        grad_c_out,
        norms[4],
        norms[5],
        grad_w_up,
        grad_w_down,
    )


def solution(mesh):
    split = Mesh(mesh.devices.reshape(2, 4, 2, 4, 2), ("xh", "z", "c", "y", "xl"))
    dp = ("xh", "z", "c")
    rows = P(dp, FS, None)
    per_row = P(dp, None)
    weight = P(FS, None)
    rep = P()
    in_specs = (
        rows, rows, per_row, per_row, per_row,
        rep, rep, weight, weight, weight, weight,
        rep, rep, weight, weight, weight, weight, weight,
        rep, rep, weight, weight, rows,
    )
    out_specs = (
        rows, rows, rows,
        rep, rep, weight, weight, weight, weight,
        rep, rep, weight, weight, weight, weight, weight,
        rep, rep, weight, weight,
    )
    return jax.shard_map(
        local, mesh=split, in_specs=in_specs, out_specs=out_specs, check_vma=False
    )
```

```python
import functools

import jax
import jax.numpy as jnp
from jax import lax
from jax.experimental import pallas as pl
from jax.experimental.pallas import tpu as pltpu
from jax.sharding import Mesh
from jax.sharding import PartitionSpec as P

HEADS = 16
HEAD = 72
D = 1152
FF = 4608
CAP_TOK = 60
TXT_OWN = 64
TXT = 8 * TXT_OWN
TOK = 256
ROW = 2048
CAP_LEN = 120
SEGS = 3
CAPS = 4
SHARD = 144
SLOT = 128
SPLIT = 1
WIN = 640
STEP = 512

bf16 = jnp.bfloat16
f32 = jnp.float32
norm_eps = 1e-06
masked_score = -1e30
scale = HEAD ** (-0.5)
log2e = 1.4426950408889634
FS = ("y", "xl")
VMEM = 60 * 1024 * 1024


def dot_nn(a, b):
    return lax.dot_general(a, b, (((1,), (0,)), ((), ())), preferred_element_type=f32)


def dot_nt(a, b):
    return lax.dot_general(a, b, (((1,), (1,)), ((), ())), preferred_element_type=f32)


def dot_tn(a, b):
    return lax.dot_general(a, b, (((0,), (0,)), ((), ())), preferred_element_type=f32)


def params():
    return pltpu.CompilerParams(vmem_limit_bytes=VMEM)


def cost(micros):
    return pl.CostEstimate(flops=int(micros * 1.15e9), bytes_accessed=0, transcendentals=0)


def shift(x, axis, by):
    n = lax.axis_size(axis)
    return lax.ppermute(x, axis, [(i, (i + by) % n) for i in range(n)])


def halves(x):
    h = (x.shape[0] // 2 + 15) // 16 * 16
    return x[:h], x[h:]


def after(x, *others):
    return lax.optimization_barrier((x, *others))[0]


def gather_first(x):
    return shift(x, "xl", 1), shift(x, "y", -1), shift(x, "y", 1)


def gather_second(x01, x10):
    return shift(x01, "y", 1), shift(x10, "y", -1), shift(x10, "xl", 1)


def gather_third(x31, x11):
    return shift(halves(x11)[0], "y", -1), shift(halves(x31)[1], "y", 1)


NEAR = ((0, 0), (0, 1), (1, 0), (3, 0))
NEXT = ((3, 1), (2, 0), (1, 1))
LAST = (2, 1)


def reduce_first(chunk):
    lo, hi = halves(chunk(2, 1))
    return shift(lo, "y", 1), shift(hi, "y", -1), shift(chunk(2, 0), "y", 1)


def reduce_second(chunk, lo, hi):
    h = lo.shape[0]
    c11, c31 = chunk(1, 1), chunk(3, 1)
    c11 = jnp.concatenate([c11[:h] + lo, c11[h:]], axis=0)
    c31 = jnp.concatenate([c31[:h], c31[h:] + hi], axis=0)
    return shift(c11, "xl", 1), shift(c31, "y", -1)


def reduce_third(chunk, c20, c11, c31):
    return (
        shift(chunk(1, 0) + c20 + c11, "y", 1),
        shift(chunk(0, 1) + c31, "xl", 1),
        shift(chunk(3, 0), "y", -1),
    )


def reduce_last(chunk, *parts):
    return sum([p.astype(f32) for p in parts], chunk(0, 0).astype(f32))


def every_peer(x, axes=FS):
    n = lax.axis_size(axes)
    copies = jnp.broadcast_to(x[None], (n, *x.shape)).reshape(n * x.shape[0], x.shape[1])
    return lax.all_to_all(copies, axes, 0, 0, tiled=True)


def peers_parts(x, axes=FS):
    return lax.all_to_all(x, axes, 0, 0, tiled=True)


def sum_parts(parts):
    return jnp.sum(parts.reshape(8, -1, parts.shape[1]).astype(f32), axis=0)


def neighbours(x):
    return x, shift(x, "z", 1), shift(x, "z", 2), shift(x, "z", -1)


def in_order(*around):
    rows, cols = around[0].shape

    def body(where, *refs):
        ins, out = refs[:4], refs[4]
        for k in range(4):
            row = pl.multiple_of(lax.rem(where[0] + 4 - k, 4) * rows, 16)
            out[pl.ds(row, rows), :] = ins[k][...]

    vmem = pl.BlockSpec(memory_space=pltpu.VMEM)
    return pl.pallas_call(
        body,
        in_specs=[pl.BlockSpec(memory_space=pltpu.SMEM)] + [vmem] * 4,
        out_specs=vmem,
        out_shape=jax.ShapeDtypeStruct((4 * rows, cols), bf16),
        compiler_params=params(),
    )(lax.axis_index("z").astype(jnp.int32)[None], *around)


def reduce_z(far, minus, plus):
    lo, hi = halves(far)
    lo, hi = shift(lo, "z", -1), shift(hi, "z", 1)
    h = lo.shape[0]
    return (
        jnp.concatenate([minus[:h] + lo, minus[h:]], axis=0),
        jnp.concatenate([plus[:h], plus[h:] + hi], axis=0),
    )


def peer(dy, dx):
    return ((lax.axis_index("y") + dy) % 4) * 2 + (lax.axis_index("xl") ^ dx)


def place_rows(own, first, second, third, gain, bias):
    lo = third[0].shape[0]
    rows, cols = own.shape
    pieces = [(x, p, 0) for x, p in zip((own, *first), NEAR)]
    pieces += [(x, p, 0) for x, p in zip(second, NEXT)]
    pieces += [(third[0], LAST, 0), (third[1], LAST, lo)]
    count = len(pieces)

    def body(where, gain, bias, *refs):
        ins, plain, normed, sem = refs[:count], refs[count], refs[count + 1], refs[-1]
        started = []
        for k, (x, _, off) in enumerate(pieces):
            row = pl.multiple_of(where[k] * rows + off, 16)
            one = pltpu.make_async_copy(ins[k], plain.at[pl.ds(row, x.shape[0])], sem.at[k])
            one.start()
            started.append(one)
        for one in started:
            one.wait()

        def step(i, carry):
            part = pl.ds(pl.multiple_of(i * rows, rows), rows)
            normed[part, :] = (plain[part, :].astype(f32) * gain[...] + bias[...]).astype(bf16)
            return carry

        lax.fori_loop(0, 8, step, 0)

    vmem = pl.BlockSpec(memory_space=pltpu.VMEM)
    return pl.pallas_call(
        body,
        in_specs=[pl.BlockSpec(memory_space=pltpu.SMEM), vmem, vmem]
        + [pl.BlockSpec(memory_space=pl.ANY)] * count,
        out_specs=[vmem, vmem],
        out_shape=[jax.ShapeDtypeStruct((8 * rows, cols), bf16)] * 2,
        scratch_shapes=[pltpu.SemaphoreType.DMA((count,))],
        compiler_params=params(),
    )(
        jnp.stack([peer(*p) for _, p, _ in pieces]).astype(jnp.int32),
        gain,
        bias,
        *[x for x, _, _ in pieces],
    )


QUARTER = 768


def place_quarters(*quarters):
    def body(where, own, minus, plus, far_lo, far_hi, out, sem):
        started = []
        half = far_lo.shape[0]
        for k, (ref, turn, row) in enumerate(
            ((own, 0, 0), (minus, 3, 0), (plus, 1, 0), (far_lo, 2, 0), (far_hi, 2, half))
        ):
            column = pl.multiple_of(lax.rem(where[0] + turn, 4) * QUARTER, 128)
            one = pltpu.make_async_copy(
                ref, out.at[pl.ds(row, ref.shape[0]), pl.ds(column, QUARTER)], sem.at[k]
            )
            one.start()
            started.append(one)
        for one in started:
            one.wait()

    return pl.pallas_call(
        body,
        in_specs=[pl.BlockSpec(memory_space=pltpu.SMEM)] + [pl.BlockSpec(memory_space=pl.ANY)] * 5,
        out_specs=pl.BlockSpec(memory_space=pltpu.VMEM),
        out_shape=jax.ShapeDtypeStruct((D, 4 * QUARTER), bf16),
        scratch_shapes=[pltpu.SemaphoreType.DMA((5,))],
        compiler_params=params(),
    )(lax.axis_index("z").astype(jnp.int32)[None], *quarters)


def pack_heads_body(wq, wk, wv, out):
    for p in range(8):
        rows = slice(SHARD * p, SHARD * (p + 1))
        out[rows, :] = jnp.concatenate([w[:, rows] for w in (wq, wk, wv)], axis=1)


def pack_heads(*weights):
    return pl.pallas_call(
        pack_heads_body,
        out_shape=jax.ShapeDtypeStruct((D, 3 * SHARD), bf16),
        compiler_params=params(),
    )(*weights)


def spread_heads_body(x, out):
    blank = jnp.zeros((D, SLOT - HEAD), bf16)
    for h in range(2):
        for k in range(3):
            first = SHARD * k + HEAD * h
            slot = SLOT * (3 * h + k)
            out[:, slot : slot + SLOT] = jnp.concatenate(
                [x[:, first : first + HEAD], blank], axis=1
            )


def spread_heads(x):
    return pl.pallas_call(
        spread_heads_body,
        out_shape=jax.ShapeDtypeStruct((D, 6 * SLOT), bf16),
        compiler_params=params(),
    )(x)


def self_forward_body(seg_q, seg_k, q, kv, out, total):
    s = dot_nt(q[:, :SLOT], kv[:, SLOT : 2 * SLOT])
    s = jnp.where(seg_q[...] == seg_k[...], s, masked_score)
    top = jnp.max(s, axis=1, keepdims=True)
    p = jnp.exp2((s - top) * (scale * log2e))
    mass = jnp.sum(p, axis=1, keepdims=True)
    out[...] = (dot_nn(p.astype(bf16), kv[:, 2 * SLOT :]) / mass)[:, :HEAD].astype(bf16)
    log_total = top * (scale * log2e) + jnp.log2(mass)
    total[...] = jnp.transpose(jnp.broadcast_to(log_total, (TOK, SLOT)))[0:1, :]


def self_forward(head, seg_q, seg_k, qkv):
    return pl.pallas_call(
        self_forward_body,
        grid=(ROW // TOK,),
        in_specs=[
            pl.BlockSpec((TOK, 1), lambda i: (i, 0)),
            pl.BlockSpec((1, ROW), lambda i: (0, 0)),
            pl.BlockSpec((TOK, 3 * SLOT), lambda i: (i, head)),
            pl.BlockSpec((ROW, 3 * SLOT), lambda i: (0, head)),
        ],
        out_specs=[
            pl.BlockSpec((TOK, HEAD), lambda i: (i, 0)),
            pl.BlockSpec((1, TOK), lambda i: (0, i)),
        ],
        out_shape=[
            jax.ShapeDtypeStruct((ROW, HEAD), bf16),
            jax.ShapeDtypeStruct((1, ROW), f32),
        ],
        compiler_params=params(),
    )(seg_q, seg_k, qkv, qkv)


def self_backward_body(head, seg_k, seg_q, total, q, kv, g, *refs):
    grad, key_sum, value_sum, key_t = refs[-4:]
    i = pl.program_id(0)

    @pl.when(i == 0)
    def _():
        key_sum[...] = jnp.zeros_like(key_sum)
        value_sum[...] = jnp.zeros_like(value_sum)
        key_t[...] = jnp.transpose(kv[:, SLOT : 2 * SLOT])

    rows = pl.ds(pl.multiple_of(i * TOK, TOK), TOK)
    q_h, k_h, v_h = q[:, :SLOT], kv[:, SLOT : 2 * SLOT], kv[:, 2 * SLOT :]
    g_both = g[...]
    g_h = jnp.concatenate(
        [g_both[:, HEAD * head : HEAD * (head + 1)], jnp.zeros((TOK, SLOT - HEAD), bf16)], axis=1
    )
    p = jnp.exp2(dot_nt(k_h, q_h) * (scale * log2e) - total[...])
    p = jnp.where(seg_k[...] == seg_q[...], p, 0.0)
    dp = dot_nt(v_h, g_h)
    ds = (p * (dp - jnp.sum(p * dp, axis=0, keepdims=True))).astype(bf16)
    value_sum[...] += dot_nn(p.astype(bf16), g_h)
    key_sum[...] += dot_nn(ds, q_h)
    grad[rows, :SLOT] = (jnp.transpose(dot_nn(key_t[...], ds)) * scale).astype(bf16)

    @pl.when(i == pl.num_programs(0) - 1)
    def _():
        grad[:, SLOT : 2 * SLOT] = (key_sum[...] * scale).astype(bf16)
        grad[:, 2 * SLOT :] = value_sum[...].astype(bf16)


def self_backward(head, seg_k, seg_q, total, qkv, g, before=()):
    return pl.pallas_call(
        functools.partial(self_backward_body, head),
        grid=(ROW // TOK,),
        in_specs=[
            pl.BlockSpec((ROW, 1), lambda i: (0, 0)),
            pl.BlockSpec((1, TOK), lambda i: (0, i)),
            pl.BlockSpec((1, TOK), lambda i: (0, i)),
            pl.BlockSpec((TOK, 3 * SLOT), lambda i: (i, head)),
            pl.BlockSpec((ROW, 3 * SLOT), lambda i: (0, head)),
            pl.BlockSpec((TOK, SHARD), lambda i: (i, 0)),
        ]
        + [pl.BlockSpec(memory_space=pl.ANY)] * len(before),
        out_specs=pl.BlockSpec((ROW, 3 * SLOT), lambda i: (0, head)),
        out_shape=jax.ShapeDtypeStruct((ROW, 6 * SLOT), bf16),
        input_output_aliases={6: 0} if before else {},
        scratch_shapes=[
            pltpu.VMEM((ROW, SLOT), f32),
            pltpu.VMEM((ROW, SLOT), f32),
            pltpu.VMEM((SLOT, ROW), bf16),
        ],
        compiler_params=params(),
    )(seg_k, seg_q, total, qkv, qkv, g, *before)


def cross_forward_body(cap_q, cap_t, q, k, v, out):
    allowed = cap_q[...] == cap_t[...]
    mixed = []
    for h in range(HEADS):
        a, b = HEAD * h, HEAD * (h + 1)
        s = dot_nt(q[:, a:b], k[:, a:b])
        s = jnp.where(allowed, s, masked_score)
        top = jnp.max(s, axis=1, keepdims=True)
        p = jnp.exp2((s - top) * (scale * log2e))
        mass = jnp.sum(p, axis=1, keepdims=True)
        mixed.append(dot_nn(p.astype(bf16), v[:, a:b]) / mass)
    out[...] = jnp.concatenate(mixed, axis=1).astype(bf16)


def cross_forward(cap_q, cap_t, q, k, v):
    return pl.pallas_call(
        cross_forward_body,
        out_shape=jax.ShapeDtypeStruct((TOK, D), bf16),
        compiler_params=params(),
    )(cap_q, cap_t, q, k, v)


def cross_backward_body(cap_t, cap_q, q, k, v, g, grad_q, grad_kv):
    allowed = cap_t[...] == cap_q[...]
    dq, dk, dv = [], [], []
    for h in range(HEADS):
        a, b = HEAD * h, HEAD * (h + 1)
        q_h, k_h, v_h, g_h = q[:, a:b], k[:, a:b], v[:, a:b], g[:, a:b]
        s = jnp.where(allowed, dot_nt(k_h, q_h), masked_score)
        top = jnp.max(s, axis=0, keepdims=True)
        p = jnp.exp2((s - top) * (scale * log2e))
        p = p / jnp.sum(p, axis=0, keepdims=True)
        dp = dot_nt(v_h, g_h)
        ds = (p * (dp - jnp.sum(p * dp, axis=0, keepdims=True))).astype(bf16)
        dv.append(dot_nn(p.astype(bf16), g_h))
        dk.append(dot_nn(ds, q_h) * scale)
        dq.append(dot_tn(ds, k_h) * scale)
    grad_q[...] = jnp.concatenate(dq, axis=1).astype(bf16)
    grad_kv[:, :D] = jnp.concatenate(dk, axis=1).astype(bf16)
    grad_kv[:, D:] = jnp.concatenate(dv, axis=1).astype(bf16)


def cross_backward(cap_t, cap_q, q, k, v, g):
    return pl.pallas_call(
        cross_backward_body,
        out_shape=[
            jax.ShapeDtypeStruct((TOK, D), bf16),
            jax.ShapeDtypeStruct((TXT, 2 * D), bf16),
        ],
        compiler_params=params(),
    )(cap_t, cap_q, q, k, v, g)


def fetch_pair(core, mine, other, first, second, sem, column=0):
    def run(a, b):
        columns = pl.ds(column, D)
        one = pltpu.make_async_copy(a.at[:, columns], first, sem.at[0])
        two = pltpu.make_async_copy(b.at[:, columns], second, sem.at[1])
        one.start()
        two.start()
        one.wait()
        two.wait()

    @pl.when(core[0] == 0)
    def _():
        run(mine, other)

    @pl.when(core[0] != 0)
    def _():
        run(other, mine)


def fetch_windows(core, mine, other, whole, sem):
    def run(a, b):
        one = pltpu.make_async_copy(
            a.at[:, pl.ds(2 * D, WIN)], whole.at[:, pl.ds(0, WIN)], sem.at[0]
        )
        two = pltpu.make_async_copy(
            b.at[:, pl.ds(2 * D + 128, STEP)], whole.at[:, pl.ds(WIN, STEP)], sem.at[1]
        )
        one.start()
        two.start()
        one.wait()
        two.wait()

    @pl.when(core[0] == 0)
    def _():
        run(mine, other)

    @pl.when(core[0] != 0)
    def _():
        run(other, mine)


def mlp_body(parts, count, core, *refs):
    xs, gs = refs[: parts * count], refs[parts * count : 2 * parts * count]
    mine, other = refs[2 * parts * count : 2 * parts * count + 2]
    outs = refs[2 * parts * count + 2 : -3]
    up, down, sem = refs[-3:]
    fetch_pair(core, mine, other, up, down, sem)
    for k in range(count):
        x = jnp.concatenate([r[...] for r in xs[parts * k : parts * (k + 1)]], axis=0)
        g = jnp.concatenate([r[...] for r in gs[parts * k : parts * (k + 1)]], axis=0)
        out, act_out, pre_out, grad_x = outs[4 * k : 4 * (k + 1)]
        pre = dot_nn(x, up[...])
        grad_act = dot_nt(g, down[...])
        cdf = 0.5 * (1.0 + lax.erf(pre * (0.5**0.5)))
        density = jnp.exp2(pre * pre * (-0.5 * log2e)) * 0.3989422804014327
        act = (pre * cdf).astype(bf16)
        grad_pre = (grad_act * (cdf + pre * density)).astype(bf16)
        act_out[...] = act
        pre_out[...] = grad_pre
        out[...] = dot_nn(act, down[...]).astype(out.dtype)
        grad_x[...] = dot_nt(grad_pre, up[...]).astype(grad_x.dtype)


def mlp(core, xs, gs, mine, other):
    parts = TOK // xs[0].shape[0]
    count = len(xs) // parts
    vmem = pl.BlockSpec(memory_space=pltpu.VMEM)
    hbm = pl.BlockSpec(memory_space=pl.ANY)
    return pl.pallas_call(
        functools.partial(mlp_body, parts, count),
        in_specs=[pl.BlockSpec(memory_space=pltpu.SMEM)]
        + [vmem] * (2 * parts * count)
        + [hbm, hbm],
        out_specs=[vmem] * (4 * count),
        out_shape=[jax.ShapeDtypeStruct((TOK, D), bf16)] * (4 * count),
        scratch_shapes=[
            pltpu.VMEM((D, D), bf16),
            pltpu.VMEM((D, D), bf16),
            pltpu.SemaphoreType.DMA((2,)),
        ],
        compiler_params=params(),
    )(core, *xs, *gs, mine, other)


def mlp_grad_body(which, core, *refs):
    out = refs[16]

    def run(xs, gs):
        out[...] = sum(dot_tn(x[...], g[...]) for x, g in zip(xs, gs)).astype(bf16)

    @pl.when(core[0] == which)
    def _():
        run(refs[:4], refs[4:8])

    @pl.when(core[0] != which)
    def _():
        run(refs[8:12], refs[12:16])


def mlp_grad(which, core, xs, pres, acts, gs):
    whole = [pl.BlockSpec((TOK, D), lambda k: (0, 0))] * 4
    part = [pl.BlockSpec((TOK, 384), lambda k: (0, k))] * 4
    return pl.pallas_call(
        functools.partial(mlp_grad_body, which),
        grid=(3,),
        in_specs=[pl.BlockSpec(memory_space=pltpu.SMEM)] + whole + part + whole + part,
        out_specs=pl.BlockSpec((D, 384), lambda k: (0, k)),
        out_shape=jax.ShapeDtypeStruct((D, D), bf16),
        compiler_params=params(),
    )(core, *xs, *pres, *acts, *gs)


def sort_hidden_body(core, mine, other, up, down):
    def run(ups, downs):
        for f in range(8):
            lanes = slice(SHARD * f, SHARD * (f + 1))
            up[:, 4 * SHARD * f : 4 * SHARD * (f + 1)] = jnp.concatenate(
                [ups[SHARD * z : SHARD * (z + 1), lanes] for z in range(4)], axis=1
            ).astype(f32)
        down[...] = downs[...].astype(f32)

    @pl.when(core[0] == 0)
    def _():
        run(mine, other)

    @pl.when(core[0] != 0)
    def _():
        run(other, mine)


def sort_hidden(core, mine, other):
    vmem = pl.BlockSpec(memory_space=pltpu.VMEM)
    return pl.pallas_call(
        sort_hidden_body,
        in_specs=[pl.BlockSpec(memory_space=pltpu.SMEM), vmem, vmem],
        out_specs=[vmem, vmem],
        out_shape=[
            jax.ShapeDtypeStruct((SHARD, FF), f32),
            jax.ShapeDtypeStruct((4 * SHARD, D), f32),
        ],
        compiler_params=params(),
    )(core, mine, other)


def normalize(x):
    center = x - jnp.mean(x, axis=-1, keepdims=True)
    inverse = lax.rsqrt(jnp.mean(center * center, axis=-1, keepdims=True) + norm_eps)
    return center * inverse, inverse


def norm_back(x, g, gain):
    plain, inverse = normalize(x)
    scaled = g * gain
    mixed = jnp.mean(scaled * plain, axis=-1, keepdims=True)
    grad = inverse * (scaled - jnp.mean(scaled, axis=-1, keepdims=True) - plain * mixed)
    sums = [jnp.sum(g * plain, axis=0, keepdims=True), jnp.sum(g, axis=0, keepdims=True)]
    return grad, sums


def call(body, ins, outs, scratch):
    spaces = {"vmem": pltpu.VMEM, "hbm": pl.ANY, "smem": pltpu.SMEM}
    return pl.pallas_call(
        body,
        in_specs=[pl.BlockSpec(memory_space=spaces[where]) for _, where in ins],
        out_specs=[pl.BlockSpec(memory_space=pltpu.VMEM)] * len(outs),
        out_shape=[jax.ShapeDtypeStruct(*o) for o in outs],
        scratch_shapes=scratch,
        compiler_params=params(),
    )(*[x for x, _ in ins])


def square_scratch(count):
    return [pltpu.VMEM((D, D), bf16)] * count + [pltpu.SemaphoreType.DMA((2,))]


def after_self_body(core, x, mixed, gain, bias, mine, other, total, normed, query, w1, w2, sem):
    fetch_pair(core, mine, other, w1, w2, sem)
    rows = x[...].astype(f32) + dot_nn(mixed[...], w1[...])
    total[...] = rows
    low = (normalize(rows)[0] * gain[...] + bias[...]).astype(bf16)
    normed[...] = low
    query[...] = dot_nn(low, w2[...]).astype(bf16)


def text_keys_body(core, context, mine, other, key, value, w1, w2, sem):
    fetch_pair(core, mine, other, w1, w2, sem, D)
    key[...] = dot_nn(context[...], w1[...]).astype(bf16)
    value[...] = dot_nn(context[...], w2[...]).astype(bf16)


def after_cross_body(core, x, mixed, gain, bias, mine, other, total, normed, w, sem):
    fetch_windows(core, mine, other, w, sem)
    rows = x[...] + dot_nn(mixed[...], w[...])
    total[...] = rows
    normed[...] = (normalize(rows)[0] * gain[...] + bias[...]).astype(bf16)


def third_back_body(core, x, g0, g1, g2, cot, gain, mine, other, grad, low, mixed, sums, w, sem):
    fetch_windows(core, mine, other, w, sem)
    g = g0[...].astype(f32) + g1[...].astype(f32) + g2[...].astype(f32)
    back, both = norm_back(x[...], g, gain[...])
    total = cot[...] + back
    grad[...] = total
    low[...] = total.astype(bf16)
    mixed[...] = dot_nt(total.astype(bf16), w[...]).astype(bf16)
    sums[...] = jnp.concatenate(both + [jnp.zeros((6, D), f32)], axis=0)


def second_back_body(core, x, gq, before, gain, mine, other, grad, low, mixed, sums, w1, w2, sem):
    fetch_pair(core, mine, other, w1, w2, sem)
    back, both = norm_back(x[...], dot_nt(gq[...], w2[...]), gain[...])
    total = before[...] + back
    grad[...] = total
    low[...] = total.astype(bf16)
    mixed[...] = dot_nt(total.astype(bf16), w1[...]).astype(bf16)
    sums[...] = jnp.concatenate(both + [jnp.zeros((6, D), f32)], axis=0)


def first_back_body(x, *refs):
    before, gain, grad = refs[SPLIT:]
    size = TOK // SPLIT
    sums = []
    for parts in refs[:SPLIT]:
        g = parts[:size, :].astype(f32)
        for k in range(1, 8):
            g = g + parts[size * k : size * (k + 1), :].astype(f32)
        sums.append(g)
    g = jnp.concatenate(sums, axis=0)
    grad[...] = before[...] + norm_back(x[...].astype(f32), g, gain[...])[0]


def text_back_body(
    core, kv, cols, text, w_text, mine, other, part, grad_text, grad_kv, w1, w2, sem
):
    fetch_pair(core, mine, other, w1, w2, sem, D)
    low = (dot_nt(kv[:, :D], w1[...]) + dot_nt(kv[:, D:], w2[...])).astype(bf16)
    part[...] = dot_nt(low, w_text[...]).astype(bf16)
    grad_text[...] = dot_tn(text[...], low).astype(bf16)
    grad_kv[...] = dot_tn(cols[...], kv[...]).astype(bf16)


def first_part_body(g, w, plain, *refs):
    rows = dot_nt(g[...], w[...])
    sums = refs[-1]
    size = TOK // SPLIT
    for k in range(SPLIT):
        refs[k][...] = rows[size * k : size * (k + 1)].astype(bf16)
    both = [
        jnp.sum(rows * plain[...].astype(f32), axis=0, keepdims=True),
        jnp.sum(rows, axis=0, keepdims=True),
        jnp.zeros((6, D), f32),
    ]
    both = jnp.concatenate(both, axis=0)

    @pl.when(pl.program_id(0) == 0)
    def _():
        sums[...] = both

    @pl.when(pl.program_id(0) != 0)
    def _():
        sums[...] += both


def first_part(g, w, plain):
    return pl.pallas_call(
        first_part_body,
        grid=(ROW // TOK,),
        in_specs=[
            pl.BlockSpec((TOK, 6 * SLOT), lambda i: (i, 0)),
            pl.BlockSpec((D, 6 * SLOT), lambda i: (0, 0)),
            pl.BlockSpec((TOK, D), lambda i: (i, 0)),
        ],
        out_specs=[
            *[pl.BlockSpec((TOK // SPLIT, D), lambda i: (i, 0))] * SPLIT,
            pl.BlockSpec((8, D), lambda i: (0, 0)),
        ],
        out_shape=[jax.ShapeDtypeStruct((ROW // SPLIT, D), bf16)] * SPLIT
        + [jax.ShapeDtypeStruct((8, D), f32)],
        cost_estimate=cost(11),
        compiler_params=params(),
    )(g, w, plain)


def heads_grad_body(x, g, out):
    grad = dot_tn(x[...], g[...]).astype(bf16)
    out[...] = jnp.concatenate(
        [
            grad[:, SLOT * (3 * h + k) : SLOT * (3 * h + k) + HEAD]
            for k in range(3)
            for h in range(2)
        ],
        axis=1,
    )


def heads_grad(x, g):
    return pl.pallas_call(
        heads_grad_body,
        grid=(3,),
        in_specs=[
            pl.BlockSpec((ROW, 384), lambda i: (0, i)),
            pl.BlockSpec((ROW, 6 * SLOT), lambda i: (0, 0)),
        ],
        out_specs=pl.BlockSpec((384, 3 * SHARD), lambda i: (i, 0)),
        out_shape=jax.ShapeDtypeStruct((D, 3 * SHARD), bf16),
        cost_estimate=cost(8),
        compiler_params=params(),
    )(x, g)


def unpack_heads_body(x, out):
    for k in range(3):
        out[SHARD * k : SHARD * (k + 1), :] = jnp.concatenate(
            [x[SHARD * p : SHARD * (p + 1), SHARD * k : SHARD * (k + 1)] for p in range(8)], axis=1
        )


def unpack_heads(x):
    return pl.pallas_call(
        unpack_heads_body,
        out_shape=jax.ShapeDtypeStruct((3 * SHARD, D), bf16),
        compiler_params=params(),
    )(x)


def row_block(x, index, rows):
    return lax.dynamic_slice_in_dim(x, index * rows, rows, axis=0)


def core_window(x, core):
    return lax.dynamic_slice_in_dim(x, core * STEP, WIN, axis=1)


def both_cores(x):
    return jnp.concatenate([x, shift(x, "c", 1)], axis=0)


def window_grad(left, right):
    core = lax.axis_index("c")
    sent = shift(core_window(right, 1 - core), "c", 1)
    rights = jnp.concatenate([core_window(right, core), sent], axis=0)
    return dot_tn(both_cores(left), rights).astype(bf16)


def sum_over(x, *axes):
    for axis in axes:
        n = lax.axis_size(axis)
        x = sum([shift(x, axis, k) for k in range(1, n)], x)
    return x


def local(
    tokens,
    text_states,
    seg_lengths,
    caption_of_segment,
    text_lengths,
    ln1_gain,
    ln1_bias,
    w_query,
    w_key,
    w_value,
    w_out,
    ln2_gain,
    ln2_bias,
    c_query,
    w_text,
    c_key,
    c_value,
    c_out,
    ln3_gain,
    ln3_bias,
    w_up,
    w_down,
    cotangent,
):
    core = lax.axis_index("c")
    first_core = core == 0
    core_index = core.astype(jnp.int32)[None]
    quarter = lax.axis_index("z")
    first_row = peer(0, 0) * TOK

    ends = jnp.cumsum(seg_lengths[0])
    positions = jnp.arange(ROW, dtype=jnp.int32)
    segment = jnp.sum((positions[:, None] >= ends[None, :]).astype(jnp.int32), axis=1)
    own_segment = lax.dynamic_slice_in_dim(segment, first_row, TOK)
    text_row = jnp.arange(TXT, dtype=jnp.int32)
    text_pos = text_row // TXT_OWN * CAP_TOK + text_row % TXT_OWN
    text_caption = text_pos // CAP_LEN
    live = jnp.sum(
        jnp.where(
            text_caption[:, None] == jnp.arange(CAPS, dtype=jnp.int32)[None, :],
            text_lengths[0][None, :],
            0,
        ),
        axis=1,
    )
    query_caption = jnp.sum(
        jnp.where(
            own_segment[:, None] == jnp.arange(SEGS, dtype=jnp.int32)[None, :],
            caption_of_segment[0][None, :],
            0,
        ),
        axis=1,
    )
    text_live = (text_row % TXT_OWN < CAP_TOK) & (text_pos % CAP_LEN < live)
    text_key = jnp.where(text_live, text_caption, -1)

    def row(x):
        return x[None, :]

    gap = jnp.zeros((SHARD, 128), bf16)
    square_pack = jnp.where(
        first_core,
        jnp.concatenate([w_out, c_key, c_out[:, :WIN], gap], axis=1),
        jnp.concatenate([c_query, c_value, c_out[:, STEP:], gap], axis=1),
    )
    square_pack = lax.dynamic_slice_in_dim(square_pack, quarter * QUARTER, QUARTER, axis=1)
    quarter_own = lax.all_gather(square_pack, FS, axis=0, tiled=True)

    rows_in = tokens[0]
    plain = normalize(rows_in.astype(f32))[0].astype(bf16)
    n01, n10, n30 = gather_first(plain)

    heads_pack = pack_heads(after(w_query, plain), w_key, w_value)
    n01, n10, n30, heads_pack = lax.optimization_barrier((n01, n10, n30, heads_pack))
    heads_w = peers_parts(heads_pack)
    n31, n20, n11 = gather_second(n01, n10)

    n31, n20, n11 = lax.optimization_barrier((n31, n20, n11))
    n21 = gather_third(n31, n11)
    plain_all, normed_all = place_rows(
        plain,
        (n01, n10, n30),
        (n31, n20, n11),
        n21,
        row(ln1_gain),
        row(ln1_bias),
    )
    heads_w = spread_heads(heads_w)
    quarter_own, normed_all, heads_w = lax.optimization_barrier((quarter_own, normed_all, heads_w))
    quarter_minus, quarter_plus = shift(quarter_own, "z", 1), shift(quarter_own, "z", -1)

    text_own = jnp.pad(after(text_states[0], normed_all), ((0, TXT_OWN - CAP_TOK), (0, 0)))
    text_columns = lax.all_to_all(text_own, FS, split_axis=1, concat_axis=0, tiled=True)

    up_own = jnp.concatenate(
        [
            lax.dynamic_slice(w_up, (0, 4 * SHARD * k + SHARD * quarter), (SHARD, SHARD))
            for k in range(8)
        ],
        axis=1,
    )
    hidden_own = jnp.where(first_core, up_own, row_block(w_down, quarter, SHARD))

    seg_col, seg_row = segment[:, None], segment[None, :]
    qkv = dot_nn(normed_all, heads_w).astype(bf16)
    text_columns, qkv = lax.optimization_barrier((text_columns, qkv))
    context_part = dot_nn(text_columns, w_text).astype(bf16)
    context_own = lax.psum_scatter(context_part, FS, scatter_dimension=0, tiled=True)
    head0, total0 = self_forward(0, seg_col, seg_row, after(qkv, context_part))
    head1, total1 = self_forward(1, seg_col, seg_row, after(qkv, head0))
    hidden_mine = every_peer(after(hidden_own, text_columns))
    quarter_minus, quarter_plus, hidden_mine, head1 = lax.optimization_barrier(
        (quarter_minus, quarter_plus, hidden_mine, head1)
    )
    quarter_far = (
        shift(halves(quarter_minus)[0], "z", 1),
        shift(halves(quarter_plus)[1], "z", -1),
    )
    attended = lax.all_to_all(
        jnp.concatenate([head0, head1], axis=1), FS, split_axis=0, concat_axis=1, tiled=True
    )
    attended, context_own, *quarter_far = lax.optimization_barrier(
        (attended, context_own, *quarter_far)
    )
    context = every_peer(context_own)
    square_mine = place_quarters(quarter_own, quarter_minus, quarter_plus, *quarter_far)
    square_other = shift(square_mine, "c", 1)
    grad_out = cotangent[0]
    grad_mlp = grad_out.astype(bf16)
    grad_sent = after(grad_mlp, square_mine)
    mlp_minus, mlp_plus = shift(grad_sent, "z", 1), shift(grad_sent, "z", -1)

    after_self, normed_two, cross_query = call(
        after_self_body,
        [
            (core_index, "smem"), (rows_in, "vmem"), (attended, "vmem"),
            (row(ln2_gain), "vmem"), (row(ln2_bias), "vmem"),
            (square_mine, "hbm"), (square_other, "hbm"),
        ],
        [((TOK, D), f32), ((TOK, D), bf16), ((TOK, D), bf16)],
        square_scratch(2),
    )
    cross_key, cross_value = call(
        text_keys_body,
        [
            (core_index, "smem"), (after(context, cross_query, mlp_minus, mlp_plus), "vmem"),
            (square_mine, "hbm"), (square_other, "hbm"),
        ],
        [((TXT, D), bf16), ((TXT, D), bf16)],
        square_scratch(2),
    )
    cross_mixed = cross_forward(
        query_caption[:, None], text_key[None, :], cross_query, cross_key, cross_value
    )
    hidden_mine = after(hidden_mine, cross_mixed)
    weights = (hidden_mine, shift(hidden_mine, "c", 1))
    after_cross, normed_three = call(
        after_cross_body,
        [
            (core_index, "smem"), (after_self, "vmem"), (cross_mixed, "vmem"),
            (row(ln3_gain), "vmem"), (row(ln3_bias), "vmem"),
            (square_mine, "hbm"), (square_other, "hbm"),
        ],
        [((TOK, D), f32), ((TOK, D), bf16)],
        square_scratch(1),
    )

    mlp_sent = lax.optimization_barrier((mlp_minus, mlp_plus, cross_query))
    mlp_far = (
        shift(halves(mlp_sent[0])[0], "z", 1),
        shift(halves(mlp_sent[1])[1], "z", -1),
    )

    three_minus, three_plus = shift(normed_three, "z", 1), shift(normed_three, "z", -1)
    out_own, act_own, pre_own, back_own = mlp(core_index, (normed_three,), (grad_mlp,), *weights)
    three_minus, three_plus, out_own = lax.optimization_barrier(
        (three_minus, three_plus, out_own)
    )
    three_far = (
        shift(halves(three_minus)[0], "z", 1),
        shift(halves(three_plus)[1], "z", -1),
    )
    near = mlp(core_index, (three_minus, three_plus), (mlp_minus, mlp_plus), *weights)
    out_m, act_m, pre_m, back_m, out_p, act_p, pre_p, back_p = near
    *three_far, out_m = lax.optimization_barrier((*three_far, out_m))
    out_far, act_far, pre_far, back_far = mlp(core_index, three_far, mlp_far, *weights)
    back_minus, back_plus = reduce_z(back_far, back_m, back_p)
    three_parts = (normed_three, three_minus, three_plus, jnp.concatenate(three_far, axis=0))
    pre_parts = (pre_own, pre_m, pre_p, pre_far)
    act_parts = (act_own, act_m, act_p, act_far)
    mlp_parts = (grad_mlp, mlp_minus, mlp_plus, jnp.concatenate(mlp_far, axis=0))
    send = mlp_grad(1, core_index, three_parts, pre_parts, act_parts, mlp_parts)
    back_minus, back_plus, send = lax.optimization_barrier((back_minus, back_plus, send))
    back_minus, back_plus = shift(back_minus, "z", -1), shift(back_plus, "z", 1)
    keep = mlp_grad(
        0, core_index, three_parts, pre_parts, act_parts, (after(grad_mlp, send), *mlp_parts[1:])
    )
    back_minus, back_plus, keep = lax.optimization_barrier((back_minus, back_plus, keep))
    hidden_sum = keep + shift(send, "c", 1)
    grad_after_cross, grad_cross_branch, grad_cross_mixed, sums_three = call(
        third_back_body,
        [
            (core_index, "smem"), (after_cross, "vmem"), (back_own, "vmem"),
            (back_minus, "vmem"), (back_plus, "vmem"), (grad_out, "vmem"),
            (after(row(ln3_gain), hidden_sum), "vmem"), (square_mine, "hbm"), (square_other, "hbm"),
        ],
        [((TOK, D), f32), ((TOK, D), bf16), ((TOK, D), bf16), ((8, D), f32)],
        square_scratch(1),
    )

    grad_cquery_rows, grad_kv = cross_backward(
        text_key[:, None],
        query_caption[None, :],
        cross_query,
        cross_key,
        cross_value,
        grad_cross_mixed,
    )
    kv_own = lax.psum_scatter(grad_kv, FS, scatter_dimension=0, tiled=True)
    grad_after_self, grad_self_branch, grad_attended, sums_two = call(
        second_back_body,
        [
            (core_index, "smem"), (after_self, "vmem"), (grad_cquery_rows, "vmem"),
            (grad_after_cross, "vmem"), (row(ln2_gain), "vmem"),
            (square_mine, "hbm"), (square_other, "hbm"),
        ],
        [((TOK, D), f32), ((TOK, D), bf16), ((TOK, D), bf16), ((8, D), f32)],
        square_scratch(2),
    )
    grad_heads = lax.all_to_all(grad_attended, FS, split_axis=1, concat_axis=0, tiled=True)

    square = jnp.concatenate(
        [
            window_grad(cross_mixed, after(grad_cross_branch, grad_attended)),
            window_grad(normed_two, after(grad_cquery_rows, grad_attended)),
            window_grad(attended, grad_self_branch),
        ],
        axis=1,
    )

    def square_chunk(dy, dx):
        return row_block(square, peer(dy, dx), SHARD)

    grad_heads, square = lax.optimization_barrier((grad_heads, square))
    grad_qkv = self_backward(0, seg_col, seg_row, total0, qkv, grad_heads)
    kv_own, square, grad_qkv = lax.optimization_barrier((kv_own, square, grad_qkv))
    s_lo, s_hi, s20 = reduce_first(square_chunk)
    kv_all = every_peer(kv_own)
    hidden_grad = lax.psum_scatter(after(hidden_sum, kv_own), FS, scatter_dimension=0, tiled=True)
    out_minus, out_plus = reduce_z(after(out_far, grad_qkv), out_m, out_p)
    grad_qkv = self_backward(
        1, seg_col, seg_row, total1, qkv, after(grad_heads, kv_own), (grad_qkv,)
    )
    s_lo, s_hi, s20, out_minus, out_plus, grad_qkv = lax.optimization_barrier(
        (s_lo, s_hi, s20, out_minus, out_plus, grad_qkv)
    )
    s11, s31 = reduce_second(square_chunk, s_lo, s_hi)

    heads_own = heads_grad(normed_all, grad_qkv)
    heads_own, s11, s31, kv_all = lax.optimization_barrier((heads_own, s11, s31, kv_all))
    heads_part = peers_parts(heads_own)
    square_parts = reduce_third(square_chunk, s20, s11, s31)
    part, sums_one = first_part(after(grad_qkv, heads_own), heads_w, plain_all)
    part, heads_part, kv_all, hidden_grad, *square_parts = lax.optimization_barrier(
        (part, heads_part, kv_all, hidden_grad, *square_parts)
    )
    sent = peers_parts(part)

    square = reduce_last(square_chunk, *square_parts).astype(bf16)
    heads_rows = unpack_heads(heads_part)
    early = row_block(heads_rows, core, 216) + shift(row_block(heads_rows, 1 - core, 216), "c", 1)
    early = jnp.concatenate([early, jnp.zeros((256 - 216, D), bf16)], axis=0)
    square = jnp.concatenate([square[:, WIN * k : WIN * (k + 1)] for k in range(3)], axis=0)
    square = jnp.concatenate([square[:216], square[216:]], axis=1)
    early = jnp.concatenate(
        [early, jnp.concatenate([square, jnp.zeros((256 - 216, 2 * WIN), bf16)], axis=0)], axis=1
    )
    early = lax.psum_scatter(early, "z", scatter_dimension=0, tiled=True)
    norms = jnp.concatenate([sums_one[:2], sums_two[:2], sums_three[:2], jnp.zeros((2, D), f32)])
    norms = sum_over(norms, "z", "c")
    own_columns = lax.dynamic_slice_in_dim(context, peer(0, 0) * SHARD, SHARD, axis=1)
    text_part, grad_w_text, grad_w_kv = call(
        text_back_body,
        [
            (core_index, "smem"), (kv_all, "vmem"), (own_columns, "vmem"),
            (text_columns, "vmem"), (w_text, "vmem"),
            (square_mine, "hbm"), (square_other, "hbm"),
        ],
        [((TXT, TXT), bf16), ((TXT, D), bf16), ((SHARD, 2 * D), bf16)],
        square_scratch(2),
    )

    def half(which):
        kv = jnp.where(which == 0, grad_w_kv[:, :D], grad_w_kv[:, D:])
        return jnp.concatenate(
            [row_block(grad_w_text, which, 256), kv, jnp.zeros((448 - 400, D), bf16)], axis=0
        )

    late = half(core) + shift(half(1 - core), "c", 1)
    late = lax.psum_scatter(late, "z", scatter_dimension=0, tiled=True)
    hidden_grad = after(hidden_grad, part)
    hidden_grad = hidden_grad + shift(hidden_grad, "xh", 1)
    part, norms, late = lax.optimization_barrier((sent, norms, late))
    early = after(early, part)
    early = early + shift(early, "xh", 1)
    hidden_grad = in_order(*neighbours(after(hidden_grad, part)))
    grad_w_up, grad_w_down = sort_hidden(core_index, hidden_grad, shift(hidden_grad, "c", 1))

    norms = sum_over(norms, "y", "xl", "xh")
    late = late + shift(late, "xh", 1)
    early = in_order(*neighbours(early))
    late = in_order(*neighbours(late))

    def by_core(x):
        other = shift(x, "c", 1)
        low, high = jnp.where(first_core, x, other), jnp.where(first_core, other, x)
        return low.astype(f32), high.astype(f32)

    low, high = by_core(early)
    grad_w_query = low[:144, :D]
    grad_w_key = jnp.concatenate([low[144:216, :D], high[:72, :D]], axis=0)
    grad_w_value = high[72:216, :D]
    low = jnp.concatenate([low[:216, D : D + WIN], low[:216, D + WIN :]], axis=0)
    high = jnp.concatenate([high[:216, D : D + WIN], high[:216, D + WIN :]], axis=0)
    grad_c_out, grad_c_query, grad_w_out = (
        jnp.concatenate(
            [low[SHARD * k : SHARD * (k + 1)], high[SHARD * k : SHARD * (k + 1), 128:]], axis=1
        )
        for k in range(3)
    )
    low, high = by_core(late)
    grad_w_text = jnp.concatenate([low[:256], high[:256]], axis=0)
    grad_c_key, grad_c_value = low[256:400], high[256:400]
    out_minus, out_plus = shift(out_minus, "z", -1), shift(out_plus, "z", 1)
    outputs = (
        after_cross + out_own.astype(f32) + out_minus.astype(f32) + out_plus.astype(f32)
    )

    grad_tokens = call(
        first_back_body,
        [
            (rows_in, "vmem"), (part, "vmem"), (grad_after_self, "vmem"),
            (row(ln1_gain), "vmem"),
        ],
        [((TOK, D), f32)],
        [],
    )[0]
    grad_text = lax.all_to_all(
        after(text_part, part), FS, split_axis=0, concat_axis=1, tiled=True
    )
    grad_text = grad_text[:CAP_TOK].astype(f32)
    return (
        outputs[None],
        grad_tokens[None],
        grad_text[None],
        norms[0],
        norms[1],
        grad_w_query,
        grad_w_key,
        grad_w_value,
        grad_w_out,
        norms[2],
        norms[3],
        grad_c_query,
        grad_w_text,
        grad_c_key,
        grad_c_value,
        grad_c_out,
        norms[4],
        norms[5],
        grad_w_up,
        grad_w_down,
    )


def solution(mesh):
    split = Mesh(mesh.devices.reshape(2, 4, 2, 4, 2), ("xh", "z", "c", "y", "xl"))
    dp = ("xh", "z", "c")
    rows = P(dp, FS, None)
    per_row = P(dp, None)
    weight = P(FS, None)
    rep = P()
    in_specs = (
        rows, rows, per_row, per_row, per_row,
        rep, rep, weight, weight, weight, weight,
        rep, rep, weight, weight, weight, weight, weight,
        rep, rep, weight, weight, rows,
    )
    out_specs = (
        rows, rows, rows,
        rep, rep, weight, weight, weight, weight,
        rep, rep, weight, weight, weight, weight, weight,
        rep, rep, weight, weight,
    )
    return jax.shard_map(
        local, mesh=split, in_specs=in_specs, out_specs=out_specs, check_vma=False
    )
```

```python
import functools

import jax
import jax.numpy as jnp
from jax import lax
from jax.experimental import pallas as pl
from jax.experimental.pallas import tpu as pltpu
from jax.sharding import Mesh
from jax.sharding import PartitionSpec as P

HEADS = 16
HEAD = 72
D = 1152
FF = 4608
CAP_TOK = 60
TXT_OWN = 64
TXT = 8 * TXT_OWN
TOK = 256
ROW = 2048
CAP_LEN = 120
SEGS = 3
CAPS = 4
SHARD = 144
SLOT = 128
SPLIT = 1
WIN = 640
STEP = 512

bf16 = jnp.bfloat16
f32 = jnp.float32
norm_eps = 1e-06
masked_score = -1e30
scale = HEAD ** (-0.5)
log2e = 1.4426950408889634
FS = ("y", "xl")
VMEM = 60 * 1024 * 1024


def dot_nn(a, b):
    return lax.dot_general(a, b, (((1,), (0,)), ((), ())), preferred_element_type=f32)


def dot_nt(a, b):
    return lax.dot_general(a, b, (((1,), (1,)), ((), ())), preferred_element_type=f32)


def dot_tn(a, b):
    return lax.dot_general(a, b, (((0,), (0,)), ((), ())), preferred_element_type=f32)


def params():
    return pltpu.CompilerParams(vmem_limit_bytes=VMEM)


def cost(micros):
    return pl.CostEstimate(flops=int(micros * 1.15e9), bytes_accessed=0, transcendentals=0)


def shift(x, axis, by):
    n = lax.axis_size(axis)
    return lax.ppermute(x, axis, [(i, (i + by) % n) for i in range(n)])


def halves(x):
    h = (x.shape[0] // 2 + 15) // 16 * 16
    return x[:h], x[h:]


def after(x, *others):
    return lax.optimization_barrier((x, *others))[0]


def gather_first(x):
    return shift(x, "xl", 1), shift(x, "y", -1), shift(x, "y", 1)


def gather_second(x01, x10):
    return shift(x01, "y", 1), shift(x10, "y", -1), shift(x10, "xl", 1)


def gather_third(x31, x11):
    return shift(halves(x11)[0], "y", -1), shift(halves(x31)[1], "y", 1)


NEAR = ((0, 0), (0, 1), (1, 0), (3, 0))
NEXT = ((3, 1), (2, 0), (1, 1))
LAST = (2, 1)


def reduce_first(chunk):
    lo, hi = halves(chunk(2, 1))
    return shift(lo, "y", 1), shift(hi, "y", -1), shift(chunk(2, 0), "y", 1)


def reduce_second(chunk, lo, hi):
    h = lo.shape[0]
    c11, c31 = chunk(1, 1), chunk(3, 1)
    c11 = jnp.concatenate([c11[:h] + lo, c11[h:]], axis=0)
    c31 = jnp.concatenate([c31[:h], c31[h:] + hi], axis=0)
    return shift(c11, "xl", 1), shift(c31, "y", -1)


def reduce_third(chunk, c20, c11, c31):
    return (
        shift(chunk(1, 0) + c20 + c11, "y", 1),
        shift(chunk(0, 1) + c31, "xl", 1),
        shift(chunk(3, 0), "y", -1),
    )


def reduce_last(chunk, *parts):
    return sum([p.astype(f32) for p in parts], chunk(0, 0).astype(f32))


def every_peer(x, axes=FS):
    n = lax.axis_size(axes)
    copies = jnp.broadcast_to(x[None], (n, *x.shape)).reshape(n * x.shape[0], x.shape[1])
    return lax.all_to_all(copies, axes, 0, 0, tiled=True)


def peers_parts(x, axes=FS):
    return lax.all_to_all(x, axes, 0, 0, tiled=True)


def sum_parts(parts):
    return jnp.sum(parts.reshape(8, -1, parts.shape[1]).astype(f32), axis=0)


def neighbours(x):
    return x, shift(x, "z", 1), shift(x, "z", 2), shift(x, "z", -1)


def in_order(*around):
    rows, cols = around[0].shape

    def body(where, *refs):
        ins, out = refs[:4], refs[4]
        for k in range(4):
            row = pl.multiple_of(lax.rem(where[0] + 4 - k, 4) * rows, 16)
            out[pl.ds(row, rows), :] = ins[k][...]

    vmem = pl.BlockSpec(memory_space=pltpu.VMEM)
    return pl.pallas_call(
        body,
        in_specs=[pl.BlockSpec(memory_space=pltpu.SMEM)] + [vmem] * 4,
        out_specs=vmem,
        out_shape=jax.ShapeDtypeStruct((4 * rows, cols), bf16),
        compiler_params=params(),
    )(lax.axis_index("z").astype(jnp.int32)[None], *around)


def reduce_z(far, minus, plus):
    lo, hi = halves(far)
    lo, hi = shift(lo, "z", -1), shift(hi, "z", 1)
    h = lo.shape[0]
    return (
        jnp.concatenate([minus[:h] + lo, minus[h:]], axis=0),
        jnp.concatenate([plus[:h], plus[h:] + hi], axis=0),
    )


def peer(dy, dx):
    return ((lax.axis_index("y") + dy) % 4) * 2 + (lax.axis_index("xl") ^ dx)


def place_rows(own, first, second, third, gain, bias):
    lo = third[0].shape[0]
    rows, cols = own.shape
    pieces = [(x, p, 0) for x, p in zip((own, *first), NEAR)]
    pieces += [(x, p, 0) for x, p in zip(second, NEXT)]
    pieces += [(third[0], LAST, 0), (third[1], LAST, lo)]
    count = len(pieces)

    def body(where, gain, bias, *refs):
        ins, plain, normed, sem = refs[:count], refs[count], refs[count + 1], refs[-1]
        started = []
        for k, (x, _, off) in enumerate(pieces):
            row = pl.multiple_of(where[k] * rows + off, 16)
            one = pltpu.make_async_copy(ins[k], plain.at[pl.ds(row, x.shape[0])], sem.at[k])
            one.start()
            started.append(one)
        for one in started:
            one.wait()

        def step(i, carry):
            part = pl.ds(pl.multiple_of(i * rows, rows), rows)
            normed[part, :] = (plain[part, :].astype(f32) * gain[...] + bias[...]).astype(bf16)
            return carry

        lax.fori_loop(0, 8, step, 0)

    vmem = pl.BlockSpec(memory_space=pltpu.VMEM)
    return pl.pallas_call(
        body,
        in_specs=[pl.BlockSpec(memory_space=pltpu.SMEM), vmem, vmem]
        + [pl.BlockSpec(memory_space=pl.ANY)] * count,
        out_specs=[vmem, vmem],
        out_shape=[jax.ShapeDtypeStruct((8 * rows, cols), bf16)] * 2,
        scratch_shapes=[pltpu.SemaphoreType.DMA((count,))],
        compiler_params=params(),
    )(
        jnp.stack([peer(*p) for _, p, _ in pieces]).astype(jnp.int32),
        gain,
        bias,
        *[x for x, _, _ in pieces],
    )


QUARTER = 768


def place_quarters(*quarters):
    def body(where, own, minus, plus, far_lo, far_hi, out, sem):
        started = []
        half = far_lo.shape[0]
        for k, (ref, turn, row) in enumerate(
            ((own, 0, 0), (minus, 3, 0), (plus, 1, 0), (far_lo, 2, 0), (far_hi, 2, half))
        ):
            column = pl.multiple_of(lax.rem(where[0] + turn, 4) * QUARTER, 128)
            one = pltpu.make_async_copy(
                ref, out.at[pl.ds(row, ref.shape[0]), pl.ds(column, QUARTER)], sem.at[k]
            )
            one.start()
            started.append(one)
        for one in started:
            one.wait()

    return pl.pallas_call(
        body,
        in_specs=[pl.BlockSpec(memory_space=pltpu.SMEM)] + [pl.BlockSpec(memory_space=pl.ANY)] * 5,
        out_specs=pl.BlockSpec(memory_space=pltpu.VMEM),
        out_shape=jax.ShapeDtypeStruct((D, 4 * QUARTER), bf16),
        scratch_shapes=[pltpu.SemaphoreType.DMA((5,))],
        compiler_params=params(),
    )(lax.axis_index("z").astype(jnp.int32)[None], *quarters)


def pack_heads_body(wq, wk, wv, out):
    for p in range(8):
        rows = slice(SHARD * p, SHARD * (p + 1))
        out[rows, :] = jnp.concatenate([w[:, rows] for w in (wq, wk, wv)], axis=1)


def pack_heads(*weights):
    return pl.pallas_call(
        pack_heads_body,
        out_shape=jax.ShapeDtypeStruct((D, 3 * SHARD), bf16),
        compiler_params=params(),
    )(*weights)


def spread_heads_body(x, out):
    blank = jnp.zeros((D, SLOT - HEAD), bf16)
    for h in range(2):
        for k in range(3):
            first = SHARD * k + HEAD * h
            slot = SLOT * (3 * h + k)
            out[:, slot : slot + SLOT] = jnp.concatenate(
                [x[:, first : first + HEAD], blank], axis=1
            )


def spread_heads(x):
    return pl.pallas_call(
        spread_heads_body,
        out_shape=jax.ShapeDtypeStruct((D, 6 * SLOT), bf16),
        compiler_params=params(),
    )(x)


def self_forward_body(seg_q, seg_k, q, kv, out, total):
    s = dot_nt(q[:, :SLOT], kv[:, SLOT : 2 * SLOT])
    s = jnp.where(seg_q[...] == seg_k[...], s, masked_score)
    top = jnp.max(s, axis=1, keepdims=True)
    p = jnp.exp2((s - top) * (scale * log2e))
    mass = jnp.sum(p, axis=1, keepdims=True)
    out[...] = (dot_nn(p.astype(bf16), kv[:, 2 * SLOT :]) / mass)[:, :HEAD].astype(bf16)
    log_total = top * (scale * log2e) + jnp.log2(mass)
    total[...] = jnp.transpose(jnp.broadcast_to(log_total, (TOK, SLOT)))[0:1, :]


def self_forward(head, seg_q, seg_k, qkv):
    return pl.pallas_call(
        self_forward_body,
        grid=(ROW // TOK,),
        in_specs=[
            pl.BlockSpec((TOK, 1), lambda i: (i, 0)),
            pl.BlockSpec((1, ROW), lambda i: (0, 0)),
            pl.BlockSpec((TOK, 3 * SLOT), lambda i: (i, head)),
            pl.BlockSpec((ROW, 3 * SLOT), lambda i: (0, head)),
        ],
        out_specs=[
            pl.BlockSpec((TOK, HEAD), lambda i: (i, 0)),
            pl.BlockSpec((1, TOK), lambda i: (0, i)),
        ],
        out_shape=[
            jax.ShapeDtypeStruct((ROW, HEAD), bf16),
            jax.ShapeDtypeStruct((1, ROW), f32),
        ],
        compiler_params=params(),
    )(seg_q, seg_k, qkv, qkv)


def self_backward_body(head, seg_k, seg_q, total, q, kv, g, *refs):
    grad, key_sum, value_sum, key_t = refs[-4:]
    i = pl.program_id(0)

    @pl.when(i == 0)
    def _():
        key_sum[...] = jnp.zeros_like(key_sum)
        value_sum[...] = jnp.zeros_like(value_sum)
        key_t[...] = jnp.transpose(kv[:, SLOT : 2 * SLOT])

    rows = pl.ds(pl.multiple_of(i * TOK, TOK), TOK)
    q_h, k_h, v_h = q[:, :SLOT], kv[:, SLOT : 2 * SLOT], kv[:, 2 * SLOT :]
    g_both = g[...]
    g_h = jnp.concatenate(
        [g_both[:, HEAD * head : HEAD * (head + 1)], jnp.zeros((TOK, SLOT - HEAD), bf16)], axis=1
    )
    p = jnp.exp2(dot_nt(k_h, q_h) * (scale * log2e) - total[...])
    p = jnp.where(seg_k[...] == seg_q[...], p, 0.0)
    dp = dot_nt(v_h, g_h)
    ds = (p * (dp - jnp.sum(p * dp, axis=0, keepdims=True))).astype(bf16)
    value_sum[...] += dot_nn(p.astype(bf16), g_h)
    key_sum[...] += dot_nn(ds, q_h)
    grad[rows, :SLOT] = (jnp.transpose(dot_nn(key_t[...], ds)) * scale).astype(bf16)

    @pl.when(i == pl.num_programs(0) - 1)
    def _():
        grad[:, SLOT : 2 * SLOT] = (key_sum[...] * scale).astype(bf16)
        grad[:, 2 * SLOT :] = value_sum[...].astype(bf16)


def self_backward(head, seg_k, seg_q, total, qkv, g, before=()):
    return pl.pallas_call(
        functools.partial(self_backward_body, head),
        grid=(ROW // TOK,),
        in_specs=[
            pl.BlockSpec((ROW, 1), lambda i: (0, 0)),
            pl.BlockSpec((1, TOK), lambda i: (0, i)),
            pl.BlockSpec((1, TOK), lambda i: (0, i)),
            pl.BlockSpec((TOK, 3 * SLOT), lambda i: (i, head)),
            pl.BlockSpec((ROW, 3 * SLOT), lambda i: (0, head)),
            pl.BlockSpec((TOK, SHARD), lambda i: (i, 0)),
        ]
        + [pl.BlockSpec(memory_space=pl.ANY)] * len(before),
        out_specs=pl.BlockSpec((ROW, 3 * SLOT), lambda i: (0, head)),
        out_shape=jax.ShapeDtypeStruct((ROW, 6 * SLOT), bf16),
        input_output_aliases={6: 0} if before else {},
        scratch_shapes=[
            pltpu.VMEM((ROW, SLOT), f32),
            pltpu.VMEM((ROW, SLOT), f32),
            pltpu.VMEM((SLOT, ROW), bf16),
        ],
        compiler_params=params(),
    )(seg_k, seg_q, total, qkv, qkv, g, *before)


def cross_forward_body(cap_q, cap_t, q, k, v, out):
    allowed = cap_q[...] == cap_t[...]
    mixed = []
    for h in range(HEADS):
        a, b = HEAD * h, HEAD * (h + 1)
        s = dot_nt(q[:, a:b], k[:, a:b])
        s = jnp.where(allowed, s, masked_score)
        top = jnp.max(s, axis=1, keepdims=True)
        p = jnp.exp2((s - top) * (scale * log2e))
        mass = jnp.sum(p, axis=1, keepdims=True)
        mixed.append(dot_nn(p.astype(bf16), v[:, a:b]) / mass)
    out[...] = jnp.concatenate(mixed, axis=1).astype(bf16)


def cross_forward(cap_q, cap_t, q, k, v):
    return pl.pallas_call(
        cross_forward_body,
        out_shape=jax.ShapeDtypeStruct((TOK, D), bf16),
        compiler_params=params(),
    )(cap_q, cap_t, q, k, v)


def cross_backward_body(cap_t, cap_q, q, k, v, g, grad_q, grad_kv):
    allowed = cap_t[...] == cap_q[...]
    dq, dk, dv = [], [], []
    for h in range(HEADS):
        a, b = HEAD * h, HEAD * (h + 1)
        q_h, k_h, v_h, g_h = q[:, a:b], k[:, a:b], v[:, a:b], g[:, a:b]
        s = jnp.where(allowed, dot_nt(k_h, q_h), masked_score)
        top = jnp.max(s, axis=0, keepdims=True)
        p = jnp.exp2((s - top) * (scale * log2e))
        p = p / jnp.sum(p, axis=0, keepdims=True)
        dp = dot_nt(v_h, g_h)
        ds = (p * (dp - jnp.sum(p * dp, axis=0, keepdims=True))).astype(bf16)
        dv.append(dot_nn(p.astype(bf16), g_h))
        dk.append(dot_nn(ds, q_h) * scale)
        dq.append(dot_tn(ds, k_h) * scale)
    grad_q[...] = jnp.concatenate(dq, axis=1).astype(bf16)
    grad_kv[:, :D] = jnp.concatenate(dk, axis=1).astype(bf16)
    grad_kv[:, D:] = jnp.concatenate(dv, axis=1).astype(bf16)


def cross_backward(cap_t, cap_q, q, k, v, g):
    return pl.pallas_call(
        cross_backward_body,
        out_shape=[
            jax.ShapeDtypeStruct((TOK, D), bf16),
            jax.ShapeDtypeStruct((TXT, 2 * D), bf16),
        ],
        compiler_params=params(),
    )(cap_t, cap_q, q, k, v, g)


def fetch_pair(core, mine, other, first, second, sem, column=0):
    def run(a, b):
        columns = pl.ds(column, D)
        one = pltpu.make_async_copy(a.at[:, columns], first, sem.at[0])
        two = pltpu.make_async_copy(b.at[:, columns], second, sem.at[1])
        one.start()
        two.start()
        one.wait()
        two.wait()

    @pl.when(core[0] == 0)
    def _():
        run(mine, other)

    @pl.when(core[0] != 0)
    def _():
        run(other, mine)


def fetch_windows(core, mine, other, whole, sem):
    def run(a, b):
        one = pltpu.make_async_copy(
            a.at[:, pl.ds(2 * D, WIN)], whole.at[:, pl.ds(0, WIN)], sem.at[0]
        )
        two = pltpu.make_async_copy(
            b.at[:, pl.ds(2 * D + 128, STEP)], whole.at[:, pl.ds(WIN, STEP)], sem.at[1]
        )
        one.start()
        two.start()
        one.wait()
        two.wait()

    @pl.when(core[0] == 0)
    def _():
        run(mine, other)

    @pl.when(core[0] != 0)
    def _():
        run(other, mine)


def mlp_body(parts, count, core, *refs):
    xs, gs = refs[: parts * count], refs[parts * count : 2 * parts * count]
    mine, other = refs[2 * parts * count : 2 * parts * count + 2]
    outs = refs[2 * parts * count + 2 : -3]
    up, down, sem = refs[-3:]
    fetch_pair(core, mine, other, up, down, sem)
    for k in range(count):
        x = jnp.concatenate([r[...] for r in xs[parts * k : parts * (k + 1)]], axis=0)
        g = jnp.concatenate([r[...] for r in gs[parts * k : parts * (k + 1)]], axis=0)
        out, act_out, pre_out, grad_x = outs[4 * k : 4 * (k + 1)]
        pre = dot_nn(x, up[...])
        grad_act = dot_nt(g, down[...])
        cdf = 0.5 * (1.0 + lax.erf(pre * (0.5**0.5)))
        density = jnp.exp2(pre * pre * (-0.5 * log2e)) * 0.3989422804014327
        act = (pre * cdf).astype(bf16)
        grad_pre = (grad_act * (cdf + pre * density)).astype(bf16)
        act_out[...] = act
        pre_out[...] = grad_pre
        out[...] = dot_nn(act, down[...]).astype(out.dtype)
        grad_x[...] = dot_nt(grad_pre, up[...]).astype(grad_x.dtype)


def mlp(core, xs, gs, mine, other):
    parts = TOK // xs[0].shape[0]
    count = len(xs) // parts
    vmem = pl.BlockSpec(memory_space=pltpu.VMEM)
    hbm = pl.BlockSpec(memory_space=pl.ANY)
    return pl.pallas_call(
        functools.partial(mlp_body, parts, count),
        in_specs=[pl.BlockSpec(memory_space=pltpu.SMEM)]
        + [vmem] * (2 * parts * count)
        + [hbm, hbm],
        out_specs=[vmem] * (4 * count),
        out_shape=[jax.ShapeDtypeStruct((TOK, D), bf16)] * (4 * count),
        scratch_shapes=[
            pltpu.VMEM((D, D), bf16),
            pltpu.VMEM((D, D), bf16),
            pltpu.SemaphoreType.DMA((2,)),
        ],
        compiler_params=params(),
    )(core, *xs, *gs, mine, other)


def mlp_grad_body(which, core, *refs):
    out = refs[16]

    def run(xs, gs):
        out[...] = sum(dot_tn(x[...], g[...]) for x, g in zip(xs, gs)).astype(bf16)

    @pl.when(core[0] == which)
    def _():
        run(refs[:4], refs[4:8])

    @pl.when(core[0] != which)
    def _():
        run(refs[8:12], refs[12:16])


def mlp_grad(which, core, xs, pres, acts, gs):
    whole = [pl.BlockSpec((TOK, D), lambda k: (0, 0))] * 4
    part = [pl.BlockSpec((TOK, 384), lambda k: (0, k))] * 4
    return pl.pallas_call(
        functools.partial(mlp_grad_body, which),
        grid=(3,),
        in_specs=[pl.BlockSpec(memory_space=pltpu.SMEM)] + whole + part + whole + part,
        out_specs=pl.BlockSpec((D, 384), lambda k: (0, k)),
        out_shape=jax.ShapeDtypeStruct((D, D), bf16),
        compiler_params=params(),
    )(core, *xs, *pres, *acts, *gs)


def sort_hidden_body(core, mine, other, up, down):
    def run(ups, downs):
        for f in range(8):
            lanes = slice(SHARD * f, SHARD * (f + 1))
            up[:, 4 * SHARD * f : 4 * SHARD * (f + 1)] = jnp.concatenate(
                [ups[SHARD * z : SHARD * (z + 1), lanes] for z in range(4)], axis=1
            ).astype(f32)
        down[...] = downs[...].astype(f32)

    @pl.when(core[0] == 0)
    def _():
        run(mine, other)

    @pl.when(core[0] != 0)
    def _():
        run(other, mine)


def sort_hidden(core, mine, other):
    vmem = pl.BlockSpec(memory_space=pltpu.VMEM)
    return pl.pallas_call(
        sort_hidden_body,
        in_specs=[pl.BlockSpec(memory_space=pltpu.SMEM), vmem, vmem],
        out_specs=[vmem, vmem],
        out_shape=[
            jax.ShapeDtypeStruct((SHARD, FF), f32),
            jax.ShapeDtypeStruct((4 * SHARD, D), f32),
        ],
        compiler_params=params(),
    )(core, mine, other)


def normalize(x):
    center = x - jnp.mean(x, axis=-1, keepdims=True)
    inverse = lax.rsqrt(jnp.mean(center * center, axis=-1, keepdims=True) + norm_eps)
    return center * inverse, inverse


def norm_back(x, g, gain):
    plain, inverse = normalize(x)
    scaled = g * gain
    mixed = jnp.mean(scaled * plain, axis=-1, keepdims=True)
    grad = inverse * (scaled - jnp.mean(scaled, axis=-1, keepdims=True) - plain * mixed)
    sums = [jnp.sum(g * plain, axis=0, keepdims=True), jnp.sum(g, axis=0, keepdims=True)]
    return grad, sums


def call(body, ins, outs, scratch):
    spaces = {"vmem": pltpu.VMEM, "hbm": pl.ANY, "smem": pltpu.SMEM}
    return pl.pallas_call(
        body,
        in_specs=[pl.BlockSpec(memory_space=spaces[where]) for _, where in ins],
        out_specs=[pl.BlockSpec(memory_space=pltpu.VMEM)] * len(outs),
        out_shape=[jax.ShapeDtypeStruct(*o) for o in outs],
        scratch_shapes=scratch,
        compiler_params=params(),
    )(*[x for x, _ in ins])


def square_scratch(count):
    return [pltpu.VMEM((D, D), bf16)] * count + [pltpu.SemaphoreType.DMA((2,))]


def after_self_body(core, x, mixed, gain, bias, mine, other, total, normed, query, w1, w2, sem):
    fetch_pair(core, mine, other, w1, w2, sem)
    rows = x[...].astype(f32) + dot_nn(mixed[...], w1[...])
    total[...] = rows
    low = (normalize(rows)[0] * gain[...] + bias[...]).astype(bf16)
    normed[...] = low
    query[...] = dot_nn(low, w2[...]).astype(bf16)


def text_keys_body(core, context, mine, other, key, value, w1, w2, sem):
    fetch_pair(core, mine, other, w1, w2, sem, D)
    key[...] = dot_nn(context[...], w1[...]).astype(bf16)
    value[...] = dot_nn(context[...], w2[...]).astype(bf16)


def after_cross_body(core, x, mixed, gain, bias, mine, other, total, normed, w, sem):
    fetch_windows(core, mine, other, w, sem)
    rows = x[...] + dot_nn(mixed[...], w[...])
    total[...] = rows
    normed[...] = (normalize(rows)[0] * gain[...] + bias[...]).astype(bf16)


def third_back_body(core, x, g0, g1, g2, cot, gain, mine, other, grad, low, mixed, sums, w, sem):
    fetch_windows(core, mine, other, w, sem)
    g = g0[...].astype(f32) + g1[...].astype(f32) + g2[...].astype(f32)
    back, both = norm_back(x[...], g, gain[...])
    total = cot[...] + back
    grad[...] = total
    low[...] = total.astype(bf16)
    mixed[...] = dot_nt(total.astype(bf16), w[...]).astype(bf16)
    sums[...] = jnp.concatenate(both + [jnp.zeros((6, D), f32)], axis=0)


def second_back_body(core, x, gq, before, gain, mine, other, grad, low, mixed, sums, w1, w2, sem):
    fetch_pair(core, mine, other, w1, w2, sem)
    back, both = norm_back(x[...], dot_nt(gq[...], w2[...]), gain[...])
    total = before[...] + back
    grad[...] = total
    low[...] = total.astype(bf16)
    mixed[...] = dot_nt(total.astype(bf16), w1[...]).astype(bf16)
    sums[...] = jnp.concatenate(both + [jnp.zeros((6, D), f32)], axis=0)


def first_back_body(x, *refs):
    before, gain, grad = refs[SPLIT:]
    size = TOK // SPLIT
    sums = []
    for parts in refs[:SPLIT]:
        g = parts[:size, :].astype(f32)
        for k in range(1, 8):
            g = g + parts[size * k : size * (k + 1), :].astype(f32)
        sums.append(g)
    g = jnp.concatenate(sums, axis=0)
    grad[...] = before[...] + norm_back(x[...].astype(f32), g, gain[...])[0]


def text_back_body(
    core, kv, cols, text, w_text, mine, other, part, grad_text, grad_kv, w1, w2, sem
):
    fetch_pair(core, mine, other, w1, w2, sem, D)
    low = (dot_nt(kv[:, :D], w1[...]) + dot_nt(kv[:, D:], w2[...])).astype(bf16)
    part[...] = dot_nt(low, w_text[...]).astype(bf16)
    grad_text[...] = dot_tn(text[...], low).astype(bf16)
    grad_kv[...] = dot_tn(cols[...], kv[...]).astype(bf16)


def first_part_body(g, w, plain, *refs):
    rows = dot_nt(g[...], w[...])
    sums = refs[-1]
    size = TOK // SPLIT
    for k in range(SPLIT):
        refs[k][...] = rows[size * k : size * (k + 1)].astype(bf16)
    both = [
        jnp.sum(rows * plain[...].astype(f32), axis=0, keepdims=True),
        jnp.sum(rows, axis=0, keepdims=True),
        jnp.zeros((6, D), f32),
    ]
    both = jnp.concatenate(both, axis=0)

    @pl.when(pl.program_id(0) == 0)
    def _():
        sums[...] = both

    @pl.when(pl.program_id(0) != 0)
    def _():
        sums[...] += both


def first_part(g, w, plain):
    return pl.pallas_call(
        first_part_body,
        grid=(ROW // TOK,),
        in_specs=[
            pl.BlockSpec((TOK, 6 * SLOT), lambda i: (i, 0)),
            pl.BlockSpec((D, 6 * SLOT), lambda i: (0, 0)),
            pl.BlockSpec((TOK, D), lambda i: (i, 0)),
        ],
        out_specs=[
            *[pl.BlockSpec((TOK // SPLIT, D), lambda i: (i, 0))] * SPLIT,
            pl.BlockSpec((8, D), lambda i: (0, 0)),
        ],
        out_shape=[jax.ShapeDtypeStruct((ROW // SPLIT, D), bf16)] * SPLIT
        + [jax.ShapeDtypeStruct((8, D), f32)],
        cost_estimate=cost(11),
        compiler_params=params(),
    )(g, w, plain)


def heads_grad_body(x, g, out):
    grad = dot_tn(x[...], g[...]).astype(bf16)
    out[...] = jnp.concatenate(
        [
            grad[:, SLOT * (3 * h + k) : SLOT * (3 * h + k) + HEAD]
            for k in range(3)
            for h in range(2)
        ],
        axis=1,
    )


def heads_grad(x, g):
    return pl.pallas_call(
        heads_grad_body,
        grid=(3,),
        in_specs=[
            pl.BlockSpec((ROW, 384), lambda i: (0, i)),
            pl.BlockSpec((ROW, 6 * SLOT), lambda i: (0, 0)),
        ],
        out_specs=pl.BlockSpec((384, 3 * SHARD), lambda i: (i, 0)),
        out_shape=jax.ShapeDtypeStruct((D, 3 * SHARD), bf16),
        cost_estimate=cost(8),
        compiler_params=params(),
    )(x, g)


def unpack_heads_body(x, out):
    for k in range(3):
        out[SHARD * k : SHARD * (k + 1), :] = jnp.concatenate(
            [x[SHARD * p : SHARD * (p + 1), SHARD * k : SHARD * (k + 1)] for p in range(8)], axis=1
        )


def unpack_heads(x):
    return pl.pallas_call(
        unpack_heads_body,
        out_shape=jax.ShapeDtypeStruct((3 * SHARD, D), bf16),
        compiler_params=params(),
    )(x)


def row_block(x, index, rows):
    return lax.dynamic_slice_in_dim(x, index * rows, rows, axis=0)


def core_window(x, core):
    return lax.dynamic_slice_in_dim(x, core * STEP, WIN, axis=1)


def both_cores(x):
    return jnp.concatenate([x, shift(x, "c", 1)], axis=0)


def window_grad(left, right):
    core = lax.axis_index("c")
    sent = shift(core_window(right, 1 - core), "c", 1)
    rights = jnp.concatenate([core_window(right, core), sent], axis=0)
    return dot_tn(both_cores(left), rights).astype(bf16)


def sum_over(x, *axes):
    for axis in axes:
        n = lax.axis_size(axis)
        x = sum([shift(x, axis, k) for k in range(1, n)], x)
    return x


def local(
    tokens,
    text_states,
    seg_lengths,
    caption_of_segment,
    text_lengths,
    ln1_gain,
    ln1_bias,
    w_query,
    w_key,
    w_value,
    w_out,
    ln2_gain,
    ln2_bias,
    c_query,
    w_text,
    c_key,
    c_value,
    c_out,
    ln3_gain,
    ln3_bias,
    w_up,
    w_down,
    cotangent,
):
    core = lax.axis_index("c")
    first_core = core == 0
    core_index = core.astype(jnp.int32)[None]
    quarter = lax.axis_index("z")
    first_row = peer(0, 0) * TOK

    ends = jnp.cumsum(seg_lengths[0])
    positions = jnp.arange(ROW, dtype=jnp.int32)
    segment = jnp.sum((positions[:, None] >= ends[None, :]).astype(jnp.int32), axis=1)
    own_segment = lax.dynamic_slice_in_dim(segment, first_row, TOK)
    text_row = jnp.arange(TXT, dtype=jnp.int32)
    text_pos = text_row // TXT_OWN * CAP_TOK + text_row % TXT_OWN
    text_caption = text_pos // CAP_LEN
    live = jnp.sum(
        jnp.where(
            text_caption[:, None] == jnp.arange(CAPS, dtype=jnp.int32)[None, :],
            text_lengths[0][None, :],
            0,
        ),
        axis=1,
    )
    query_caption = jnp.sum(
        jnp.where(
            own_segment[:, None] == jnp.arange(SEGS, dtype=jnp.int32)[None, :],
            caption_of_segment[0][None, :],
            0,
        ),
        axis=1,
    )
    text_live = (text_row % TXT_OWN < CAP_TOK) & (text_pos % CAP_LEN < live)
    text_key = jnp.where(text_live, text_caption, -1)

    def row(x):
        return x[None, :]

    gap = jnp.zeros((SHARD, 128), bf16)
    square_pack = jnp.where(
        first_core,
        jnp.concatenate([w_out, c_key, c_out[:, :WIN], gap], axis=1),
        jnp.concatenate([c_query, c_value, c_out[:, STEP:], gap], axis=1),
    )
    square_pack = lax.dynamic_slice_in_dim(square_pack, quarter * QUARTER, QUARTER, axis=1)
    quarter_own = lax.all_gather(square_pack, FS, axis=0, tiled=True)

    rows_in = tokens[0]
    plain = normalize(rows_in.astype(f32))[0].astype(bf16)
    n01, n10, n30 = gather_first(plain)

    heads_pack = pack_heads(after(w_query, plain), w_key, w_value)
    n01, n10, n30, heads_pack = lax.optimization_barrier((n01, n10, n30, heads_pack))
    heads_w = peers_parts(heads_pack)
    n31, n20, n11 = gather_second(n01, n10)

    n31, n20, n11 = lax.optimization_barrier((n31, n20, n11))
    n21 = gather_third(n31, n11)
    plain_all, normed_all = place_rows(
        plain,
        (n01, n10, n30),
        (n31, n20, n11),
        n21,
        row(ln1_gain),
        row(ln1_bias),
    )
    heads_w = spread_heads(heads_w)
    quarter_own, normed_all, heads_w = lax.optimization_barrier((quarter_own, normed_all, heads_w))
    quarter_minus, quarter_plus = shift(quarter_own, "z", 1), shift(quarter_own, "z", -1)

    text_own = jnp.pad(after(text_states[0], normed_all), ((0, TXT_OWN - CAP_TOK), (0, 0)))
    text_columns = lax.all_to_all(text_own, FS, split_axis=1, concat_axis=0, tiled=True)

    up_own = jnp.concatenate(
        [
            lax.dynamic_slice(w_up, (0, 4 * SHARD * k + SHARD * quarter), (SHARD, SHARD))
            for k in range(8)
        ],
        axis=1,
    )
    hidden_own = jnp.where(first_core, up_own, row_block(w_down, quarter, SHARD))

    seg_col, seg_row = segment[:, None], segment[None, :]
    qkv = dot_nn(normed_all, heads_w).astype(bf16)
    text_columns, qkv = lax.optimization_barrier((text_columns, qkv))
    context_part = dot_nn(text_columns, w_text).astype(bf16)
    context_own = lax.psum_scatter(context_part, FS, scatter_dimension=0, tiled=True)
    head0, total0 = self_forward(0, seg_col, seg_row, after(qkv, context_part))
    head1, total1 = self_forward(1, seg_col, seg_row, after(qkv, head0))
    hidden_mine = every_peer(after(hidden_own, text_columns))
    quarter_minus, quarter_plus, hidden_mine, head1 = lax.optimization_barrier(
        (quarter_minus, quarter_plus, hidden_mine, head1)
    )
    quarter_far = (
        shift(halves(quarter_minus)[0], "z", 1),
        shift(halves(quarter_plus)[1], "z", -1),
    )
    attended = lax.all_to_all(
        jnp.concatenate([head0, head1], axis=1), FS, split_axis=0, concat_axis=1, tiled=True
    )
    attended, context_own, *quarter_far = lax.optimization_barrier(
        (attended, context_own, *quarter_far)
    )
    context = every_peer(context_own)
    square_mine = place_quarters(quarter_own, quarter_minus, quarter_plus, *quarter_far)
    square_other = shift(square_mine, "c", 1)
    grad_out = cotangent[0]
    grad_mlp = grad_out.astype(bf16)
    grad_sent = after(grad_mlp, square_mine)
    mlp_minus, mlp_plus = shift(grad_sent, "z", 1), shift(grad_sent, "z", -1)

    after_self, normed_two, cross_query = call(
        after_self_body,
        [
            (core_index, "smem"), (rows_in, "vmem"), (attended, "vmem"),
            (row(ln2_gain), "vmem"), (row(ln2_bias), "vmem"),
            (square_mine, "hbm"), (square_other, "hbm"),
        ],
        [((TOK, D), f32), ((TOK, D), bf16), ((TOK, D), bf16)],
        square_scratch(2),
    )
    cross_key, cross_value = call(
        text_keys_body,
        [
            (core_index, "smem"), (after(context, cross_query, mlp_minus, mlp_plus), "vmem"),
            (square_mine, "hbm"), (square_other, "hbm"),
        ],
        [((TXT, D), bf16), ((TXT, D), bf16)],
        square_scratch(2),
    )
    cross_mixed = cross_forward(
        query_caption[:, None], text_key[None, :], cross_query, cross_key, cross_value
    )
    hidden_mine = after(hidden_mine, cross_mixed)
    weights = (hidden_mine, shift(hidden_mine, "c", 1))
    after_cross, normed_three = call(
        after_cross_body,
        [
            (core_index, "smem"), (after_self, "vmem"), (cross_mixed, "vmem"),
            (row(ln3_gain), "vmem"), (row(ln3_bias), "vmem"),
            (square_mine, "hbm"), (square_other, "hbm"),
        ],
        [((TOK, D), f32), ((TOK, D), bf16)],
        square_scratch(1),
    )

    mlp_sent = lax.optimization_barrier((mlp_minus, mlp_plus, cross_query))
    mlp_far = (
        shift(halves(mlp_sent[0])[0], "z", 1),
        shift(halves(mlp_sent[1])[1], "z", -1),
    )

    three_minus, three_plus = shift(normed_three, "z", 1), shift(normed_three, "z", -1)
    out_own, act_own, pre_own, back_own = mlp(core_index, (normed_three,), (grad_mlp,), *weights)
    three_minus, three_plus, out_own = lax.optimization_barrier(
        (three_minus, three_plus, out_own)
    )
    three_far = (
        shift(halves(three_minus)[0], "z", 1),
        shift(halves(three_plus)[1], "z", -1),
    )
    near = mlp(core_index, (three_minus, three_plus), (mlp_minus, mlp_plus), *weights)
    out_m, act_m, pre_m, back_m, out_p, act_p, pre_p, back_p = near
    *three_far, out_m = lax.optimization_barrier((*three_far, out_m))
    out_far, act_far, pre_far, back_far = mlp(core_index, three_far, mlp_far, *weights)
    back_minus, back_plus = reduce_z(back_far, back_m, back_p)
    three_parts = (normed_three, three_minus, three_plus, jnp.concatenate(three_far, axis=0))
    pre_parts = (pre_own, pre_m, pre_p, pre_far)
    act_parts = (act_own, act_m, act_p, act_far)
    mlp_parts = (grad_mlp, mlp_minus, mlp_plus, jnp.concatenate(mlp_far, axis=0))
    send = mlp_grad(1, core_index, three_parts, pre_parts, act_parts, mlp_parts)
    back_minus, back_plus, send = lax.optimization_barrier((back_minus, back_plus, send))
    back_minus, back_plus = shift(back_minus, "z", -1), shift(back_plus, "z", 1)
    keep = mlp_grad(
        0, core_index, three_parts, pre_parts, act_parts, (after(grad_mlp, send), *mlp_parts[1:])
    )
    back_minus, back_plus, keep = lax.optimization_barrier((back_minus, back_plus, keep))
    hidden_sum = keep + shift(send, "c", 1)
    hidden_grad = lax.psum_scatter(hidden_sum, FS, scatter_dimension=0, tiled=True)
    grad_after_cross, grad_cross_branch, grad_cross_mixed, sums_three = call(
        third_back_body,
        [
            (core_index, "smem"), (after_cross, "vmem"), (back_own, "vmem"),
            (back_minus, "vmem"), (back_plus, "vmem"), (grad_out, "vmem"),
            (after(row(ln3_gain), hidden_sum), "vmem"), (square_mine, "hbm"), (square_other, "hbm"),
        ],
        [((TOK, D), f32), ((TOK, D), bf16), ((TOK, D), bf16), ((8, D), f32)],
        square_scratch(1),
    )

    grad_cquery_rows, grad_kv = cross_backward(
        text_key[:, None],
        query_caption[None, :],
        cross_query,
        cross_key,
        cross_value,
        grad_cross_mixed,
    )
    grad_after_self, grad_self_branch, grad_attended, sums_two = call(
        second_back_body,
        [
            (core_index, "smem"), (after_self, "vmem"), (grad_cquery_rows, "vmem"),
            (grad_after_cross, "vmem"), (row(ln2_gain), "vmem"),
            (square_mine, "hbm"), (square_other, "hbm"),
        ],
        [((TOK, D), f32), ((TOK, D), bf16), ((TOK, D), bf16), ((8, D), f32)],
        square_scratch(2),
    )
    grad_heads = lax.all_to_all(grad_attended, FS, split_axis=1, concat_axis=0, tiled=True)

    square = jnp.concatenate(
        [
            window_grad(cross_mixed, after(grad_cross_branch, grad_attended)),
            window_grad(normed_two, after(grad_cquery_rows, grad_attended)),
            window_grad(attended, grad_self_branch),
        ],
        axis=1,
    )

    def square_chunk(dy, dx):
        return row_block(square, peer(dy, dx), SHARD)

    grad_heads, square = lax.optimization_barrier((grad_heads, square))
    grad_qkv = self_backward(0, seg_col, seg_row, total0, qkv, grad_heads)
    square, hidden_grad, grad_kv, grad_qkv = lax.optimization_barrier(
        (square, hidden_grad, grad_kv, grad_qkv)
    )
    kv_own = lax.psum_scatter(grad_kv, FS, scatter_dimension=0, tiled=True)
    s_lo, s_hi, s20 = reduce_first(square_chunk)
    hidden_grad = hidden_grad + shift(hidden_grad, "xh", 1)
    out_minus, out_plus = reduce_z(after(out_far, grad_qkv), out_m, out_p)
    grad_qkv = self_backward(1, seg_col, seg_row, total1, qkv, grad_heads, (grad_qkv,))
    s_lo, s_hi, s20, out_minus, out_plus, grad_qkv = lax.optimization_barrier(
        (s_lo, s_hi, s20, out_minus, out_plus, grad_qkv)
    )
    s11, s31 = reduce_second(square_chunk, s_lo, s_hi)

    heads_own = heads_grad(normed_all, grad_qkv)
    heads_own, kv_own = lax.optimization_barrier((heads_own, kv_own))
    heads_part = peers_parts(heads_own)
    kv_all = lax.all_gather(kv_own, FS, axis=0, tiled=True)
    part, sums_one = first_part(after(grad_qkv, heads_own), heads_w, plain_all)
    part, heads_part, s11, s31, hidden_grad = lax.optimization_barrier(
        (part, heads_part, s11, s31, hidden_grad)
    )
    sent = peers_parts(part)

    square_parts = reduce_third(square_chunk, s20, s11, s31)
    hidden_z = neighbours(after(hidden_grad, part))
    heads_rows = unpack_heads(heads_part)
    early = row_block(heads_rows, core, 216) + shift(row_block(heads_rows, 1 - core, 216), "c", 1)
    norms = jnp.concatenate([sums_one[:2], sums_two[:2], sums_three[:2], jnp.zeros((2, D), f32)])
    norms = sum_over(norms, "z", "c")
    part, early, norms, kv_all, *rest = lax.optimization_barrier(
        (sent, early, norms, kv_all, *square_parts, *hidden_z)
    )
    square_parts, hidden_z = rest[:3], rest[3:]

    square = reduce_last(square_chunk, *square_parts).astype(bf16)
    square = jnp.concatenate([square[:, WIN * k : WIN * (k + 1)] for k in range(3)], axis=0)
    square = jnp.concatenate([square[:216], square[216:]], axis=1)
    early = jnp.concatenate([early, square], axis=1)
    early = jnp.concatenate([early, jnp.zeros((256 - 216, D + 2 * WIN), bf16)], axis=0)
    early = lax.psum_scatter(early, "z", scatter_dimension=0, tiled=True)
    early = early + shift(early, "xh", 1)
    own_columns = lax.dynamic_slice_in_dim(context, peer(0, 0) * SHARD, SHARD, axis=1)
    text_part, grad_w_text, grad_w_kv = call(
        text_back_body,
        [
            (core_index, "smem"), (kv_all, "vmem"), (own_columns, "vmem"),
            (text_columns, "vmem"), (w_text, "vmem"),
            (square_mine, "hbm"), (square_other, "hbm"),
        ],
        [((TXT, TXT), bf16), ((TXT, D), bf16), ((SHARD, 2 * D), bf16)],
        square_scratch(2),
    )

    def half(which):
        kv = jnp.where(which == 0, grad_w_kv[:, :D], grad_w_kv[:, D:])
        return jnp.concatenate(
            [row_block(grad_w_text, which, 256), kv, jnp.zeros((448 - 400, D), bf16)], axis=0
        )

    late = half(core) + shift(half(1 - core), "c", 1)
    late = lax.psum_scatter(late, "z", scatter_dimension=0, tiled=True)
    hidden_grad = in_order(*hidden_z)
    grad_w_up, grad_w_down = sort_hidden(core_index, hidden_grad, shift(hidden_grad, "c", 1))

    norms = sum_over(norms, "y", "xl", "xh")
    late = late + shift(late, "xh", 1)
    early = in_order(*neighbours(early))
    late = in_order(*neighbours(late))

    def by_core(x):
        other = shift(x, "c", 1)
        low, high = jnp.where(first_core, x, other), jnp.where(first_core, other, x)
        return low.astype(f32), high.astype(f32)

    low, high = by_core(early)
    grad_w_query = low[:144, :D]
    grad_w_key = jnp.concatenate([low[144:216, :D], high[:72, :D]], axis=0)
    grad_w_value = high[72:216, :D]
    low = jnp.concatenate([low[:216, D : D + WIN], low[:216, D + WIN :]], axis=0)
    high = jnp.concatenate([high[:216, D : D + WIN], high[:216, D + WIN :]], axis=0)
    grad_c_out, grad_c_query, grad_w_out = (
        jnp.concatenate(
            [low[SHARD * k : SHARD * (k + 1)], high[SHARD * k : SHARD * (k + 1), 128:]], axis=1
        )
        for k in range(3)
    )
    low, high = by_core(late)
    grad_w_text = jnp.concatenate([low[:256], high[:256]], axis=0)
    grad_c_key, grad_c_value = low[256:400], high[256:400]
    out_minus, out_plus = shift(out_minus, "z", -1), shift(out_plus, "z", 1)
    outputs = (
        after_cross + out_own.astype(f32) + out_minus.astype(f32) + out_plus.astype(f32)
    )

    grad_tokens = call(
        first_back_body,
        [
            (rows_in, "vmem"), (part, "vmem"), (grad_after_self, "vmem"),
            (row(ln1_gain), "vmem"),
        ],
        [((TOK, D), f32)],
        [],
    )[0]
    grad_text = lax.all_to_all(
        after(text_part, part), FS, split_axis=0, concat_axis=1, tiled=True
    )
    grad_text = grad_text[:CAP_TOK].astype(f32)
    return (
        outputs[None],
        grad_tokens[None],
        grad_text[None],
        norms[0],
        norms[1],
        grad_w_query,
        grad_w_key,
        grad_w_value,
        grad_w_out,
        norms[2],
        norms[3],
        grad_c_query,
        grad_w_text,
        grad_c_key,
        grad_c_value,
        grad_c_out,
        norms[4],
        norms[5],
        grad_w_up,
        grad_w_down,
    )


def solution(mesh):
    split = Mesh(mesh.devices.reshape(2, 4, 2, 4, 2), ("xh", "z", "c", "y", "xl"))
    dp = ("xh", "z", "c")
    rows = P(dp, FS, None)
    per_row = P(dp, None)
    weight = P(FS, None)
    rep = P()
    in_specs = (
        rows, rows, per_row, per_row, per_row,
        rep, rep, weight, weight, weight, weight,
        rep, rep, weight, weight, weight, weight, weight,
        rep, rep, weight, weight, rows,
    )
    out_specs = (
        rows, rows, rows,
        rep, rep, weight, weight, weight, weight,
        rep, rep, weight, weight, weight, weight, weight,
        rep, rep, weight, weight,
    )
    return jax.shard_map(
        local, mesh=split, in_specs=in_specs, out_specs=out_specs, check_vma=False
    )
```

```python
import functools

import jax
import jax.numpy as jnp
from jax import lax
from jax.experimental import pallas as pl
from jax.experimental.pallas import tpu as pltpu
from jax.sharding import Mesh
from jax.sharding import PartitionSpec as P

HEADS = 16
HEAD = 72
D = 1152
FF = 4608
CAP_TOK = 60
TXT_OWN = 64
TXT = 8 * TXT_OWN
TOK = 256
ROW = 2048
CAP_LEN = 120
SEGS = 3
CAPS = 4
SHARD = 144
SLOT = 128
SPLIT = 1
WIN = 640
STEP = 512

bf16 = jnp.bfloat16
f32 = jnp.float32
norm_eps = 1e-06
masked_score = -1e30
scale = HEAD ** (-0.5)
log2e = 1.4426950408889634
FS = ("y", "xl")
VMEM = 60 * 1024 * 1024


def dot_nn(a, b):
    return lax.dot_general(a, b, (((1,), (0,)), ((), ())), preferred_element_type=f32)


def dot_nt(a, b):
    return lax.dot_general(a, b, (((1,), (1,)), ((), ())), preferred_element_type=f32)


def dot_tn(a, b):
    return lax.dot_general(a, b, (((0,), (0,)), ((), ())), preferred_element_type=f32)


def params():
    return pltpu.CompilerParams(vmem_limit_bytes=VMEM)


def cost(micros):
    return pl.CostEstimate(flops=int(micros * 1.15e9), bytes_accessed=0, transcendentals=0)


def shift(x, axis, by):
    n = lax.axis_size(axis)
    return lax.ppermute(x, axis, [(i, (i + by) % n) for i in range(n)])


def halves(x):
    h = (x.shape[0] // 2 + 15) // 16 * 16
    return x[:h], x[h:]


def after(x, *others):
    return lax.optimization_barrier((x, *others))[0]


def gather_first(x):
    return shift(x, "xl", 1), shift(x, "y", -1), shift(x, "y", 1)


def gather_second(x01, x10):
    return shift(x01, "y", 1), shift(x10, "y", -1), shift(x10, "xl", 1)


def gather_third(x31, x11):
    return shift(halves(x11)[0], "y", -1), shift(halves(x31)[1], "y", 1)


NEAR = ((0, 0), (0, 1), (1, 0), (3, 0))
NEXT = ((3, 1), (2, 0), (1, 1))
LAST = (2, 1)


def reduce_first(chunk):
    lo, hi = halves(chunk(2, 1))
    return shift(lo, "y", 1), shift(hi, "y", -1), shift(chunk(2, 0), "y", 1)


def reduce_second(chunk, lo, hi):
    h = lo.shape[0]
    c11, c31 = chunk(1, 1), chunk(3, 1)
    c11 = jnp.concatenate([c11[:h] + lo, c11[h:]], axis=0)
    c31 = jnp.concatenate([c31[:h], c31[h:] + hi], axis=0)
    return shift(c11, "xl", 1), shift(c31, "y", -1)


def reduce_third(chunk, c20, c11, c31):
    return (
        shift(chunk(1, 0) + c20 + c11, "y", 1),
        shift(chunk(0, 1) + c31, "xl", 1),
        shift(chunk(3, 0), "y", -1),
    )


def reduce_last(chunk, *parts):
    return sum([p.astype(f32) for p in parts], chunk(0, 0).astype(f32))


def every_peer(x, axes=FS):
    n = lax.axis_size(axes)
    copies = jnp.broadcast_to(x[None], (n, *x.shape)).reshape(n * x.shape[0], x.shape[1])
    return lax.all_to_all(copies, axes, 0, 0, tiled=True)


def peers_parts(x, axes=FS):
    return lax.all_to_all(x, axes, 0, 0, tiled=True)


def sum_parts(parts):
    return jnp.sum(parts.reshape(8, -1, parts.shape[1]).astype(f32), axis=0)


def neighbours(x):
    return x, shift(x, "z", 1), shift(x, "z", 2), shift(x, "z", -1)


def in_order(*around):
    rows, cols = around[0].shape

    def body(where, *refs):
        ins, out = refs[:4], refs[4]
        for k in range(4):
            row = pl.multiple_of(lax.rem(where[0] + 4 - k, 4) * rows, 16)
            out[pl.ds(row, rows), :] = ins[k][...]

    vmem = pl.BlockSpec(memory_space=pltpu.VMEM)
    return pl.pallas_call(
        body,
        in_specs=[pl.BlockSpec(memory_space=pltpu.SMEM)] + [vmem] * 4,
        out_specs=vmem,
        out_shape=jax.ShapeDtypeStruct((4 * rows, cols), bf16),
        compiler_params=params(),
    )(lax.axis_index("z").astype(jnp.int32)[None], *around)


def reduce_z(far, minus, plus):
    lo, hi = halves(far)
    lo, hi = shift(lo, "z", -1), shift(hi, "z", 1)
    h = lo.shape[0]
    return (
        jnp.concatenate([minus[:h] + lo, minus[h:]], axis=0),
        jnp.concatenate([plus[:h], plus[h:] + hi], axis=0),
    )


def peer(dy, dx):
    return ((lax.axis_index("y") + dy) % 4) * 2 + (lax.axis_index("xl") ^ dx)


def place_rows(own, first, second, third, gain, bias):
    lo = third[0].shape[0]
    rows, cols = own.shape
    pieces = [(x, p, 0) for x, p in zip((own, *first), NEAR)]
    pieces += [(x, p, 0) for x, p in zip(second, NEXT)]
    pieces += [(third[0], LAST, 0), (third[1], LAST, lo)]
    count = len(pieces)

    def body(where, gain, bias, *refs):
        ins, plain, normed, sem = refs[:count], refs[count], refs[count + 1], refs[-1]
        started = []
        for k, (x, _, off) in enumerate(pieces):
            row = pl.multiple_of(where[k] * rows + off, 16)
            one = pltpu.make_async_copy(ins[k], plain.at[pl.ds(row, x.shape[0])], sem.at[k])
            one.start()
            started.append(one)
        for one in started:
            one.wait()

        def step(i, carry):
            part = pl.ds(pl.multiple_of(i * rows, rows), rows)
            normed[part, :] = (plain[part, :].astype(f32) * gain[...] + bias[...]).astype(bf16)
            return carry

        lax.fori_loop(0, 8, step, 0)

    vmem = pl.BlockSpec(memory_space=pltpu.VMEM)
    return pl.pallas_call(
        body,
        in_specs=[pl.BlockSpec(memory_space=pltpu.SMEM), vmem, vmem]
        + [pl.BlockSpec(memory_space=pl.ANY)] * count,
        out_specs=[vmem, vmem],
        out_shape=[jax.ShapeDtypeStruct((8 * rows, cols), bf16)] * 2,
        scratch_shapes=[pltpu.SemaphoreType.DMA((count,))],
        compiler_params=params(),
    )(
        jnp.stack([peer(*p) for _, p, _ in pieces]).astype(jnp.int32),
        gain,
        bias,
        *[x for x, _, _ in pieces],
    )


QUARTER = 768


def place_quarters(*quarters):
    def body(where, own, minus, plus, far_lo, far_hi, out, sem):
        started = []
        half = far_lo.shape[0]
        for k, (ref, turn, row) in enumerate(
            ((own, 0, 0), (minus, 3, 0), (plus, 1, 0), (far_lo, 2, 0), (far_hi, 2, half))
        ):
            column = pl.multiple_of(lax.rem(where[0] + turn, 4) * QUARTER, 128)
            one = pltpu.make_async_copy(
                ref, out.at[pl.ds(row, ref.shape[0]), pl.ds(column, QUARTER)], sem.at[k]
            )
            one.start()
            started.append(one)
        for one in started:
            one.wait()

    return pl.pallas_call(
        body,
        in_specs=[pl.BlockSpec(memory_space=pltpu.SMEM)] + [pl.BlockSpec(memory_space=pl.ANY)] * 5,
        out_specs=pl.BlockSpec(memory_space=pltpu.VMEM),
        out_shape=jax.ShapeDtypeStruct((D, 4 * QUARTER), bf16),
        scratch_shapes=[pltpu.SemaphoreType.DMA((5,))],
        compiler_params=params(),
    )(lax.axis_index("z").astype(jnp.int32)[None], *quarters)


def pack_heads_body(wq, wk, wv, out):
    for p in range(8):
        rows = slice(SHARD * p, SHARD * (p + 1))
        out[rows, :] = jnp.concatenate([w[:, rows] for w in (wq, wk, wv)], axis=1)


def pack_heads(*weights):
    return pl.pallas_call(
        pack_heads_body,
        out_shape=jax.ShapeDtypeStruct((D, 3 * SHARD), bf16),
        compiler_params=params(),
    )(*weights)


def spread_heads_body(x, out):
    blank = jnp.zeros((D, SLOT - HEAD), bf16)
    for h in range(2):
        for k in range(3):
            first = SHARD * k + HEAD * h
            slot = SLOT * (3 * h + k)
            out[:, slot : slot + SLOT] = jnp.concatenate(
                [x[:, first : first + HEAD], blank], axis=1
            )


def spread_heads(x):
    return pl.pallas_call(
        spread_heads_body,
        out_shape=jax.ShapeDtypeStruct((D, 6 * SLOT), bf16),
        compiler_params=params(),
    )(x)


def self_forward_body(seg_q, seg_k, q, kv, out, total):
    s = dot_nt(q[:, :SLOT], kv[:, SLOT : 2 * SLOT])
    s = jnp.where(seg_q[...] == seg_k[...], s, masked_score)
    top = jnp.max(s, axis=1, keepdims=True)
    p = jnp.exp2((s - top) * (scale * log2e))
    mass = jnp.sum(p, axis=1, keepdims=True)
    out[...] = (dot_nn(p.astype(bf16), kv[:, 2 * SLOT :]) / mass)[:, :HEAD].astype(bf16)
    log_total = top * (scale * log2e) + jnp.log2(mass)
    total[...] = jnp.transpose(jnp.broadcast_to(log_total, (TOK, SLOT)))[0:1, :]


def self_forward(head, seg_q, seg_k, qkv):
    return pl.pallas_call(
        self_forward_body,
        grid=(ROW // TOK,),
        in_specs=[
            pl.BlockSpec((TOK, 1), lambda i: (i, 0)),
            pl.BlockSpec((1, ROW), lambda i: (0, 0)),
            pl.BlockSpec((TOK, 3 * SLOT), lambda i: (i, head)),
            pl.BlockSpec((ROW, 3 * SLOT), lambda i: (0, head)),
        ],
        out_specs=[
            pl.BlockSpec((TOK, HEAD), lambda i: (i, 0)),
            pl.BlockSpec((1, TOK), lambda i: (0, i)),
        ],
        out_shape=[
            jax.ShapeDtypeStruct((ROW, HEAD), bf16),
            jax.ShapeDtypeStruct((1, ROW), f32),
        ],
        compiler_params=params(),
    )(seg_q, seg_k, qkv, qkv)


def self_backward_body(head, seg_k, seg_q, total, q, kv, g, *refs):
    grad, key_sum, value_sum, key_t = refs[-4:]
    i = pl.program_id(0)

    @pl.when(i == 0)
    def _():
        key_sum[...] = jnp.zeros_like(key_sum)
        value_sum[...] = jnp.zeros_like(value_sum)
        key_t[...] = jnp.transpose(kv[:, SLOT : 2 * SLOT])

    rows = pl.ds(pl.multiple_of(i * TOK, TOK), TOK)
    q_h, k_h, v_h = q[:, :SLOT], kv[:, SLOT : 2 * SLOT], kv[:, 2 * SLOT :]
    g_both = g[...]
    g_h = jnp.concatenate(
        [g_both[:, HEAD * head : HEAD * (head + 1)], jnp.zeros((TOK, SLOT - HEAD), bf16)], axis=1
    )
    p = jnp.exp2(dot_nt(k_h, q_h) * (scale * log2e) - total[...])
    p = jnp.where(seg_k[...] == seg_q[...], p, 0.0)
    dp = dot_nt(v_h, g_h)
    ds = (p * (dp - jnp.sum(p * dp, axis=0, keepdims=True))).astype(bf16)
    value_sum[...] += dot_nn(p.astype(bf16), g_h)
    key_sum[...] += dot_nn(ds, q_h)
    grad[rows, :SLOT] = (jnp.transpose(dot_nn(key_t[...], ds)) * scale).astype(bf16)

    @pl.when(i == pl.num_programs(0) - 1)
    def _():
        grad[:, SLOT : 2 * SLOT] = (key_sum[...] * scale).astype(bf16)
        grad[:, 2 * SLOT :] = value_sum[...].astype(bf16)


def self_backward(head, seg_k, seg_q, total, qkv, g, before=()):
    return pl.pallas_call(
        functools.partial(self_backward_body, head),
        grid=(ROW // TOK,),
        in_specs=[
            pl.BlockSpec((ROW, 1), lambda i: (0, 0)),
            pl.BlockSpec((1, TOK), lambda i: (0, i)),
            pl.BlockSpec((1, TOK), lambda i: (0, i)),
            pl.BlockSpec((TOK, 3 * SLOT), lambda i: (i, head)),
            pl.BlockSpec((ROW, 3 * SLOT), lambda i: (0, head)),
            pl.BlockSpec((TOK, SHARD), lambda i: (i, 0)),
        ]
        + [pl.BlockSpec(memory_space=pl.ANY)] * len(before),
        out_specs=pl.BlockSpec((ROW, 3 * SLOT), lambda i: (0, head)),
        out_shape=jax.ShapeDtypeStruct((ROW, 6 * SLOT), bf16),
        input_output_aliases={6: 0} if before else {},
        scratch_shapes=[
            pltpu.VMEM((ROW, SLOT), f32),
            pltpu.VMEM((ROW, SLOT), f32),
            pltpu.VMEM((SLOT, ROW), bf16),
        ],
        compiler_params=params(),
    )(seg_k, seg_q, total, qkv, qkv, g, *before)


def cross_forward_body(cap_q, cap_t, q, k, v, out):
    allowed = cap_q[...] == cap_t[...]
    mixed = []
    for h in range(HEADS):
        a, b = HEAD * h, HEAD * (h + 1)
        s = dot_nt(q[:, a:b], k[:, a:b])
        s = jnp.where(allowed, s, masked_score)
        top = jnp.max(s, axis=1, keepdims=True)
        p = jnp.exp2((s - top) * (scale * log2e))
        mass = jnp.sum(p, axis=1, keepdims=True)
        mixed.append(dot_nn(p.astype(bf16), v[:, a:b]) / mass)
    out[...] = jnp.concatenate(mixed, axis=1).astype(bf16)


def cross_forward(cap_q, cap_t, q, k, v):
    return pl.pallas_call(
        cross_forward_body,
        out_shape=jax.ShapeDtypeStruct((TOK, D), bf16),
        compiler_params=params(),
    )(cap_q, cap_t, q, k, v)


def cross_backward_body(cap_t, cap_q, q, k, v, g, grad_q, grad_kv):
    allowed = cap_t[...] == cap_q[...]
    dq, dk, dv = [], [], []
    for h in range(HEADS):
        a, b = HEAD * h, HEAD * (h + 1)
        q_h, k_h, v_h, g_h = q[:, a:b], k[:, a:b], v[:, a:b], g[:, a:b]
        s = jnp.where(allowed, dot_nt(k_h, q_h), masked_score)
        top = jnp.max(s, axis=0, keepdims=True)
        p = jnp.exp2((s - top) * (scale * log2e))
        p = p / jnp.sum(p, axis=0, keepdims=True)
        dp = dot_nt(v_h, g_h)
        ds = (p * (dp - jnp.sum(p * dp, axis=0, keepdims=True))).astype(bf16)
        dv.append(dot_nn(p.astype(bf16), g_h))
        dk.append(dot_nn(ds, q_h) * scale)
        dq.append(dot_tn(ds, k_h) * scale)
    grad_q[...] = jnp.concatenate(dq, axis=1).astype(bf16)
    grad_kv[:, :D] = jnp.concatenate(dk, axis=1).astype(bf16)
    grad_kv[:, D:] = jnp.concatenate(dv, axis=1).astype(bf16)


def cross_backward(cap_t, cap_q, q, k, v, g):
    return pl.pallas_call(
        cross_backward_body,
        out_shape=[
            jax.ShapeDtypeStruct((TOK, D), bf16),
            jax.ShapeDtypeStruct((TXT, 2 * D), bf16),
        ],
        compiler_params=params(),
    )(cap_t, cap_q, q, k, v, g)


def fetch_pair(core, mine, other, first, second, sem, column=0):
    def run(a, b):
        columns = pl.ds(column, D)
        one = pltpu.make_async_copy(a.at[:, columns], first, sem.at[0])
        two = pltpu.make_async_copy(b.at[:, columns], second, sem.at[1])
        one.start()
        two.start()
        one.wait()
        two.wait()

    @pl.when(core[0] == 0)
    def _():
        run(mine, other)

    @pl.when(core[0] != 0)
    def _():
        run(other, mine)


def fetch_windows(core, mine, other, whole, sem):
    def run(a, b):
        one = pltpu.make_async_copy(
            a.at[:, pl.ds(2 * D, WIN)], whole.at[:, pl.ds(0, WIN)], sem.at[0]
        )
        two = pltpu.make_async_copy(
            b.at[:, pl.ds(2 * D + 128, STEP)], whole.at[:, pl.ds(WIN, STEP)], sem.at[1]
        )
        one.start()
        two.start()
        one.wait()
        two.wait()

    @pl.when(core[0] == 0)
    def _():
        run(mine, other)

    @pl.when(core[0] != 0)
    def _():
        run(other, mine)


def mlp_body(parts, count, core, *refs):
    xs, gs = refs[: parts * count], refs[parts * count : 2 * parts * count]
    mine, other = refs[2 * parts * count : 2 * parts * count + 2]
    outs = refs[2 * parts * count + 2 : -3]
    up, down, sem = refs[-3:]
    fetch_pair(core, mine, other, up, down, sem)
    for k in range(count):
        x = jnp.concatenate([r[...] for r in xs[parts * k : parts * (k + 1)]], axis=0)
        g = jnp.concatenate([r[...] for r in gs[parts * k : parts * (k + 1)]], axis=0)
        out, act_out, pre_out, grad_x = outs[4 * k : 4 * (k + 1)]
        pre = dot_nn(x, up[...])
        grad_act = dot_nt(g, down[...])
        cdf = 0.5 * (1.0 + lax.erf(pre * (0.5**0.5)))
        density = jnp.exp2(pre * pre * (-0.5 * log2e)) * 0.3989422804014327
        act = (pre * cdf).astype(bf16)
        grad_pre = (grad_act * (cdf + pre * density)).astype(bf16)
        act_out[...] = act
        pre_out[...] = grad_pre
        out[...] = dot_nn(act, down[...]).astype(out.dtype)
        grad_x[...] = dot_nt(grad_pre, up[...]).astype(grad_x.dtype)


def mlp(core, xs, gs, mine, other):
    parts = TOK // xs[0].shape[0]
    count = len(xs) // parts
    vmem = pl.BlockSpec(memory_space=pltpu.VMEM)
    hbm = pl.BlockSpec(memory_space=pl.ANY)
    return pl.pallas_call(
        functools.partial(mlp_body, parts, count),
        in_specs=[pl.BlockSpec(memory_space=pltpu.SMEM)]
        + [vmem] * (2 * parts * count)
        + [hbm, hbm],
        out_specs=[vmem] * (4 * count),
        out_shape=[jax.ShapeDtypeStruct((TOK, D), bf16)] * (4 * count),
        scratch_shapes=[
            pltpu.VMEM((D, D), bf16),
            pltpu.VMEM((D, D), bf16),
            pltpu.SemaphoreType.DMA((2,)),
        ],
        compiler_params=params(),
    )(core, *xs, *gs, mine, other)


def mlp_grad_body(which, core, *refs):
    out = refs[16]

    def run(xs, gs):
        out[...] = sum(dot_tn(x[...], g[...]) for x, g in zip(xs, gs)).astype(bf16)

    @pl.when(core[0] == which)
    def _():
        run(refs[:4], refs[4:8])

    @pl.when(core[0] != which)
    def _():
        run(refs[8:12], refs[12:16])


def mlp_grad(which, core, xs, pres, acts, gs):
    whole = [pl.BlockSpec((TOK, D), lambda k: (0, 0))] * 4
    part = [pl.BlockSpec((TOK, 384), lambda k: (0, k))] * 4
    return pl.pallas_call(
        functools.partial(mlp_grad_body, which),
        grid=(3,),
        in_specs=[pl.BlockSpec(memory_space=pltpu.SMEM)] + whole + part + whole + part,
        out_specs=pl.BlockSpec((D, 384), lambda k: (0, k)),
        out_shape=jax.ShapeDtypeStruct((D, D), bf16),
        compiler_params=params(),
    )(core, *xs, *pres, *acts, *gs)


def sort_hidden_body(core, mine, other, up, down):
    def run(ups, downs):
        for f in range(8):
            lanes = slice(SHARD * f, SHARD * (f + 1))
            up[:, 4 * SHARD * f : 4 * SHARD * (f + 1)] = jnp.concatenate(
                [ups[SHARD * z : SHARD * (z + 1), lanes] for z in range(4)], axis=1
            ).astype(f32)
        down[...] = downs[...].astype(f32)

    @pl.when(core[0] == 0)
    def _():
        run(mine, other)

    @pl.when(core[0] != 0)
    def _():
        run(other, mine)


def sort_hidden(core, mine, other):
    vmem = pl.BlockSpec(memory_space=pltpu.VMEM)
    return pl.pallas_call(
        sort_hidden_body,
        in_specs=[pl.BlockSpec(memory_space=pltpu.SMEM), vmem, vmem],
        out_specs=[vmem, vmem],
        out_shape=[
            jax.ShapeDtypeStruct((SHARD, FF), f32),
            jax.ShapeDtypeStruct((4 * SHARD, D), f32),
        ],
        compiler_params=params(),
    )(core, mine, other)


def normalize(x):
    center = x - jnp.mean(x, axis=-1, keepdims=True)
    inverse = lax.rsqrt(jnp.mean(center * center, axis=-1, keepdims=True) + norm_eps)
    return center * inverse, inverse


def norm_back(x, g, gain):
    plain, inverse = normalize(x)
    scaled = g * gain
    mixed = jnp.mean(scaled * plain, axis=-1, keepdims=True)
    grad = inverse * (scaled - jnp.mean(scaled, axis=-1, keepdims=True) - plain * mixed)
    sums = [jnp.sum(g * plain, axis=0, keepdims=True), jnp.sum(g, axis=0, keepdims=True)]
    return grad, sums


def call(body, ins, outs, scratch):
    spaces = {"vmem": pltpu.VMEM, "hbm": pl.ANY, "smem": pltpu.SMEM}
    return pl.pallas_call(
        body,
        in_specs=[pl.BlockSpec(memory_space=spaces[where]) for _, where in ins],
        out_specs=[pl.BlockSpec(memory_space=pltpu.VMEM)] * len(outs),
        out_shape=[jax.ShapeDtypeStruct(*o) for o in outs],
        scratch_shapes=scratch,
        compiler_params=params(),
    )(*[x for x, _ in ins])


def square_scratch(count):
    return [pltpu.VMEM((D, D), bf16)] * count + [pltpu.SemaphoreType.DMA((2,))]


def after_self_body(core, x, mixed, gain, bias, mine, other, total, normed, query, w1, w2, sem):
    fetch_pair(core, mine, other, w1, w2, sem)
    rows = x[...].astype(f32) + dot_nn(mixed[...], w1[...])
    total[...] = rows
    low = (normalize(rows)[0] * gain[...] + bias[...]).astype(bf16)
    normed[...] = low
    query[...] = dot_nn(low, w2[...]).astype(bf16)


def text_keys_body(core, context, mine, other, key, value, w1, w2, sem):
    fetch_pair(core, mine, other, w1, w2, sem, D)
    key[...] = dot_nn(context[...], w1[...]).astype(bf16)
    value[...] = dot_nn(context[...], w2[...]).astype(bf16)


def after_cross_body(core, x, mixed, gain, bias, mine, other, total, normed, w, sem):
    fetch_windows(core, mine, other, w, sem)
    rows = x[...] + dot_nn(mixed[...], w[...])
    total[...] = rows
    normed[...] = (normalize(rows)[0] * gain[...] + bias[...]).astype(bf16)


def third_back_body(core, x, g0, g1, g2, cot, gain, mine, other, grad, low, mixed, sums, w, sem):
    fetch_windows(core, mine, other, w, sem)
    g = g0[...].astype(f32) + g1[...].astype(f32) + g2[...].astype(f32)
    back, both = norm_back(x[...], g, gain[...])
    total = cot[...] + back
    grad[...] = total
    low[...] = total.astype(bf16)
    mixed[...] = dot_nt(total.astype(bf16), w[...]).astype(bf16)
    sums[...] = jnp.concatenate(both + [jnp.zeros((6, D), f32)], axis=0)


def second_back_body(core, x, gq, before, gain, mine, other, grad, low, mixed, sums, w1, w2, sem):
    fetch_pair(core, mine, other, w1, w2, sem)
    back, both = norm_back(x[...], dot_nt(gq[...], w2[...]), gain[...])
    total = before[...] + back
    grad[...] = total
    low[...] = total.astype(bf16)
    mixed[...] = dot_nt(total.astype(bf16), w1[...]).astype(bf16)
    sums[...] = jnp.concatenate(both + [jnp.zeros((6, D), f32)], axis=0)


def first_back_body(x, *refs):
    before, gain, grad = refs[SPLIT:]
    size = TOK // SPLIT
    sums = []
    for parts in refs[:SPLIT]:
        g = parts[:size, :].astype(f32)
        for k in range(1, 8):
            g = g + parts[size * k : size * (k + 1), :].astype(f32)
        sums.append(g)
    g = jnp.concatenate(sums, axis=0)
    grad[...] = before[...] + norm_back(x[...].astype(f32), g, gain[...])[0]


def text_back_body(
    core, kv, cols, text, w_text, mine, other, part, grad_text, grad_kv, w1, w2, sem
):
    fetch_pair(core, mine, other, w1, w2, sem, D)
    low = (dot_nt(kv[:, :D], w1[...]) + dot_nt(kv[:, D:], w2[...])).astype(bf16)
    part[...] = dot_nt(low, w_text[...]).astype(bf16)
    grad_text[...] = dot_tn(text[...], low).astype(bf16)
    grad_kv[...] = dot_tn(cols[...], kv[...]).astype(bf16)


def first_part_body(g, w, plain, *refs):
    rows = dot_nt(g[...], w[...])
    sums = refs[-1]
    size = TOK // SPLIT
    for k in range(SPLIT):
        refs[k][...] = rows[size * k : size * (k + 1)].astype(bf16)
    both = [
        jnp.sum(rows * plain[...].astype(f32), axis=0, keepdims=True),
        jnp.sum(rows, axis=0, keepdims=True),
        jnp.zeros((6, D), f32),
    ]
    both = jnp.concatenate(both, axis=0)

    @pl.when(pl.program_id(0) == 0)
    def _():
        sums[...] = both

    @pl.when(pl.program_id(0) != 0)
    def _():
        sums[...] += both


def first_part(g, w, plain):
    return pl.pallas_call(
        first_part_body,
        grid=(ROW // TOK,),
        in_specs=[
            pl.BlockSpec((TOK, 6 * SLOT), lambda i: (i, 0)),
            pl.BlockSpec((D, 6 * SLOT), lambda i: (0, 0)),
            pl.BlockSpec((TOK, D), lambda i: (i, 0)),
        ],
        out_specs=[
            *[pl.BlockSpec((TOK // SPLIT, D), lambda i: (i, 0))] * SPLIT,
            pl.BlockSpec((8, D), lambda i: (0, 0)),
        ],
        out_shape=[jax.ShapeDtypeStruct((ROW // SPLIT, D), bf16)] * SPLIT
        + [jax.ShapeDtypeStruct((8, D), f32)],
        cost_estimate=cost(11),
        compiler_params=params(),
    )(g, w, plain)


def heads_grad_body(x, g, out):
    grad = dot_tn(x[...], g[...]).astype(bf16)
    out[...] = jnp.concatenate(
        [
            grad[:, SLOT * (3 * h + k) : SLOT * (3 * h + k) + HEAD]
            for k in range(3)
            for h in range(2)
        ],
        axis=1,
    )


def heads_grad(x, g):
    return pl.pallas_call(
        heads_grad_body,
        grid=(3,),
        in_specs=[
            pl.BlockSpec((ROW, 384), lambda i: (0, i)),
            pl.BlockSpec((ROW, 6 * SLOT), lambda i: (0, 0)),
        ],
        out_specs=pl.BlockSpec((384, 3 * SHARD), lambda i: (i, 0)),
        out_shape=jax.ShapeDtypeStruct((D, 3 * SHARD), bf16),
        cost_estimate=cost(8),
        compiler_params=params(),
    )(x, g)


def unpack_heads_body(x, out):
    for k in range(3):
        out[SHARD * k : SHARD * (k + 1), :] = jnp.concatenate(
            [x[SHARD * p : SHARD * (p + 1), SHARD * k : SHARD * (k + 1)] for p in range(8)], axis=1
        )


def unpack_heads(x):
    return pl.pallas_call(
        unpack_heads_body,
        out_shape=jax.ShapeDtypeStruct((3 * SHARD, D), bf16),
        compiler_params=params(),
    )(x)


def row_block(x, index, rows):
    return lax.dynamic_slice_in_dim(x, index * rows, rows, axis=0)


def core_window(x, core):
    return lax.dynamic_slice_in_dim(x, core * STEP, WIN, axis=1)


def both_cores(x):
    return jnp.concatenate([x, shift(x, "c", 1)], axis=0)


def window_grad(left, right):
    core = lax.axis_index("c")
    sent = shift(core_window(right, 1 - core), "c", 1)
    rights = jnp.concatenate([core_window(right, core), sent], axis=0)
    return dot_tn(both_cores(left), rights).astype(bf16)


def sum_over(x, *axes):
    for axis in axes:
        n = lax.axis_size(axis)
        x = sum([shift(x, axis, k) for k in range(1, n)], x)
    return x


def local(
    tokens,
    text_states,
    seg_lengths,
    caption_of_segment,
    text_lengths,
    ln1_gain,
    ln1_bias,
    w_query,
    w_key,
    w_value,
    w_out,
    ln2_gain,
    ln2_bias,
    c_query,
    w_text,
    c_key,
    c_value,
    c_out,
    ln3_gain,
    ln3_bias,
    w_up,
    w_down,
    cotangent,
):
    core = lax.axis_index("c")
    first_core = core == 0
    core_index = core.astype(jnp.int32)[None]
    quarter = lax.axis_index("z")
    first_row = peer(0, 0) * TOK

    ends = jnp.cumsum(seg_lengths[0])
    positions = jnp.arange(ROW, dtype=jnp.int32)
    segment = jnp.sum((positions[:, None] >= ends[None, :]).astype(jnp.int32), axis=1)
    own_segment = lax.dynamic_slice_in_dim(segment, first_row, TOK)
    text_row = jnp.arange(TXT, dtype=jnp.int32)
    text_pos = text_row // TXT_OWN * CAP_TOK + text_row % TXT_OWN
    text_caption = text_pos // CAP_LEN
    live = jnp.sum(
        jnp.where(
            text_caption[:, None] == jnp.arange(CAPS, dtype=jnp.int32)[None, :],
            text_lengths[0][None, :],
            0,
        ),
        axis=1,
    )
    query_caption = jnp.sum(
        jnp.where(
            own_segment[:, None] == jnp.arange(SEGS, dtype=jnp.int32)[None, :],
            caption_of_segment[0][None, :],
            0,
        ),
        axis=1,
    )
    text_live = (text_row % TXT_OWN < CAP_TOK) & (text_pos % CAP_LEN < live)
    text_key = jnp.where(text_live, text_caption, -1)

    def row(x):
        return x[None, :]

    gap = jnp.zeros((SHARD, 128), bf16)
    square_pack = jnp.where(
        first_core,
        jnp.concatenate([w_out, c_key, c_out[:, :WIN], gap], axis=1),
        jnp.concatenate([c_query, c_value, c_out[:, STEP:], gap], axis=1),
    )
    square_pack = lax.dynamic_slice_in_dim(square_pack, quarter * QUARTER, QUARTER, axis=1)
    quarter_own = lax.all_gather(square_pack, FS, axis=0, tiled=True)

    rows_in = tokens[0]
    plain = normalize(rows_in.astype(f32))[0].astype(bf16)
    n01, n10, n30 = gather_first(plain)

    heads_pack = pack_heads(after(w_query, plain), w_key, w_value)
    n01, n10, n30, heads_pack = lax.optimization_barrier((n01, n10, n30, heads_pack))
    heads_w = peers_parts(heads_pack)
    n31, n20, n11 = gather_second(n01, n10)

    n31, n20, n11 = lax.optimization_barrier((n31, n20, n11))
    n21 = gather_third(n31, n11)
    plain_all, normed_all = place_rows(
        plain,
        (n01, n10, n30),
        (n31, n20, n11),
        n21,
        row(ln1_gain),
        row(ln1_bias),
    )
    heads_w = spread_heads(heads_w)
    quarter_own, normed_all, heads_w = lax.optimization_barrier((quarter_own, normed_all, heads_w))
    quarter_minus, quarter_plus = shift(quarter_own, "z", 1), shift(quarter_own, "z", -1)

    text_own = jnp.pad(after(text_states[0], normed_all), ((0, TXT_OWN - CAP_TOK), (0, 0)))
    text_columns = lax.all_to_all(text_own, FS, split_axis=1, concat_axis=0, tiled=True)

    up_own = jnp.concatenate(
        [
            lax.dynamic_slice(w_up, (0, 4 * SHARD * k + SHARD * quarter), (SHARD, SHARD))
            for k in range(8)
        ],
        axis=1,
    )
    hidden_own = jnp.where(first_core, up_own, row_block(w_down, quarter, SHARD))

    seg_col, seg_row = segment[:, None], segment[None, :]
    qkv = dot_nn(normed_all, heads_w).astype(bf16)
    text_columns, qkv = lax.optimization_barrier((text_columns, qkv))
    context_part = dot_nn(text_columns, w_text).astype(bf16)
    context_own = lax.psum_scatter(context_part, FS, scatter_dimension=0, tiled=True)
    head0, total0 = self_forward(0, seg_col, seg_row, after(qkv, context_part))
    head1, total1 = self_forward(1, seg_col, seg_row, after(qkv, head0))
    hidden_mine = every_peer(after(hidden_own, text_columns))
    quarter_minus, quarter_plus, hidden_mine, head1 = lax.optimization_barrier(
        (quarter_minus, quarter_plus, hidden_mine, head1)
    )
    quarter_far = (
        shift(halves(quarter_minus)[0], "z", 1),
        shift(halves(quarter_plus)[1], "z", -1),
    )
    attended = lax.all_to_all(
        jnp.concatenate([head0, head1], axis=1), FS, split_axis=0, concat_axis=1, tiled=True
    )
    attended, context_own, *quarter_far = lax.optimization_barrier(
        (attended, context_own, *quarter_far)
    )
    context = every_peer(context_own)
    square_mine = place_quarters(quarter_own, quarter_minus, quarter_plus, *quarter_far)
    square_other = shift(square_mine, "c", 1)
    grad_out = cotangent[0]
    grad_mlp = grad_out.astype(bf16)
    grad_sent = after(grad_mlp, square_mine)
    mlp_minus, mlp_plus = shift(grad_sent, "z", 1), shift(grad_sent, "z", -1)

    after_self, normed_two, cross_query = call(
        after_self_body,
        [
            (core_index, "smem"), (rows_in, "vmem"), (attended, "vmem"),
            (row(ln2_gain), "vmem"), (row(ln2_bias), "vmem"),
            (square_mine, "hbm"), (square_other, "hbm"),
        ],
        [((TOK, D), f32), ((TOK, D), bf16), ((TOK, D), bf16)],
        square_scratch(2),
    )
    cross_key, cross_value = call(
        text_keys_body,
        [
            (core_index, "smem"), (after(context, cross_query, mlp_minus, mlp_plus), "vmem"),
            (square_mine, "hbm"), (square_other, "hbm"),
        ],
        [((TXT, D), bf16), ((TXT, D), bf16)],
        square_scratch(2),
    )
    cross_mixed = cross_forward(
        query_caption[:, None], text_key[None, :], cross_query, cross_key, cross_value
    )
    hidden_mine = after(hidden_mine, cross_mixed)
    weights = (hidden_mine, shift(hidden_mine, "c", 1))
    after_cross, normed_three = call(
        after_cross_body,
        [
            (core_index, "smem"), (after_self, "vmem"), (cross_mixed, "vmem"),
            (row(ln3_gain), "vmem"), (row(ln3_bias), "vmem"),
            (square_mine, "hbm"), (square_other, "hbm"),
        ],
        [((TOK, D), f32), ((TOK, D), bf16)],
        square_scratch(1),
    )

    mlp_sent = lax.optimization_barrier((mlp_minus, mlp_plus, cross_query))
    mlp_far = (
        shift(halves(mlp_sent[0])[0], "z", 1),
        shift(halves(mlp_sent[1])[1], "z", -1),
    )

    three_minus, three_plus = shift(normed_three, "z", 1), shift(normed_three, "z", -1)
    out_own, act_own, pre_own, back_own = mlp(core_index, (normed_three,), (grad_mlp,), *weights)
    three_minus, three_plus, out_own = lax.optimization_barrier(
        (three_minus, three_plus, out_own)
    )
    three_far = (
        shift(halves(three_minus)[0], "z", 1),
        shift(halves(three_plus)[1], "z", -1),
    )
    near = mlp(core_index, (three_minus, three_plus), (mlp_minus, mlp_plus), *weights)
    out_m, act_m, pre_m, back_m, out_p, act_p, pre_p, back_p = near
    *three_far, out_m = lax.optimization_barrier((*three_far, out_m))
    out_far, act_far, pre_far, back_far = mlp(core_index, three_far, mlp_far, *weights)
    back_minus, back_plus = reduce_z(back_far, back_m, back_p)
    three_parts = (normed_three, three_minus, three_plus, jnp.concatenate(three_far, axis=0))
    pre_parts = (pre_own, pre_m, pre_p, pre_far)
    act_parts = (act_own, act_m, act_p, act_far)
    mlp_parts = (grad_mlp, mlp_minus, mlp_plus, jnp.concatenate(mlp_far, axis=0))
    send = mlp_grad(1, core_index, three_parts, pre_parts, act_parts, mlp_parts)
    back_minus, back_plus, send = lax.optimization_barrier((back_minus, back_plus, send))
    back_minus, back_plus = shift(back_minus, "z", -1), shift(back_plus, "z", 1)
    keep = mlp_grad(
        0, core_index, three_parts, pre_parts, act_parts, (after(grad_mlp, send), *mlp_parts[1:])
    )
    back_minus, back_plus, keep = lax.optimization_barrier((back_minus, back_plus, keep))
    hidden_sum = keep + shift(send, "c", 1)
    grad_after_cross, grad_cross_branch, grad_cross_mixed, sums_three = call(
        third_back_body,
        [
            (core_index, "smem"), (after_cross, "vmem"), (back_own, "vmem"),
            (back_minus, "vmem"), (back_plus, "vmem"), (grad_out, "vmem"),
            (after(row(ln3_gain), hidden_sum), "vmem"), (square_mine, "hbm"), (square_other, "hbm"),
        ],
        [((TOK, D), f32), ((TOK, D), bf16), ((TOK, D), bf16), ((8, D), f32)],
        square_scratch(1),
    )

    grad_cquery_rows, grad_kv = cross_backward(
        text_key[:, None],
        query_caption[None, :],
        cross_query,
        cross_key,
        cross_value,
        grad_cross_mixed,
    )
    kv_own = lax.psum_scatter(grad_kv, FS, scatter_dimension=0, tiled=True)
    grad_after_self, grad_self_branch, grad_attended, sums_two = call(
        second_back_body,
        [
            (core_index, "smem"), (after_self, "vmem"), (grad_cquery_rows, "vmem"),
            (grad_after_cross, "vmem"), (row(ln2_gain), "vmem"),
            (square_mine, "hbm"), (square_other, "hbm"),
        ],
        [((TOK, D), f32), ((TOK, D), bf16), ((TOK, D), bf16), ((8, D), f32)],
        square_scratch(2),
    )
    grad_heads = lax.all_to_all(grad_attended, FS, split_axis=1, concat_axis=0, tiled=True)

    square = jnp.concatenate(
        [
            window_grad(cross_mixed, after(grad_cross_branch, grad_attended)),
            window_grad(normed_two, after(grad_cquery_rows, grad_attended)),
            window_grad(attended, grad_self_branch),
        ],
        axis=1,
    )

    def square_chunk(dy, dx):
        return row_block(square, peer(dy, dx), SHARD)

    grad_heads, square = lax.optimization_barrier((grad_heads, square))
    grad_qkv = self_backward(0, seg_col, seg_row, total0, qkv, grad_heads)
    kv_own, square, grad_qkv = lax.optimization_barrier((kv_own, square, grad_qkv))
    s_lo, s_hi, s20 = reduce_first(square_chunk)
    kv_all = every_peer(kv_own)
    hidden_grad = lax.psum_scatter(after(hidden_sum, kv_own), FS, scatter_dimension=0, tiled=True)
    out_minus, out_plus = reduce_z(after(out_far, grad_qkv), out_m, out_p)
    grad_qkv = self_backward(
        1, seg_col, seg_row, total1, qkv, after(grad_heads, kv_own), (grad_qkv,)
    )
    s_lo, s_hi, s20, out_minus, out_plus, grad_qkv = lax.optimization_barrier(
        (s_lo, s_hi, s20, out_minus, out_plus, grad_qkv)
    )
    s11, s31 = reduce_second(square_chunk, s_lo, s_hi)

    heads_own = heads_grad(normed_all, grad_qkv)
    heads_own, kv_all = lax.optimization_barrier((heads_own, kv_all))
    heads_part = peers_parts(heads_own)
    part, sums_one = first_part(after(grad_qkv, heads_own), heads_w, plain_all)
    part, heads_part, kv_all, hidden_grad, s11, s31 = lax.optimization_barrier(
        (part, heads_part, kv_all, hidden_grad, s11, s31)
    )
    sent = peers_parts(part)
    square_parts = reduce_third(square_chunk, s20, s11, s31)

    square = reduce_last(square_chunk, *square_parts).astype(bf16)
    heads_rows = unpack_heads(heads_part)
    early = row_block(heads_rows, core, 216) + shift(row_block(heads_rows, 1 - core, 216), "c", 1)
    early = jnp.concatenate([early, jnp.zeros((256 - 216, D), bf16)], axis=0)
    square = jnp.concatenate([square[:, WIN * k : WIN * (k + 1)] for k in range(3)], axis=0)
    square = jnp.concatenate([square[:216], square[216:]], axis=1)
    early = jnp.concatenate(
        [early, jnp.concatenate([square, jnp.zeros((256 - 216, 2 * WIN), bf16)], axis=0)], axis=1
    )
    early = lax.psum_scatter(early, "z", scatter_dimension=0, tiled=True)
    norms = jnp.concatenate([sums_one[:2], sums_two[:2], sums_three[:2], jnp.zeros((2, D), f32)])
    norms = sum_over(norms, "z", "c")
    own_columns = lax.dynamic_slice_in_dim(context, peer(0, 0) * SHARD, SHARD, axis=1)
    text_part, grad_w_text, grad_w_kv = call(
        text_back_body,
        [
            (core_index, "smem"), (kv_all, "vmem"), (own_columns, "vmem"),
            (text_columns, "vmem"), (w_text, "vmem"),
            (square_mine, "hbm"), (square_other, "hbm"),
        ],
        [((TXT, TXT), bf16), ((TXT, D), bf16), ((SHARD, 2 * D), bf16)],
        square_scratch(2),
    )

    def half(which):
        kv = jnp.where(which == 0, grad_w_kv[:, :D], grad_w_kv[:, D:])
        return jnp.concatenate(
            [row_block(grad_w_text, which, 256), kv, jnp.zeros((448 - 400, D), bf16)], axis=0
        )

    late = half(core) + shift(half(1 - core), "c", 1)
    late = lax.psum_scatter(late, "z", scatter_dimension=0, tiled=True)
    hidden_grad = after(hidden_grad, part)
    hidden_grad = hidden_grad + shift(hidden_grad, "xh", 1)
    part, norms, late = lax.optimization_barrier((sent, norms, late))
    early = after(early, part)
    early = early + shift(early, "xh", 1)
    hidden_grad = in_order(*neighbours(after(hidden_grad, part)))
    grad_w_up, grad_w_down = sort_hidden(core_index, hidden_grad, shift(hidden_grad, "c", 1))

    norms = sum_over(norms, "y", "xl", "xh")
    late = late + shift(late, "xh", 1)
    early = in_order(*neighbours(early))
    late = in_order(*neighbours(late))

    def by_core(x):
        other = shift(x, "c", 1)
        low, high = jnp.where(first_core, x, other), jnp.where(first_core, other, x)
        return low.astype(f32), high.astype(f32)

    low, high = by_core(early)
    grad_w_query = low[:144, :D]
    grad_w_key = jnp.concatenate([low[144:216, :D], high[:72, :D]], axis=0)
    grad_w_value = high[72:216, :D]
    low = jnp.concatenate([low[:216, D : D + WIN], low[:216, D + WIN :]], axis=0)
    high = jnp.concatenate([high[:216, D : D + WIN], high[:216, D + WIN :]], axis=0)
    grad_c_out, grad_c_query, grad_w_out = (
        jnp.concatenate(
            [low[SHARD * k : SHARD * (k + 1)], high[SHARD * k : SHARD * (k + 1), 128:]], axis=1
        )
        for k in range(3)
    )
    low, high = by_core(late)
    grad_w_text = jnp.concatenate([low[:256], high[:256]], axis=0)
    grad_c_key, grad_c_value = low[256:400], high[256:400]
    out_minus, out_plus = shift(out_minus, "z", -1), shift(out_plus, "z", 1)
    outputs = (
        after_cross + out_own.astype(f32) + out_minus.astype(f32) + out_plus.astype(f32)
    )

    grad_tokens = call(
        first_back_body,
        [
            (rows_in, "vmem"), (part, "vmem"), (grad_after_self, "vmem"),
            (row(ln1_gain), "vmem"),
        ],
        [((TOK, D), f32)],
        [],
    )[0]
    grad_text = lax.all_to_all(
        after(text_part, part), FS, split_axis=0, concat_axis=1, tiled=True
    )
    grad_text = grad_text[:CAP_TOK].astype(f32)
    return (
        outputs[None],
        grad_tokens[None],
        grad_text[None],
        norms[0],
        norms[1],
        grad_w_query,
        grad_w_key,
        grad_w_value,
        grad_w_out,
        norms[2],
        norms[3],
        grad_c_query,
        grad_w_text,
        grad_c_key,
        grad_c_value,
        grad_c_out,
        norms[4],
        norms[5],
        grad_w_up,
        grad_w_down,
    )


def solution(mesh):
    split = Mesh(mesh.devices.reshape(2, 4, 2, 4, 2), ("xh", "z", "c", "y", "xl"))
    dp = ("xh", "z", "c")
    rows = P(dp, FS, None)
    per_row = P(dp, None)
    weight = P(FS, None)
    rep = P()
    in_specs = (
        rows, rows, per_row, per_row, per_row,
        rep, rep, weight, weight, weight, weight,
        rep, rep, weight, weight, weight, weight, weight,
        rep, rep, weight, weight, rows,
    )
    out_specs = (
        rows, rows, rows,
        rep, rep, weight, weight, weight, weight,
        rep, rep, weight, weight, weight, weight, weight,
        rep, rep, weight, weight,
    )
    return jax.shard_map(
        local, mesh=split, in_specs=in_specs, out_specs=out_specs, check_vma=False
    )
```

```python
import functools

import jax
import jax.numpy as jnp
from jax import lax
from jax.experimental import pallas as pl
from jax.experimental.pallas import tpu as pltpu
from jax.sharding import Mesh
from jax.sharding import PartitionSpec as P

HEADS = 16
HEAD = 72
D = 1152
FF = 4608
CAP_TOK = 60
TXT_OWN = 64
TXT = 8 * TXT_OWN
TOK = 256
ROW = 2048
CAP_LEN = 120
SEGS = 3
CAPS = 4
SHARD = 144
SLOT = 128
SPLIT = 1
WIN = 640
STEP = 512

bf16 = jnp.bfloat16
f32 = jnp.float32
norm_eps = 1e-06
masked_score = -1e30
scale = HEAD ** (-0.5)
log2e = 1.4426950408889634
FS = ("y", "xl")
VMEM = 60 * 1024 * 1024


def dot_nn(a, b):
    return lax.dot_general(a, b, (((1,), (0,)), ((), ())), preferred_element_type=f32)


def dot_nt(a, b):
    return lax.dot_general(a, b, (((1,), (1,)), ((), ())), preferred_element_type=f32)


def dot_tn(a, b):
    return lax.dot_general(a, b, (((0,), (0,)), ((), ())), preferred_element_type=f32)


def params():
    return pltpu.CompilerParams(vmem_limit_bytes=VMEM)


def cost(micros):
    return pl.CostEstimate(flops=int(micros * 1.15e9), bytes_accessed=0, transcendentals=0)


def shift(x, axis, by):
    n = lax.axis_size(axis)
    return lax.ppermute(x, axis, [(i, (i + by) % n) for i in range(n)])


def halves(x):
    h = (x.shape[0] // 2 + 15) // 16 * 16
    return x[:h], x[h:]


def after(x, *others):
    return lax.optimization_barrier((x, *others))[0]


def gather_first(x):
    return shift(x, "xl", 1), shift(x, "y", -1), shift(x, "y", 1)


def gather_second(x01, x10):
    return shift(x01, "y", 1), shift(x10, "y", -1), shift(x10, "xl", 1)


def gather_third(x31, x11):
    return shift(halves(x11)[0], "y", -1), shift(halves(x31)[1], "y", 1)


NEAR = ((0, 0), (0, 1), (1, 0), (3, 0))
NEXT = ((3, 1), (2, 0), (1, 1))
LAST = (2, 1)


def reduce_first(chunk):
    lo, hi = halves(chunk(2, 1))
    return shift(lo, "y", 1), shift(hi, "y", -1), shift(chunk(2, 0), "y", 1)


def reduce_second(chunk, lo, hi):
    h = lo.shape[0]
    c11, c31 = chunk(1, 1), chunk(3, 1)
    c11 = jnp.concatenate([c11[:h] + lo, c11[h:]], axis=0)
    c31 = jnp.concatenate([c31[:h], c31[h:] + hi], axis=0)
    return shift(c11, "xl", 1), shift(c31, "y", -1)


def reduce_third(chunk, c20, c11, c31):
    return (
        shift(chunk(1, 0) + c20 + c11, "y", 1),
        shift(chunk(0, 1) + c31, "xl", 1),
        shift(chunk(3, 0), "y", -1),
    )


def reduce_last(chunk, *parts):
    return sum([p.astype(f32) for p in parts], chunk(0, 0).astype(f32))


def every_peer(x, axes=FS):
    n = lax.axis_size(axes)
    copies = jnp.broadcast_to(x[None], (n, *x.shape)).reshape(n * x.shape[0], x.shape[1])
    return lax.all_to_all(copies, axes, 0, 0, tiled=True)


def peers_parts(x, axes=FS):
    return lax.all_to_all(x, axes, 0, 0, tiled=True)


def sum_parts(parts):
    return jnp.sum(parts.reshape(8, -1, parts.shape[1]).astype(f32), axis=0)


def neighbours(x):
    return x, shift(x, "z", 1), shift(x, "z", 2), shift(x, "z", -1)


def in_order(*around):
    rows, cols = around[0].shape

    def body(where, *refs):
        ins, out = refs[:4], refs[4]
        for k in range(4):
            row = pl.multiple_of(lax.rem(where[0] + 4 - k, 4) * rows, 16)
            out[pl.ds(row, rows), :] = ins[k][...]

    vmem = pl.BlockSpec(memory_space=pltpu.VMEM)
    return pl.pallas_call(
        body,
        in_specs=[pl.BlockSpec(memory_space=pltpu.SMEM)] + [vmem] * 4,
        out_specs=vmem,
        out_shape=jax.ShapeDtypeStruct((4 * rows, cols), bf16),
        compiler_params=params(),
    )(lax.axis_index("z").astype(jnp.int32)[None], *around)


def reduce_z(far, minus, plus):
    lo, hi = halves(far)
    lo, hi = shift(lo, "z", -1), shift(hi, "z", 1)
    h = lo.shape[0]
    return (
        jnp.concatenate([minus[:h] + lo, minus[h:]], axis=0),
        jnp.concatenate([plus[:h], plus[h:] + hi], axis=0),
    )


def peer(dy, dx):
    return ((lax.axis_index("y") + dy) % 4) * 2 + (lax.axis_index("xl") ^ dx)


def place_rows(own, first, second, third, gain, bias):
    lo = third[0].shape[0]
    rows, cols = own.shape
    pieces = [(x, p, 0) for x, p in zip((own, *first), NEAR)]
    pieces += [(x, p, 0) for x, p in zip(second, NEXT)]
    pieces += [(third[0], LAST, 0), (third[1], LAST, lo)]
    count = len(pieces)

    def body(where, gain, bias, *refs):
        ins, plain, normed, sem = refs[:count], refs[count], refs[count + 1], refs[-1]
        started = []
        for k, (x, _, off) in enumerate(pieces):
            row = pl.multiple_of(where[k] * rows + off, 16)
            one = pltpu.make_async_copy(ins[k], plain.at[pl.ds(row, x.shape[0])], sem.at[k])
            one.start()
            started.append(one)
        for one in started:
            one.wait()

        def step(i, carry):
            part = pl.ds(pl.multiple_of(i * rows, rows), rows)
            normed[part, :] = (plain[part, :].astype(f32) * gain[...] + bias[...]).astype(bf16)
            return carry

        lax.fori_loop(0, 8, step, 0)

    vmem = pl.BlockSpec(memory_space=pltpu.VMEM)
    return pl.pallas_call(
        body,
        in_specs=[pl.BlockSpec(memory_space=pltpu.SMEM), vmem, vmem]
        + [pl.BlockSpec(memory_space=pl.ANY)] * count,
        out_specs=[vmem, vmem],
        out_shape=[jax.ShapeDtypeStruct((8 * rows, cols), bf16)] * 2,
        scratch_shapes=[pltpu.SemaphoreType.DMA((count,))],
        compiler_params=params(),
    )(
        jnp.stack([peer(*p) for _, p, _ in pieces]).astype(jnp.int32),
        gain,
        bias,
        *[x for x, _, _ in pieces],
    )


QUARTER = 768


def place_quarters(*quarters):
    def body(where, own, minus, plus, far_lo, far_hi, out, sem):
        started = []
        half = far_lo.shape[0]
        for k, (ref, turn, row) in enumerate(
            ((own, 0, 0), (minus, 3, 0), (plus, 1, 0), (far_lo, 2, 0), (far_hi, 2, half))
        ):
            column = pl.multiple_of(lax.rem(where[0] + turn, 4) * QUARTER, 128)
            one = pltpu.make_async_copy(
                ref, out.at[pl.ds(row, ref.shape[0]), pl.ds(column, QUARTER)], sem.at[k]
            )
            one.start()
            started.append(one)
        for one in started:
            one.wait()

    return pl.pallas_call(
        body,
        in_specs=[pl.BlockSpec(memory_space=pltpu.SMEM)] + [pl.BlockSpec(memory_space=pl.ANY)] * 5,
        out_specs=pl.BlockSpec(memory_space=pltpu.VMEM),
        out_shape=jax.ShapeDtypeStruct((D, 4 * QUARTER), bf16),
        scratch_shapes=[pltpu.SemaphoreType.DMA((5,))],
        compiler_params=params(),
    )(lax.axis_index("z").astype(jnp.int32)[None], *quarters)


def pack_heads_body(wq, wk, wv, out):
    for p in range(8):
        rows = slice(SHARD * p, SHARD * (p + 1))
        out[rows, :] = jnp.concatenate([w[:, rows] for w in (wq, wk, wv)], axis=1)


def pack_heads(*weights):
    return pl.pallas_call(
        pack_heads_body,
        out_shape=jax.ShapeDtypeStruct((D, 3 * SHARD), bf16),
        compiler_params=params(),
    )(*weights)


def spread_heads_body(x, out):
    blank = jnp.zeros((D, SLOT - HEAD), bf16)
    for h in range(2):
        for k in range(3):
            first = SHARD * k + HEAD * h
            slot = SLOT * (3 * h + k)
            out[:, slot : slot + SLOT] = jnp.concatenate(
                [x[:, first : first + HEAD], blank], axis=1
            )


def spread_heads(x):
    return pl.pallas_call(
        spread_heads_body,
        out_shape=jax.ShapeDtypeStruct((D, 6 * SLOT), bf16),
        compiler_params=params(),
    )(x)


def self_forward_body(seg_q, seg_k, q, kv, out, total):
    s = dot_nt(q[:, :SLOT], kv[:, SLOT : 2 * SLOT])
    s = jnp.where(seg_q[...] == seg_k[...], s, masked_score)
    top = jnp.max(s, axis=1, keepdims=True)
    p = jnp.exp2((s - top) * (scale * log2e))
    mass = jnp.sum(p, axis=1, keepdims=True)
    out[...] = (dot_nn(p.astype(bf16), kv[:, 2 * SLOT :]) / mass)[:, :HEAD].astype(bf16)
    log_total = top * (scale * log2e) + jnp.log2(mass)
    total[...] = jnp.transpose(jnp.broadcast_to(log_total, (TOK, SLOT)))[0:1, :]


def self_forward(head, seg_q, seg_k, qkv):
    return pl.pallas_call(
        self_forward_body,
        grid=(ROW // TOK,),
        in_specs=[
            pl.BlockSpec((TOK, 1), lambda i: (i, 0)),
            pl.BlockSpec((1, ROW), lambda i: (0, 0)),
            pl.BlockSpec((TOK, 3 * SLOT), lambda i: (i, head)),
            pl.BlockSpec((ROW, 3 * SLOT), lambda i: (0, head)),
        ],
        out_specs=[
            pl.BlockSpec((TOK, HEAD), lambda i: (i, 0)),
            pl.BlockSpec((1, TOK), lambda i: (0, i)),
        ],
        out_shape=[
            jax.ShapeDtypeStruct((ROW, HEAD), bf16),
            jax.ShapeDtypeStruct((1, ROW), f32),
        ],
        compiler_params=params(),
    )(seg_q, seg_k, qkv, qkv)


def self_backward_body(head, seg_k, seg_q, total, q, kv, g, *refs):
    grad, key_sum, value_sum, key_t = refs[-4:]
    i = pl.program_id(0)

    @pl.when(i == 0)
    def _():
        key_sum[...] = jnp.zeros_like(key_sum)
        value_sum[...] = jnp.zeros_like(value_sum)
        key_t[...] = jnp.transpose(kv[:, SLOT : 2 * SLOT])

    rows = pl.ds(pl.multiple_of(i * TOK, TOK), TOK)
    q_h, k_h, v_h = q[:, :SLOT], kv[:, SLOT : 2 * SLOT], kv[:, 2 * SLOT :]
    g_both = g[...]
    g_h = jnp.concatenate(
        [g_both[:, HEAD * head : HEAD * (head + 1)], jnp.zeros((TOK, SLOT - HEAD), bf16)], axis=1
    )
    p = jnp.exp2(dot_nt(k_h, q_h) * (scale * log2e) - total[...])
    p = jnp.where(seg_k[...] == seg_q[...], p, 0.0)
    dp = dot_nt(v_h, g_h)
    ds = (p * (dp - jnp.sum(p * dp, axis=0, keepdims=True))).astype(bf16)
    value_sum[...] += dot_nn(p.astype(bf16), g_h)
    key_sum[...] += dot_nn(ds, q_h)
    grad[rows, :SLOT] = (jnp.transpose(dot_nn(key_t[...], ds)) * scale).astype(bf16)

    @pl.when(i == pl.num_programs(0) - 1)
    def _():
        grad[:, SLOT : 2 * SLOT] = (key_sum[...] * scale).astype(bf16)
        grad[:, 2 * SLOT :] = value_sum[...].astype(bf16)


def self_backward(head, seg_k, seg_q, total, qkv, g, before=()):
    return pl.pallas_call(
        functools.partial(self_backward_body, head),
        grid=(ROW // TOK,),
        in_specs=[
            pl.BlockSpec((ROW, 1), lambda i: (0, 0)),
            pl.BlockSpec((1, TOK), lambda i: (0, i)),
            pl.BlockSpec((1, TOK), lambda i: (0, i)),
            pl.BlockSpec((TOK, 3 * SLOT), lambda i: (i, head)),
            pl.BlockSpec((ROW, 3 * SLOT), lambda i: (0, head)),
            pl.BlockSpec((TOK, SHARD), lambda i: (i, 0)),
        ]
        + [pl.BlockSpec(memory_space=pl.ANY)] * len(before),
        out_specs=pl.BlockSpec((ROW, 3 * SLOT), lambda i: (0, head)),
        out_shape=jax.ShapeDtypeStruct((ROW, 6 * SLOT), bf16),
        input_output_aliases={6: 0} if before else {},
        scratch_shapes=[
            pltpu.VMEM((ROW, SLOT), f32),
            pltpu.VMEM((ROW, SLOT), f32),
            pltpu.VMEM((SLOT, ROW), bf16),
        ],
        compiler_params=params(),
    )(seg_k, seg_q, total, qkv, qkv, g, *before)


def cross_forward_body(cap_q, cap_t, q, k, v, out):
    allowed = cap_q[...] == cap_t[...]
    mixed = []
    for h in range(HEADS):
        a, b = HEAD * h, HEAD * (h + 1)
        s = dot_nt(q[:, a:b], k[:, a:b])
        s = jnp.where(allowed, s, masked_score)
        top = jnp.max(s, axis=1, keepdims=True)
        p = jnp.exp2((s - top) * (scale * log2e))
        mass = jnp.sum(p, axis=1, keepdims=True)
        mixed.append(dot_nn(p.astype(bf16), v[:, a:b]) / mass)
    out[...] = jnp.concatenate(mixed, axis=1).astype(bf16)


def cross_forward(cap_q, cap_t, q, k, v):
    return pl.pallas_call(
        cross_forward_body,
        out_shape=jax.ShapeDtypeStruct((TOK, D), bf16),
        compiler_params=params(),
    )(cap_q, cap_t, q, k, v)


def cross_backward_body(cap_t, cap_q, q, k, v, g, grad_q, grad_kv):
    allowed = cap_t[...] == cap_q[...]
    dq, dk, dv = [], [], []
    for h in range(HEADS):
        a, b = HEAD * h, HEAD * (h + 1)
        q_h, k_h, v_h, g_h = q[:, a:b], k[:, a:b], v[:, a:b], g[:, a:b]
        s = jnp.where(allowed, dot_nt(k_h, q_h), masked_score)
        top = jnp.max(s, axis=0, keepdims=True)
        p = jnp.exp2((s - top) * (scale * log2e))
        p = p / jnp.sum(p, axis=0, keepdims=True)
        dp = dot_nt(v_h, g_h)
        ds = (p * (dp - jnp.sum(p * dp, axis=0, keepdims=True))).astype(bf16)
        dv.append(dot_nn(p.astype(bf16), g_h))
        dk.append(dot_nn(ds, q_h) * scale)
        dq.append(dot_tn(ds, k_h) * scale)
    grad_q[...] = jnp.concatenate(dq, axis=1).astype(bf16)
    grad_kv[:, :D] = jnp.concatenate(dk, axis=1).astype(bf16)
    grad_kv[:, D:] = jnp.concatenate(dv, axis=1).astype(bf16)


def cross_backward(cap_t, cap_q, q, k, v, g):
    return pl.pallas_call(
        cross_backward_body,
        out_shape=[
            jax.ShapeDtypeStruct((TOK, D), bf16),
            jax.ShapeDtypeStruct((TXT, 2 * D), bf16),
        ],
        compiler_params=params(),
    )(cap_t, cap_q, q, k, v, g)


def fetch_pair(core, mine, other, first, second, sem, column=0):
    def run(a, b):
        columns = pl.ds(column, D)
        one = pltpu.make_async_copy(a.at[:, columns], first, sem.at[0])
        two = pltpu.make_async_copy(b.at[:, columns], second, sem.at[1])
        one.start()
        two.start()
        one.wait()
        two.wait()

    @pl.when(core[0] == 0)
    def _():
        run(mine, other)

    @pl.when(core[0] != 0)
    def _():
        run(other, mine)


def fetch_windows(core, mine, other, whole, sem):
    def run(a, b):
        one = pltpu.make_async_copy(
            a.at[:, pl.ds(2 * D, WIN)], whole.at[:, pl.ds(0, WIN)], sem.at[0]
        )
        two = pltpu.make_async_copy(
            b.at[:, pl.ds(2 * D + 128, STEP)], whole.at[:, pl.ds(WIN, STEP)], sem.at[1]
        )
        one.start()
        two.start()
        one.wait()
        two.wait()

    @pl.when(core[0] == 0)
    def _():
        run(mine, other)

    @pl.when(core[0] != 0)
    def _():
        run(other, mine)


def mlp_body(parts, count, core, *refs):
    xs, gs = refs[: parts * count], refs[parts * count : 2 * parts * count]
    mine, other = refs[2 * parts * count : 2 * parts * count + 2]
    outs = refs[2 * parts * count + 2 : -3]
    up, down, sem = refs[-3:]
    fetch_pair(core, mine, other, up, down, sem)
    for k in range(count):
        x = jnp.concatenate([r[...] for r in xs[parts * k : parts * (k + 1)]], axis=0)
        g = jnp.concatenate([r[...] for r in gs[parts * k : parts * (k + 1)]], axis=0)
        out, act_out, pre_out, grad_x = outs[4 * k : 4 * (k + 1)]
        pre = dot_nn(x, up[...])
        grad_act = dot_nt(g, down[...])
        cdf = 0.5 * (1.0 + lax.erf(pre * (0.5**0.5)))
        density = jnp.exp2(pre * pre * (-0.5 * log2e)) * 0.3989422804014327
        act = (pre * cdf).astype(bf16)
        grad_pre = (grad_act * (cdf + pre * density)).astype(bf16)
        act_out[...] = act
        pre_out[...] = grad_pre
        out[...] = dot_nn(act, down[...]).astype(out.dtype)
        grad_x[...] = dot_nt(grad_pre, up[...]).astype(grad_x.dtype)


def mlp(core, xs, gs, mine, other):
    parts = TOK // xs[0].shape[0]
    count = len(xs) // parts
    vmem = pl.BlockSpec(memory_space=pltpu.VMEM)
    hbm = pl.BlockSpec(memory_space=pl.ANY)
    return pl.pallas_call(
        functools.partial(mlp_body, parts, count),
        in_specs=[pl.BlockSpec(memory_space=pltpu.SMEM)]
        + [vmem] * (2 * parts * count)
        + [hbm, hbm],
        out_specs=[vmem] * (4 * count),
        out_shape=[jax.ShapeDtypeStruct((TOK, D), bf16)] * (4 * count),
        scratch_shapes=[
            pltpu.VMEM((D, D), bf16),
            pltpu.VMEM((D, D), bf16),
            pltpu.SemaphoreType.DMA((2,)),
        ],
        compiler_params=params(),
    )(core, *xs, *gs, mine, other)


def mlp_grad_body(which, core, *refs):
    out = refs[16]

    def run(xs, gs):
        out[...] = sum(dot_tn(x[...], g[...]) for x, g in zip(xs, gs)).astype(bf16)

    @pl.when(core[0] == which)
    def _():
        run(refs[:4], refs[4:8])

    @pl.when(core[0] != which)
    def _():
        run(refs[8:12], refs[12:16])


def mlp_grad(which, core, xs, pres, acts, gs):
    whole = [pl.BlockSpec((TOK, D), lambda k: (0, 0))] * 4
    part = [pl.BlockSpec((TOK, 384), lambda k: (0, k))] * 4
    return pl.pallas_call(
        functools.partial(mlp_grad_body, which),
        grid=(3,),
        in_specs=[pl.BlockSpec(memory_space=pltpu.SMEM)] + whole + part + whole + part,
        out_specs=pl.BlockSpec((D, 384), lambda k: (0, k)),
        out_shape=jax.ShapeDtypeStruct((D, D), bf16),
        compiler_params=params(),
    )(core, *xs, *pres, *acts, *gs)


def sort_hidden_body(core, mine, other, up, down):
    def run(ups, downs):
        for f in range(8):
            lanes = slice(SHARD * f, SHARD * (f + 1))
            up[:, 4 * SHARD * f : 4 * SHARD * (f + 1)] = jnp.concatenate(
                [ups[SHARD * z : SHARD * (z + 1), lanes] for z in range(4)], axis=1
            ).astype(f32)
        down[...] = downs[...].astype(f32)

    @pl.when(core[0] == 0)
    def _():
        run(mine, other)

    @pl.when(core[0] != 0)
    def _():
        run(other, mine)


def sort_hidden(core, mine, other):
    vmem = pl.BlockSpec(memory_space=pltpu.VMEM)
    return pl.pallas_call(
        sort_hidden_body,
        in_specs=[pl.BlockSpec(memory_space=pltpu.SMEM), vmem, vmem],
        out_specs=[vmem, vmem],
        out_shape=[
            jax.ShapeDtypeStruct((SHARD, FF), f32),
            jax.ShapeDtypeStruct((4 * SHARD, D), f32),
        ],
        compiler_params=params(),
    )(core, mine, other)


def normalize(x):
    center = x - jnp.mean(x, axis=-1, keepdims=True)
    inverse = lax.rsqrt(jnp.mean(center * center, axis=-1, keepdims=True) + norm_eps)
    return center * inverse, inverse


def norm_back(x, g, gain):
    plain, inverse = normalize(x)
    scaled = g * gain
    mixed = jnp.mean(scaled * plain, axis=-1, keepdims=True)
    grad = inverse * (scaled - jnp.mean(scaled, axis=-1, keepdims=True) - plain * mixed)
    sums = [jnp.sum(g * plain, axis=0, keepdims=True), jnp.sum(g, axis=0, keepdims=True)]
    return grad, sums


def call(body, ins, outs, scratch):
    spaces = {"vmem": pltpu.VMEM, "hbm": pl.ANY, "smem": pltpu.SMEM}
    return pl.pallas_call(
        body,
        in_specs=[pl.BlockSpec(memory_space=spaces[where]) for _, where in ins],
        out_specs=[pl.BlockSpec(memory_space=pltpu.VMEM)] * len(outs),
        out_shape=[jax.ShapeDtypeStruct(*o) for o in outs],
        scratch_shapes=scratch,
        compiler_params=params(),
    )(*[x for x, _ in ins])


def square_scratch(count):
    return [pltpu.VMEM((D, D), bf16)] * count + [pltpu.SemaphoreType.DMA((2,))]


def after_self_body(core, x, mixed, gain, bias, mine, other, total, normed, query, w1, w2, sem):
    fetch_pair(core, mine, other, w1, w2, sem)
    rows = x[...].astype(f32) + dot_nn(mixed[...], w1[...])
    total[...] = rows
    low = (normalize(rows)[0] * gain[...] + bias[...]).astype(bf16)
    normed[...] = low
    query[...] = dot_nn(low, w2[...]).astype(bf16)


def text_keys_body(core, context, mine, other, key, value, w1, w2, sem):
    fetch_pair(core, mine, other, w1, w2, sem, D)
    key[...] = dot_nn(context[...], w1[...]).astype(bf16)
    value[...] = dot_nn(context[...], w2[...]).astype(bf16)


def after_cross_body(core, x, mixed, gain, bias, mine, other, total, normed, w, sem):
    fetch_windows(core, mine, other, w, sem)
    rows = x[...] + dot_nn(mixed[...], w[...])
    total[...] = rows
    normed[...] = (normalize(rows)[0] * gain[...] + bias[...]).astype(bf16)


def third_back_body(core, x, g0, g1, g2, cot, gain, mine, other, grad, low, mixed, sums, w, sem):
    fetch_windows(core, mine, other, w, sem)
    g = g0[...].astype(f32) + g1[...].astype(f32) + g2[...].astype(f32)
    back, both = norm_back(x[...], g, gain[...])
    total = cot[...] + back
    grad[...] = total
    low[...] = total.astype(bf16)
    mixed[...] = dot_nt(total.astype(bf16), w[...]).astype(bf16)
    sums[...] = jnp.concatenate(both + [jnp.zeros((6, D), f32)], axis=0)


def second_back_body(core, x, gq, before, gain, mine, other, grad, low, mixed, sums, w1, w2, sem):
    fetch_pair(core, mine, other, w1, w2, sem)
    back, both = norm_back(x[...], dot_nt(gq[...], w2[...]), gain[...])
    total = before[...] + back
    grad[...] = total
    low[...] = total.astype(bf16)
    mixed[...] = dot_nt(total.astype(bf16), w1[...]).astype(bf16)
    sums[...] = jnp.concatenate(both + [jnp.zeros((6, D), f32)], axis=0)


def first_back_body(x, *refs):
    before, gain, grad = refs[SPLIT:]
    size = TOK // SPLIT
    sums = []
    for parts in refs[:SPLIT]:
        g = parts[:size, :].astype(f32)
        for k in range(1, 8):
            g = g + parts[size * k : size * (k + 1), :].astype(f32)
        sums.append(g)
    g = jnp.concatenate(sums, axis=0)
    grad[...] = before[...] + norm_back(x[...].astype(f32), g, gain[...])[0]


def text_back_body(
    core, kv, cols, text, w_text, mine, other, part, grad_text, grad_kv, w1, w2, sem
):
    fetch_pair(core, mine, other, w1, w2, sem, D)
    low = (dot_nt(kv[:, :D], w1[...]) + dot_nt(kv[:, D:], w2[...])).astype(bf16)
    part[...] = dot_nt(low, w_text[...]).astype(bf16)
    grad_text[...] = dot_tn(text[...], low).astype(bf16)
    grad_kv[...] = dot_tn(cols[...], kv[...]).astype(bf16)


def first_part_body(g, w, plain, *refs):
    rows = dot_nt(g[...], w[...])
    sums = refs[-1]
    size = TOK // SPLIT
    for k in range(SPLIT):
        refs[k][...] = rows[size * k : size * (k + 1)].astype(bf16)
    both = [
        jnp.sum(rows * plain[...].astype(f32), axis=0, keepdims=True),
        jnp.sum(rows, axis=0, keepdims=True),
        jnp.zeros((6, D), f32),
    ]
    both = jnp.concatenate(both, axis=0)

    @pl.when(pl.program_id(0) == 0)
    def _():
        sums[...] = both

    @pl.when(pl.program_id(0) != 0)
    def _():
        sums[...] += both


def first_part(g, w, plain):
    return pl.pallas_call(
        first_part_body,
        grid=(ROW // TOK,),
        in_specs=[
            pl.BlockSpec((TOK, 6 * SLOT), lambda i: (i, 0)),
            pl.BlockSpec((D, 6 * SLOT), lambda i: (0, 0)),
            pl.BlockSpec((TOK, D), lambda i: (i, 0)),
        ],
        out_specs=[
            *[pl.BlockSpec((TOK // SPLIT, D), lambda i: (i, 0))] * SPLIT,
            pl.BlockSpec((8, D), lambda i: (0, 0)),
        ],
        out_shape=[jax.ShapeDtypeStruct((ROW // SPLIT, D), bf16)] * SPLIT
        + [jax.ShapeDtypeStruct((8, D), f32)],
        cost_estimate=cost(11),
        compiler_params=params(),
    )(g, w, plain)


def heads_grad_body(x, g, out):
    grad = dot_tn(x[...], g[...]).astype(bf16)
    out[...] = jnp.concatenate(
        [
            grad[:, SLOT * (3 * h + k) : SLOT * (3 * h + k) + HEAD]
            for k in range(3)
            for h in range(2)
        ],
        axis=1,
    )


def heads_grad(x, g):
    return pl.pallas_call(
        heads_grad_body,
        grid=(3,),
        in_specs=[
            pl.BlockSpec((ROW, 384), lambda i: (0, i)),
            pl.BlockSpec((ROW, 6 * SLOT), lambda i: (0, 0)),
        ],
        out_specs=pl.BlockSpec((384, 3 * SHARD), lambda i: (i, 0)),
        out_shape=jax.ShapeDtypeStruct((D, 3 * SHARD), bf16),
        cost_estimate=cost(8),
        compiler_params=params(),
    )(x, g)


def unpack_heads_body(x, out):
    for k in range(3):
        out[SHARD * k : SHARD * (k + 1), :] = jnp.concatenate(
            [x[SHARD * p : SHARD * (p + 1), SHARD * k : SHARD * (k + 1)] for p in range(8)], axis=1
        )


def unpack_heads(x):
    return pl.pallas_call(
        unpack_heads_body,
        out_shape=jax.ShapeDtypeStruct((3 * SHARD, D), bf16),
        compiler_params=params(),
    )(x)


def row_block(x, index, rows):
    return lax.dynamic_slice_in_dim(x, index * rows, rows, axis=0)


def core_window(x, core):
    return lax.dynamic_slice_in_dim(x, core * STEP, WIN, axis=1)


def both_cores(x):
    return jnp.concatenate([x, shift(x, "c", 1)], axis=0)


def window_grad(left, right):
    core = lax.axis_index("c")
    sent = shift(core_window(right, 1 - core), "c", 1)
    rights = jnp.concatenate([core_window(right, core), sent], axis=0)
    return dot_tn(both_cores(left), rights).astype(bf16)


def sum_over(x, *axes):
    for axis in axes:
        n = lax.axis_size(axis)
        x = sum([shift(x, axis, k) for k in range(1, n)], x)
    return x


def local(
    tokens,
    text_states,
    seg_lengths,
    caption_of_segment,
    text_lengths,
    ln1_gain,
    ln1_bias,
    w_query,
    w_key,
    w_value,
    w_out,
    ln2_gain,
    ln2_bias,
    c_query,
    w_text,
    c_key,
    c_value,
    c_out,
    ln3_gain,
    ln3_bias,
    w_up,
    w_down,
    cotangent,
):
    core = lax.axis_index("c")
    first_core = core == 0
    core_index = core.astype(jnp.int32)[None]
    quarter = lax.axis_index("z")
    first_row = peer(0, 0) * TOK

    ends = jnp.cumsum(seg_lengths[0])
    positions = jnp.arange(ROW, dtype=jnp.int32)
    segment = jnp.sum((positions[:, None] >= ends[None, :]).astype(jnp.int32), axis=1)
    own_segment = lax.dynamic_slice_in_dim(segment, first_row, TOK)
    text_row = jnp.arange(TXT, dtype=jnp.int32)
    text_pos = text_row // TXT_OWN * CAP_TOK + text_row % TXT_OWN
    text_caption = text_pos // CAP_LEN
    live = jnp.sum(
        jnp.where(
            text_caption[:, None] == jnp.arange(CAPS, dtype=jnp.int32)[None, :],
            text_lengths[0][None, :],
            0,
        ),
        axis=1,
    )
    query_caption = jnp.sum(
        jnp.where(
            own_segment[:, None] == jnp.arange(SEGS, dtype=jnp.int32)[None, :],
            caption_of_segment[0][None, :],
            0,
        ),
        axis=1,
    )
    text_live = (text_row % TXT_OWN < CAP_TOK) & (text_pos % CAP_LEN < live)
    text_key = jnp.where(text_live, text_caption, -1)

    def row(x):
        return x[None, :]

    gap = jnp.zeros((SHARD, 128), bf16)
    square_pack = jnp.where(
        first_core,
        jnp.concatenate([w_out, c_key, c_out[:, :WIN], gap], axis=1),
        jnp.concatenate([c_query, c_value, c_out[:, STEP:], gap], axis=1),
    )
    square_pack = lax.dynamic_slice_in_dim(square_pack, quarter * QUARTER, QUARTER, axis=1)
    quarter_own = lax.all_gather(square_pack, FS, axis=0, tiled=True)

    rows_in = tokens[0]
    plain = normalize(rows_in.astype(f32))[0].astype(bf16)
    n01, n10, n30 = gather_first(plain)

    heads_pack = pack_heads(after(w_query, plain), w_key, w_value)
    n01, n10, n30, heads_pack = lax.optimization_barrier((n01, n10, n30, heads_pack))
    heads_w = peers_parts(heads_pack)
    n31, n20, n11 = gather_second(n01, n10)

    n31, n20, n11 = lax.optimization_barrier((n31, n20, n11))
    n21 = gather_third(n31, n11)
    plain_all, normed_all = place_rows(
        plain,
        (n01, n10, n30),
        (n31, n20, n11),
        n21,
        row(ln1_gain),
        row(ln1_bias),
    )
    heads_w = spread_heads(heads_w)
    quarter_own, normed_all, heads_w = lax.optimization_barrier((quarter_own, normed_all, heads_w))
    quarter_minus, quarter_plus = shift(quarter_own, "z", 1), shift(quarter_own, "z", -1)

    text_own = jnp.pad(after(text_states[0], normed_all), ((0, TXT_OWN - CAP_TOK), (0, 0)))
    text_columns = lax.all_to_all(text_own, FS, split_axis=1, concat_axis=0, tiled=True)

    up_own = jnp.concatenate(
        [
            lax.dynamic_slice(w_up, (0, 4 * SHARD * k + SHARD * quarter), (SHARD, SHARD))
            for k in range(8)
        ],
        axis=1,
    )
    hidden_own = jnp.where(first_core, up_own, row_block(w_down, quarter, SHARD))

    seg_col, seg_row = segment[:, None], segment[None, :]
    qkv = dot_nn(normed_all, heads_w).astype(bf16)
    text_columns, qkv = lax.optimization_barrier((text_columns, qkv))
    context_part = dot_nn(text_columns, w_text).astype(bf16)
    context_own = lax.psum_scatter(context_part, FS, scatter_dimension=0, tiled=True)
    head0, total0 = self_forward(0, seg_col, seg_row, after(qkv, context_part))
    head1, total1 = self_forward(1, seg_col, seg_row, after(qkv, head0))
    hidden_mine = every_peer(after(hidden_own, text_columns))
    quarter_minus, quarter_plus, hidden_mine, head1 = lax.optimization_barrier(
        (quarter_minus, quarter_plus, hidden_mine, head1)
    )
    quarter_far = (
        shift(halves(quarter_minus)[0], "z", 1),
        shift(halves(quarter_plus)[1], "z", -1),
    )
    attended = lax.all_to_all(
        jnp.concatenate([head0, head1], axis=1), FS, split_axis=0, concat_axis=1, tiled=True
    )
    attended, context_own, *quarter_far = lax.optimization_barrier(
        (attended, context_own, *quarter_far)
    )
    context = every_peer(context_own)
    square_mine = place_quarters(quarter_own, quarter_minus, quarter_plus, *quarter_far)
    square_other = shift(square_mine, "c", 1)
    grad_out = cotangent[0]
    grad_mlp = grad_out.astype(bf16)
    grad_sent = after(grad_mlp, square_mine)
    mlp_minus, mlp_plus = shift(grad_sent, "z", 1), shift(grad_sent, "z", -1)

    after_self, normed_two, cross_query = call(
        after_self_body,
        [
            (core_index, "smem"), (rows_in, "vmem"), (attended, "vmem"),
            (row(ln2_gain), "vmem"), (row(ln2_bias), "vmem"),
            (square_mine, "hbm"), (square_other, "hbm"),
        ],
        [((TOK, D), f32), ((TOK, D), bf16), ((TOK, D), bf16)],
        square_scratch(2),
    )
    cross_key, cross_value = call(
        text_keys_body,
        [
            (core_index, "smem"), (after(context, cross_query, mlp_minus, mlp_plus), "vmem"),
            (square_mine, "hbm"), (square_other, "hbm"),
        ],
        [((TXT, D), bf16), ((TXT, D), bf16)],
        square_scratch(2),
    )
    cross_mixed = cross_forward(
        query_caption[:, None], text_key[None, :], cross_query, cross_key, cross_value
    )
    hidden_mine = after(hidden_mine, cross_mixed)
    weights = (hidden_mine, shift(hidden_mine, "c", 1))
    after_cross, normed_three = call(
        after_cross_body,
        [
            (core_index, "smem"), (after_self, "vmem"), (cross_mixed, "vmem"),
            (row(ln3_gain), "vmem"), (row(ln3_bias), "vmem"),
            (square_mine, "hbm"), (square_other, "hbm"),
        ],
        [((TOK, D), f32), ((TOK, D), bf16)],
        square_scratch(1),
    )

    mlp_sent = lax.optimization_barrier((mlp_minus, mlp_plus, cross_query))
    mlp_far = (
        shift(halves(mlp_sent[0])[0], "z", 1),
        shift(halves(mlp_sent[1])[1], "z", -1),
    )

    three_minus, three_plus = shift(normed_three, "z", 1), shift(normed_three, "z", -1)
    out_own, act_own, pre_own, back_own = mlp(core_index, (normed_three,), (grad_mlp,), *weights)
    three_minus, three_plus, out_own = lax.optimization_barrier(
        (three_minus, three_plus, out_own)
    )
    three_far = (
        shift(halves(three_minus)[0], "z", 1),
        shift(halves(three_plus)[1], "z", -1),
    )
    near = mlp(core_index, (three_minus, three_plus), (mlp_minus, mlp_plus), *weights)
    out_m, act_m, pre_m, back_m, out_p, act_p, pre_p, back_p = near
    *three_far, out_m = lax.optimization_barrier((*three_far, out_m))
    out_far, act_far, pre_far, back_far = mlp(core_index, three_far, mlp_far, *weights)
    back_minus, back_plus = reduce_z(back_far, back_m, back_p)
    three_parts = (normed_three, three_minus, three_plus, jnp.concatenate(three_far, axis=0))
    pre_parts = (pre_own, pre_m, pre_p, pre_far)
    act_parts = (act_own, act_m, act_p, act_far)
    mlp_parts = (grad_mlp, mlp_minus, mlp_plus, jnp.concatenate(mlp_far, axis=0))
    send = mlp_grad(1, core_index, three_parts, pre_parts, act_parts, mlp_parts)
    back_minus, back_plus, send = lax.optimization_barrier((back_minus, back_plus, send))
    back_minus, back_plus = shift(back_minus, "z", -1), shift(back_plus, "z", 1)
    keep = mlp_grad(
        0, core_index, three_parts, pre_parts, act_parts, (after(grad_mlp, send), *mlp_parts[1:])
    )
    back_minus, back_plus, keep = lax.optimization_barrier((back_minus, back_plus, keep))
    hidden_sum = keep + shift(send, "c", 1)
    grad_after_cross, grad_cross_branch, grad_cross_mixed, sums_three = call(
        third_back_body,
        [
            (core_index, "smem"), (after_cross, "vmem"), (back_own, "vmem"),
            (back_minus, "vmem"), (back_plus, "vmem"), (grad_out, "vmem"),
            (after(row(ln3_gain), hidden_sum), "vmem"), (square_mine, "hbm"), (square_other, "hbm"),
        ],
        [((TOK, D), f32), ((TOK, D), bf16), ((TOK, D), bf16), ((8, D), f32)],
        square_scratch(1),
    )

    grad_cquery_rows, grad_kv = cross_backward(
        text_key[:, None],
        query_caption[None, :],
        cross_query,
        cross_key,
        cross_value,
        grad_cross_mixed,
    )
    kv_own = lax.psum_scatter(grad_kv, FS, scatter_dimension=0, tiled=True)
    grad_after_self, grad_self_branch, grad_attended, sums_two = call(
        second_back_body,
        [
            (core_index, "smem"), (after_self, "vmem"), (grad_cquery_rows, "vmem"),
            (grad_after_cross, "vmem"), (row(ln2_gain), "vmem"),
            (square_mine, "hbm"), (square_other, "hbm"),
        ],
        [((TOK, D), f32), ((TOK, D), bf16), ((TOK, D), bf16), ((8, D), f32)],
        square_scratch(2),
    )
    grad_heads = lax.all_to_all(grad_attended, FS, split_axis=1, concat_axis=0, tiled=True)

    square = jnp.concatenate(
        [
            window_grad(cross_mixed, after(grad_cross_branch, grad_attended)),
            window_grad(normed_two, after(grad_cquery_rows, grad_attended)),
            window_grad(attended, grad_self_branch),
        ],
        axis=1,
    )

    def square_chunk(dy, dx):
        return row_block(square, peer(dy, dx), SHARD)

    grad_heads, square = lax.optimization_barrier((grad_heads, square))
    grad_qkv = self_backward(0, seg_col, seg_row, total0, qkv, grad_heads)
    kv_own, square, grad_qkv = lax.optimization_barrier((kv_own, square, grad_qkv))
    s_lo, s_hi, s20 = reduce_first(square_chunk)
    kv_all = every_peer(kv_own)
    out_minus, out_plus = reduce_z(after(out_far, grad_qkv), out_m, out_p)
    grad_qkv = self_backward(
        1, seg_col, seg_row, total1, qkv, after(grad_heads, kv_own), (grad_qkv,)
    )
    s_lo, s_hi, s20, out_minus, out_plus, grad_qkv = lax.optimization_barrier(
        (s_lo, s_hi, s20, out_minus, out_plus, grad_qkv)
    )
    s11, s31 = reduce_second(square_chunk, s_lo, s_hi)

    heads_own = heads_grad(normed_all, grad_qkv)
    heads_own, s11, s31, kv_all = lax.optimization_barrier((heads_own, s11, s31, kv_all))
    heads_part = peers_parts(heads_own)
    square_parts = reduce_third(square_chunk, s20, s11, s31)
    part, sums_one = first_part(after(grad_qkv, heads_own), heads_w, plain_all)
    part, heads_part, kv_all, *square_parts = lax.optimization_barrier(
        (part, heads_part, kv_all, *square_parts)
    )
    sent = peers_parts(part)

    square = reduce_last(square_chunk, *square_parts).astype(bf16)
    heads_rows = unpack_heads(heads_part)
    early = row_block(heads_rows, core, 216) + shift(row_block(heads_rows, 1 - core, 216), "c", 1)
    early = jnp.concatenate([early, jnp.zeros((256 - 216, D), bf16)], axis=0)
    square = jnp.concatenate([square[:, WIN * k : WIN * (k + 1)] for k in range(3)], axis=0)
    square = jnp.concatenate([square[:216], square[216:]], axis=1)
    early = jnp.concatenate(
        [early, jnp.concatenate([square, jnp.zeros((256 - 216, 2 * WIN), bf16)], axis=0)], axis=1
    )
    early = lax.psum_scatter(early, "z", scatter_dimension=0, tiled=True)
    norms = jnp.concatenate([sums_one[:2], sums_two[:2], sums_three[:2], jnp.zeros((2, D), f32)])
    norms = sum_over(norms, "z", "c")
    own_columns = lax.dynamic_slice_in_dim(context, peer(0, 0) * SHARD, SHARD, axis=1)
    text_part, grad_w_text, grad_w_kv = call(
        text_back_body,
        [
            (core_index, "smem"), (kv_all, "vmem"), (own_columns, "vmem"),
            (text_columns, "vmem"), (w_text, "vmem"),
            (square_mine, "hbm"), (square_other, "hbm"),
        ],
        [((TXT, TXT), bf16), ((TXT, D), bf16), ((SHARD, 2 * D), bf16)],
        square_scratch(2),
    )

    def half(which):
        kv = jnp.where(which == 0, grad_w_kv[:, :D], grad_w_kv[:, D:])
        return jnp.concatenate(
            [row_block(grad_w_text, which, 256), kv, jnp.zeros((448 - 400, D), bf16)], axis=0
        )

    late = half(core) + shift(half(1 - core), "c", 1)
    late = lax.psum_scatter(late, "z", scatter_dimension=0, tiled=True)
    part, norms, late = lax.optimization_barrier((sent, norms, late))
    hidden_parts = peers_parts(after(hidden_sum, part))
    hidden_grad = sum_parts(hidden_parts).astype(bf16)
    hidden_grad = hidden_grad + shift(hidden_grad, "xh", 1)
    early = after(early, part)
    early = early + shift(early, "xh", 1)
    hidden_grad = in_order(*neighbours(hidden_grad))
    grad_w_up, grad_w_down = sort_hidden(core_index, hidden_grad, shift(hidden_grad, "c", 1))

    norms = sum_over(norms, "y", "xl", "xh")
    late = late + shift(late, "xh", 1)
    early = in_order(*neighbours(early))
    late = in_order(*neighbours(late))

    def by_core(x):
        other = shift(x, "c", 1)
        low, high = jnp.where(first_core, x, other), jnp.where(first_core, other, x)
        return low.astype(f32), high.astype(f32)

    low, high = by_core(early)
    grad_w_query = low[:144, :D]
    grad_w_key = jnp.concatenate([low[144:216, :D], high[:72, :D]], axis=0)
    grad_w_value = high[72:216, :D]
    low = jnp.concatenate([low[:216, D : D + WIN], low[:216, D + WIN :]], axis=0)
    high = jnp.concatenate([high[:216, D : D + WIN], high[:216, D + WIN :]], axis=0)
    grad_c_out, grad_c_query, grad_w_out = (
        jnp.concatenate(
            [low[SHARD * k : SHARD * (k + 1)], high[SHARD * k : SHARD * (k + 1), 128:]], axis=1
        )
        for k in range(3)
    )
    low, high = by_core(late)
    grad_w_text = jnp.concatenate([low[:256], high[:256]], axis=0)
    grad_c_key, grad_c_value = low[256:400], high[256:400]
    out_minus, out_plus = shift(out_minus, "z", -1), shift(out_plus, "z", 1)
    outputs = (
        after_cross + out_own.astype(f32) + out_minus.astype(f32) + out_plus.astype(f32)
    )

    grad_tokens = call(
        first_back_body,
        [
            (rows_in, "vmem"), (part, "vmem"), (grad_after_self, "vmem"),
            (row(ln1_gain), "vmem"),
        ],
        [((TOK, D), f32)],
        [],
    )[0]
    grad_text = lax.all_to_all(
        after(text_part, hidden_parts), FS, split_axis=0, concat_axis=1, tiled=True
    )
    grad_text = grad_text[:CAP_TOK].astype(f32)
    return (
        outputs[None],
        grad_tokens[None],
        grad_text[None],
        norms[0],
        norms[1],
        grad_w_query,
        grad_w_key,
        grad_w_value,
        grad_w_out,
        norms[2],
        norms[3],
        grad_c_query,
        grad_w_text,
        grad_c_key,
        grad_c_value,
        grad_c_out,
        norms[4],
        norms[5],
        grad_w_up,
        grad_w_down,
    )


def solution(mesh):
    split = Mesh(mesh.devices.reshape(2, 4, 2, 4, 2), ("xh", "z", "c", "y", "xl"))
    dp = ("xh", "z", "c")
    rows = P(dp, FS, None)
    per_row = P(dp, None)
    weight = P(FS, None)
    rep = P()
    in_specs = (
        rows, rows, per_row, per_row, per_row,
        rep, rep, weight, weight, weight, weight,
        rep, rep, weight, weight, weight, weight, weight,
        rep, rep, weight, weight, rows,
    )
    out_specs = (
        rows, rows, rows,
        rep, rep, weight, weight, weight, weight,
        rep, rep, weight, weight, weight, weight, weight,
        rep, rep, weight, weight,
    )
    return jax.shard_map(
        local, mesh=split, in_specs=in_specs, out_specs=out_specs, check_vma=False
    )
```
